32 devices in a mesh: groups: 2 (over x), seq: 8 (over z, y), tp: 2 (over core).
Axes of the slice: x: 2, y: 2, z: 4, core: 2. Of those that a mesh axis runs over, the one named last changes fastest.
Arguments:
- tokens: bfloat16 [8192, 4096], P(('groups', 'seq')), parts along dimension 0, may hold values from -6 to 6
- gain: float32 [4096], replicated, may hold values from 0.1 to 1.9
- segments: int32 [8192], P(('groups', 'seq')), parts along dimension 0, may hold values from 0 to 3, never falling along the last dimension, each value on 1 to 2048 neighbouring positions
- w_query: bfloat16 [4096, 512], P(None, 'tp')
- w_keyval: bfloat16 [4096, 512], P(None, 'tp')
- w_out: bfloat16 [512, 4096], P('tp'), may hold values from -2.109375 to 2.109375
- sum_exps: int32 [8192, 32], P(('groups', 'seq')), parts along dimension 0, may hold values from -9 to -5
- out_exps: int32 [8192, 32], P(('groups', 'seq')), parts along dimension 0, may hold values from -9 to -5
Outputs:
- mixed: bfloat16 [8192, 4096], P(('groups', 'seq')), parts along dimension 0
The draws below stay inside these ranges and needn't reach their ends.
There are 2 independent parts, one for each index of `groups`. The reference program is written for one: setup_inputs(seed, part) draws one part's arguments, and reference() takes and returns one part's arrays. A program takes and returns all parts, laid end to end along the dimension named above; an argument that names none is the same for every part. Nothing has to cross between parts.
All inputs are finite; a program needn't handle non-finite values.
Results may differ from the reference program's by a relative error of at most 0.007.
The reference program's roundings to bfloat16 on the way count: a program that leaves them out, or rounds other values in their place, can miss the bound.
Values may be sent and summed in bfloat16 or wider, within the bound.
No kernel may reach another device: no remote copies, remote signals or barrier semaphores. Data moves between devices by JAX's collectives and lax.ppermute only.
A program may use at most 128 MiB of HBM per device.

```python
import math
import jax
import jax.numpy as jnp
import numpy as np
from jax import lax

D = 4096
HEADS = 2
HD = 256
TOK_DEV = 512
TOKENS = 4096
N_TP = 2


def query_base(key):
    return jax.random.normal(key, (D, HEADS * HD), jnp.float32)


def draw_w_query(key, part):
    shared = query_base(key)
    return (shared * D ** (-0.5)).astype(jnp.bfloat16)


def draw_w_keyval(key, part):
    key = jax.random.fold_in(key, 7)
    fresh = jax.random.normal(key, (D, 2 * HD), jnp.float32) * D ** (-0.5)
    return fresh.astype(jnp.bfloat16)


def set_ends(entries, rng, smallest, top_value):
    dims = entries.shape
    spot = [jax.random.randint(jax.random.fold_in(rng, axis), (), 0, dims[axis]) for axis in range(len(dims))]
    entries = entries.at[tuple(spot)].set(smallest)
    longest = dims.index(max(dims))
    spot[longest] = (spot[longest] + 1) % dims[longest]
    return entries.at[tuple(spot)].set(top_value)


def block_levels(own_key, extent, cuts, smallest, high):
    factor_of, own = 1.0, jax.random.fold_in(own_key, 6)
    for position, shards_of in cuts:
        heights = jnp.exp(jax.random.uniform(jax.random.fold_in(own, position), (shards_of,), jnp.float32, smallest / len(cuts), high / len(cuts)))
        factor_of = factor_of * jnp.repeat(heights, extent[position] // shards_of).reshape([-1 if axis == position else 1 for axis in range(len(extent))])
    return factor_of


def length_profile(count, total, most, skew):
    portions = [(1 << 20) // math.isqrt(rank ** skew) + 1 for rank in range(2, count + 1)]
    surplus, given = total - most - (count - 1), [1] * (count - 1)
    while surplus > 0:
        free = [i for i in range(count - 1) if given[i] < most]
        mass, left = sum([portions[i] for i in free]), surplus
        for i in free:
            extra = min(most - given[i], max(1, left * portions[i] // mass), surplus)
            given[i] = given[i] + extra
            surplus = surplus - extra
    return np.array([most] + given)


def uneven_parts(stream_key, count, total, reach, skew):
    if count == 2:
        one = jax.random.randint(stream_key, (), max(1, total - reach), min(reach, total - 1) + 1)
        return jnp.stack([one, total - one])
    lengths = jnp.asarray(length_profile(count, total, reach, skew), jnp.int32)
    couples = (count - 1) // 2
    source_of, sink = lengths[1:1 + 2 * couples:2], lengths[2:2 + 2 * couples:2]
    slack = jnp.minimum(source_of - 1, reach - sink)
    moved = jax.random.randint(jax.random.fold_in(stream_key, 1), (couples,), 0, 1 << 20) % (slack + 1)
    lengths = lengths.at[1:1 + 2 * couples:2].set(source_of - moved).at[2:2 + 2 * couples:2].set(sink + moved)
    return lengths[jax.random.permutation(jax.random.fold_in(stream_key, 2), count)]


def gaussian(own_key, extent, deviation, bound, pieces=(), kind=jnp.bfloat16):
    drawn = jax.random.normal(own_key, extent, jnp.float32) * deviation
    if len(pieces) > 0:
        drawn = block_levels(own_key, extent, pieces, -0.22, 0.18) * drawn
    return jnp.clip(drawn, min=-bound, max=bound).astype(kind)


def setup_inputs(seed: int = 0, part: int = 0) -> dict:
    streams_of = jax.random.split(jax.random.key(seed), 9)
    part_splits = jax.random.split(jax.random.fold_in(streams_of[8], part), 9)
    return {
        "tokens": gaussian(part_splits[0], (TOKENS, D), 1.0, 6.0, ((0, 8),)),
        "gain": jnp.clip(1.0 + 0.18 * jax.random.normal(streams_of[1], (D,), jnp.float32), 0.1, 1.9),
        "segments": jnp.searchsorted(jnp.cumsum(uneven_parts(part_splits[2], 4, TOKENS, TOKENS // 2, 0)), jnp.arange(TOKENS), side="right").astype(jnp.int32),
        "w_query": draw_w_query(jax.random.fold_in(streams_of[8], 71), part),
        "w_keyval": draw_w_keyval(jax.random.fold_in(streams_of[8], 71), part),
        "w_out": gaussian(streams_of[5], (HEADS * HD, D), (8.0 * (HEADS * HD) ** -0.5), 2.109375, ((0, 2),)),
        "sum_exps": set_ends(jax.random.randint(part_splits[6], (TOKENS, D // 128), -9, -4), jax.random.fold_in(part_splits[6], 1), -9, (-4) - 1).astype(jnp.int32),
        "out_exps": set_ends(jax.random.randint(part_splits[7], (TOKENS, D // 128), -9, -4), jax.random.fold_in(part_splits[7], 1), -9, (-4) - 1).astype(jnp.int32),
    }


def reference(tokens, gain, segments, w_query, w_keyval, w_out, sum_exps, out_exps):
    wide_tokens = tokens.astype(jnp.float32)
    center = wide_tokens - lax.optimization_barrier(jnp.mean(wide_tokens, axis=1, keepdims=True))
    spread = lax.optimization_barrier(jnp.mean(center * center, axis=1, keepdims=True))
    normed = (center * lax.rsqrt(spread + 1e-05) * gain).astype(jnp.bfloat16)
    query = jnp.dot(normed, w_query, preferred_element_type=jnp.float32).astype(jnp.bfloat16)
    keyval = jnp.dot(normed, w_keyval, preferred_element_type=jnp.float32).astype(jnp.bfloat16)
    key_rows = keyval[:, :HD].astype(jnp.float32)
    value_rows = keyval[:, HD:].astype(jnp.float32)
    positions = jnp.arange(TOKENS, dtype=jnp.int32)
    factor = HD ** (-0.5)

    def attend(index):
        start = (index * TOK_DEV).astype(jnp.int32)
        query_block = lax.dynamic_slice_in_dim(query, start, TOK_DEV, 0).astype(jnp.float32).reshape(TOK_DEV, HEADS, HD)
        query_seg = lax.dynamic_slice_in_dim(segments, start, TOK_DEV, 0)
        query_pos = start + jnp.arange(TOK_DEV, dtype=jnp.int32)
        scores = jnp.einsum('qhd,kd->hqk', query_block, key_rows) * factor
        allowed = ((query_seg[:, None] == segments[None, :]) & (positions[None, :] <= query_pos[:, None]))[None]
        top = lax.optimization_barrier(jnp.max(jnp.where(allowed, scores, -1e+30), axis=2, keepdims=True))
        weights = jnp.where(allowed, jnp.exp(scores - top), 0.0)
        total = lax.optimization_barrier(jnp.sum(weights, axis=2))
        probs = lax.optimization_barrier(weights.astype(jnp.bfloat16)).astype(jnp.float32)
        summed = jnp.einsum('hqk,kd->qhd', probs, value_rows)
        return (summed / jnp.transpose(total)[:, :, None]).astype(jnp.bfloat16)
    blocks = lax.map(attend, jnp.arange(TOKENS // TOK_DEV, dtype=jnp.int32))
    attended = blocks.reshape(TOKENS, HEADS * HD)
    sum_scale = jnp.repeat(jnp.exp2(sum_exps.astype(jnp.float32)), 128, axis=1)
    out_scale = jnp.repeat(jnp.exp2(out_exps.astype(jnp.float32)), 128, axis=1)
    head_cols = HEADS * HD // N_TP
    accumulated = jnp.zeros((TOKENS, D), jnp.float32)
    for member in range(N_TP):
        heads_part = attended[:, member * head_cols:(member + 1) * head_cols]
        term = jnp.dot(heads_part, w_out[member * head_cols:(member + 1) * head_cols], preferred_element_type=jnp.float32)
        quant = jnp.clip(term / sum_scale, -448.0, 448.0).astype(jnp.bfloat16)
        accumulated = accumulated + quant.astype(jnp.float32)
    combined = wide_tokens + sum_scale * accumulated
    coded = lax.optimization_barrier(jnp.clip(combined / out_scale, -448.0, 448.0).astype(jnp.bfloat16))
    return (coded.astype(jnp.float32) * out_scale).astype(jnp.bfloat16)
```

```python
import functools

import jax
import jax.numpy as jnp
from jax import lax
from jax.experimental import pallas as pl
from jax.experimental.pallas import tpu as pltpu
from jax.sharding import PartitionSpec as P

HD = 256
LANES = 128
SEG_ROWS = 16
LIMIT = 448.0
MIN_EXP = -9
NEG = -1e30
VMEM_BYTES = 56 * 1024 * 1024
NT = (((1,), (1,)), ((), ()))


def norm_kv_kernel(x_ref, gain_ref, w_ref, seg_ref, msg_ref, normed_ref):
    step = pl.program_id(0)
    rows = x_ref.shape[0]
    count = msg_ref.shape[0] - SEG_ROWS
    x = x_ref[...].astype(jnp.float32)
    center = x - jnp.mean(x, axis=1, keepdims=True)
    spread = jnp.mean(center * center, axis=1, keepdims=True)
    normed = (center * lax.rsqrt(spread + 1e-05) * gain_ref[...]).astype(jnp.bfloat16)
    normed_ref[...] = normed
    kv = jnp.dot(normed, w_ref[...], preferred_element_type=jnp.float32)
    msg_ref[pl.ds(pl.multiple_of(step * rows, rows), rows), :] = kv.astype(jnp.bfloat16)

    @pl.when(step == 0)
    def _():
        seg = seg_ref[...].astype(jnp.float32)
        low = jnp.broadcast_to(seg[:, :HD], (8, HD))
        high = jnp.broadcast_to(seg[:, HD:], (8, HD))
        msg_ref[pl.ds(count, SEG_ROWS), :] = jnp.concatenate([low, high], axis=0).astype(jnp.bfloat16)


def norm_kv(tokens, gain, w_keyval, segments, tile):
    rows, width = tokens.shape
    cols = w_keyval.shape[1]
    return pl.pallas_call(
        norm_kv_kernel,
        grid=(rows // tile,),
        in_specs=[
            pl.BlockSpec((tile, width), lambda i: (i, 0)),
            pl.BlockSpec((1, width), lambda i: (0, 0)),
            pl.BlockSpec((width, cols), lambda i: (0, 0)),
            pl.BlockSpec((1, rows), lambda i: (0, 0)),
        ],
        out_specs=[
            pl.BlockSpec((rows + SEG_ROWS, cols), lambda i: (0, 0)),
            pl.BlockSpec((tile, width), lambda i: (i, 0)),
        ],
        out_shape=[
            jax.ShapeDtypeStruct((rows + SEG_ROWS, cols), jnp.bfloat16),
            jax.ShapeDtypeStruct((rows, width), jnp.bfloat16),
        ],
        compiler_params=pltpu.CompilerParams(vmem_limit_bytes=VMEM_BYTES),
        cost_estimate=pl.CostEstimate(
            flops=2 * rows * width * cols + 10 * rows * width, bytes_accessed=4 * rows * width + 2 * width * cols, transcendentals=rows
        ),
        name="norm_kv",
    )(tokens, gain.reshape(1, width), w_keyval, segments.reshape(1, rows))


def query_kernel(x_ref, w_ref, out_ref):
    out_ref[...] = jnp.dot(x_ref[...], w_ref[...], preferred_element_type=jnp.float32).astype(jnp.bfloat16)


def project_query(normed, w_query):
    rows, width = normed.shape
    cols = w_query.shape[1]
    tile = rows // 2
    return pl.pallas_call(
        query_kernel,
        grid=(rows // tile,),
        in_specs=[pl.BlockSpec((tile, width), lambda i: (i, 0)), pl.BlockSpec((width, cols), lambda i: (0, 0))],
        out_specs=pl.BlockSpec((tile, cols), lambda i: (i, 0)),
        out_shape=jax.ShapeDtypeStruct((rows, cols), jnp.bfloat16),
        compiler_params=pltpu.CompilerParams(vmem_limit_bytes=VMEM_BYTES),
        cost_estimate=pl.CostEstimate(
            flops=2 * rows * width * cols, bytes_accessed=2 * rows * width + 2 * width * cols, transcendentals=0
        ),
        name="project_query",
    )(normed, w_query)


def attend_kernel(count, blocks, q_ref, seg_ref, *refs):
    mine, other = refs[:blocks + 1], refs[blocks + 1:2 * blocks + 2]
    out_ref, keys, values, segs, scores, sems = refs[2 * blocks + 2:]
    rows = q_ref.shape[0]
    part = lax.axis_index("tp")
    place = lax.axis_index("seq")
    odd = lax.rem(place, 2)

    def pieces(here, there, slot):
        return (
            (here.at[pl.ds(0, rows)], keys.at[slot], there.at[pl.ds(0, rows)], values.at[slot]),
            (there.at[pl.ds(0, rows)], keys.at[slot], here.at[pl.ds(0, rows)], values.at[slot]),
        )

    def fetch(here, there, slot):
        for value, (key_src, key_dst, val_src, val_dst) in enumerate(pieces(here, there, slot)):
            @pl.when(part == value)
            def _():
                pltpu.make_async_copy(key_src, key_dst, sems.at[0, slot]).start()
                pltpu.make_async_copy(val_src, val_dst, sems.at[1, slot]).start()

        pltpu.make_async_copy(here.at[pl.ds(rows, SEG_ROWS)], segs.at[slot], sems.at[2, slot]).start()

    for slot in range(blocks - 1):
        fetch(mine[slot], other[slot], slot)
    for value in range(2):
        @pl.when(odd == 1 - value)
        def _():
            fetch(mine[blocks - 1 + value], other[blocks - 1 + value], blocks - 1)

    evens = blocks // 2
    back = [0] + [2 * k for k in range(1, evens + 1)]
    back += [2 * k - 1 + 2 * odd for k in range(1, evens)] + [(2 * evens - 1) - (2 * evens - 2) * odd]
    wide = jnp.broadcast_to(seg_ref[...].astype(jnp.float32), (8, rows))
    own_seg = jnp.transpose(wide)[:, 0:1]
    top = jnp.full((rows, 1), NEG, jnp.float32)
    for slot in range(blocks):
        pltpu.make_async_copy(mine[0].at[pl.ds(0, rows)], keys.at[slot], sems.at[0, slot]).wait()
        pltpu.make_async_copy(mine[0].at[pl.ds(0, rows)], values.at[slot], sems.at[1, slot]).wait()
        pltpu.make_async_copy(mine[0].at[pl.ds(rows, SEG_ROWS)], segs.at[slot], sems.at[2, slot]).wait()
        raw = lax.dot_general(q_ref[...], keys[slot], NT, preferred_element_type=jnp.float32)
        packed = segs[slot].astype(jnp.float32)
        key_seg = jnp.concatenate([packed[0:1, :], packed[8:9, :]], axis=1)
        if slot == 0:
            row_pos = lax.broadcasted_iota(jnp.int32, (rows, rows), 0)
            col_pos = lax.broadcasted_iota(jnp.int32, (rows, rows), 1)
            allowed = (key_seg == own_seg) & (col_pos <= row_pos)
        else:
            key_seg = jnp.where(place >= back[slot], key_seg, -1.0)
            allowed = key_seg == own_seg
        masked = jnp.where(allowed, raw, NEG)
        scores[slot] = masked
        top = jnp.maximum(top, jnp.max(masked, axis=1, keepdims=True))
    factor = HD ** (-0.5) * 1.4426950408889634
    total = jnp.zeros((rows, 1), jnp.float32)
    weighted = jnp.zeros((rows, HD), jnp.float32)
    for slot in range(blocks):
        weights = jnp.exp2((scores[slot] - top) * factor)
        total = total + jnp.sum(weights, axis=1, keepdims=True)
        weighted = weighted + jnp.dot(weights.astype(jnp.bfloat16), values[slot], preferred_element_type=jnp.float32)
    out_ref[...] = (weighted / total).astype(jnp.bfloat16)


def attend(query, segments, mine, other, blocks):
    rows = query.shape[0]
    operands = 2 * (blocks + 1)
    return pl.pallas_call(
        functools.partial(attend_kernel, rows, blocks),
        in_specs=[pl.BlockSpec(memory_space=pltpu.VMEM)] * 2 + [pl.BlockSpec(memory_space=pl.ANY)] * operands,
        out_specs=pl.BlockSpec(memory_space=pltpu.VMEM),
        out_shape=jax.ShapeDtypeStruct((rows, HD), jnp.bfloat16),
        scratch_shapes=[
            pltpu.VMEM((blocks, rows, HD), jnp.bfloat16),
            pltpu.VMEM((blocks, rows, HD), jnp.bfloat16),
            pltpu.VMEM((blocks, SEG_ROWS, HD), jnp.bfloat16),
            pltpu.VMEM((blocks, rows, rows), jnp.float32),
            pltpu.SemaphoreType.DMA((3, blocks)),
        ],
        compiler_params=pltpu.CompilerParams(vmem_limit_bytes=VMEM_BYTES),
        cost_estimate=pl.CostEstimate(
            flops=4 * rows * rows * blocks * HD, bytes_accessed=4 * rows * blocks * HD, transcendentals=rows * rows * blocks
        ),
        name="attend",
    )(query, segments.reshape(1, rows), *mine, *other)


def output_kernel(a_ref, b_ref, wa_ref, wb_ref, x_ref, sum_ref, out_exp_ref, out_ref):
    width = x_ref.shape[1]
    groups = sum_ref.shape[0]

    def bounds(ref):
        power = jnp.left_shift(jnp.int32(1), ref[...] - MIN_EXP).astype(jnp.float32)
        return jnp.transpose(power * (LIMIT * 2.0 ** MIN_EXP))

    sum_bound, out_bound = bounds(sum_ref), bounds(out_exp_ref)
    per = width // groups
    chunk = 2 * per
    a, b = a_ref[...], b_ref[...]
    for start in range(0, width, chunk):
        term_a = jnp.dot(a, wa_ref[:, start:start + chunk], preferred_element_type=jnp.float32)
        term_b = jnp.dot(b, wb_ref[:, start:start + chunk], preferred_element_type=jnp.float32)
        for part in range(2):
            cols = slice(part * per, (part + 1) * per)
            group = (start + part * per) // per
            bound = sum_bound[:, group:group + 1]
            quant_a = jnp.clip(term_a[:, cols], -bound, bound).astype(jnp.bfloat16).astype(jnp.float32)
            quant_b = jnp.clip(term_b[:, cols], -bound, bound).astype(jnp.bfloat16).astype(jnp.float32)
            span = slice(start + part * per, start + (part + 1) * per)
            combined = x_ref[:, span].astype(jnp.float32) + (quant_a + quant_b)
            last = out_bound[:, group:group + 1]
            out_ref[:, span] = jnp.clip(combined, -last, last).astype(jnp.bfloat16)


def project_out(att_a, att_b, w_a, w_b, tokens, sum_exps, out_exps):
    rows, width = tokens.shape
    depth = att_a.shape[1]
    groups = sum_exps.shape[1]
    steps = groups // 8
    tile = width // steps
    whole = pl.BlockSpec((rows, depth), lambda i: (0, 0))
    weight = pl.BlockSpec((depth, tile), lambda i: (0, i))
    wide = pl.BlockSpec((rows, tile), lambda i: (0, i))
    exps = pl.BlockSpec((groups // steps, rows), lambda i: (i, 0))
    return pl.pallas_call(
        output_kernel,
        grid=(steps,),
        in_specs=[whole, whole, weight, weight, wide, exps, exps],
        out_specs=wide,
        out_shape=jax.ShapeDtypeStruct((rows, width), jnp.bfloat16),
        compiler_params=pltpu.CompilerParams(vmem_limit_bytes=VMEM_BYTES),
        cost_estimate=pl.CostEstimate(
            flops=4 * rows * width * depth, bytes_accessed=4 * rows * width + 4 * width * depth, transcendentals=0
        ),
        name="project_out",
    )(att_a, att_b, w_a, w_b, tokens, sum_exps.T, out_exps.T)


def on_device(seq_size, tokens, gain, segments, w_query, w_keyval, w_out, sum_exps, out_exps):
    window = seq_size // 2
    ahead = [(i, i + 2) for i in range(seq_size - 2)]
    across = [(i, i ^ 1) for i in range(seq_size)]
    to_odd = [(i, i + 1) for i in range(0, seq_size, 2)]
    to_even = [(i + 1, i) for i in range(0, seq_size, 2)]

    def swap(x):
        return lax.ppermute(x, "tp", [(0, 1), (1, 0)])

    w_other = swap(w_out)
    message, normed = norm_kv(tokens, gain, w_keyval, segments, 128)
    evens, odds = [], []
    held = message
    pair = lax.ppermute(message, "seq", to_odd)
    for k in range(window // 2):
        held = lax.ppermute(held, "seq", ahead)
        evens.append(held)
        if k < window // 2 - 1:
            odds.append(lax.ppermute(held, "seq", across))
    far = lax.ppermute(held, "seq", to_even)
    mine = [message] + evens + odds + [pair, far]
    other = [swap(m) for m in mine]
    query = project_query(normed, w_query)
    attended = attend(query, segments, mine, other, window + 1)
    return project_out(attended, swap(attended), w_out, w_other, tokens, sum_exps, out_exps)


def solution(mesh):
    in_specs = (
        P(("groups", "seq"), None),
        P(),
        P(("groups", "seq")),
        P(None, "tp"),
        P(None, "tp"),
        P("tp", None),
        P(("groups", "seq"), None),
        P(("groups", "seq"), None),
    )
    out_specs = P(("groups", "seq"), None)
    return jax.shard_map(
        functools.partial(on_device, mesh.shape["seq"]),
        mesh=mesh, in_specs=in_specs, out_specs=out_specs, check_vma=False,
    )
```

```python
import functools

import jax
import jax.numpy as jnp
from jax import lax
from jax.experimental import pallas as pl
from jax.experimental.pallas import tpu as pltpu
from jax.sharding import PartitionSpec as P

HD = 256
LANES = 128
SEG_ROWS = 16
LIMIT = 448.0
MIN_EXP = -9
NEG = -1e30
MIB = 1024 * 1024
NT = (((1,), (1,)), ((), ()))
FACTOR = HD ** (-0.5) * 1.4426950408889634


def norm_kv_kernel(x_ref, gain_ref, w_ref, seg_ref, msg_ref, normed_ref):
    step = pl.program_id(0)
    rows, width = x_ref.shape
    count = msg_ref.shape[0] - SEG_ROWS

    def wide(start):
        return x_ref[:, start:start + LANES].astype(jnp.float32)

    total = wide(0)
    for start in range(LANES, width, LANES):
        total = total + wide(start)
    mean = jnp.broadcast_to(jnp.sum(total, axis=1, keepdims=True) * (1.0 / width), (rows, LANES))
    square = jnp.zeros((rows, LANES), jnp.float32)
    for start in range(0, width, LANES):
        center = wide(start) - mean
        square = square + center * center
    spread = jnp.sum(square, axis=1, keepdims=True) * (1.0 / width)
    scale = jnp.broadcast_to(lax.rsqrt(spread + 1e-05), (rows, LANES))
    kv = jnp.zeros((rows, w_ref.shape[1]), jnp.float32)
    for start in range(0, width, HD):
        for at in (start, start + LANES):
            normed = (wide(at) - mean) * scale * gain_ref[:, at:at + LANES]
            normed_ref[:, at:at + LANES] = normed.astype(jnp.bfloat16)
        kv = kv + jnp.dot(
            normed_ref[:, start:start + HD], w_ref[start:start + HD, :], preferred_element_type=jnp.float32
        )
    msg_ref[pl.ds(pl.multiple_of(step * rows, rows), rows), :] = kv.astype(jnp.bfloat16)

    @pl.when(step == 0)
    def _():
        seg = seg_ref[...].astype(jnp.float32)
        low = jnp.broadcast_to(seg[:, :HD], (8, HD))
        high = jnp.broadcast_to(seg[:, HD:], (8, HD))
        msg_ref[pl.ds(count, SEG_ROWS), :] = jnp.concatenate([low, high], axis=0).astype(jnp.bfloat16)


def norm_kv(tokens, gain, w_keyval, segments, tile):
    rows, width = tokens.shape
    cols = w_keyval.shape[1]
    return pl.pallas_call(
        norm_kv_kernel,
        grid=(rows // tile,),
        in_specs=[
            pl.BlockSpec((tile, width), lambda i: (i, 0)),
            pl.BlockSpec((1, width), lambda i: (0, 0)),
            pl.BlockSpec((width, cols), lambda i: (0, 0)),
            pl.BlockSpec((1, rows), lambda i: (0, 0)),
        ],
        out_specs=[
            pl.BlockSpec((rows + SEG_ROWS, cols), lambda i: (0, 0)),
            pl.BlockSpec((tile, width), lambda i: (i, 0)),
        ],
        out_shape=[
            jax.ShapeDtypeStruct((rows + SEG_ROWS, cols), jnp.bfloat16),
            jax.ShapeDtypeStruct((rows, width), jnp.bfloat16),
        ],
        compiler_params=pltpu.CompilerParams(vmem_limit_bytes=24 * MIB),
        cost_estimate=pl.CostEstimate(
            flops=2 * rows * width * cols, bytes_accessed=4 * rows * width + 2 * width * cols, transcendentals=0
        ),
        name="norm_kv",
    )(tokens, gain.reshape(1, width), w_keyval, segments.reshape(1, rows))


def turn():
    return lax.rem(lax.div(lax.axis_index("seq"), 2), 2)


def query_kernel(x_ref, w_ref, out_ref, turn_ref):
    out_ref[...] = jnp.dot(x_ref[...], w_ref[...], preferred_element_type=jnp.float32).astype(jnp.bfloat16)
    turn_ref[...] = jnp.full(turn_ref.shape, turn(), jnp.int32)


def project_query(normed, w_query):
    rows, width = normed.shape
    cols = w_query.shape[1]
    tile = rows // 2
    return pl.pallas_call(
        query_kernel,
        grid=(rows // tile,),
        in_specs=[pl.BlockSpec((tile, width), lambda i: (i, 0)), pl.BlockSpec((width, cols), lambda i: (0, 0))],
        out_specs=[pl.BlockSpec((tile, cols), lambda i: (i, 0)), pl.BlockSpec((8, LANES), lambda i: (0, 0))],
        out_shape=[jax.ShapeDtypeStruct((rows, cols), jnp.bfloat16), jax.ShapeDtypeStruct((8, LANES), jnp.int32)],
        compiler_params=pltpu.CompilerParams(vmem_limit_bytes=20 * MIB),
        cost_estimate=pl.CostEstimate(
            flops=2 * rows * width * cols, bytes_accessed=2 * rows * width + 2 * width * cols, transcendentals=0
        ),
        name="project_query",
    )(normed, w_query)


def attend_kernel(plan, first, last, *refs):
    blocks = len(plan)
    q_ref, seg_ref = refs[:2]
    mine, other = refs[2:2 + blocks], refs[2 + blocks:2 + 2 * blocks]
    refs = refs[2 + 2 * blocks:]
    state_ref = None
    if not first:
        state_ref, refs = refs[0], refs[1:]
    out_ref, refs = refs[0], refs[1:]
    if not last:
        turn_ref, refs = refs[0], refs[1:]
        turn_ref[...] = jnp.full(turn_ref.shape, turn(), jnp.int32)
    keys, values, segs, scores, sems = refs
    rows = q_ref.shape[0]
    tile = rows // 2
    part = lax.axis_index("tp")
    place = lax.axis_index("seq")
    odd = lax.rem(place, 2)

    for slot in range(blocks):
        for value in range(2):
            key_src, val_src = (mine[slot], other[slot]) if value == 0 else (other[slot], mine[slot])

            @pl.when(part == value)
            def _():
                pltpu.make_async_copy(key_src.at[pl.ds(0, rows)], keys.at[slot], sems.at[0, slot]).start()
                pltpu.make_async_copy(val_src.at[pl.ds(0, rows)], values.at[slot], sems.at[1, slot]).start()

        pltpu.make_async_copy(mine[slot].at[pl.ds(rows, SEG_ROWS)], segs.at[slot], sems.at[2, slot]).start()

    own_seg = jnp.transpose(jnp.broadcast_to(seg_ref[...].astype(jnp.float32), (8, rows)))[:, 0:1]
    for slot in range(blocks):
        pltpu.make_async_copy(mine[slot].at[pl.ds(0, rows)], keys.at[slot], sems.at[0, slot]).wait()
        pltpu.make_async_copy(mine[slot].at[pl.ds(0, rows)], values.at[slot], sems.at[1, slot]).wait()
        pltpu.make_async_copy(mine[slot].at[pl.ds(rows, SEG_ROWS)], segs.at[slot], sems.at[2, slot]).wait()
    key_segs = []
    for slot, kind in enumerate(plan):
        packed = segs[slot].astype(jnp.float32)
        key_seg = jnp.concatenate([packed[0:1, :], packed[8:9, :]], axis=1)
        if kind != "own":
            back = jnp.where(odd == 1, kind[1], kind[0])
            key_seg = jnp.where((back > 0) & (place >= back), key_seg, -1.0)
        key_segs.append(key_seg)

    for start in range(0, rows, tile):
        span = slice(start, start + tile)
        query = q_ref[span, :]
        best = None if first else state_ref[span, HD:HD + LANES]
        bounds = []
        for slot, kind in enumerate(plan):
            low, high = 0, rows
            if kind == "own":
                high = start + tile
            elif kind[2]:
                low = start
            bounds.append((low, high))
            raw = lax.dot_general(query, keys[slot, low:high, :], NT, preferred_element_type=jnp.float32)
            allowed = key_segs[slot][:, low:high] == own_seg[span, :]
            if kind == "own":
                row_pos = start + lax.broadcasted_iota(jnp.int32, raw.shape, 0)
                allowed = allowed & (lax.broadcasted_iota(jnp.int32, raw.shape, 1) <= row_pos)
            masked = jnp.where(allowed, raw, NEG)
            scores[slot, :, low:high] = masked
            for at in range(0, high - low, LANES):
                piece = masked[:, at:at + LANES]
                best = piece if best is None else jnp.maximum(best, piece)
        top = jnp.broadcast_to(jnp.max(best, axis=1, keepdims=True), (tile, LANES))
        if first:
            total = jnp.zeros((tile, LANES), jnp.float32)
            weighted = jnp.zeros((tile, HD), jnp.float32)
        else:
            shrink = jnp.exp2((state_ref[span, HD:HD + LANES] - top) * FACTOR)
            total = state_ref[span, HD + LANES:] * shrink
            weighted = state_ref[span, :HD] * jnp.concatenate([shrink, shrink], axis=1)
        for slot in range(blocks):
            low, high = bounds[slot]
            pieces = []
            for at in range(low, high, LANES):
                weights = jnp.exp2((scores[slot, :, at:at + LANES] - top) * FACTOR)
                total = total + weights
                pieces.append(weights.astype(jnp.bfloat16))
            probs = jnp.concatenate(pieces, axis=1)
            weighted = weighted + jnp.dot(probs, values[slot, low:high, :], preferred_element_type=jnp.float32)
        if last:
            out_ref[span, :] = (weighted / jnp.sum(total, axis=1, keepdims=True)).astype(jnp.bfloat16)
        else:
            out_ref[span, :HD] = weighted
            out_ref[span, HD:HD + LANES] = top
            out_ref[span, HD + LANES:] = total


def attend(query, segments, plan, mine, other, state, last):
    rows = query.shape[0]
    blocks = len(plan)
    vmem = pl.BlockSpec(memory_space=pltpu.VMEM)
    first = state is None
    operands = [query, segments.reshape(1, rows), *mine, *other] + ([] if first else [state])
    if last:
        out_shape = jax.ShapeDtypeStruct((rows, HD), jnp.bfloat16)
        out_specs = vmem
    else:
        out_shape = [
            jax.ShapeDtypeStruct((rows, HD + 2 * LANES), jnp.float32),
            jax.ShapeDtypeStruct((8, LANES), jnp.int32),
        ]
        out_specs = [vmem, vmem]
    return pl.pallas_call(
        functools.partial(attend_kernel, plan, first, last),
        in_specs=[vmem] * 2 + [pl.BlockSpec(memory_space=pl.ANY)] * (2 * blocks) + ([] if first else [vmem]),
        out_specs=out_specs,
        out_shape=out_shape,
        scratch_shapes=[
            pltpu.VMEM((blocks, rows, HD), jnp.bfloat16),
            pltpu.VMEM((blocks, rows, HD), jnp.bfloat16),
            pltpu.VMEM((blocks, SEG_ROWS, HD), jnp.bfloat16),
            pltpu.VMEM((blocks, rows // 2, rows), jnp.float32),
            pltpu.SemaphoreType.DMA((3, blocks)),
        ],
        compiler_params=pltpu.CompilerParams(vmem_limit_bytes=(12 + 2 * blocks) * MIB),
        cost_estimate=pl.CostEstimate(
            flops=4 * rows * rows * blocks * HD, bytes_accessed=4 * rows * blocks * HD, transcendentals=rows * rows * blocks
        ),
        name="attend_last" if last else "attend_first" if first else "attend_more",
    )(*operands)


def output_kernel(a_ref, b_ref, wa_ref, wb_ref, x_ref, sum_ref, out_exp_ref, out_ref):
    rows, width = x_ref.shape
    groups = sum_ref.shape[0]

    def bounds(ref):
        power = jnp.left_shift(jnp.int32(1), ref[...] - MIN_EXP).astype(jnp.float32)
        return jnp.transpose(power * (LIMIT * 2.0 ** MIN_EXP))

    def clip(value, bound):
        return jnp.minimum(jnp.maximum(value.astype(jnp.bfloat16), -bound), bound)

    sum_bound, out_bound = bounds(sum_ref), bounds(out_exp_ref)
    per = width // groups
    chunk = 2 * per
    a, b = a_ref[...], b_ref[...]
    for start in range(0, width, chunk):
        term_a = jnp.dot(a, wa_ref[:, start:start + chunk], preferred_element_type=jnp.float32)
        term_b = jnp.dot(b, wb_ref[:, start:start + chunk], preferred_element_type=jnp.float32)
        for part in range(2):
            cols = slice(part * per, (part + 1) * per)
            group = (start + part * per) // per
            span = slice(start + part * per, start + (part + 1) * per)
            bound = jnp.broadcast_to(sum_bound[:, group:group + 1], (rows, per)).astype(jnp.bfloat16)
            last = jnp.broadcast_to(out_bound[:, group:group + 1], (rows, per)).astype(jnp.bfloat16)
            quant_a = clip(term_a[:, cols], bound).astype(jnp.float32)
            quant_b = clip(term_b[:, cols], bound).astype(jnp.float32)
            combined = x_ref[:, span].astype(jnp.float32) + (quant_a + quant_b)
            out_ref[:, span] = clip(combined, last)


def project_out(att_a, att_b, w_a, w_b, tokens, sum_exps, out_exps):
    rows, width = tokens.shape
    depth = att_a.shape[1]
    groups = sum_exps.shape[1]
    steps = groups // 8
    tile = width // steps
    whole = pl.BlockSpec((rows, depth), lambda i: (0, 0))
    weight = pl.BlockSpec((depth, tile), lambda i: (0, i))
    wide = pl.BlockSpec((rows, tile), lambda i: (0, i))
    exps = pl.BlockSpec((groups // steps, rows), lambda i: (i, 0))
    return pl.pallas_call(
        output_kernel,
        grid=(steps,),
        in_specs=[whole, whole, weight, weight, wide, exps, exps],
        out_specs=wide,
        out_shape=jax.ShapeDtypeStruct((rows, width), jnp.bfloat16),
        compiler_params=pltpu.CompilerParams(vmem_limit_bytes=20 * MIB),
        cost_estimate=pl.CostEstimate(
            flops=4 * rows * width * depth, bytes_accessed=4 * rows * width + 4 * width * depth, transcendentals=0
        ),
        name="project_out",
    )(att_a, att_b, w_a, w_b, tokens, sum_exps.T, out_exps.T)


def on_device(seq_size, tokens, gain, segments, w_query, w_keyval, w_out, sum_exps, out_exps):
    window = seq_size // 2

    def swap_cores(x):
        return lax.ppermute(x, "tp", [(0, 1), (1, 0)])

    def swap_pair(x):
        return lax.ppermute(x, "seq", [(i, i ^ 1) for i in range(seq_size)])

    def exchange(x, colour):
        low = [i for i in range(seq_size - 2) if (i // 2) % 2 == colour]
        return lax.ppermute(x, "seq", [(i, i + 2) for i in low] + [(i + 2, i) for i in low])

    def pick(flag, if_odd, if_even):
        return jnp.where(flag[:1, :1] == 1, if_odd, if_even)

    w_other = swap_cores(w_out)
    message, normed = norm_kv(tokens, gain, w_keyval, segments, 256)
    at_odd, at_even = exchange(message, 0), exchange(message, 1)
    pair = swap_pair(message)
    query, flag = project_query(normed, w_query)
    state = None
    mine, plan = [message, pair], ["own", (0, 1, False)]
    for k in range(1, window // 2 + 1):
        held = pick(flag, at_odd, at_even)
        mine.append(held)
        plan.append((2 * k, 2 * k, 2 * k == window))
        if k < window // 2:
            at_odd, at_even = exchange(at_even, 0), exchange(at_odd, 1)
        beside = swap_pair(held)
        if k == 1 or k == window // 2:
            state, flag = attend(query, segments, plan, mine, [swap_cores(m) for m in mine], state, False)
            mine, plan = [], []
        mine.append(beside)
        plan.append((2 * k - 1, 2 * k + 1 if k < window // 2 else 0, False))
    attended = attend(query, segments, plan, mine, [swap_cores(m) for m in mine], state, True)
    return project_out(attended, swap_cores(attended), w_out, w_other, tokens, sum_exps, out_exps)


def solution(mesh):
    in_specs = (
        P(("groups", "seq"), None),
        P(),
        P(("groups", "seq")),
        P(None, "tp"),
        P(None, "tp"),
        P("tp", None),
        P(("groups", "seq"), None),
        P(("groups", "seq"), None),
    )
    out_specs = P(("groups", "seq"), None)
    return jax.shard_map(
        functools.partial(on_device, mesh.shape["seq"]),
        mesh=mesh, in_specs=in_specs, out_specs=out_specs, check_vma=False,
    )
```

```python
import functools

import jax
import jax.numpy as jnp
from jax import lax
from jax.experimental import pallas as pl
from jax.experimental.pallas import tpu as pltpu
from jax.sharding import PartitionSpec as P

HD = 256
LANES = 128
SEG_ROWS = 16
LIMIT = 448.0
MIN_EXP = -9
NEG = -1e30
MIB = 1024 * 1024
NT = (((1,), (1,)), ((), ()))
FACTOR = HD ** (-0.5) * 1.4426950408889634


def norm_kv_kernel(x_ref, gain_ref, w_ref, seg_ref, msg_ref, normed_ref, xs, ws, sems):
    rows, width = xs.shape
    tile, part = rows // 2, rows // 4

    def tokens_copy(i):
        return pltpu.make_async_copy(x_ref.at[pl.ds(i * part, part)], xs.at[pl.ds(i * part, part)], sems.at[i])

    def weights_copy():
        return pltpu.make_async_copy(w_ref, ws, sems.at[4])

    tokens_copy(0).start()
    tokens_copy(1).start()
    weights_copy().start()
    tokens_copy(2).start()
    tokens_copy(3).start()
    seg = seg_ref[...].astype(jnp.float32)
    low = jnp.broadcast_to(seg[:, :HD], (8, HD))
    high = jnp.broadcast_to(seg[:, HD:], (8, HD))
    msg_ref[rows:, :] = jnp.concatenate([low, high], axis=0).astype(jnp.bfloat16)

    def wide(first, count, start):
        return xs[first:first + count, start:start + LANES].astype(jnp.float32)

    def stats(first):
        total = wide(first, part, 0)
        for start in range(LANES, width, LANES):
            total = total + wide(first, part, start)
        mean = jnp.broadcast_to(jnp.sum(total, axis=1, keepdims=True) * (1.0 / width), (part, LANES))
        square = jnp.zeros((part, LANES), jnp.float32)
        for start in range(0, width, LANES):
            center = wide(first, part, start) - mean
            square = square + center * center
        spread = jnp.sum(square, axis=1, keepdims=True) * (1.0 / width)
        return mean, jnp.broadcast_to(lax.rsqrt(spread + 1e-05), (part, LANES))

    for first in range(0, rows, tile):
        halves = []
        for at in range(first, first + tile, part):
            tokens_copy(at // part).wait()
            halves.append(stats(at))
        mean = jnp.concatenate([h[0] for h in halves], axis=0)
        scale = jnp.concatenate([h[1] for h in halves], axis=0)
        if first == 0:
            weights_copy().wait()
        kv = jnp.zeros((tile, ws.shape[1]), jnp.float32)
        span = slice(first, first + tile)
        for start in range(0, width, HD):
            for at in (start, start + LANES):
                normed = (wide(first, tile, at) - mean) * scale * gain_ref[:, at:at + LANES]
                normed_ref[span, at:at + LANES] = normed.astype(jnp.bfloat16)
            kv = kv + jnp.dot(
                normed_ref[span, start:start + HD], ws[start:start + HD, :], preferred_element_type=jnp.float32
            )
        msg_ref[span, :] = kv.astype(jnp.bfloat16)


def norm_kv(tokens, gain, w_keyval, segments):
    rows, width = tokens.shape
    cols = w_keyval.shape[1]
    vmem, hbm = pl.BlockSpec(memory_space=pltpu.VMEM), pl.BlockSpec(memory_space=pltpu.HBM)
    return pl.pallas_call(
        norm_kv_kernel,
        in_specs=[hbm, vmem, hbm, vmem],
        out_specs=[vmem, vmem],
        out_shape=[
            jax.ShapeDtypeStruct((rows + SEG_ROWS, cols), jnp.bfloat16),
            jax.ShapeDtypeStruct((rows, width), jnp.bfloat16),
        ],
        scratch_shapes=[
            pltpu.VMEM((rows, width), jnp.bfloat16),
            pltpu.VMEM((width, cols), jnp.bfloat16),
            pltpu.SemaphoreType.DMA((5,)),
        ],
        compiler_params=pltpu.CompilerParams(vmem_limit_bytes=56 * MIB),
        cost_estimate=pl.CostEstimate(
            flops=40 * rows * width * cols, bytes_accessed=4 * rows * width + 2 * width * cols, transcendentals=0
        ),
        name="norm_kv",
    )(tokens, gain.reshape(1, width), w_keyval, segments.reshape(1, rows))


def query_kernel(x_ref, w_ref, out_ref):
    out_ref[...] = jnp.dot(x_ref[...], w_ref[...], preferred_element_type=jnp.float32).astype(jnp.bfloat16)


def project_query(normed, w_query):
    rows, width = normed.shape
    cols = w_query.shape[1]
    tile = rows // 2
    return pl.pallas_call(
        query_kernel,
        grid=(rows // tile,),
        in_specs=[pl.BlockSpec((tile, width), lambda i: (i, 0)), pl.BlockSpec((width, cols), lambda i: (0, 0))],
        out_specs=pl.BlockSpec((tile, cols), lambda i: (i, 0)),
        out_shape=jax.ShapeDtypeStruct((rows, cols), jnp.bfloat16),
        compiler_params=pltpu.CompilerParams(vmem_limit_bytes=20 * MIB),
        cost_estimate=pl.CostEstimate(
            flops=20 * rows * width * cols, bytes_accessed=2 * rows * width + 2 * width * cols, transcendentals=0
        ),
        name="project_query",
    )(normed, w_query)


def attend_kernel(plan, first, last, *refs):
    blocks = len(plan)
    q_ref, seg_ref = refs[:2]
    mine, other = refs[2:2 + blocks], refs[2 + blocks:2 + 2 * blocks]
    refs = refs[2 + 2 * blocks:]
    state_ref = None
    if not first:
        state_ref, refs = refs[0], refs[1:]
    out_ref, refs = refs[0], refs[1:]
    keys, values, segs, scores, sems = refs
    rows = q_ref.shape[0]
    tile = rows // 2
    part = lax.axis_index("tp")
    place = lax.axis_index("seq")
    odd = lax.rem(place, 2)

    for slot in range(blocks):
        for value in range(2):
            key_src, val_src = (mine[slot], other[slot]) if value == 0 else (other[slot], mine[slot])

            @pl.when(part == value)
            def _():
                pltpu.make_async_copy(key_src.at[pl.ds(0, rows)], keys.at[slot], sems.at[0, slot]).start()
                pltpu.make_async_copy(val_src.at[pl.ds(0, rows)], values.at[slot], sems.at[1, slot]).start()

        pltpu.make_async_copy(mine[slot].at[pl.ds(rows, SEG_ROWS)], segs.at[slot], sems.at[2, slot]).start()

    own_seg = jnp.transpose(jnp.broadcast_to(seg_ref[...].astype(jnp.float32), (8, rows)))[:, 0:1]
    for slot in range(blocks):
        pltpu.make_async_copy(mine[slot].at[pl.ds(0, rows)], keys.at[slot], sems.at[0, slot]).wait()
        pltpu.make_async_copy(mine[slot].at[pl.ds(0, rows)], values.at[slot], sems.at[1, slot]).wait()
        pltpu.make_async_copy(mine[slot].at[pl.ds(rows, SEG_ROWS)], segs.at[slot], sems.at[2, slot]).wait()
    key_segs = []
    for slot, kind in enumerate(plan):
        packed = segs[slot].astype(jnp.float32)
        key_seg = jnp.concatenate([packed[0:1, :], packed[8:9, :]], axis=1)
        if kind != "own":
            back = jnp.where(odd == 1, kind[1], kind[0])
            key_seg = jnp.where((back > 0) & (place >= back), key_seg, -1.0)
        key_segs.append(key_seg)

    for start in range(0, rows, tile):
        span = slice(start, start + tile)
        query = q_ref[span, :]
        best = None if first else state_ref[span, HD:HD + LANES]
        bounds = []
        for slot, kind in enumerate(plan):
            low, high = 0, rows
            if kind == "own":
                high = start + tile
            elif kind[2]:
                low = start
            bounds.append((low, high))
            raw = lax.dot_general(query, keys[slot, low:high, :], NT, preferred_element_type=jnp.float32)
            allowed = key_segs[slot][:, low:high] == own_seg[span, :]
            if kind == "own":
                row_pos = start + lax.broadcasted_iota(jnp.int32, raw.shape, 0)
                allowed = allowed & (lax.broadcasted_iota(jnp.int32, raw.shape, 1) <= row_pos)
            masked = jnp.where(allowed, raw, NEG)
            scores[slot, :, low:high] = masked
            for at in range(0, high - low, LANES):
                piece = masked[:, at:at + LANES]
                best = piece if best is None else jnp.maximum(best, piece)
        top = jnp.broadcast_to(jnp.max(best, axis=1, keepdims=True), (tile, LANES))
        if first:
            total = jnp.zeros((tile, LANES), jnp.float32)
            weighted = jnp.zeros((tile, HD), jnp.float32)
        else:
            shrink = jnp.exp2((state_ref[span, HD:HD + LANES] - top) * FACTOR)
            total = state_ref[span, HD + LANES:] * shrink
            weighted = state_ref[span, :HD] * jnp.concatenate([shrink, shrink], axis=1)
        for slot in range(blocks):
            low, high = bounds[slot]
            pieces = []
            for at in range(low, high, LANES):
                weights = jnp.exp2((scores[slot, :, at:at + LANES] - top) * FACTOR)
                total = total + weights
                pieces.append(weights.astype(jnp.bfloat16))
            probs = jnp.concatenate(pieces, axis=1)
            weighted = weighted + jnp.dot(probs, values[slot, low:high, :], preferred_element_type=jnp.float32)
        if last:
            out_ref[span, :] = (weighted / jnp.sum(total, axis=1, keepdims=True)).astype(jnp.bfloat16)
        else:
            out_ref[span, :HD] = weighted
            out_ref[span, HD:HD + LANES] = top
            out_ref[span, HD + LANES:] = total


def attend(query, segments, plan, mine, other, state, last):
    rows = query.shape[0]
    blocks = len(plan)
    vmem = pl.BlockSpec(memory_space=pltpu.VMEM)
    first = state is None
    operands = [query, segments.reshape(1, rows), *mine, *other] + ([] if first else [state])
    if last:
        out_shape = jax.ShapeDtypeStruct((rows, HD), jnp.bfloat16)
    else:
        out_shape = jax.ShapeDtypeStruct((rows, HD + 2 * LANES), jnp.float32)
    return pl.pallas_call(
        functools.partial(attend_kernel, plan, first, last),
        in_specs=[vmem] * 2 + [pl.BlockSpec(memory_space=pl.ANY)] * (2 * blocks) + ([] if first else [vmem]),
        out_specs=vmem,
        out_shape=out_shape,
        scratch_shapes=[
            pltpu.VMEM((blocks, rows, HD), jnp.bfloat16),
            pltpu.VMEM((blocks, rows, HD), jnp.bfloat16),
            pltpu.VMEM((blocks, SEG_ROWS, HD), jnp.bfloat16),
            pltpu.VMEM((blocks, rows // 2, rows), jnp.float32),
            pltpu.SemaphoreType.DMA((3, blocks)),
        ],
        compiler_params=pltpu.CompilerParams(vmem_limit_bytes=(12 + 2 * blocks) * MIB),
        cost_estimate=pl.CostEstimate(
            flops=80 * rows * rows * blocks * HD, bytes_accessed=4 * rows * blocks * HD, transcendentals=rows * rows * blocks
        ),
        name="attend_last" if last else "attend_first" if first else "attend_more",
    )(*operands)


def output_kernel(a_ref, b_ref, wa_ref, wb_ref, x_ref, sum_ref, out_exp_ref, out_ref):
    rows, width = x_ref.shape
    groups = sum_ref.shape[0]

    def bounds(ref):
        power = jnp.left_shift(jnp.int32(1), ref[...] - MIN_EXP).astype(jnp.float32)
        return jnp.transpose(power * (LIMIT * 2.0 ** MIN_EXP))

    def clip(value, bound):
        return jnp.minimum(jnp.maximum(value.astype(jnp.bfloat16), -bound), bound)

    sum_bound, out_bound = bounds(sum_ref), bounds(out_exp_ref)
    per = width // groups
    chunk = 2 * per
    a, b = a_ref[...], b_ref[...]
    for start in range(0, width, chunk):
        term_a = jnp.dot(a, wa_ref[:, start:start + chunk], preferred_element_type=jnp.float32)
        term_b = jnp.dot(b, wb_ref[:, start:start + chunk], preferred_element_type=jnp.float32)
        for part in range(2):
            cols = slice(part * per, (part + 1) * per)
            group = (start + part * per) // per
            span = slice(start + part * per, start + (part + 1) * per)
            bound = jnp.broadcast_to(sum_bound[:, group:group + 1], (rows, per)).astype(jnp.bfloat16)
            last = jnp.broadcast_to(out_bound[:, group:group + 1], (rows, per)).astype(jnp.bfloat16)
            quant_a = clip(term_a[:, cols], bound).astype(jnp.float32)
            quant_b = clip(term_b[:, cols], bound).astype(jnp.float32)
            combined = x_ref[:, span].astype(jnp.float32) + (quant_a + quant_b)
            out_ref[:, span] = clip(combined, last)


def project_out(att_a, att_b, w_a, w_b, tokens, sum_exps, out_exps):
    rows, width = tokens.shape
    depth = att_a.shape[1]
    groups = sum_exps.shape[1]
    steps = groups // 8
    tile = width // steps
    whole = pl.BlockSpec((rows, depth), lambda i: (0, 0))
    weight = pl.BlockSpec((depth, tile), lambda i: (0, i))
    wide = pl.BlockSpec((rows, tile), lambda i: (0, i))
    exps = pl.BlockSpec((groups // steps, rows), lambda i: (i, 0))
    return pl.pallas_call(
        output_kernel,
        grid=(steps,),
        in_specs=[whole, whole, weight, weight, wide, exps, exps],
        out_specs=wide,
        out_shape=jax.ShapeDtypeStruct((rows, width), jnp.bfloat16),
        compiler_params=pltpu.CompilerParams(vmem_limit_bytes=20 * MIB),
        cost_estimate=pl.CostEstimate(
            flops=4 * rows * width * depth, bytes_accessed=4 * rows * width + 4 * width * depth, transcendentals=0
        ),
        name="project_out",
    )(att_a, att_b, w_a, w_b, tokens, sum_exps.T, out_exps.T)


def on_device(seq_size, tokens, gain, segments, w_query, w_keyval, w_out, sum_exps, out_exps):
    window = seq_size // 2

    def swap_cores(x):
        return lax.ppermute(x, "tp", [(0, 1), (1, 0)])

    def swap_pair(x):
        return lax.ppermute(x, "seq", [(i, i ^ 1) for i in range(seq_size)])

    def shift(x):
        return lax.ppermute(x, "seq", [(i, (i + 2) % seq_size) for i in range(seq_size)])

    w_other = swap_cores(w_out)
    message, normed = norm_kv(tokens, gain, w_keyval, segments)
    held = shift(message)
    pair = swap_pair(message)
    query = project_query(normed, w_query)
    state = None
    mine, plan = [message, pair], ["own", (0, 1, False)]
    for k in range(1, window // 2 + 1):
        mine.append(held)
        plan.append((2 * k, 2 * k, 2 * k == window))
        beside = swap_pair(held)
        if k < window // 2:
            held = shift(held)
        if k == 1 or k == window // 2:
            state = attend(query, segments, plan, mine, [swap_cores(m) for m in mine], state, False)
            mine, plan = [], []
        mine.append(beside)
        plan.append((2 * k - 1, 2 * k + 1 if k < window // 2 else 0, False))
    attended = attend(query, segments, plan, mine, [swap_cores(m) for m in mine], state, True)
    return project_out(attended, swap_cores(attended), w_out, w_other, tokens, sum_exps, out_exps)


def solution(mesh):
    in_specs = (
        P(("groups", "seq"), None),
        P(),
        P(("groups", "seq")),
        P(None, "tp"),
        P(None, "tp"),
        P("tp", None),
        P(("groups", "seq"), None),
        P(("groups", "seq"), None),
    )
    out_specs = P(("groups", "seq"), None)
    return jax.shard_map(
        functools.partial(on_device, mesh.shape["seq"]),
        mesh=mesh, in_specs=in_specs, out_specs=out_specs, check_vma=False,
    )
```

```python
import functools

import jax
import jax.numpy as jnp
from jax import lax
from jax.experimental import pallas as pl
from jax.experimental.pallas import tpu as pltpu
from jax.sharding import PartitionSpec as P

HD = 256
LANES = 128
SEG_ROWS = 16
LIMIT = 448.0
MIN_EXP = -9
NEG = -1e30
MIB = 1024 * 1024
NT = (((1,), (1,)), ((), ()))
FACTOR = HD ** (-0.5) * 1.4426950408889634


def norm_kv_kernel(x_ref, gain_hbm, w_ref, seg_hbm, msg_ref, normed_ref, xs, ws, gain_ref, seg_ref, sems):
    rows, width = xs.shape
    tile, part = rows // 2, rows // 4

    def tokens_copy(i):
        return pltpu.make_async_copy(x_ref.at[pl.ds(i * part, part)], xs.at[pl.ds(i * part, part)], sems.at[i])

    def weights_copy():
        return pltpu.make_async_copy(w_ref, ws, sems.at[4])

    def gain_copy():
        return pltpu.make_async_copy(gain_hbm, gain_ref, sems.at[5])

    def segments_copy():
        return pltpu.make_async_copy(seg_hbm, seg_ref, sems.at[6])

    tokens_copy(0).start()
    tokens_copy(1).start()
    gain_copy().start()
    segments_copy().start()
    weights_copy().start()
    tokens_copy(2).start()
    tokens_copy(3).start()
    def wide(first, count, start):
        return xs[first:first + count, start:start + LANES].astype(jnp.float32)

    def stats(first):
        total = wide(first, part, 0)
        for start in range(LANES, width, LANES):
            total = total + wide(first, part, start)
        mean = jnp.broadcast_to(jnp.sum(total, axis=1, keepdims=True) * (1.0 / width), (part, LANES))
        square = jnp.zeros((part, LANES), jnp.float32)
        for start in range(0, width, LANES):
            center = wide(first, part, start) - mean
            square = square + center * center
        spread = jnp.sum(square, axis=1, keepdims=True) * (1.0 / width)
        return mean, jnp.broadcast_to(lax.rsqrt(spread + 1e-05), (part, LANES))

    for first in range(0, rows, tile):
        halves = []
        for at in range(first, first + tile, part):
            tokens_copy(at // part).wait()
            halves.append(stats(at))
        mean = jnp.concatenate([h[0] for h in halves], axis=0)
        scale = jnp.concatenate([h[1] for h in halves], axis=0)
        if first == 0:
            gain_copy().wait()
            weights_copy().wait()
        kv = jnp.zeros((tile, ws.shape[1]), jnp.float32)
        span = slice(first, first + tile)
        for start in range(0, width, HD):
            for at in (start, start + LANES):
                normed = (wide(first, tile, at) - mean) * scale * gain_ref[:, at:at + LANES]
                normed_ref[span, at:at + LANES] = normed.astype(jnp.bfloat16)
            kv = kv + jnp.dot(
                normed_ref[span, start:start + HD], ws[start:start + HD, :], preferred_element_type=jnp.float32
            )
        msg_ref[span, :] = kv.astype(jnp.bfloat16)
    segments_copy().wait()
    seg = seg_ref[...].astype(jnp.float32)
    low = jnp.broadcast_to(seg[:, :HD], (8, HD))
    high = jnp.broadcast_to(seg[:, HD:], (8, HD))
    msg_ref[rows:, :] = jnp.concatenate([low, high], axis=0).astype(jnp.bfloat16)


def in_hbm(x):
    return pltpu.with_memory_space_constraint(x, pltpu.HBM)


def norm_kv(tokens, gain, w_keyval, segments):
    rows, width = tokens.shape
    cols = w_keyval.shape[1]
    vmem, hbm = pl.BlockSpec(memory_space=pltpu.VMEM), pl.BlockSpec(memory_space=pltpu.HBM)
    return pl.pallas_call(
        norm_kv_kernel,
        in_specs=[hbm] * 4,
        out_specs=[vmem, vmem],
        out_shape=[pltpu.VMEM((rows + SEG_ROWS, cols), jnp.bfloat16), pltpu.VMEM((rows, width), jnp.bfloat16)],
        scratch_shapes=[
            pltpu.VMEM((rows, width), jnp.bfloat16),
            pltpu.VMEM((width, cols), jnp.bfloat16),
            pltpu.VMEM((1, width), jnp.float32),
            pltpu.VMEM((1, rows), jnp.int32),
            pltpu.SemaphoreType.DMA((7,)),
        ],
        compiler_params=pltpu.CompilerParams(vmem_limit_bytes=24 * MIB),
        cost_estimate=pl.CostEstimate(
            flops=40 * rows * width * cols, bytes_accessed=4 * rows * width + 2 * width * cols, transcendentals=0
        ),
        name="norm_kv",
    )(in_hbm(tokens), in_hbm(gain.reshape(1, width)), in_hbm(w_keyval), in_hbm(segments.reshape(1, rows)))


def query_kernel(x_ref, w_ref, out_ref):
    out_ref[...] = jnp.dot(x_ref[...], w_ref[...], preferred_element_type=jnp.float32).astype(jnp.bfloat16)


def project_query(normed, w_query):
    rows, width = normed.shape
    cols = w_query.shape[1]
    tile = rows // 2
    return pl.pallas_call(
        query_kernel,
        grid=(rows // tile,),
        in_specs=[pl.BlockSpec((tile, width), lambda i: (i, 0)), pl.BlockSpec((width, cols), lambda i: (0, 0))],
        out_specs=pl.BlockSpec((tile, cols), lambda i: (i, 0)),
        out_shape=jax.ShapeDtypeStruct((rows, cols), jnp.bfloat16),
        compiler_params=pltpu.CompilerParams(vmem_limit_bytes=20 * MIB),
        cost_estimate=pl.CostEstimate(
            flops=20 * rows * width * cols, bytes_accessed=2 * rows * width + 2 * width * cols, transcendentals=0
        ),
        name="project_query",
    )(normed, w_query)


def attend_kernel(plan, first, last, *refs):
    blocks = len(plan)
    q_ref, seg_ref = refs[:2]
    mine, other = refs[2:2 + blocks], refs[2 + blocks:2 + 2 * blocks]
    refs = refs[2 + 2 * blocks:]
    state_ref = None
    if not first:
        state_ref, refs = refs[0], refs[1:]
    out_ref, refs = refs[0], refs[1:]
    keys, values, segs, scores, sems = refs
    rows = q_ref.shape[0]
    tile = rows // 2
    part = lax.axis_index("tp")
    place = lax.axis_index("seq")
    odd = lax.rem(place, 2)

    for slot in range(blocks):
        for value in range(2):
            key_src, val_src = (mine[slot], other[slot]) if value == 0 else (other[slot], mine[slot])

            @pl.when(part == value)
            def _():
                pltpu.make_async_copy(key_src.at[pl.ds(0, rows)], keys.at[slot], sems.at[0, slot]).start()
                pltpu.make_async_copy(val_src.at[pl.ds(0, rows)], values.at[slot], sems.at[1, slot]).start()

        pltpu.make_async_copy(mine[slot].at[pl.ds(rows, SEG_ROWS)], segs.at[slot], sems.at[2, slot]).start()

    own_seg = jnp.transpose(jnp.broadcast_to(seg_ref[...].astype(jnp.float32), (8, rows)))[:, 0:1]
    for slot in range(blocks):
        pltpu.make_async_copy(mine[slot].at[pl.ds(0, rows)], keys.at[slot], sems.at[0, slot]).wait()
        pltpu.make_async_copy(mine[slot].at[pl.ds(0, rows)], values.at[slot], sems.at[1, slot]).wait()
        pltpu.make_async_copy(mine[slot].at[pl.ds(rows, SEG_ROWS)], segs.at[slot], sems.at[2, slot]).wait()
    key_segs = []
    for slot, kind in enumerate(plan):
        packed = segs[slot].astype(jnp.float32)
        key_seg = jnp.concatenate([packed[0:1, :], packed[8:9, :]], axis=1)
        if kind != "own":
            back = jnp.where(odd == 1, kind[1], kind[0])
            key_seg = jnp.where((back > 0) & (place >= back), key_seg, -1.0)
        key_segs.append(key_seg)

    for start in range(0, rows, tile):
        span = slice(start, start + tile)
        query = q_ref[span, :]
        best = None if first else state_ref[span, HD:HD + LANES]
        bounds = []
        for slot, kind in enumerate(plan):
            low, high = 0, rows
            if kind == "own":
                high = start + tile
            elif kind[2]:
                low = start
            bounds.append((low, high))
            raw = lax.dot_general(query, keys[slot, low:high, :], NT, preferred_element_type=jnp.float32)
            allowed = key_segs[slot][:, low:high] == own_seg[span, :]
            if kind == "own":
                row_pos = start + lax.broadcasted_iota(jnp.int32, raw.shape, 0)
                allowed = allowed & (lax.broadcasted_iota(jnp.int32, raw.shape, 1) <= row_pos)
            masked = jnp.where(allowed, raw, NEG)
            scores[slot, :, low:high] = masked
            for at in range(0, high - low, LANES):
                piece = masked[:, at:at + LANES]
                best = piece if best is None else jnp.maximum(best, piece)
        top = jnp.broadcast_to(jnp.max(best, axis=1, keepdims=True), (tile, LANES))
        if first:
            total = jnp.zeros((tile, LANES), jnp.float32)
            weighted = jnp.zeros((tile, HD), jnp.float32)
        else:
            shrink = jnp.exp2((state_ref[span, HD:HD + LANES] - top) * FACTOR)
            total = state_ref[span, HD + LANES:] * shrink
            weighted = state_ref[span, :HD] * jnp.concatenate([shrink, shrink], axis=1)
        for slot in range(blocks):
            low, high = bounds[slot]
            pieces = []
            for at in range(low, high, LANES):
                weights = jnp.exp2((scores[slot, :, at:at + LANES] - top) * FACTOR)
                total = total + weights
                pieces.append(weights.astype(jnp.bfloat16))
            probs = jnp.concatenate(pieces, axis=1)
            weighted = weighted + jnp.dot(probs, values[slot, low:high, :], preferred_element_type=jnp.float32)
        if last:
            out_ref[span, :] = (weighted / jnp.sum(total, axis=1, keepdims=True)).astype(jnp.bfloat16)
        else:
            out_ref[span, :HD] = weighted
            out_ref[span, HD:HD + LANES] = top
            out_ref[span, HD + LANES:] = total


def attend(query, segments, plan, mine, other, state, last):
    rows = query.shape[0]
    blocks = len(plan)
    vmem = pl.BlockSpec(memory_space=pltpu.VMEM)
    first = state is None
    operands = [query, segments.reshape(1, rows), *mine, *other] + ([] if first else [state])
    if last:
        out_shape = jax.ShapeDtypeStruct((rows, HD), jnp.bfloat16)
    else:
        out_shape = jax.ShapeDtypeStruct((rows, HD + 2 * LANES), jnp.float32)
    return pl.pallas_call(
        functools.partial(attend_kernel, plan, first, last),
        in_specs=[vmem] * 2 + [pl.BlockSpec(memory_space=pl.ANY)] * (2 * blocks) + ([] if first else [vmem]),
        out_specs=vmem,
        out_shape=out_shape,
        scratch_shapes=[
            pltpu.VMEM((blocks, rows, HD), jnp.bfloat16),
            pltpu.VMEM((blocks, rows, HD), jnp.bfloat16),
            pltpu.VMEM((blocks, SEG_ROWS, HD), jnp.bfloat16),
            pltpu.VMEM((blocks, rows // 2, rows), jnp.float32),
            pltpu.SemaphoreType.DMA((3, blocks)),
        ],
        compiler_params=pltpu.CompilerParams(vmem_limit_bytes=(12 + 2 * blocks) * MIB),
        cost_estimate=pl.CostEstimate(
            flops=80 * rows * rows * blocks * HD, bytes_accessed=4 * rows * blocks * HD, transcendentals=rows * rows * blocks
        ),
        name="attend_last" if last else "attend_first" if first else "attend_more",
    )(*operands)


def output_kernel(a_ref, b_ref, wa_ref, wb_ref, x_ref, sum_ref, out_exp_ref, out_ref):
    rows, width = x_ref.shape
    groups = sum_ref.shape[0]

    def bounds(ref):
        power = jnp.left_shift(jnp.int32(1), ref[...] - MIN_EXP).astype(jnp.float32)
        return jnp.transpose(power * (LIMIT * 2.0 ** MIN_EXP))

    def clip(value, bound):
        return jnp.minimum(jnp.maximum(value.astype(jnp.bfloat16), -bound), bound)

    sum_bound, out_bound = bounds(sum_ref), bounds(out_exp_ref)
    per = width // groups
    chunk = 2 * per
    a, b = a_ref[...], b_ref[...]
    for start in range(0, width, chunk):
        term_a = jnp.dot(a, wa_ref[:, start:start + chunk], preferred_element_type=jnp.float32)
        term_b = jnp.dot(b, wb_ref[:, start:start + chunk], preferred_element_type=jnp.float32)
        for part in range(2):
            cols = slice(part * per, (part + 1) * per)
            group = (start + part * per) // per
            span = slice(start + part * per, start + (part + 1) * per)
            bound = jnp.broadcast_to(sum_bound[:, group:group + 1], (rows, per)).astype(jnp.bfloat16)
            last = jnp.broadcast_to(out_bound[:, group:group + 1], (rows, per)).astype(jnp.bfloat16)
            quant_a = clip(term_a[:, cols], bound).astype(jnp.float32)
            quant_b = clip(term_b[:, cols], bound).astype(jnp.float32)
            combined = x_ref[:, span].astype(jnp.float32) + (quant_a + quant_b)
            out_ref[:, span] = clip(combined, last)


def project_out(att_a, att_b, w_a, w_b, tokens, sum_exps, out_exps):
    rows, width = tokens.shape
    depth = att_a.shape[1]
    groups = sum_exps.shape[1]
    steps = groups // 8
    tile = width // steps
    whole = pl.BlockSpec((rows, depth), lambda i: (0, 0))
    weight = pl.BlockSpec((depth, tile), lambda i: (0, i))
    wide = pl.BlockSpec((rows, tile), lambda i: (0, i))
    exps = pl.BlockSpec((groups // steps, rows), lambda i: (i, 0))
    return pl.pallas_call(
        output_kernel,
        grid=(steps,),
        in_specs=[whole, whole, weight, weight, wide, exps, exps],
        out_specs=wide,
        out_shape=jax.ShapeDtypeStruct((rows, width), jnp.bfloat16),
        compiler_params=pltpu.CompilerParams(vmem_limit_bytes=20 * MIB),
        cost_estimate=pl.CostEstimate(
            flops=4 * rows * width * depth, bytes_accessed=4 * rows * width + 4 * width * depth, transcendentals=0
        ),
        name="project_out",
    )(att_a, att_b, w_a, w_b, tokens, sum_exps.T, out_exps.T)


def on_device(seq_size, tokens, gain, segments, w_query, w_keyval, w_out, sum_exps, out_exps):
    window = seq_size // 2

    def swap_cores(x):
        return lax.ppermute(x, "tp", [(0, 1), (1, 0)])

    def swap_pair(x, first):
        return lax.ppermute(x, "seq", [(i, i ^ 1 if i >= first else i) for i in range(seq_size)])

    def shift(x, first):
        cycle = seq_size - first
        return lax.ppermute(x, "seq", [(i, first + (i - first + 2) % cycle if i >= first else i) for i in range(seq_size)])

    w_other = swap_cores(w_out)
    message, normed = norm_kv(tokens, gain, w_keyval, segments)
    held = shift(message, 0)
    pair = swap_pair(message, 0)
    query = project_query(normed, w_query)
    state = None
    mine, plan = [message, pair], ["own", (0, 1, False)]
    for k in range(1, window // 2 + 1):
        mine.append(held)
        plan.append((2 * k, 2 * k, 2 * k == window))
        beside = swap_pair(held, 2 * k)
        if k < window // 2:
            held = shift(held, 2 * k)
        if k == 1 or k == window // 2:
            state = attend(query, segments, plan, mine, [swap_cores(m) for m in mine], state, False)
            mine, plan = [], []
        mine.append(beside)
        plan.append((2 * k - 1, 2 * k + 1 if k < window // 2 else 0, False))
    attended = attend(query, segments, plan, mine, [swap_cores(m) for m in mine], state, True)
    return project_out(attended, swap_cores(attended), w_out, w_other, tokens, sum_exps, out_exps)


def solution(mesh):
    in_specs = (
        P(("groups", "seq"), None),
        P(),
        P(("groups", "seq")),
        P(None, "tp"),
        P(None, "tp"),
        P("tp", None),
        P(("groups", "seq"), None),
        P(("groups", "seq"), None),
    )
    out_specs = P(("groups", "seq"), None)
    return jax.shard_map(
        functools.partial(on_device, mesh.shape["seq"]),
        mesh=mesh, in_specs=in_specs, out_specs=out_specs, check_vma=False,
    )
```

```python
import functools

import jax
import jax.numpy as jnp
from jax import lax
from jax.experimental import pallas as pl
from jax.experimental.pallas import tpu as pltpu
from jax.sharding import PartitionSpec as P

HD = 256
LANES = 128
SEG_ROWS = 16
LIMIT = 448.0
MIN_EXP = -9
NEG = -1e30
MIB = 1024 * 1024
NT = (((1,), (1,)), ((), ()))
FACTOR = HD ** (-0.5) * 1.4426950408889634


def norm_kv_kernel(x_ref, gain_hbm, w_ref, seg_hbm, msg_ref, normed_ref, xs, ws, gain_ref, seg_ref, sems):
    rows, width = xs.shape
    tile, part = rows // 2, rows // 4

    def tokens_copy(i):
        return pltpu.make_async_copy(x_ref.at[pl.ds(i * part, part)], xs.at[pl.ds(i * part, part)], sems.at[i])

    def weights_copy():
        return pltpu.make_async_copy(w_ref, ws, sems.at[4])

    def gain_copy():
        return pltpu.make_async_copy(gain_hbm, gain_ref, sems.at[5])

    def segments_copy():
        return pltpu.make_async_copy(seg_hbm, seg_ref, sems.at[6])

    tokens_copy(0).start()
    tokens_copy(1).start()
    gain_copy().start()
    segments_copy().start()
    weights_copy().start()
    tokens_copy(2).start()
    tokens_copy(3).start()
    def wide(first, count, start):
        return xs[first:first + count, start:start + LANES].astype(jnp.float32)

    def stats(first):
        total = wide(first, part, 0)
        for start in range(LANES, width, LANES):
            total = total + wide(first, part, start)
        mean = jnp.broadcast_to(jnp.sum(total, axis=1, keepdims=True) * (1.0 / width), (part, LANES))
        square = jnp.zeros((part, LANES), jnp.float32)
        for start in range(0, width, LANES):
            center = wide(first, part, start) - mean
            square = square + center * center
        spread = jnp.sum(square, axis=1, keepdims=True) * (1.0 / width)
        return mean, jnp.broadcast_to(lax.rsqrt(spread + 1e-05), (part, LANES))

    for first in range(0, rows, tile):
        halves = []
        for at in range(first, first + tile, part):
            tokens_copy(at // part).wait()
            halves.append(stats(at))
        mean = jnp.concatenate([h[0] for h in halves], axis=0)
        scale = jnp.concatenate([h[1] for h in halves], axis=0)
        if first == 0:
            gain_copy().wait()
            weights_copy().wait()
        kv = jnp.zeros((tile, ws.shape[1]), jnp.float32)
        span = slice(first, first + tile)
        for start in range(0, width, HD):
            for at in (start, start + LANES):
                normed = (wide(first, tile, at) - mean) * scale * gain_ref[:, at:at + LANES]
                normed_ref[span, at:at + LANES] = normed.astype(jnp.bfloat16)
            kv = kv + jnp.dot(
                normed_ref[span, start:start + HD], ws[start:start + HD, :], preferred_element_type=jnp.float32
            )
        msg_ref[span, :] = kv.astype(jnp.bfloat16)
    segments_copy().wait()
    seg = seg_ref[...].astype(jnp.float32)
    low = jnp.broadcast_to(seg[:, :HD], (8, HD))
    high = jnp.broadcast_to(seg[:, HD:], (8, HD))
    msg_ref[rows:, :] = jnp.concatenate([low, high], axis=0).astype(jnp.bfloat16)


def in_hbm(x):
    return pltpu.with_memory_space_constraint(x, pltpu.HBM)


def norm_kv(tokens, gain, w_keyval, segments):
    rows, width = tokens.shape
    cols = w_keyval.shape[1]
    vmem, hbm = pl.BlockSpec(memory_space=pltpu.VMEM), pl.BlockSpec(memory_space=pltpu.HBM)
    return pl.pallas_call(
        norm_kv_kernel,
        in_specs=[hbm] * 4,
        out_specs=[vmem, vmem],
        out_shape=[pltpu.VMEM((rows + SEG_ROWS, cols), jnp.bfloat16), pltpu.VMEM((rows, width), jnp.bfloat16)],
        scratch_shapes=[
            pltpu.VMEM((rows, width), jnp.bfloat16),
            pltpu.VMEM((width, cols), jnp.bfloat16),
            pltpu.VMEM((1, width), jnp.float32),
            pltpu.VMEM((1, rows), jnp.int32),
            pltpu.SemaphoreType.DMA((7,)),
        ],
        compiler_params=pltpu.CompilerParams(vmem_limit_bytes=24 * MIB),
        cost_estimate=pl.CostEstimate(
            flops=2 * rows * width * cols, bytes_accessed=4 * rows * width + 2 * width * cols, transcendentals=0
        ),
        name="norm_kv",
    )(in_hbm(tokens), in_hbm(gain.reshape(1, width)), in_hbm(w_keyval), in_hbm(segments.reshape(1, rows)))


def query_kernel(x_ref, w_ref, out_ref):
    out_ref[...] = jnp.dot(x_ref[...], w_ref[...], preferred_element_type=jnp.float32).astype(jnp.bfloat16)


def project_query(normed, w_query):
    rows, width = normed.shape
    cols = w_query.shape[1]
    tile = rows // 2
    return pl.pallas_call(
        query_kernel,
        grid=(rows // tile,),
        in_specs=[pl.BlockSpec((tile, width), lambda i: (i, 0)), pl.BlockSpec((width, cols), lambda i: (0, 0))],
        out_specs=pl.BlockSpec((tile, cols), lambda i: (i, 0)),
        out_shape=jax.ShapeDtypeStruct((rows, cols), jnp.bfloat16),
        compiler_params=pltpu.CompilerParams(vmem_limit_bytes=20 * MIB),
        cost_estimate=pl.CostEstimate(
            flops=2 * rows * width * cols, bytes_accessed=2 * rows * width + 2 * width * cols, transcendentals=0
        ),
        name="project_query",
    )(normed, w_query)


def attend_kernel(plan, first, last, *refs):
    blocks = len(plan)
    q_ref, seg_ref = refs[:2]
    mine, other = refs[2:2 + blocks], refs[2 + blocks:2 + 2 * blocks]
    refs = refs[2 + 2 * blocks:]
    state_ref = None
    if not first:
        state_ref, refs = refs[0], refs[1:]
    out_ref, refs = refs[0], refs[1:]
    keys, values, segs, scores, sems = refs
    rows = q_ref.shape[0]
    tile = rows // 2
    part = lax.axis_index("tp")
    place = lax.axis_index("seq")

    for slot in range(blocks):
        for value in range(2):
            key_src, val_src = (mine[slot], other[slot]) if value == 0 else (other[slot], mine[slot])

            @pl.when(part == value)
            def _():
                pltpu.make_async_copy(key_src.at[pl.ds(0, rows)], keys.at[slot], sems.at[0, slot]).start()
                pltpu.make_async_copy(val_src.at[pl.ds(0, rows)], values.at[slot], sems.at[1, slot]).start()

        pltpu.make_async_copy(mine[slot].at[pl.ds(rows, SEG_ROWS)], segs.at[slot], sems.at[2, slot]).start()

    own_seg = jnp.transpose(jnp.broadcast_to(seg_ref[...].astype(jnp.float32), (8, rows)))[:, 0:1]
    for slot in range(blocks):
        pltpu.make_async_copy(mine[slot].at[pl.ds(0, rows)], keys.at[slot], sems.at[0, slot]).wait()
        pltpu.make_async_copy(mine[slot].at[pl.ds(0, rows)], values.at[slot], sems.at[1, slot]).wait()
        pltpu.make_async_copy(mine[slot].at[pl.ds(rows, SEG_ROWS)], segs.at[slot], sems.at[2, slot]).wait()
    key_segs = []
    for slot, (back, _) in enumerate(plan):
        packed = segs[slot].astype(jnp.float32)
        key_seg = jnp.concatenate([packed[0:1, :], packed[8:9, :]], axis=1)
        if back > 0:
            key_seg = jnp.where(place >= back, key_seg, -1.0)
        key_segs.append(key_seg)

    for start in range(0, rows, tile):
        span = slice(start, start + tile)
        query = q_ref[span, :]
        best = None if first else state_ref[span, HD:HD + LANES]
        bounds = []
        for slot, (back, furthest) in enumerate(plan):
            low, high = 0, rows
            if back == 0:
                high = start + tile
            elif furthest:
                low = start
            bounds.append((low, high))
            raw = lax.dot_general(query, keys[slot, low:high, :], NT, preferred_element_type=jnp.float32)
            allowed = key_segs[slot][:, low:high] == own_seg[span, :]
            if back == 0:
                row_pos = start + lax.broadcasted_iota(jnp.int32, raw.shape, 0)
                allowed = allowed & (lax.broadcasted_iota(jnp.int32, raw.shape, 1) <= row_pos)
            masked = jnp.where(allowed, raw, NEG)
            scores[slot, :, low:high] = masked
            for at in range(0, high - low, LANES):
                piece = masked[:, at:at + LANES]
                best = piece if best is None else jnp.maximum(best, piece)
        top = jnp.broadcast_to(jnp.max(best, axis=1, keepdims=True), (tile, LANES))
        if first:
            total = jnp.zeros((tile, LANES), jnp.float32)
            weighted = jnp.zeros((tile, HD), jnp.float32)
        else:
            shrink = jnp.exp2((state_ref[span, HD:HD + LANES] - top) * FACTOR)
            total = state_ref[span, HD + LANES:] * shrink
            weighted = state_ref[span, :HD] * jnp.concatenate([shrink, shrink], axis=1)
        for slot in range(blocks):
            low, high = bounds[slot]
            pieces = []
            for at in range(low, high, LANES):
                weights = jnp.exp2((scores[slot, :, at:at + LANES] - top) * FACTOR)
                total = total + weights
                pieces.append(weights.astype(jnp.bfloat16))
            probs = jnp.concatenate(pieces, axis=1)
            weighted = weighted + jnp.dot(probs, values[slot, low:high, :], preferred_element_type=jnp.float32)
        if last:
            out_ref[span, :] = (weighted / jnp.sum(total, axis=1, keepdims=True)).astype(jnp.bfloat16)
        else:
            out_ref[span, :HD] = weighted
            out_ref[span, HD:HD + LANES] = top
            out_ref[span, HD + LANES:] = total


def attend(query, segments, plan, mine, other, state, last):
    rows = query.shape[0]
    blocks = len(plan)
    vmem = pl.BlockSpec(memory_space=pltpu.VMEM)
    first = state is None
    operands = [query, segments.reshape(1, rows), *mine, *other] + ([] if first else [state])
    if last:
        out_shape = jax.ShapeDtypeStruct((rows, HD), jnp.bfloat16)
    else:
        out_shape = jax.ShapeDtypeStruct((rows, HD + 2 * LANES), jnp.float32)
    return pl.pallas_call(
        functools.partial(attend_kernel, plan, first, last),
        in_specs=[vmem] * 2 + [pl.BlockSpec(memory_space=pl.ANY)] * (2 * blocks) + ([] if first else [vmem]),
        out_specs=vmem,
        out_shape=out_shape,
        scratch_shapes=[
            pltpu.VMEM((blocks, rows, HD), jnp.bfloat16),
            pltpu.VMEM((blocks, rows, HD), jnp.bfloat16),
            pltpu.VMEM((blocks, SEG_ROWS, HD), jnp.bfloat16),
            pltpu.VMEM((blocks, rows // 2, rows), jnp.float32),
            pltpu.SemaphoreType.DMA((3, blocks)),
        ],
        compiler_params=pltpu.CompilerParams(vmem_limit_bytes=(12 + 2 * blocks) * MIB),
        cost_estimate=pl.CostEstimate(
            flops=4 * rows * rows * blocks * HD, bytes_accessed=4 * rows * blocks * HD, transcendentals=rows * rows * blocks
        ),
        name="attend_last" if last else "attend_first" if first else "attend_more",
    )(*operands)


def output_kernel(a_ref, b_ref, wa_ref, wb_ref, x_ref, sum_ref, out_exp_ref, out_ref):
    rows, width = x_ref.shape
    groups = sum_ref.shape[0]

    def bounds(ref):
        power = jnp.left_shift(jnp.int32(1), ref[...] - MIN_EXP).astype(jnp.float32)
        return jnp.transpose(power * (LIMIT * 2.0 ** MIN_EXP))

    def clip(value, bound):
        return jnp.minimum(jnp.maximum(value.astype(jnp.bfloat16), -bound), bound)

    sum_bound, out_bound = bounds(sum_ref), bounds(out_exp_ref)
    per = width // groups
    chunk = 2 * per
    a, b = a_ref[...], b_ref[...]
    for start in range(0, width, chunk):
        term_a = jnp.dot(a, wa_ref[:, start:start + chunk], preferred_element_type=jnp.float32)
        term_b = jnp.dot(b, wb_ref[:, start:start + chunk], preferred_element_type=jnp.float32)
        for part in range(2):
            cols = slice(part * per, (part + 1) * per)
            group = (start + part * per) // per
            span = slice(start + part * per, start + (part + 1) * per)
            bound = jnp.broadcast_to(sum_bound[:, group:group + 1], (rows, per)).astype(jnp.bfloat16)
            last = jnp.broadcast_to(out_bound[:, group:group + 1], (rows, per)).astype(jnp.bfloat16)
            quant_a = clip(term_a[:, cols], bound).astype(jnp.float32)
            quant_b = clip(term_b[:, cols], bound).astype(jnp.float32)
            combined = x_ref[:, span].astype(jnp.float32) + (quant_a + quant_b)
            out_ref[:, span] = clip(combined, last)


def project_out(att_a, att_b, w_a, w_b, tokens, sum_exps, out_exps):
    rows, width = tokens.shape
    depth = att_a.shape[1]
    groups = sum_exps.shape[1]
    steps = groups // 8
    tile = width // steps
    whole = pl.BlockSpec((rows, depth), lambda i: (0, 0))
    weight = pl.BlockSpec((depth, tile), lambda i: (0, i))
    wide = pl.BlockSpec((rows, tile), lambda i: (0, i))
    exps = pl.BlockSpec((groups // steps, rows), lambda i: (i, 0))
    return pl.pallas_call(
        output_kernel,
        grid=(steps,),
        in_specs=[whole, whole, weight, weight, wide, exps, exps],
        out_specs=wide,
        out_shape=jax.ShapeDtypeStruct((rows, width), jnp.bfloat16),
        compiler_params=pltpu.CompilerParams(vmem_limit_bytes=20 * MIB),
        cost_estimate=pl.CostEstimate(
            flops=4 * rows * width * depth, bytes_accessed=4 * rows * width + 4 * width * depth, transcendentals=0
        ),
        name="project_out",
    )(att_a, att_b, w_a, w_b, tokens, sum_exps.T, out_exps.T)


def on_device(seq_size, tokens, gain, segments, w_query, w_keyval, w_out, sum_exps, out_exps):
    window = seq_size // 2

    def swap_cores(x):
        return lax.ppermute(x, "tp", [(0, 1), (1, 0)])

    def shift(x, step):
        return lax.ppermute(x, "seq", [(i, (i + step) % seq_size) for i in range(seq_size)])

    w_other = swap_cores(w_out)
    message, normed = norm_kv(tokens, gain, w_keyval, segments)
    query = project_query(normed, w_query)
    held, query = lax.optimization_barrier((shift(message, 2), query))
    odd = lax.rem(lax.axis_index("seq"), 2) == 1
    beside = lax.ppermute(jnp.where(odd, held, message), "seq", [(i, i ^ 1) for i in range(seq_size)])
    parts = [[(0, message), (2, held)], [(1, beside)]]
    for back in range(2, window, 2):
        parts[-1].append((back + 1, shift(held, 1)))
        held = shift(held, 2)
        if back + 2 < window:
            parts[-1].append((back + 2, held))
        else:
            parts.append([(window, held)])
    state = None
    for number, blocks in enumerate(parts):
        plan = [(back, back == window) for back, _ in blocks]
        mine = [block for _, block in blocks]
        if number == len(parts) - 1:
            mine[0], early = lax.optimization_barrier((mine[0], early))
        early = state
        state = attend(query, segments, plan, mine, [swap_cores(m) for m in mine], state, number == len(parts) - 1)
    return project_out(state, swap_cores(state), w_out, w_other, tokens, sum_exps, out_exps)


def solution(mesh):
    in_specs = (
        P(("groups", "seq"), None),
        P(),
        P(("groups", "seq")),
        P(None, "tp"),
        P(None, "tp"),
        P("tp", None),
        P(("groups", "seq"), None),
        P(("groups", "seq"), None),
    )
    out_specs = P(("groups", "seq"), None)
    return jax.shard_map(
        functools.partial(on_device, mesh.shape["seq"]),
        mesh=mesh, in_specs=in_specs, out_specs=out_specs, check_vma=False,
    )
```

```python
import functools

import jax
import jax.numpy as jnp
from jax import lax
from jax.experimental import pallas as pl
from jax.experimental.pallas import tpu as pltpu
from jax.sharding import PartitionSpec as P

HD = 256
LANES = 128
SEG_ROWS = 16
LIMIT = 448.0
MIN_EXP = -9
NEG = -1e30
MIB = 1024 * 1024
NT = (((1,), (1,)), ((), ()))
FACTOR = HD ** (-0.5) * 1.4426950408889634


def norm_kv_kernel(x_ref, gain_hbm, w_ref, seg_hbm, msg_ref, normed_ref, xs, ws, gain_ref, seg_ref, sems):
    rows, width = xs.shape
    tile, part = rows // 2, rows // 4

    def tokens_copy(i):
        return pltpu.make_async_copy(x_ref.at[pl.ds(i * part, part)], xs.at[pl.ds(i * part, part)], sems.at[i])

    def weights_copy():
        return pltpu.make_async_copy(w_ref, ws, sems.at[4])

    def gain_copy():
        return pltpu.make_async_copy(gain_hbm, gain_ref, sems.at[5])

    def segments_copy():
        return pltpu.make_async_copy(seg_hbm, seg_ref, sems.at[6])

    tokens_copy(0).start()
    tokens_copy(1).start()
    gain_copy().start()
    segments_copy().start()
    weights_copy().start()
    tokens_copy(2).start()
    tokens_copy(3).start()
    def wide(first, count, start):
        return xs[first:first + count, start:start + LANES].astype(jnp.float32)

    ones = jnp.ones((width, LANES), jnp.bfloat16)

    def stats(first):
        total = jnp.dot(xs[first:first + part, :], ones, preferred_element_type=jnp.float32)
        mean = total * (1.0 / width)
        square = jnp.zeros((part, LANES), jnp.float32)
        for start in range(0, width, LANES):
            center = wide(first, part, start) - mean
            square = square + center * center
        spread = jnp.sum(square, axis=1, keepdims=True) * (1.0 / width)
        return mean, jnp.broadcast_to(lax.rsqrt(spread + 1e-05), (part, LANES))

    for first in range(0, rows, tile):
        halves = []
        for at in range(first, first + tile, part):
            tokens_copy(at // part).wait()
            halves.append(stats(at))
        mean = jnp.concatenate([h[0] for h in halves], axis=0)
        scale = jnp.concatenate([h[1] for h in halves], axis=0)
        if first == 0:
            gain_copy().wait()
            weights_copy().wait()
        kv = jnp.zeros((tile, ws.shape[1]), jnp.float32)
        span = slice(first, first + tile)
        for start in range(0, width, HD):
            for at in (start, start + LANES):
                normed = (wide(first, tile, at) - mean) * scale * gain_ref[:, at:at + LANES]
                normed_ref[span, at:at + LANES] = normed.astype(jnp.bfloat16)
            kv = kv + jnp.dot(
                normed_ref[span, start:start + HD], ws[start:start + HD, :], preferred_element_type=jnp.float32
            )
        msg_ref[span, :] = kv.astype(jnp.bfloat16)
    segments_copy().wait()
    seg = seg_ref[...].astype(jnp.float32)
    low = jnp.broadcast_to(seg[:, :HD], (8, HD))
    high = jnp.broadcast_to(seg[:, HD:], (8, HD))
    msg_ref[rows:, :] = jnp.concatenate([low, high], axis=0).astype(jnp.bfloat16)


def in_hbm(x):
    return pltpu.with_memory_space_constraint(x, pltpu.HBM)


def in_vmem(x):
    return pltpu.with_memory_space_constraint(x, pltpu.VMEM)


def norm_kv(tokens, gain, w_keyval, segments):
    rows, width = tokens.shape
    cols = w_keyval.shape[1]
    vmem, hbm = pl.BlockSpec(memory_space=pltpu.VMEM), pl.BlockSpec(memory_space=pltpu.HBM)
    return pl.pallas_call(
        norm_kv_kernel,
        in_specs=[hbm] * 4,
        out_specs=[vmem, vmem],
        out_shape=[pltpu.VMEM((rows + SEG_ROWS, cols), jnp.bfloat16), pltpu.VMEM((rows, width), jnp.bfloat16)],
        scratch_shapes=[
            pltpu.VMEM((rows, width), jnp.bfloat16),
            pltpu.VMEM((width, cols), jnp.bfloat16),
            pltpu.VMEM((1, width), jnp.float32),
            pltpu.VMEM((1, rows), jnp.int32),
            pltpu.SemaphoreType.DMA((7,)),
        ],
        compiler_params=pltpu.CompilerParams(vmem_limit_bytes=24 * MIB),
        cost_estimate=pl.CostEstimate(
            flops=2 * rows * width * cols, bytes_accessed=4 * rows * width + 2 * width * cols, transcendentals=0
        ),
        name="norm_kv",
    )(in_hbm(tokens), in_hbm(gain.reshape(1, width)), in_hbm(w_keyval), in_hbm(segments.reshape(1, rows)))


def query_kernel(x_ref, w_ref, out_ref):
    out_ref[...] = jnp.dot(x_ref[...], w_ref[...], preferred_element_type=jnp.float32).astype(jnp.bfloat16)


def project_query(normed, w_query):
    rows, width = normed.shape
    cols = w_query.shape[1]
    vmem = pl.BlockSpec(memory_space=pltpu.VMEM)
    return pl.pallas_call(
        query_kernel,
        in_specs=[vmem, vmem],
        out_specs=vmem,
        out_shape=pltpu.VMEM((rows, cols), jnp.bfloat16),
        compiler_params=pltpu.CompilerParams(vmem_limit_bytes=8 * MIB),
        cost_estimate=pl.CostEstimate(
            flops=2 * rows * width * cols, bytes_accessed=2 * rows * width + 2 * width * cols, transcendentals=0
        ),
        name="project_query",
    )(in_vmem(normed), in_vmem(w_query))


def attend_kernel(plan, first, last, *refs):
    blocks = len(plan)
    q_ref, seg_ref = refs[:2]
    mine, other = refs[2:2 + blocks], refs[2 + blocks:2 + 2 * blocks]
    refs = refs[2 + 2 * blocks:]
    state_ref = None
    if not first:
        state_ref, refs = refs[0], refs[1:]
    out_ref, scores = refs
    rows = q_ref.shape[0]
    tile = rows // 2
    part = lax.axis_index("tp")
    place = lax.axis_index("seq")

    def finish(span, weighted, total):
        out_ref[span, :] = (weighted / jnp.sum(total, axis=1, keepdims=True)).astype(jnp.bfloat16)

    def update(count, keys, values):
        own_seg = jnp.transpose(jnp.broadcast_to(seg_ref[...].astype(jnp.float32), (8, rows)))[:, 0:1]
        key_segs = []
        for slot in range(count):
            packed = mine[slot][rows:, :].astype(jnp.float32)
            key_segs.append(jnp.concatenate([packed[0:1, :], packed[8:9, :]], axis=1))
        for start in range(0, rows, tile):
            span = slice(start, start + tile)
            query = q_ref[span, :]
            best = None if first else state_ref[span, HD:HD + LANES]
            bounds = []
            for slot, (back, furthest) in enumerate(plan[:count]):
                low, high = 0, rows
                if back == 0:
                    high = start + tile
                elif furthest:
                    low = start
                bounds.append((low, high))
                raw = lax.dot_general(query, keys[slot][low:high, :], NT, preferred_element_type=jnp.float32)
                allowed = key_segs[slot][:, low:high] == own_seg[span, :]
                if back == 0:
                    row_pos = start + lax.broadcasted_iota(jnp.int32, raw.shape, 0)
                    allowed = allowed & (lax.broadcasted_iota(jnp.int32, raw.shape, 1) <= row_pos)
                masked = jnp.where(allowed, raw, NEG)
                scores[slot, :, low:high] = masked
                for at in range(0, high - low, LANES):
                    piece = masked[:, at:at + LANES]
                    best = piece if best is None else jnp.maximum(best, piece)
            top = jnp.broadcast_to(jnp.max(best, axis=1, keepdims=True), (tile, LANES))
            if first:
                total = jnp.zeros((tile, LANES), jnp.float32)
                weighted = jnp.zeros((tile, HD), jnp.float32)
            else:
                shrink = jnp.exp2((state_ref[span, HD:HD + LANES] - top) * FACTOR)
                total = state_ref[span, HD + LANES:] * shrink
                weighted = state_ref[span, :HD] * jnp.concatenate([shrink, shrink], axis=1)
            for slot in range(count):
                low, high = bounds[slot]
                pieces = []
                for at in range(low, high, LANES):
                    weights = jnp.exp2((scores[slot, :, at:at + LANES] - top) * FACTOR)
                    total = total + weights
                    pieces.append(weights.astype(jnp.bfloat16))
                probs = jnp.concatenate(pieces, axis=1)
                weighted = weighted + jnp.dot(probs, values[slot][low:high, :], preferred_element_type=jnp.float32)
            if last:
                finish(span, weighted, total)
            else:
                out_ref[span, :HD] = weighted
                out_ref[span, HD:HD + LANES] = top
                out_ref[span, HD + LANES:] = total

    for count in range(1 if first else 0, blocks + 1):
        reached = place >= (plan[count - 1][0] if count > 0 else 0)
        if count < blocks:
            reached = reached & (place < plan[count][0])
        if count > 0:
            pl.when(reached & (part == 0))(functools.partial(update, count, mine, other))
            pl.when(reached & (part == 1))(functools.partial(update, count, other, mine))
        elif last:

            @pl.when(reached)
            def _():
                finish(slice(0, rows), state_ref[:, :HD], state_ref[:, HD + LANES:])


def attend(query, segments, plan, mine, other, state, last):
    rows = query.shape[0]
    blocks = len(plan)
    vmem = pl.BlockSpec(memory_space=pltpu.VMEM)
    first = state is None
    operands = [query, segments.reshape(1, rows), *mine, *other] + ([] if first else [state])
    return pl.pallas_call(
        functools.partial(attend_kernel, plan, first, last),
        in_specs=[vmem] * len(operands),
        out_specs=vmem,
        out_shape=pltpu.VMEM((rows, HD), jnp.bfloat16) if last else pltpu.VMEM((rows, HD + 2 * LANES), jnp.float32),
        scratch_shapes=[pltpu.VMEM((blocks, rows // 2, rows), jnp.float32)],
        input_output_aliases={} if first or last else {len(operands) - 1: 0},
        compiler_params=pltpu.CompilerParams(vmem_limit_bytes=12 * MIB),
        cost_estimate=pl.CostEstimate(
            flops=4 * rows * rows * blocks * HD, bytes_accessed=4 * rows * blocks * HD, transcendentals=rows * rows * blocks
        ),
        name="attend_last" if last else "attend_first" if first else "attend_more",
    )(*[in_vmem(operand) for operand in operands])


def bounds_kernel(sum_ref, out_exp_ref, sum_bound_ref, out_bound_ref):
    groups, rows = sum_ref.shape
    per = sum_bound_ref.shape[1] // groups
    for exps, bound_ref in ((sum_ref, sum_bound_ref), (out_exp_ref, out_bound_ref)):
        power = jnp.left_shift(jnp.int32(1), exps[...] - MIN_EXP).astype(jnp.float32)
        bound = jnp.transpose(power * (LIMIT * 2.0 ** MIN_EXP))
        for group in range(groups):
            wide = jnp.broadcast_to(bound[:, group:group + 1], (rows, per))
            bound_ref[:, group * per:(group + 1) * per] = wide.astype(jnp.bfloat16)


def spread_bounds(sum_exps, out_exps, width):
    rows, groups = sum_exps.shape
    vmem = pl.BlockSpec(memory_space=pltpu.VMEM)
    return pl.pallas_call(
        bounds_kernel,
        in_specs=[vmem, vmem],
        out_specs=[vmem, vmem],
        out_shape=[pltpu.VMEM((rows, width), jnp.bfloat16)] * 2,
        compiler_params=pltpu.CompilerParams(vmem_limit_bytes=8 * MIB),
        cost_estimate=pl.CostEstimate(flops=8 * rows * width, bytes_accessed=8 * rows * groups, transcendentals=0),
        name="spread_bounds",
    )(sum_exps.T, out_exps.T)


def output_kernel(a_ref, b_ref, wa_ref, wb_ref, x_ref, sum_ref, last_ref, out_ref, staged, sems):
    rows, width = x_ref.shape
    steps = sems.shape[0]
    chunk = width // steps
    tile = rows // 2

    def clip(value, bound):
        return jnp.minimum(jnp.maximum(value.astype(jnp.bfloat16), -bound), bound)

    def copy(step):
        span = pl.ds(pl.multiple_of(step * chunk, chunk), chunk)
        return pltpu.make_async_copy(staged.at[:, span], out_ref.at[:, span], sems.at[step])

    def body(step, carry):
        for at in range(0, chunk, HD):
            cols = pl.ds(pl.multiple_of(step * chunk + at, HD), HD)
            weights_a, weights_b = wa_ref[:, cols], wb_ref[:, cols]
            for start in range(0, rows, tile):
                span = slice(start, start + tile)
                term_a = jnp.dot(a_ref[span, :], weights_a, preferred_element_type=jnp.float32)
                term_b = jnp.dot(b_ref[span, :], weights_b, preferred_element_type=jnp.float32)
                bound = sum_ref[span, cols]
                quant = clip(term_a, bound).astype(jnp.float32) + clip(term_b, bound).astype(jnp.float32)
                staged[span, cols] = clip(x_ref[span, cols].astype(jnp.float32) + quant, last_ref[span, cols])
        copy(step).start()
        return carry

    lax.fori_loop(0, steps, body, 0)
    for step in range(steps):
        copy(step).wait()


def project_out(att_a, att_b, w_a, w_b, tokens, sum_bound, out_bound):
    rows, width = tokens.shape
    depth = att_a.shape[1]
    steps = 4
    vmem = pl.BlockSpec(memory_space=pltpu.VMEM)
    operands = [att_a, att_b, w_a, w_b, tokens, sum_bound, out_bound]
    return pl.pallas_call(
        output_kernel,
        in_specs=[vmem] * len(operands),
        out_specs=pl.BlockSpec(memory_space=pltpu.HBM),
        out_shape=jax.ShapeDtypeStruct((rows, width), jnp.bfloat16),
        scratch_shapes=[pltpu.VMEM((rows, width), jnp.bfloat16), pltpu.SemaphoreType.DMA((steps,))],
        compiler_params=pltpu.CompilerParams(vmem_limit_bytes=12 * MIB),
        cost_estimate=pl.CostEstimate(
            flops=4 * rows * width * depth, bytes_accessed=4 * rows * width + 4 * width * depth, transcendentals=0
        ),
        name="project_out",
    )(*[in_vmem(operand) for operand in operands])


def on_device(seq_size, tokens, gain, segments, w_query, w_keyval, w_out, sum_exps, out_exps):
    window = seq_size // 2

    def swap_cores(x):
        return lax.ppermute(x, "tp", [(0, 1), (1, 0)])

    def shift(x, step):
        return lax.ppermute(x, "seq", [(i, (i + step) % seq_size) for i in range(seq_size)])

    w_other = swap_cores(w_out)
    message, normed = norm_kv(tokens, gain, w_keyval, segments)
    query = project_query(normed, w_query)
    held, query = lax.optimization_barrier((shift(message, 2), query))
    odd = lax.rem(lax.axis_index("seq"), 2) == 1
    beside = lax.ppermute(jnp.where(odd, held, message), "seq", [(i, i ^ 1) for i in range(seq_size)])
    parts = [[(0, message), (2, held)]]
    for back in range(2, window, 2):
        step = shift(held, 1)
        held = shift(held, 2)
        parts.append([(back + 1, step)] + ([(back + 2, held)] if back + 2 < window else []))
    parts.append([(1, beside), (window, held)])
    exps = lax.optimization_barrier((sum_exps, out_exps, query))[:2]
    bounds = spread_bounds(*exps, tokens.shape[1])
    state = None
    for number, blocks in enumerate(parts):
        plan = [(back, back == window) for back, _ in blocks]
        mine = [block for _, block in blocks]
        if number == 1:
            bounds, state = early = lax.optimization_barrier((bounds, state))
        if number > 0:
            mine = [lax.optimization_barrier((block, early))[0] for block in mine]
        other = [swap_cores(m) for m in mine]
        state = attend(query, segments, plan, mine, other, state, number == len(parts) - 1)
    return project_out(state, swap_cores(state), w_out, w_other, tokens, *bounds)


def solution(mesh):
    in_specs = (
        P(("groups", "seq"), None),
        P(),
        P(("groups", "seq")),
        P(None, "tp"),
        P(None, "tp"),
        P("tp", None),
        P(("groups", "seq"), None),
        P(("groups", "seq"), None),
    )
    out_specs = P(("groups", "seq"), None)
    return jax.shard_map(
        functools.partial(on_device, mesh.shape["seq"]),
        mesh=mesh, in_specs=in_specs, out_specs=out_specs, check_vma=False,
    )
```

```python
import functools

import jax
import jax.numpy as jnp
from jax import lax
from jax.experimental import pallas as pl
from jax.experimental.pallas import tpu as pltpu
from jax.sharding import PartitionSpec as P

HD = 256
LANES = 128
SEG_ROWS = 16
LIMIT = 448.0
MIN_EXP = -9
NEG = -1e30
MIB = 1024 * 1024
NT = (((1,), (1,)), ((), ()))
FACTOR = HD ** (-0.5) * 1.4426950408889634


def norm_kv_kernel(x_ref, gain_hbm, w_ref, seg_hbm, msg_ref, normed_ref, xs, ws, gain_ref, seg_ref, sems):
    rows, width = xs.shape
    tile, part = rows // 2, rows // 8
    pieces = 4
    deep = width // pieces

    def tokens_copy(i):
        return pltpu.make_async_copy(x_ref.at[pl.ds(i * part, part)], xs.at[pl.ds(i * part, part)], sems.at[i])

    def weights_copy(i):
        return pltpu.make_async_copy(w_ref.at[pl.ds(i * deep, deep)], ws.at[pl.ds(i * deep, deep)], sems.at[8 + i])

    def gain_copy():
        return pltpu.make_async_copy(gain_hbm, gain_ref, sems.at[12])

    def segments_copy():
        return pltpu.make_async_copy(seg_hbm, seg_ref, sems.at[13])

    for i in range(4):
        tokens_copy(i).start()
    gain_copy().start()
    for i in range(pieces):
        weights_copy(i).start()
    for i in range(4, 8):
        tokens_copy(i).start()
    segments_copy().start()

    def wide(first, count, start):
        return xs[first:first + count, start:start + LANES].astype(jnp.float32)

    def stats(first):
        total = wide(first, part, 0)
        for start in range(LANES, width, LANES):
            total = total + wide(first, part, start)
        mean = jnp.broadcast_to(jnp.sum(total, axis=1, keepdims=True) * (1.0 / width), (part, LANES))
        square = jnp.zeros((part, LANES), jnp.float32)
        for start in range(0, width, LANES):
            center = wide(first, part, start) - mean
            square = square + center * center
        spread = jnp.sum(square, axis=1, keepdims=True) * (1.0 / width)
        return mean, jnp.broadcast_to(lax.rsqrt(spread + 1e-05), (part, LANES))

    for first in range(0, rows, tile):
        halves = []
        for at in range(first, first + tile, part):
            tokens_copy(at // part).wait()
            halves.append(stats(at))
        mean = jnp.concatenate([h[0] for h in halves], axis=0)
        scale = jnp.concatenate([h[1] for h in halves], axis=0)
        if first == 0:
            gain_copy().wait()
            for i in range(pieces):
                weights_copy(i).wait()
        kv = jnp.zeros((tile, ws.shape[1]), jnp.float32)
        span = slice(first, first + tile)
        for start in range(0, width, HD):
            for at in (start, start + LANES):
                normed = (wide(first, tile, at) - mean) * scale * gain_ref[:, at:at + LANES]
                normed_ref[span, at:at + LANES] = normed.astype(jnp.bfloat16)
            kv = kv + jnp.dot(
                normed_ref[span, start:start + HD], ws[start:start + HD, :], preferred_element_type=jnp.float32
            )
        msg_ref[span, :] = kv.astype(jnp.bfloat16)
    segments_copy().wait()
    seg = seg_ref[...].astype(jnp.float32)
    low = jnp.broadcast_to(seg[:, :HD], (8, HD))
    high = jnp.broadcast_to(seg[:, HD:], (8, HD))
    msg_ref[rows:, :] = jnp.concatenate([low, high], axis=0).astype(jnp.bfloat16)


def in_hbm(x):
    return pltpu.with_memory_space_constraint(x, pltpu.HBM)


def in_vmem(x):
    return pltpu.with_memory_space_constraint(x, pltpu.VMEM)


def norm_kv(tokens, gain, w_keyval, segments):
    rows, width = tokens.shape
    cols = w_keyval.shape[1]
    vmem, hbm = pl.BlockSpec(memory_space=pltpu.VMEM), pl.BlockSpec(memory_space=pltpu.HBM)
    return pl.pallas_call(
        norm_kv_kernel,
        in_specs=[hbm] * 4,
        out_specs=[vmem, vmem],
        out_shape=[pltpu.VMEM((rows + SEG_ROWS, cols), jnp.bfloat16), pltpu.VMEM((rows, width), jnp.bfloat16)],
        scratch_shapes=[
            pltpu.VMEM((rows, width), jnp.bfloat16),
            pltpu.VMEM((width, cols), jnp.bfloat16),
            pltpu.VMEM((1, width), jnp.float32),
            pltpu.VMEM((1, rows), jnp.int32),
            pltpu.SemaphoreType.DMA((14,)),
        ],
        compiler_params=pltpu.CompilerParams(vmem_limit_bytes=24 * MIB),
        cost_estimate=pl.CostEstimate(
            flops=2 * rows * width * cols, bytes_accessed=4 * rows * width + 2 * width * cols, transcendentals=0
        ),
        name="norm_kv",
    )(in_hbm(tokens), in_hbm(gain.reshape(1, width)), in_hbm(w_keyval), in_hbm(segments.reshape(1, rows)))


def query_kernel(x_ref, w_ref, out_ref):
    out_ref[...] = jnp.dot(x_ref[...], w_ref[...], preferred_element_type=jnp.float32).astype(jnp.bfloat16)


def project_query(normed, w_query):
    rows, width = normed.shape
    cols = w_query.shape[1]
    vmem = pl.BlockSpec(memory_space=pltpu.VMEM)
    return pl.pallas_call(
        query_kernel,
        in_specs=[vmem, vmem],
        out_specs=vmem,
        out_shape=pltpu.VMEM((rows, cols), jnp.bfloat16),
        compiler_params=pltpu.CompilerParams(vmem_limit_bytes=8 * MIB),
        cost_estimate=pl.CostEstimate(
            flops=2 * rows * width * cols, bytes_accessed=2 * rows * width + 2 * width * cols, transcendentals=0
        ),
        name="project_query",
    )(in_vmem(normed), in_vmem(w_query))


def attend_kernel(plan, first, last, *refs):
    blocks = len(plan)
    q_ref, seg_ref = refs[:2]
    mine, other = refs[2:2 + blocks], refs[2 + blocks:2 + 2 * blocks]
    refs = refs[2 + 2 * blocks:]
    state_ref = None
    if not first:
        state_ref, refs = refs[0], refs[1:]
    out_ref, scores = refs
    rows = q_ref.shape[0]
    tile = rows // 2
    part = lax.axis_index("tp")
    place = lax.axis_index("seq")

    def finish(span, weighted, total):
        out_ref[span, :] = (weighted / jnp.sum(total, axis=1, keepdims=True)).astype(jnp.bfloat16)

    def update(count, keys, values):
        own_seg = jnp.transpose(jnp.broadcast_to(seg_ref[...].astype(jnp.float32), (8, rows)))[:, 0:1]
        key_segs = []
        for slot in range(count):
            packed = mine[slot][rows:, :].astype(jnp.float32)
            key_segs.append(jnp.concatenate([packed[0:1, :], packed[8:9, :]], axis=1))
        for start in range(0, rows, tile):
            span = slice(start, start + tile)
            query = q_ref[span, :]
            best = None if first else state_ref[span, HD:HD + LANES]
            bounds = []
            for slot, (back, furthest) in enumerate(plan[:count]):
                low, high = 0, rows
                if back == 0:
                    high = start + tile
                elif furthest:
                    low = start
                bounds.append((low, high))
                raw = lax.dot_general(query, keys[slot][low:high, :], NT, preferred_element_type=jnp.float32)
                allowed = key_segs[slot][:, low:high] == own_seg[span, :]
                if back == 0:
                    row_pos = start + lax.broadcasted_iota(jnp.int32, raw.shape, 0)
                    allowed = allowed & (lax.broadcasted_iota(jnp.int32, raw.shape, 1) <= row_pos)
                masked = jnp.where(allowed, raw, NEG)
                scores[slot, :, low:high] = masked
                for at in range(0, high - low, LANES):
                    piece = masked[:, at:at + LANES]
                    best = piece if best is None else jnp.maximum(best, piece)
            top = jnp.broadcast_to(jnp.max(best, axis=1, keepdims=True), (tile, LANES))
            if first:
                total = jnp.zeros((tile, LANES), jnp.float32)
                weighted = jnp.zeros((tile, HD), jnp.float32)
            else:
                shrink = jnp.exp2((state_ref[span, HD:HD + LANES] - top) * FACTOR)
                total = state_ref[span, HD + LANES:] * shrink
                weighted = state_ref[span, :HD] * jnp.concatenate([shrink, shrink], axis=1)
            for slot in range(count):
                low, high = bounds[slot]
                pieces = []
                for at in range(low, high, LANES):
                    weights = jnp.exp2((scores[slot, :, at:at + LANES] - top) * FACTOR)
                    total = total + weights
                    pieces.append(weights.astype(jnp.bfloat16))
                probs = jnp.concatenate(pieces, axis=1)
                weighted = weighted + jnp.dot(probs, values[slot][low:high, :], preferred_element_type=jnp.float32)
            if last:
                finish(span, weighted, total)
            else:
                out_ref[span, :HD] = weighted
                out_ref[span, HD:HD + LANES] = top
                out_ref[span, HD + LANES:] = total

    for count in range(1 if first else 0, blocks + 1):
        reached = place >= (plan[count - 1][0] if count > 0 else 0)
        if count < blocks:
            reached = reached & (place < plan[count][0])
        if count > 0:
            pl.when(reached & (part == 0))(functools.partial(update, count, mine, other))
            pl.when(reached & (part == 1))(functools.partial(update, count, other, mine))
        elif last:

            @pl.when(reached)
            def _():
                finish(slice(0, rows), state_ref[:, :HD], state_ref[:, HD + LANES:])


def attend(query, segments, plan, mine, other, state, last):
    rows = query.shape[0]
    blocks = len(plan)
    vmem = pl.BlockSpec(memory_space=pltpu.VMEM)
    first = state is None
    operands = [query, segments.reshape(1, rows), *mine, *other] + ([] if first else [state])
    return pl.pallas_call(
        functools.partial(attend_kernel, plan, first, last),
        in_specs=[vmem] * len(operands),
        out_specs=vmem,
        out_shape=pltpu.VMEM((rows, HD), jnp.bfloat16) if last else pltpu.VMEM((rows, HD + 2 * LANES), jnp.float32),
        scratch_shapes=[pltpu.VMEM((blocks, rows // 2, rows), jnp.float32)],
        input_output_aliases={} if first or last else {len(operands) - 1: 0},
        compiler_params=pltpu.CompilerParams(vmem_limit_bytes=12 * MIB),
        cost_estimate=pl.CostEstimate(
            flops=4 * rows * rows * blocks * HD, bytes_accessed=4 * rows * blocks * HD, transcendentals=rows * rows * blocks
        ),
        name="attend_last" if last else "attend_first" if first else "attend_more",
    )(*[in_vmem(operand) for operand in operands])


def bounds_kernel(sum_ref, out_exp_ref, x_ref, sum_bound_ref, out_bound_ref, near_ref, sem):
    groups, rows = sum_ref.shape
    fetch = pltpu.make_async_copy(x_ref, near_ref, sem)
    fetch.start()
    per = sum_bound_ref.shape[1] // groups
    for exps, bound_ref in ((sum_ref, sum_bound_ref), (out_exp_ref, out_bound_ref)):
        power = jnp.left_shift(jnp.int32(1), exps[...] - MIN_EXP).astype(jnp.float32)
        bound = jnp.transpose(power * (LIMIT * 2.0 ** MIN_EXP))
        for group in range(groups):
            wide = jnp.broadcast_to(bound[:, group:group + 1], (rows, per))
            bound_ref[:, group * per:(group + 1) * per] = wide.astype(jnp.bfloat16)
    fetch.wait()


def spread_bounds(sum_exps, out_exps, tokens):
    rows, width = tokens.shape
    groups = sum_exps.shape[1]
    vmem = pl.BlockSpec(memory_space=pltpu.VMEM)
    return pl.pallas_call(
        bounds_kernel,
        in_specs=[vmem, vmem, pl.BlockSpec(memory_space=pltpu.HBM)],
        out_specs=[vmem] * 3,
        out_shape=[pltpu.VMEM((rows, width), jnp.bfloat16)] * 3,
        scratch_shapes=[pltpu.SemaphoreType.DMA(())],
        compiler_params=pltpu.CompilerParams(vmem_limit_bytes=8 * MIB),
        cost_estimate=pl.CostEstimate(flops=8 * rows * width, bytes_accessed=8 * rows * groups, transcendentals=0),
        name="spread_bounds",
    )(in_vmem(sum_exps.T), in_vmem(out_exps.T), in_hbm(tokens))


def clip(value, bound):
    return jnp.minimum(jnp.maximum(value.astype(jnp.bfloat16), -bound), bound)


def own_kernel(a_ref, w_ref, sum_ref, out_ref):
    rows, width = out_ref.shape
    tile = rows // 2
    chunk = width // 4

    def body(step, carry):
        for at in range(0, chunk, HD):
            cols = pl.ds(pl.multiple_of(step * chunk + at, HD), HD)
            weights = w_ref[:, cols]
            for start in range(0, rows, tile):
                span = slice(start, start + tile)
                term = jnp.dot(a_ref[span, :], weights, preferred_element_type=jnp.float32)
                out_ref[span, cols] = clip(term, sum_ref[span, cols])
        return carry

    lax.fori_loop(0, 4, body, 0)


def project_own(attended, w_out, sum_bound):
    rows, depth = attended.shape
    width = w_out.shape[1]
    vmem = pl.BlockSpec(memory_space=pltpu.VMEM)
    return pl.pallas_call(
        own_kernel,
        in_specs=[vmem] * 3,
        out_specs=vmem,
        out_shape=pltpu.VMEM((rows, width), jnp.bfloat16),
        compiler_params=pltpu.CompilerParams(vmem_limit_bytes=8 * MIB),
        cost_estimate=pl.CostEstimate(
            flops=2 * rows * width * depth, bytes_accessed=4 * rows * width + 2 * width * depth, transcendentals=0
        ),
        name="project_own",
    )(in_vmem(attended), in_vmem(w_out), in_vmem(sum_bound))


def output_kernel(b_ref, wb_ref, quant_ref, x_ref, sum_ref, last_ref, out_ref, staged, sems):
    rows, width = x_ref.shape
    steps = sems.shape[0]
    chunk = width // steps
    tile = rows // 2

    def copy(step):
        span = pl.ds(pl.multiple_of(step * chunk, chunk), chunk)
        return pltpu.make_async_copy(staged.at[:, span], out_ref.at[:, span], sems.at[step])

    def body(step, carry):
        for at in range(0, chunk, HD):
            cols = pl.ds(pl.multiple_of(step * chunk + at, HD), HD)
            weights = wb_ref[:, cols]
            for start in range(0, rows, tile):
                span = slice(start, start + tile)
                term = jnp.dot(b_ref[span, :], weights, preferred_element_type=jnp.float32)
                quant = clip(term, sum_ref[span, cols]).astype(jnp.float32) + quant_ref[span, cols].astype(jnp.float32)
                staged[span, cols] = clip(x_ref[span, cols].astype(jnp.float32) + quant, last_ref[span, cols])
        copy(step).start()
        return carry

    lax.fori_loop(0, steps, body, 0)
    for step in range(steps):
        copy(step).wait()


def project_out(att_other, w_other, quant_own, sum_bound, out_bound, tokens):
    rows, width = tokens.shape
    depth = att_other.shape[1]
    steps = 4
    vmem = pl.BlockSpec(memory_space=pltpu.VMEM)
    operands = [att_other, w_other, quant_own, tokens, sum_bound, out_bound]
    return pl.pallas_call(
        output_kernel,
        in_specs=[vmem] * len(operands),
        out_specs=pl.BlockSpec(memory_space=pltpu.HBM),
        out_shape=jax.ShapeDtypeStruct((rows, width), jnp.bfloat16),
        scratch_shapes=[pltpu.VMEM((rows, width), jnp.bfloat16), pltpu.SemaphoreType.DMA((steps,))],
        compiler_params=pltpu.CompilerParams(vmem_limit_bytes=12 * MIB),
        cost_estimate=pl.CostEstimate(
            flops=2 * rows * width * depth, bytes_accessed=4 * rows * width + 2 * width * depth, transcendentals=0
        ),
        name="project_out",
    )(*[in_vmem(operand) for operand in operands])


def on_device(seq_size, tokens, gain, segments, w_query, w_keyval, w_out, sum_exps, out_exps):
    window = seq_size // 2

    def swap_cores(x):
        return lax.ppermute(x, "tp", [(0, 1), (1, 0)])

    def shift(x, step, first):
        cycle = seq_size - first
        pairs = []
        for i in range(seq_size):
            for core in range(2):
                after = 2 * (first + (i - first + step) % cycle) + core if i >= first else 2 * i + 1 - core
                pairs.append((2 * i + core, after))
        return lax.ppermute(x, ("seq", "tp"), pairs)

    w_other = swap_cores(w_out)
    message, normed = norm_kv(tokens, gain, w_keyval, segments)
    query = project_query(normed, w_query)
    held, query = lax.optimization_barrier((shift(message, 2, 0), query))
    odd = lax.rem(lax.axis_index("seq"), 2) == 1
    beside = lax.ppermute(jnp.where(odd, held, message), "seq", [(i, i ^ 1) for i in range(seq_size)])
    parts = [[(0, message), (2, held)]]
    for back in range(2, window, 2):
        step = shift(held, 1, back)
        held = shift(held, 2, back)
        parts.append([(back + 1, step)] + ([(back + 2, held)] if back + 2 < window else []))
    parts.append([(1, beside), (window, held)])
    exps = lax.optimization_barrier((sum_exps, out_exps, query))[:2]
    bounds = spread_bounds(*exps, tokens)
    state = None
    for number, blocks in enumerate(parts):
        plan = [(back, back == window) for back, _ in blocks]
        mine = [block for _, block in blocks]
        if number == 1:
            bounds, state = early = lax.optimization_barrier((bounds, state))
        if number > 0:
            mine = [lax.optimization_barrier((block, early))[0] for block in mine]
        other = [swap_cores(m) for m in mine]
        state = attend(query, segments, plan, mine, other, state, number == len(parts) - 1)
    quant_own = project_own(state, w_out, bounds[0])
    return project_out(swap_cores(state), w_other, quant_own, *bounds)


def solution(mesh):
    in_specs = (
        P(("groups", "seq"), None),
        P(),
        P(("groups", "seq")),
        P(None, "tp"),
        P(None, "tp"),
        P("tp", None),
        P(("groups", "seq"), None),
        P(("groups", "seq"), None),
    )
    out_specs = P(("groups", "seq"), None)
    return jax.shard_map(
        functools.partial(on_device, mesh.shape["seq"]),
        mesh=mesh, in_specs=in_specs, out_specs=out_specs, check_vma=False,
    )
```

```python
import functools

import jax
import jax.numpy as jnp
from jax import lax
from jax.experimental import pallas as pl
from jax.experimental.pallas import tpu as pltpu
from jax.sharding import PartitionSpec as P

HD = 256
LANES = 128
SEG_ROWS = 16
LIMIT = 448.0
MIN_EXP = -9
NEG = -1e30
MIB = 1024 * 1024
NT = (((1,), (1,)), ((), ()))
FACTOR = HD ** (-0.5) * 1.4426950408889634


def norm_kv_kernel(x_ref, gain_hbm, w_ref, seg_hbm, msg_ref, normed_ref, xs, ws, gain_ref, seg_ref, sems):
    rows, width = xs.shape
    tile, part = rows // 2, rows // 8
    pieces = 4
    deep = width // pieces

    def tokens_copy(i):
        return pltpu.make_async_copy(x_ref.at[pl.ds(i * part, part)], xs.at[pl.ds(i * part, part)], sems.at[i])

    def weights_copy(i):
        return pltpu.make_async_copy(w_ref.at[pl.ds(i * deep, deep)], ws.at[pl.ds(i * deep, deep)], sems.at[8 + i])

    def gain_copy():
        return pltpu.make_async_copy(gain_hbm, gain_ref, sems.at[12])

    def segments_copy():
        return pltpu.make_async_copy(seg_hbm, seg_ref, sems.at[13])

    for i in range(4):
        tokens_copy(i).start()
    gain_copy().start()
    for i in range(pieces):
        weights_copy(i).start()
    for i in range(4, 8):
        tokens_copy(i).start()
    segments_copy().start()

    def wide(first, count, start):
        return xs[first:first + count, start:start + LANES].astype(jnp.float32)

    def stats(first):
        total = wide(first, part, 0)
        for start in range(LANES, width, LANES):
            total = total + wide(first, part, start)
        mean = jnp.broadcast_to(jnp.sum(total, axis=1, keepdims=True) * (1.0 / width), (part, LANES))
        square = jnp.zeros((part, LANES), jnp.float32)
        for start in range(0, width, LANES):
            center = wide(first, part, start) - mean
            square = square + center * center
        spread = jnp.sum(square, axis=1, keepdims=True) * (1.0 / width)
        return mean, jnp.broadcast_to(lax.rsqrt(spread + 1e-05), (part, LANES))

    def project(first):
        span = slice(first, first + tile)
        kv = jnp.dot(normed_ref[span, :], ws[...], preferred_element_type=jnp.float32)
        msg_ref[span, :] = kv.astype(jnp.bfloat16)

    for at in range(0, rows, part):
        tokens_copy(at // part).wait()
        mean, scale = stats(at)
        if at == 0:
            gain_copy().wait()
        for start in range(0, width, LANES):
            normed = (wide(at, part, start) - mean) * scale * gain_ref[:, start:start + LANES]
            normed_ref[at:at + part, start:start + LANES] = normed.astype(jnp.bfloat16)
        if at + part == rows - tile:
            for i in range(pieces):
                weights_copy(i).wait()
            project(0)
    project(rows - tile)
    segments_copy().wait()
    seg = seg_ref[...].astype(jnp.float32)
    low = jnp.broadcast_to(seg[:, :HD], (8, HD))
    high = jnp.broadcast_to(seg[:, HD:], (8, HD))
    msg_ref[rows:, :] = jnp.concatenate([low, high], axis=0).astype(jnp.bfloat16)


def in_hbm(x):
    return pltpu.with_memory_space_constraint(x, pltpu.HBM)


def in_vmem(x):
    return pltpu.with_memory_space_constraint(x, pltpu.VMEM)


def norm_kv(tokens, gain, w_keyval, segments):
    rows, width = tokens.shape
    cols = w_keyval.shape[1]
    vmem, hbm = pl.BlockSpec(memory_space=pltpu.VMEM), pl.BlockSpec(memory_space=pltpu.HBM)
    return pl.pallas_call(
        norm_kv_kernel,
        in_specs=[hbm] * 4,
        out_specs=[vmem, vmem],
        out_shape=[pltpu.VMEM((rows + SEG_ROWS, cols), jnp.bfloat16), pltpu.VMEM((rows, width), jnp.bfloat16)],
        scratch_shapes=[
            pltpu.VMEM((rows, width), jnp.bfloat16),
            pltpu.VMEM((width, cols), jnp.bfloat16),
            pltpu.VMEM((1, width), jnp.float32),
            pltpu.VMEM((1, rows), jnp.int32),
            pltpu.SemaphoreType.DMA((14,)),
        ],
        compiler_params=pltpu.CompilerParams(vmem_limit_bytes=24 * MIB),
        cost_estimate=pl.CostEstimate(
            flops=2 * rows * width * cols, bytes_accessed=4 * rows * width + 2 * width * cols, transcendentals=0
        ),
        name="norm_kv",
    )(in_hbm(tokens), in_hbm(gain.reshape(1, width)), in_hbm(w_keyval), in_hbm(segments.reshape(1, rows)))


def query_kernel(x_ref, w_ref, out_ref):
    out_ref[...] = jnp.dot(x_ref[...], w_ref[...], preferred_element_type=jnp.float32).astype(jnp.bfloat16)


def project_query(normed, w_query):
    rows, width = normed.shape
    cols = w_query.shape[1]
    vmem = pl.BlockSpec(memory_space=pltpu.VMEM)
    return pl.pallas_call(
        query_kernel,
        in_specs=[vmem, vmem],
        out_specs=vmem,
        out_shape=pltpu.VMEM((rows, cols), jnp.bfloat16),
        compiler_params=pltpu.CompilerParams(vmem_limit_bytes=8 * MIB),
        cost_estimate=pl.CostEstimate(
            flops=2 * rows * width * cols, bytes_accessed=2 * rows * width + 2 * width * cols, transcendentals=0
        ),
        name="project_query",
    )(in_vmem(normed), in_vmem(w_query))


def attend_kernel(plan, first, last, *refs):
    blocks = len(plan)
    q_ref, seg_ref = refs[:2]
    mine, other = refs[2:2 + blocks], refs[2 + blocks:2 + 2 * blocks]
    refs = refs[2 + 2 * blocks:]
    state_ref = None
    if not first:
        state_ref, refs = refs[0], refs[1:]
    out_ref, scores = refs
    rows = q_ref.shape[0]
    tile = rows // 2
    part = lax.axis_index("tp")
    place = lax.axis_index("seq")

    def finish(span, weighted, total):
        out_ref[span, :] = (weighted / jnp.sum(total, axis=1, keepdims=True)).astype(jnp.bfloat16)

    def update(count, keys, values):
        own_seg = jnp.transpose(jnp.broadcast_to(seg_ref[...].astype(jnp.float32), (8, rows)))[:, 0:1]
        key_segs = []
        for slot in range(count):
            packed = mine[slot][rows:, :].astype(jnp.float32)
            key_segs.append(jnp.concatenate([packed[0:1, :], packed[8:9, :]], axis=1))
        for start in range(0, rows, tile):
            span = slice(start, start + tile)
            query = q_ref[span, :]
            best = None if first else state_ref[span, HD:HD + LANES]
            bounds = []
            for slot, (back, furthest) in enumerate(plan[:count]):
                low, high = 0, rows
                if back == 0:
                    high = start + tile
                elif furthest:
                    low = start
                bounds.append((low, high))
                raw = lax.dot_general(query, keys[slot][low:high, :], NT, preferred_element_type=jnp.float32)
                allowed = key_segs[slot][:, low:high] == own_seg[span, :]
                if back == 0:
                    row_pos = start + lax.broadcasted_iota(jnp.int32, raw.shape, 0)
                    allowed = allowed & (lax.broadcasted_iota(jnp.int32, raw.shape, 1) <= row_pos)
                masked = jnp.where(allowed, raw, NEG)
                scores[slot, :, low:high] = masked
                for at in range(0, high - low, LANES):
                    piece = masked[:, at:at + LANES]
                    best = piece if best is None else jnp.maximum(best, piece)
            top = jnp.broadcast_to(jnp.max(best, axis=1, keepdims=True), (tile, LANES))
            if first:
                total = jnp.zeros((tile, LANES), jnp.float32)
                weighted = jnp.zeros((tile, HD), jnp.float32)
            else:
                shrink = jnp.exp2((state_ref[span, HD:HD + LANES] - top) * FACTOR)
                total = state_ref[span, HD + LANES:] * shrink
                weighted = state_ref[span, :HD] * jnp.concatenate([shrink, shrink], axis=1)
            for slot in range(count):
                low, high = bounds[slot]
                pieces = []
                for at in range(low, high, LANES):
                    weights = jnp.exp2((scores[slot, :, at:at + LANES] - top) * FACTOR)
                    total = total + weights
                    pieces.append(weights.astype(jnp.bfloat16))
                probs = jnp.concatenate(pieces, axis=1)
                weighted = weighted + jnp.dot(probs, values[slot][low:high, :], preferred_element_type=jnp.float32)
            if last:
                finish(span, weighted, total)
            else:
                out_ref[span, :HD] = weighted
                out_ref[span, HD:HD + LANES] = top
                out_ref[span, HD + LANES:] = total

    for count in range(1 if first else 0, blocks + 1):
        reached = place >= (plan[count - 1][0] if count > 0 else 0)
        if count < blocks:
            reached = reached & (place < plan[count][0])
        if count > 0:
            pl.when(reached & (part == 0))(functools.partial(update, count, mine, other))
            pl.when(reached & (part == 1))(functools.partial(update, count, other, mine))
        elif last:

            @pl.when(reached)
            def _():
                finish(slice(0, rows), state_ref[:, :HD], state_ref[:, HD + LANES:])


def attend(query, segments, plan, mine, other, state, last):
    rows = query.shape[0]
    blocks = len(plan)
    vmem = pl.BlockSpec(memory_space=pltpu.VMEM)
    first = state is None
    operands = [query, segments.reshape(1, rows), *mine, *other] + ([] if first else [state])
    return pl.pallas_call(
        functools.partial(attend_kernel, plan, first, last),
        in_specs=[vmem] * len(operands),
        out_specs=vmem,
        out_shape=pltpu.VMEM((rows, HD), jnp.bfloat16) if last else pltpu.VMEM((rows, HD + 2 * LANES), jnp.float32),
        scratch_shapes=[pltpu.VMEM((blocks, rows // 2, rows), jnp.float32)],
        input_output_aliases={} if first or last else {len(operands) - 1: 0},
        compiler_params=pltpu.CompilerParams(vmem_limit_bytes=12 * MIB),
        cost_estimate=pl.CostEstimate(
            flops=4 * rows * rows * blocks * HD, bytes_accessed=4 * rows * blocks * HD, transcendentals=rows * rows * blocks
        ),
        name="attend_last" if last else "attend_first" if first else "attend_more",
    )(*[in_vmem(operand) for operand in operands])


def bounds_kernel(sum_ref, out_exp_ref, x_ref, sum_bound_ref, out_bound_ref, near_ref, sem):
    groups, rows = sum_ref.shape
    fetch = pltpu.make_async_copy(x_ref, near_ref, sem)
    fetch.start()
    per = sum_bound_ref.shape[1] // groups
    for exps, bound_ref in ((sum_ref, sum_bound_ref), (out_exp_ref, out_bound_ref)):
        power = jnp.left_shift(jnp.int32(1), exps[...] - MIN_EXP).astype(jnp.float32)
        bound = jnp.transpose(power * (LIMIT * 2.0 ** MIN_EXP))
        for group in range(groups):
            wide = jnp.broadcast_to(bound[:, group:group + 1], (rows, per))
            bound_ref[:, group * per:(group + 1) * per] = wide.astype(jnp.bfloat16)
    fetch.wait()


def spread_bounds(sum_exps, out_exps, tokens):
    rows, width = tokens.shape
    groups = sum_exps.shape[1]
    vmem = pl.BlockSpec(memory_space=pltpu.VMEM)
    return pl.pallas_call(
        bounds_kernel,
        in_specs=[vmem, vmem, pl.BlockSpec(memory_space=pltpu.HBM)],
        out_specs=[vmem] * 3,
        out_shape=[pltpu.VMEM((rows, width), jnp.bfloat16)] * 3,
        scratch_shapes=[pltpu.SemaphoreType.DMA(())],
        compiler_params=pltpu.CompilerParams(vmem_limit_bytes=8 * MIB),
        cost_estimate=pl.CostEstimate(flops=8 * rows * width, bytes_accessed=8 * rows * groups, transcendentals=0),
        name="spread_bounds",
    )(in_vmem(sum_exps.T), in_vmem(out_exps.T), in_hbm(tokens))


def clip(value, bound):
    return jnp.minimum(jnp.maximum(value.astype(jnp.bfloat16), -bound), bound)


def in_tiles(a_ref, w_ref, first, count, tile, finish):
    waiting = None
    for at in range(0, count, HD):
        cols = pl.ds(pl.multiple_of(first + at, HD), HD)
        weights = w_ref[:, cols]
        for start in range(0, a_ref.shape[0], tile):
            span = slice(start, start + tile)
            term = jnp.dot(a_ref[span, :], weights, preferred_element_type=jnp.float32)
            if waiting is not None:
                finish(*waiting)
            waiting = (span, cols, term)
    finish(*waiting)


def own_kernel(a_ref, w_ref, sum_ref, out_ref):
    rows, width = out_ref.shape
    tile = rows // 2
    chunk = width // 4

    def body(step, carry):
        def finish(span, cols, term):
            out_ref[span, cols] = clip(term, sum_ref[span, cols])

        in_tiles(a_ref, w_ref, step * chunk, chunk, tile, finish)
        return carry

    lax.fori_loop(0, 4, body, 0)


def project_own(attended, w_out, sum_bound):
    rows, depth = attended.shape
    width = w_out.shape[1]
    vmem = pl.BlockSpec(memory_space=pltpu.VMEM)
    return pl.pallas_call(
        own_kernel,
        in_specs=[vmem] * 3,
        out_specs=vmem,
        out_shape=pltpu.VMEM((rows, width), jnp.bfloat16),
        compiler_params=pltpu.CompilerParams(vmem_limit_bytes=8 * MIB),
        cost_estimate=pl.CostEstimate(
            flops=2 * rows * width * depth, bytes_accessed=4 * rows * width + 2 * width * depth, transcendentals=0
        ),
        name="project_own",
    )(in_vmem(attended), in_vmem(w_out), in_vmem(sum_bound))


def output_kernel(b_ref, wb_ref, quant_ref, x_ref, sum_ref, last_ref, out_ref, staged, sems):
    rows, width = x_ref.shape
    steps = sems.shape[0]
    chunk = width // steps
    tile = rows // 2

    def copy(step):
        span = pl.ds(pl.multiple_of(step * chunk, chunk), chunk)
        return pltpu.make_async_copy(staged.at[:, span], out_ref.at[:, span], sems.at[step])

    def body(step, carry):
        def finish(span, cols, term):
            quant = clip(term, sum_ref[span, cols]).astype(jnp.float32) + quant_ref[span, cols].astype(jnp.float32)
            staged[span, cols] = clip(x_ref[span, cols].astype(jnp.float32) + quant, last_ref[span, cols])

        in_tiles(b_ref, wb_ref, step * chunk, chunk, tile, finish)
        copy(step).start()
        return carry

    lax.fori_loop(0, steps, body, 0)
    for step in range(steps):
        copy(step).wait()


def project_out(att_other, w_other, quant_own, sum_bound, out_bound, tokens):
    rows, width = tokens.shape
    depth = att_other.shape[1]
    steps = 8
    vmem = pl.BlockSpec(memory_space=pltpu.VMEM)
    operands = [att_other, w_other, quant_own, tokens, sum_bound, out_bound]
    return pl.pallas_call(
        output_kernel,
        in_specs=[vmem] * len(operands),
        out_specs=pl.BlockSpec(memory_space=pltpu.HBM),
        out_shape=jax.ShapeDtypeStruct((rows, width), jnp.bfloat16),
        scratch_shapes=[pltpu.VMEM((rows, width), jnp.bfloat16), pltpu.SemaphoreType.DMA((steps,))],
        compiler_params=pltpu.CompilerParams(vmem_limit_bytes=12 * MIB),
        cost_estimate=pl.CostEstimate(
            flops=2 * rows * width * depth, bytes_accessed=4 * rows * width + 2 * width * depth, transcendentals=0
        ),
        name="project_out",
    )(*[in_vmem(operand) for operand in operands])


def on_device(seq_size, tokens, gain, segments, w_query, w_keyval, w_out, sum_exps, out_exps):
    window = seq_size // 2

    def swap_cores(x):
        return lax.ppermute(x, "tp", [(0, 1), (1, 0)])

    def shift(x, step, first):
        cycle = seq_size - first
        pairs = []
        for i in range(seq_size):
            for core in range(2):
                after = 2 * (first + (i - first + step) % cycle) + core if i >= first else 2 * i + 1 - core
                pairs.append((2 * i + core, after))
        return lax.ppermute(x, ("seq", "tp"), pairs)

    w_other = swap_cores(w_out)
    message, normed = norm_kv(tokens, gain, w_keyval, segments)
    query = project_query(normed, w_query)
    held, query = lax.optimization_barrier((shift(message, 2, 0), query))
    odd = lax.rem(lax.axis_index("seq"), 2) == 1
    beside = lax.ppermute(jnp.where(odd, held, message), "seq", [(i, i ^ 1) for i in range(seq_size)])
    parts = [[(0, message), (2, held)]]
    for back in range(2, window, 2):
        step = shift(held, 1, back)
        held = shift(held, 2, back)
        parts.append([(back + 1, step)] + ([(back + 2, held)] if back + 2 < window else []))
    parts.append([(1, beside), (window, held)])
    exps = lax.optimization_barrier((sum_exps, out_exps, query))[:2]
    bounds = spread_bounds(*exps, tokens)
    state = None
    for number, blocks in enumerate(parts):
        plan = [(back, back == window) for back, _ in blocks]
        mine = [block for _, block in blocks]
        if number == 1:
            bounds, state = early = lax.optimization_barrier((bounds, state))
        if number > 0:
            mine = [lax.optimization_barrier((block, early))[0] for block in mine]
        other = [swap_cores(m) for m in mine]
        state = attend(query, segments, plan, mine, other, state, number == len(parts) - 1)
    quant_own = project_own(state, w_out, bounds[0])
    return project_out(swap_cores(state), w_other, quant_own, *bounds)


def solution(mesh):
    in_specs = (
        P(("groups", "seq"), None),
        P(),
        P(("groups", "seq")),
        P(None, "tp"),
        P(None, "tp"),
        P("tp", None),
        P(("groups", "seq"), None),
        P(("groups", "seq"), None),
    )
    out_specs = P(("groups", "seq"), None)
    return jax.shard_map(
        functools.partial(on_device, mesh.shape["seq"]),
        mesh=mesh, in_specs=in_specs, out_specs=out_specs, check_vma=False,
    )
```

```python
import functools

import jax
import jax.numpy as jnp
from jax import lax
from jax.experimental import pallas as pl
from jax.experimental.pallas import tpu as pltpu
from jax.sharding import PartitionSpec as P

HD = 256
LANES = 128
SEG_ROWS = 16
LIMIT = 448.0
MIN_EXP = -9
NEG = -1e30
MIB = 1024 * 1024
NT = (((1,), (1,)), ((), ()))
FACTOR = HD ** (-0.5) * 1.4426950408889634


def norm_kv_kernel(x_ref, gain_hbm, w_ref, seg_hbm, msg_ref, normed_ref, xs, ws, gain_ref, seg_ref, sems):
    rows, width = xs.shape
    tile, part = rows // 2, rows // 8
    pieces = 4
    deep = width // pieces

    def tokens_copy(i):
        return pltpu.make_async_copy(x_ref.at[pl.ds(i * part, part)], xs.at[pl.ds(i * part, part)], sems.at[i])

    def weights_copy(i):
        return pltpu.make_async_copy(w_ref.at[pl.ds(i * deep, deep)], ws.at[pl.ds(i * deep, deep)], sems.at[8 + i])

    def gain_copy():
        return pltpu.make_async_copy(gain_hbm, gain_ref, sems.at[12])

    def segments_copy():
        return pltpu.make_async_copy(seg_hbm, seg_ref, sems.at[13])

    for i in range(4):
        tokens_copy(i).start()
    gain_copy().start()
    for i in range(pieces):
        weights_copy(i).start()
    for i in range(4, 8):
        tokens_copy(i).start()
    segments_copy().start()

    def wide(first, count, start):
        return xs[first:first + count, start:start + LANES].astype(jnp.float32)

    for first in range(0, rows, tile):
        for at in range(first, first + tile, part):
            tokens_copy(at // part).wait()
        total = wide(first, tile, 0)
        for start in range(LANES, width, LANES):
            total = total + wide(first, tile, start)
        mean = jnp.broadcast_to(jnp.sum(total, axis=1, keepdims=True) * (1.0 / width), (tile, LANES))
        square = jnp.zeros((tile, LANES), jnp.float32)
        for start in range(0, width, LANES):
            center = wide(first, tile, start) - mean
            square = square + center * center
        spread = jnp.sum(square, axis=1, keepdims=True) * (1.0 / width)
        scale = jnp.broadcast_to(lax.rsqrt(spread + 1e-05), (tile, LANES))
        if first == 0:
            gain_copy().wait()
            for i in range(pieces):
                weights_copy(i).wait()
        kv = jnp.zeros((tile, ws.shape[1]), jnp.float32)
        span = slice(first, first + tile)
        for start in range(0, width, HD):
            for at in (start, start + LANES):
                normed = (wide(first, tile, at) - mean) * scale * gain_ref[:, at:at + LANES]
                normed_ref[span, at:at + LANES] = normed.astype(jnp.bfloat16)
            kv = kv + jnp.dot(
                normed_ref[span, start:start + HD], ws[start:start + HD, :], preferred_element_type=jnp.float32
            )
        msg_ref[span, :] = kv.astype(jnp.bfloat16)
    segments_copy().wait()
    seg = seg_ref[...].astype(jnp.float32)
    low = jnp.broadcast_to(seg[:, :HD], (8, HD))
    high = jnp.broadcast_to(seg[:, HD:], (8, HD))
    msg_ref[rows:, :] = jnp.concatenate([low, high], axis=0).astype(jnp.bfloat16)


def in_hbm(x):
    return pltpu.with_memory_space_constraint(x, pltpu.HBM)


def in_vmem(x):
    return pltpu.with_memory_space_constraint(x, pltpu.VMEM)


def norm_kv(tokens, gain, w_keyval, segments):
    rows, width = tokens.shape
    cols = w_keyval.shape[1]
    vmem, hbm = pl.BlockSpec(memory_space=pltpu.VMEM), pl.BlockSpec(memory_space=pltpu.HBM)
    return pl.pallas_call(
        norm_kv_kernel,
        in_specs=[hbm] * 4,
        out_specs=[vmem, vmem],
        out_shape=[pltpu.VMEM((rows + SEG_ROWS, cols), jnp.bfloat16), pltpu.VMEM((rows, width), jnp.bfloat16)],
        scratch_shapes=[
            pltpu.VMEM((rows, width), jnp.bfloat16),
            pltpu.VMEM((width, cols), jnp.bfloat16),
            pltpu.VMEM((1, width), jnp.float32),
            pltpu.VMEM((1, rows), jnp.int32),
            pltpu.SemaphoreType.DMA((14,)),
        ],
        compiler_params=pltpu.CompilerParams(vmem_limit_bytes=24 * MIB),
        cost_estimate=pl.CostEstimate(
            flops=2 * rows * width * cols, bytes_accessed=4 * rows * width + 2 * width * cols, transcendentals=0
        ),
        name="norm_kv",
    )(in_hbm(tokens), in_hbm(gain.reshape(1, width)), in_hbm(w_keyval), in_hbm(segments.reshape(1, rows)))


def query_kernel(x_ref, w_ref, out_ref):
    out_ref[...] = jnp.dot(x_ref[...], w_ref[...], preferred_element_type=jnp.float32).astype(jnp.bfloat16)


def project_query(normed, w_query):
    rows, width = normed.shape
    cols = w_query.shape[1]
    vmem = pl.BlockSpec(memory_space=pltpu.VMEM)
    return pl.pallas_call(
        query_kernel,
        in_specs=[vmem, vmem],
        out_specs=vmem,
        out_shape=pltpu.VMEM((rows, cols), jnp.bfloat16),
        compiler_params=pltpu.CompilerParams(vmem_limit_bytes=8 * MIB),
        cost_estimate=pl.CostEstimate(
            flops=2 * rows * width * cols, bytes_accessed=2 * rows * width + 2 * width * cols, transcendentals=0
        ),
        name="project_query",
    )(in_vmem(normed), in_vmem(w_query))


def attend_kernel(plan, first, last, *refs):
    blocks = len(plan)
    q_ref, seg_ref = refs[:2]
    mine, other = refs[2:2 + blocks], refs[2 + blocks:2 + 2 * blocks]
    refs = refs[2 + 2 * blocks:]
    state_ref = None
    if not first:
        state_ref, refs = refs[0], refs[1:]
    out_ref, scores = refs
    rows = q_ref.shape[0]
    tile = rows // 2
    part = lax.axis_index("tp")
    place = lax.axis_index("seq")

    def finish(span, weighted, total):
        out_ref[span, :] = (weighted / jnp.sum(total, axis=1, keepdims=True)).astype(jnp.bfloat16)

    def update(count, keys, values):
        own_seg = jnp.transpose(jnp.broadcast_to(seg_ref[...].astype(jnp.float32), (8, rows)))[:, 0:1]
        key_segs = []
        for slot in range(count):
            packed = mine[slot][rows:, :].astype(jnp.float32)
            key_segs.append(jnp.concatenate([packed[0:1, :], packed[8:9, :]], axis=1))
        for start in range(0, rows, tile):
            span = slice(start, start + tile)
            query = q_ref[span, :]
            best = None if first else state_ref[span, HD:HD + LANES]
            bounds = []
            for slot, (back, furthest) in enumerate(plan[:count]):
                low, high = 0, rows
                if back == 0:
                    high = start + tile
                elif furthest:
                    low = start
                bounds.append((low, high))
                raw = lax.dot_general(query, keys[slot][low:high, :], NT, preferred_element_type=jnp.float32)
                allowed = key_segs[slot][:, low:high] == own_seg[span, :]
                if back == 0:
                    row_pos = start + lax.broadcasted_iota(jnp.int32, raw.shape, 0)
                    allowed = allowed & (lax.broadcasted_iota(jnp.int32, raw.shape, 1) <= row_pos)
                masked = jnp.where(allowed, raw, NEG)
                scores[slot, :, low:high] = masked
                for at in range(0, high - low, LANES):
                    piece = masked[:, at:at + LANES]
                    best = piece if best is None else jnp.maximum(best, piece)
            top = jnp.broadcast_to(jnp.max(best, axis=1, keepdims=True), (tile, LANES))
            if first:
                total = jnp.zeros((tile, LANES), jnp.float32)
                weighted = jnp.zeros((tile, HD), jnp.float32)
            else:
                shrink = jnp.exp2((state_ref[span, HD:HD + LANES] - top) * FACTOR)
                total = state_ref[span, HD + LANES:] * shrink
                weighted = state_ref[span, :HD] * jnp.concatenate([shrink, shrink], axis=1)
            for slot in range(count):
                low, high = bounds[slot]
                pieces = []
                for at in range(low, high, LANES):
                    weights = jnp.exp2((scores[slot, :, at:at + LANES] - top) * FACTOR)
                    total = total + weights
                    pieces.append(weights.astype(jnp.bfloat16))
                probs = jnp.concatenate(pieces, axis=1)
                weighted = weighted + jnp.dot(probs, values[slot][low:high, :], preferred_element_type=jnp.float32)
            if last:
                finish(span, weighted, total)
            else:
                out_ref[span, :HD] = weighted
                out_ref[span, HD:HD + LANES] = top
                out_ref[span, HD + LANES:] = total

    for count in range(1 if first else 0, blocks + 1):
        reached = place >= (plan[count - 1][0] if count > 0 else 0)
        if count < blocks:
            reached = reached & (place < plan[count][0])
        if count > 0:
            pl.when(reached & (part == 0))(functools.partial(update, count, mine, other))
            pl.when(reached & (part == 1))(functools.partial(update, count, other, mine))
        elif last:

            @pl.when(reached)
            def _():
                finish(slice(0, rows), state_ref[:, :HD], state_ref[:, HD + LANES:])


def attend(query, segments, plan, mine, other, state, last):
    rows = query.shape[0]
    blocks = len(plan)
    vmem = pl.BlockSpec(memory_space=pltpu.VMEM)
    first = state is None
    operands = [query, segments.reshape(1, rows), *mine, *other] + ([] if first else [state])
    return pl.pallas_call(
        functools.partial(attend_kernel, plan, first, last),
        in_specs=[vmem] * len(operands),
        out_specs=vmem,
        out_shape=pltpu.VMEM((rows, HD), jnp.bfloat16) if last else pltpu.VMEM((rows, HD + 2 * LANES), jnp.float32),
        scratch_shapes=[pltpu.VMEM((blocks, rows // 2, rows), jnp.float32)],
        input_output_aliases={} if first or last else {len(operands) - 1: 0},
        compiler_params=pltpu.CompilerParams(vmem_limit_bytes=12 * MIB),
        cost_estimate=pl.CostEstimate(
            flops=4 * rows * rows * blocks * HD, bytes_accessed=4 * rows * blocks * HD, transcendentals=rows * rows * blocks
        ),
        name="attend_last" if last else "attend_first" if first else "attend_more",
    )(*[in_vmem(operand) for operand in operands])


def bounds_kernel(sum_ref, out_exp_ref, x_ref, sum_bound_ref, out_bound_ref, wide_ref, near, sem):
    groups, rows = sum_ref.shape
    fetch = pltpu.make_async_copy(x_ref, near, sem)
    fetch.start()
    per = sum_bound_ref.shape[1] // groups
    for exps, bound_ref in ((sum_ref, sum_bound_ref), (out_exp_ref, out_bound_ref)):
        power = jnp.left_shift(jnp.int32(1), exps[...] - MIN_EXP).astype(jnp.float32)
        bound = jnp.transpose(power * (LIMIT * 2.0 ** MIN_EXP))
        for group in range(groups):
            wide = jnp.broadcast_to(bound[:, group:group + 1], (rows, per)).astype(jnp.bfloat16)
            bound_ref[:, group * per:(group + 1) * per] = wide
    fetch.wait()

    def widen(step, carry):
        span = pl.ds(pl.multiple_of(step * 64, 64), 64)
        wide_ref[span, :] = near[span, :].astype(jnp.float32)
        return carry

    lax.fori_loop(0, rows // 64, widen, 0)


def spread_bounds(sum_exps, out_exps, tokens):
    rows, width = tokens.shape
    groups = sum_exps.shape[1]
    vmem = pl.BlockSpec(memory_space=pltpu.VMEM)
    return pl.pallas_call(
        bounds_kernel,
        in_specs=[vmem, vmem, pl.BlockSpec(memory_space=pltpu.HBM)],
        out_specs=[vmem] * 3,
        out_shape=[pltpu.VMEM((rows, width), jnp.bfloat16)] * 2 + [pltpu.VMEM((rows, width), jnp.float32)],
        scratch_shapes=[pltpu.VMEM((rows, width), jnp.bfloat16), pltpu.SemaphoreType.DMA(())],
        compiler_params=pltpu.CompilerParams(vmem_limit_bytes=10 * MIB),
        cost_estimate=pl.CostEstimate(flops=8 * rows * width, bytes_accessed=8 * rows * groups, transcendentals=0),
        name="spread_bounds",
    )(in_vmem(sum_exps.T), in_vmem(out_exps.T), in_hbm(tokens))


def clip(value, bound):
    return jnp.minimum(jnp.maximum(value.astype(jnp.bfloat16), -bound), bound)


def own_kernel(a_ref, w_ref, sum_ref, out_ref):
    rows, width = out_ref.shape
    tile = rows // 2
    chunk = width // 4

    def body(step, carry):
        for at in range(0, chunk, HD):
            cols = pl.ds(pl.multiple_of(step * chunk + at, HD), HD)
            weights = w_ref[:, cols]
            for start in range(0, rows, tile):
                span = slice(start, start + tile)
                term = jnp.dot(a_ref[span, :], weights, preferred_element_type=jnp.float32)
                out_ref[span, cols] = clip(term, sum_ref[span, cols])
        return carry

    lax.fori_loop(0, 4, body, 0)


def project_own(attended, w_out, sum_bound):
    rows, depth = attended.shape
    width = w_out.shape[1]
    vmem = pl.BlockSpec(memory_space=pltpu.VMEM)
    return pl.pallas_call(
        own_kernel,
        in_specs=[vmem] * 3,
        out_specs=vmem,
        out_shape=pltpu.VMEM((rows, width), jnp.bfloat16),
        compiler_params=pltpu.CompilerParams(vmem_limit_bytes=8 * MIB),
        cost_estimate=pl.CostEstimate(
            flops=2 * rows * width * depth, bytes_accessed=4 * rows * width + 2 * width * depth, transcendentals=0
        ),
        name="project_own",
    )(in_vmem(attended), in_vmem(w_out), in_vmem(sum_bound))


def output_kernel(b_ref, wb_ref, quant_ref, x_ref, sum_ref, last_ref, out_ref, staged, sems):
    rows, width = x_ref.shape
    pieces = sems.shape[0]
    piece = width // pieces
    chunk = width // 2
    tile = rows // 2

    def copy(index):
        span = pl.ds(pl.multiple_of(index * piece, piece), piece)
        return pltpu.make_async_copy(staged.at[:, span], out_ref.at[:, span], sems.at[index])

    def body(step, carry):
        for at in range(0, chunk, HD):
            cols = pl.ds(pl.multiple_of(step * chunk + at, HD), HD)
            weights = wb_ref[:, cols]
            for start in range(0, rows, tile):
                span = slice(start, start + tile)
                term = jnp.dot(b_ref[span, :], weights, preferred_element_type=jnp.float32)
                other = clip(term, sum_ref[span, cols])
                quant = other.astype(jnp.float32) + quant_ref[span, cols].astype(jnp.float32)
                staged[span, cols] = clip(x_ref[span, cols] + quant, last_ref[span, cols])
            if (at + HD) % piece == 0:
                copy(step * (chunk // piece) + at // piece).start()
        return carry

    lax.fori_loop(0, width // chunk, body, 0)
    for index in range(pieces):
        copy(index).wait()


def project_out(att_other, w_other, quant_own, sum_bound, out_bound, tokens):
    rows, width = tokens.shape
    depth = att_other.shape[1]
    pieces = 8
    vmem = pl.BlockSpec(memory_space=pltpu.VMEM)
    operands = [att_other, w_other, quant_own, tokens, sum_bound, out_bound]
    return pl.pallas_call(
        output_kernel,
        in_specs=[vmem] * len(operands),
        out_specs=pl.BlockSpec(memory_space=pltpu.HBM),
        out_shape=jax.ShapeDtypeStruct((rows, width), jnp.bfloat16),
        scratch_shapes=[pltpu.VMEM((rows, width), jnp.bfloat16), pltpu.SemaphoreType.DMA((pieces,))],
        compiler_params=pltpu.CompilerParams(vmem_limit_bytes=10 * MIB),
        cost_estimate=pl.CostEstimate(
            flops=2 * rows * width * depth, bytes_accessed=4 * rows * width + 2 * width * depth, transcendentals=0
        ),
        name="project_out",
    )(*[in_vmem(operand) for operand in operands])


def on_device(seq_size, tokens, gain, segments, w_query, w_keyval, w_out, sum_exps, out_exps):
    window = seq_size // 2

    def swap_cores(x):
        return lax.ppermute(x, "tp", [(0, 1), (1, 0)])

    def shift(x, step, first):
        cycle = seq_size - first
        pairs = []
        for i in range(seq_size):
            for core in range(2):
                after = 2 * (first + (i - first + step) % cycle) + core if i >= first else 2 * i + 1 - core
                pairs.append((2 * i + core, after))
        return lax.ppermute(x, ("seq", "tp"), pairs)

    w_other = swap_cores(w_out)
    message, normed = norm_kv(tokens, gain, w_keyval, segments)
    query = project_query(normed, w_query)
    held, query = lax.optimization_barrier((shift(message, 2, 0), query))
    odd = lax.rem(lax.axis_index("seq"), 2) == 1
    beside = lax.ppermute(jnp.where(odd, held, message), "seq", [(i, i ^ 1) for i in range(seq_size)])
    parts = [[(0, message), (2, held)]]
    for back in range(2, window, 2):
        step = shift(held, 1, back)
        held = shift(held, 2, back)
        parts.append([(back + 1, step)] + ([(back + 2, held)] if back + 2 < window else []))
    parts.append([(1, beside), (window, held)])
    exps = lax.optimization_barrier((sum_exps, out_exps, query))[:2]
    bounds = spread_bounds(*exps, tokens)
    state = None
    for number, blocks in enumerate(parts):
        plan = [(back, back == window) for back, _ in blocks]
        mine = [block for _, block in blocks]
        if number == 1:
            bounds, state = early = lax.optimization_barrier((bounds, state))
        if number > 0:
            mine = [lax.optimization_barrier((block, early))[0] for block in mine]
        other = [swap_cores(m) for m in mine]
        state = attend(query, segments, plan, mine, other, state, number == len(parts) - 1)
    quant_own = project_own(state, w_out, bounds[0])
    return project_out(swap_cores(state), w_other, quant_own, *bounds)


def solution(mesh):
    in_specs = (
        P(("groups", "seq"), None),
        P(),
        P(("groups", "seq")),
        P(None, "tp"),
        P(None, "tp"),
        P("tp", None),
        P(("groups", "seq"), None),
        P(("groups", "seq"), None),
    )
    out_specs = P(("groups", "seq"), None)
    return jax.shard_map(
        functools.partial(on_device, mesh.shape["seq"]),
        mesh=mesh, in_specs=in_specs, out_specs=out_specs, check_vma=False,
    )
```

```python
import functools

import jax
import jax.numpy as jnp
from jax import lax
from jax.experimental import pallas as pl
from jax.experimental.pallas import tpu as pltpu
from jax.sharding import PartitionSpec as P

HD = 256
LANES = 128
SEG_ROWS = 16
LIMIT = 448.0
MIN_EXP = -9
NEG = -1e30
MIB = 1024 * 1024
NT = (((1,), (1,)), ((), ()))
EVEN, ODD, ALL, FURTHEST = 0, 1, 2, 3
FACTOR = HD ** (-0.5) * 1.4426950408889634


def norm_kv_kernel(x_ref, gain_hbm, w_ref, seg_hbm, next_ref, msg_ref, normed_ref, near_ref, xs, ws, gain_ref, seg_ref, sems):
    rows, width = xs.shape
    tile, part = rows // 2, rows // 8
    pieces = 4
    deep = width // pieces

    def tokens_copy(i):
        return pltpu.make_async_copy(x_ref.at[pl.ds(i * part, part)], xs.at[pl.ds(i * part, part)], sems.at[i])

    def weights_copy(i):
        return pltpu.make_async_copy(w_ref.at[pl.ds(i * deep, deep)], ws.at[pl.ds(i * deep, deep)], sems.at[8 + i])

    def gain_copy():
        return pltpu.make_async_copy(gain_hbm, gain_ref, sems.at[12])

    def segments_copy():
        return pltpu.make_async_copy(seg_hbm, seg_ref, sems.at[13])

    def next_copy():
        return pltpu.make_async_copy(next_ref, near_ref, sems.at[14])

    for i in range(4):
        tokens_copy(i).start()
    gain_copy().start()
    for i in range(pieces):
        weights_copy(i).start()
    for i in range(4, 8):
        tokens_copy(i).start()
    segments_copy().start()
    next_copy().start()

    def wide(first, count, start):
        return xs[first:first + count, start:start + LANES].astype(jnp.float32)

    for first in range(0, rows, tile):
        for at in range(first, first + tile, part):
            tokens_copy(at // part).wait()
        total = wide(first, tile, 0)
        for start in range(LANES, width, LANES):
            total = total + wide(first, tile, start)
        mean = jnp.broadcast_to(jnp.sum(total, axis=1, keepdims=True) * (1.0 / width), (tile, LANES))
        square = jnp.zeros((tile, LANES), jnp.float32)
        for start in range(0, width, LANES):
            center = wide(first, tile, start) - mean
            square = square + center * center
        spread = jnp.sum(square, axis=1, keepdims=True) * (1.0 / width)
        scale = jnp.broadcast_to(lax.rsqrt(spread + 1e-05), (tile, LANES))
        if first == 0:
            gain_copy().wait()
            for i in range(pieces):
                weights_copy(i).wait()
        kv = jnp.zeros((tile, ws.shape[1]), jnp.float32)
        span = slice(first, first + tile)
        for start in range(0, width, HD):
            for at in (start, start + LANES):
                normed = (wide(first, tile, at) - mean) * scale * gain_ref[:, at:at + LANES]
                normed_ref[span, at:at + LANES] = normed.astype(jnp.bfloat16)
            kv = kv + jnp.dot(
                normed_ref[span, start:start + HD], ws[start:start + HD, :], preferred_element_type=jnp.float32
            )
        msg_ref[span, :] = kv.astype(jnp.bfloat16)
    segments_copy().wait()
    seg = seg_ref[...].astype(jnp.float32)
    low = jnp.broadcast_to(seg[:, :HD], (8, HD))
    high = jnp.broadcast_to(seg[:, HD:], (8, HD))
    msg_ref[rows:, :] = jnp.concatenate([low, high], axis=0).astype(jnp.bfloat16)
    next_copy().wait()


def in_hbm(x):
    return pltpu.with_memory_space_constraint(x, pltpu.HBM)


def in_vmem(x):
    return pltpu.with_memory_space_constraint(x, pltpu.VMEM)


def norm_kv(tokens, gain, w_keyval, segments, w_next):
    rows, width = tokens.shape
    cols = w_keyval.shape[1]
    vmem, hbm = pl.BlockSpec(memory_space=pltpu.VMEM), pl.BlockSpec(memory_space=pltpu.HBM)
    return pl.pallas_call(
        norm_kv_kernel,
        in_specs=[hbm] * 5,
        out_specs=[vmem] * 3,
        out_shape=[
            pltpu.VMEM((rows + SEG_ROWS, cols), jnp.bfloat16),
            pltpu.VMEM((rows, width), jnp.bfloat16),
            pltpu.VMEM(w_next.shape, w_next.dtype),
        ],
        scratch_shapes=[
            pltpu.VMEM((rows, width), jnp.bfloat16),
            pltpu.VMEM((width, cols), jnp.bfloat16),
            pltpu.VMEM((1, width), jnp.float32),
            pltpu.VMEM((1, rows), jnp.int32),
            pltpu.SemaphoreType.DMA((15,)),
        ],
        compiler_params=pltpu.CompilerParams(vmem_limit_bytes=24 * MIB),
        cost_estimate=pl.CostEstimate(
            flops=2 * rows * width * cols, bytes_accessed=4 * rows * width + 2 * width * cols, transcendentals=0
        ),
        name="norm_kv",
    )(*[in_hbm(x) for x in (tokens, gain.reshape(1, width), w_keyval, segments.reshape(1, rows), w_next)])


def query_kernel(x_ref, w_ref, out_ref):
    out_ref[...] = jnp.dot(x_ref[...], w_ref[...], preferred_element_type=jnp.float32).astype(jnp.bfloat16)


def project_query(normed, w_query):
    rows, width = normed.shape
    cols = w_query.shape[1]
    vmem = pl.BlockSpec(memory_space=pltpu.VMEM)
    return pl.pallas_call(
        query_kernel,
        in_specs=[vmem, vmem],
        out_specs=vmem,
        out_shape=pltpu.VMEM((rows, cols), jnp.bfloat16),
        compiler_params=pltpu.CompilerParams(vmem_limit_bytes=8 * MIB),
        cost_estimate=pl.CostEstimate(
            flops=2 * rows * width * cols, bytes_accessed=2 * rows * width + 2 * width * cols, transcendentals=0
        ),
        name="project_query",
    )(in_vmem(normed), in_vmem(w_query))


def attend_kernel(plan, first, last, *refs):
    blocks = len(plan)
    q_ref, seg_ref = refs[:2]
    mine, other = refs[2:2 + blocks], refs[2 + blocks:2 + 2 * blocks]
    refs = refs[2 + 2 * blocks:]
    state_ref = None
    if not first:
        state_ref, refs = refs[0], refs[1:]
    out_ref, scores = refs
    rows = q_ref.shape[0]
    tile = rows // 2
    part = lax.axis_index("tp")
    place = lax.axis_index("seq")

    def finish(span, weighted, total):
        out_ref[span, :] = (weighted / jnp.sum(total, axis=1, keepdims=True)).astype(jnp.bfloat16)

    def update(slots, keys, values):
        own_seg = jnp.transpose(jnp.broadcast_to(seg_ref[...].astype(jnp.float32), (8, rows)))[:, 0:1]
        key_segs = {}
        for slot in slots:
            packed = mine[slot][rows:, :].astype(jnp.float32)
            key_segs[slot] = jnp.concatenate([packed[0:1, :], packed[8:9, :]], axis=1)
        for start in range(0, rows, tile):
            span = slice(start, start + tile)
            query = q_ref[span, :]
            best = None if first else state_ref[span, HD:HD + LANES]
            bounds = {}
            for slot in slots:
                back, kind = plan[slot]
                low, high = 0, rows
                if back == 0:
                    high = start + tile
                elif kind == FURTHEST:
                    low = start
                bounds[slot] = (low, high)
                raw = lax.dot_general(query, keys[slot][low:high, :], NT, preferred_element_type=jnp.float32)
                allowed = key_segs[slot][:, low:high] == own_seg[span, :]
                if back == 0:
                    row_pos = start + lax.broadcasted_iota(jnp.int32, raw.shape, 0)
                    allowed = allowed & (lax.broadcasted_iota(jnp.int32, raw.shape, 1) <= row_pos)
                masked = jnp.where(allowed, raw, NEG)
                scores[slot, :, low:high] = masked
                for at in range(0, high - low, LANES):
                    piece = masked[:, at:at + LANES]
                    best = piece if best is None else jnp.maximum(best, piece)
            top = jnp.broadcast_to(jnp.max(best, axis=1, keepdims=True), (tile, LANES))
            if first:
                total = jnp.zeros((tile, LANES), jnp.float32)
                weighted = jnp.zeros((tile, HD), jnp.float32)
            else:
                shrink = jnp.exp2((state_ref[span, HD:HD + LANES] - top) * FACTOR)
                total = state_ref[span, HD + LANES:] * shrink
                weighted = state_ref[span, :HD] * jnp.concatenate([shrink, shrink], axis=1)
            for slot in slots:
                low, high = bounds[slot]
                pieces = []
                for at in range(low, high, LANES):
                    weights = jnp.exp2((scores[slot, :, at:at + LANES] - top) * FACTOR)
                    total = total + weights
                    pieces.append(weights.astype(jnp.bfloat16))
                probs = jnp.concatenate(pieces, axis=1)
                weighted = weighted + jnp.dot(probs, values[slot][low:high, :], preferred_element_type=jnp.float32)
            if last:
                finish(span, weighted, total)
            else:
                out_ref[span, :HD] = weighted
                out_ref[span, HD:HD + LANES] = top
                out_ref[span, HD + LANES:] = total

    for parity in (0, 1):
        slots = [slot for slot, (_, kind) in enumerate(plan) if kind in (ALL, FURTHEST, parity)]
        for count in range(len(slots) + 1):
            reached = lax.rem(place, 2) == parity
            if count > 0:
                reached = reached & (place >= plan[slots[count - 1]][0])
            if count < len(slots):
                reached = reached & (place < plan[slots[count]][0])
            if count > 0:
                pl.when(reached & (part == 0))(functools.partial(update, slots[:count], mine, other))
                pl.when(reached & (part == 1))(functools.partial(update, slots[:count], other, mine))
            elif last:

                @pl.when(reached)
                def _():
                    finish(slice(0, rows), state_ref[:, :HD], state_ref[:, HD + LANES:])


def attend(query, segments, plan, mine, other, state, last):
    rows = query.shape[0]
    blocks = len(plan)
    vmem = pl.BlockSpec(memory_space=pltpu.VMEM)
    first = state is None
    operands = [query, segments.reshape(1, rows), *mine, *other] + ([] if first else [state])
    return pl.pallas_call(
        functools.partial(attend_kernel, plan, first, last),
        in_specs=[vmem] * len(operands),
        out_specs=vmem,
        out_shape=pltpu.VMEM((rows, HD), jnp.bfloat16) if last else pltpu.VMEM((rows, HD + 2 * LANES), jnp.float32),
        scratch_shapes=[pltpu.VMEM((blocks, rows // 2, rows), jnp.float32)],
        input_output_aliases={} if first or last else {len(operands) - 1: 0},
        compiler_params=pltpu.CompilerParams(vmem_limit_bytes=12 * MIB),
        cost_estimate=pl.CostEstimate(
            flops=4 * rows * rows * blocks * HD, bytes_accessed=4 * rows * blocks * HD, transcendentals=rows * rows * blocks
        ),
        name="attend_last" if last else "attend_first" if first else "attend_more",
    )(*[in_vmem(operand) for operand in operands])


def bounds_kernel(sum_ref, out_exp_ref, x_ref, sum_bound_ref, out_bound_ref, wide_ref, near, sem):
    groups, rows = sum_ref.shape
    fetch = pltpu.make_async_copy(x_ref, near, sem)
    fetch.start()
    per = sum_bound_ref.shape[1] // groups
    for exps, bound_ref in ((sum_ref, sum_bound_ref), (out_exp_ref, out_bound_ref)):
        power = jnp.left_shift(jnp.int32(1), exps[...] - MIN_EXP).astype(jnp.float32)
        bound = jnp.transpose(power * (LIMIT * 2.0 ** MIN_EXP))
        for group in range(groups):
            wide = jnp.broadcast_to(bound[:, group:group + 1], (rows, per)).astype(jnp.bfloat16)
            bound_ref[:, group * per:(group + 1) * per] = wide
    fetch.wait()

    def widen(step, carry):
        span = pl.ds(pl.multiple_of(step * 64, 64), 64)
        wide_ref[span, :] = near[span, :].astype(jnp.float32)
        return carry

    lax.fori_loop(0, rows // 64, widen, 0)


def spread_bounds(sum_exps, out_exps, tokens):
    rows, width = tokens.shape
    groups = sum_exps.shape[1]
    vmem = pl.BlockSpec(memory_space=pltpu.VMEM)
    return pl.pallas_call(
        bounds_kernel,
        in_specs=[vmem, vmem, pl.BlockSpec(memory_space=pltpu.HBM)],
        out_specs=[vmem] * 3,
        out_shape=[pltpu.VMEM((rows, width), jnp.bfloat16)] * 2 + [pltpu.VMEM((rows, width), jnp.float32)],
        scratch_shapes=[pltpu.VMEM((rows, width), jnp.bfloat16), pltpu.SemaphoreType.DMA(())],
        compiler_params=pltpu.CompilerParams(vmem_limit_bytes=10 * MIB),
        cost_estimate=pl.CostEstimate(flops=8 * rows * width, bytes_accessed=8 * rows * groups, transcendentals=0),
        name="spread_bounds",
    )(in_vmem(sum_exps.T), in_vmem(out_exps.T), in_hbm(tokens))


def clip(value, bound):
    return jnp.minimum(jnp.maximum(value.astype(jnp.bfloat16), -bound), bound)


def own_kernel(a_ref, w_ref, sum_ref, out_ref):
    rows, width = out_ref.shape
    tile = rows // 2
    chunk = width // 4

    def body(step, carry):
        for at in range(0, chunk, HD):
            cols = pl.ds(pl.multiple_of(step * chunk + at, HD), HD)
            weights = w_ref[:, cols]
            for start in range(0, rows, tile):
                span = slice(start, start + tile)
                term = jnp.dot(a_ref[span, :], weights, preferred_element_type=jnp.float32)
                out_ref[span, cols] = clip(term, sum_ref[span, cols])
        return carry

    lax.fori_loop(0, 4, body, 0)


def project_own(attended, w_out, sum_bound):
    rows, depth = attended.shape
    width = w_out.shape[1]
    vmem = pl.BlockSpec(memory_space=pltpu.VMEM)
    return pl.pallas_call(
        own_kernel,
        in_specs=[vmem] * 3,
        out_specs=vmem,
        out_shape=pltpu.VMEM((rows, width), jnp.bfloat16),
        compiler_params=pltpu.CompilerParams(vmem_limit_bytes=8 * MIB),
        cost_estimate=pl.CostEstimate(
            flops=2 * rows * width * depth, bytes_accessed=4 * rows * width + 2 * width * depth, transcendentals=0
        ),
        name="project_own",
    )(in_vmem(attended), in_vmem(w_out), in_vmem(sum_bound))


def output_kernel(b_ref, wb_ref, quant_ref, x_ref, sum_ref, last_ref, out_ref, staged, sems):
    rows, width = x_ref.shape
    pieces = sems.shape[0]
    piece = width // pieces
    chunk = width // 2
    tile = rows // 2

    def copy(index):
        span = pl.ds(pl.multiple_of(index * piece, piece), piece)
        return pltpu.make_async_copy(staged.at[:, span], out_ref.at[:, span], sems.at[index])

    def body(step, carry):
        for at in range(0, chunk, HD):
            cols = pl.ds(pl.multiple_of(step * chunk + at, HD), HD)
            weights = wb_ref[:, cols]
            for start in range(0, rows, tile):
                span = slice(start, start + tile)
                term = jnp.dot(b_ref[span, :], weights, preferred_element_type=jnp.float32)
                other = clip(term, sum_ref[span, cols])
                quant = other.astype(jnp.float32) + quant_ref[span, cols].astype(jnp.float32)
                staged[span, cols] = clip(x_ref[span, cols] + quant, last_ref[span, cols])
            if (at + HD) % piece == 0:
                copy(step * (chunk // piece) + at // piece).start()
        return carry

    lax.fori_loop(0, width // chunk, body, 0)
    for index in range(pieces):
        copy(index).wait()


def project_out(att_other, w_other, quant_own, sum_bound, out_bound, tokens):
    rows, width = tokens.shape
    depth = att_other.shape[1]
    pieces = 16
    vmem = pl.BlockSpec(memory_space=pltpu.VMEM)
    operands = [att_other, w_other, quant_own, tokens, sum_bound, out_bound]
    return pl.pallas_call(
        output_kernel,
        in_specs=[vmem] * len(operands),
        out_specs=pl.BlockSpec(memory_space=pltpu.HBM),
        out_shape=jax.ShapeDtypeStruct((rows, width), jnp.bfloat16),
        scratch_shapes=[pltpu.VMEM((rows, width), jnp.bfloat16), pltpu.SemaphoreType.DMA((pieces,))],
        compiler_params=pltpu.CompilerParams(vmem_limit_bytes=10 * MIB),
        cost_estimate=pl.CostEstimate(
            flops=2 * rows * width * depth, bytes_accessed=4 * rows * width + 2 * width * depth, transcendentals=0
        ),
        name="project_out",
    )(*[in_vmem(operand) for operand in operands])


def on_device(seq_size, tokens, gain, segments, w_query, w_keyval, w_out, sum_exps, out_exps):
    window = seq_size // 2

    def swap_cores(x):
        return lax.ppermute(x, "tp", [(0, 1), (1, 0)])

    def shift(x, step, first):
        cycle = seq_size - first
        pairs = []
        for i in range(seq_size):
            for core in range(2):
                after = 2 * (first + (i - first + step) % cycle) + core if i >= first else 2 * i + 1 - core
                pairs.append((2 * i + core, after))
        return lax.ppermute(x, ("seq", "tp"), pairs)

    w_other = swap_cores(w_out)
    message, normed, w_near = norm_kv(tokens, gain, w_keyval, segments, w_query)
    query = project_query(normed, w_near)
    held, query = lax.optimization_barrier((shift(message, 2, 0), query))
    pair = lax.ppermute(message, "seq", [(i, i ^ 1) for i in range(seq_size)])
    along = [(i, min(i + 2, seq_size - 1)) for i in range(0, seq_size, 2)] + [(i, max(i - 2, 0)) for i in range(1, seq_size, 2)]
    pair, held = lax.optimization_barrier((pair, held))
    beside = lax.ppermute(pair, "seq", along)
    parts = [[(0, ALL, message), (1, ODD, pair), (2, ALL, held)], [(1, EVEN, beside)]]
    for back in range(2, window, 2):
        parts[-1].append((back + 1, ALL, shift(held, 1, back)))
        held = shift(held, 2, back)
        parts.append([(back + 2, ALL if back + 2 < window else FURTHEST, held)])
    exps = lax.optimization_barrier((sum_exps, out_exps, query))[:2]
    bounds = spread_bounds(*exps, tokens)
    state = None
    for number, blocks in enumerate(parts):
        plan = [(back, kind) for back, kind, _ in blocks]
        mine = [block for _, _, block in blocks]
        if number == 1:
            bounds, state = early = lax.optimization_barrier((bounds, state))
        if number > 0:
            mine = [lax.optimization_barrier((block, early))[0] for block in mine]
        other = [swap_cores(m) for m in mine]
        state = attend(query, segments, plan, mine, other, state, number == len(parts) - 1)
    quant_own = project_own(state, w_out, bounds[0])
    return project_out(swap_cores(state), w_other, quant_own, *bounds)


def solution(mesh):
    in_specs = (
        P(("groups", "seq"), None),
        P(),
        P(("groups", "seq")),
        P(None, "tp"),
        P(None, "tp"),
        P("tp", None),
        P(("groups", "seq"), None),
        P(("groups", "seq"), None),
    )
    out_specs = P(("groups", "seq"), None)
    return jax.shard_map(
        functools.partial(on_device, mesh.shape["seq"]),
        mesh=mesh, in_specs=in_specs, out_specs=out_specs, check_vma=False,
    )
```

```python
import functools

import jax
import jax.numpy as jnp
from jax import lax
from jax.experimental import pallas as pl
from jax.experimental.pallas import tpu as pltpu
from jax.sharding import PartitionSpec as P

HD = 256
LANES = 128
SEG_ROWS = 16
LIMIT = 448.0
MIN_EXP = -9
NEG = -1e30
MIB = 1024 * 1024
NT = (((1,), (1,)), ((), ()))
FACTOR = HD ** (-0.5) * 1.4426950408889634


def norm_kv_kernel(x_ref, gain_hbm, w_ref, seg_hbm, msg_ref, normed_ref, xs, ws, gain_ref, seg_ref, sems):
    rows, width = xs.shape
    tile, part = rows // 2, rows // 8
    pieces = 4
    deep = width // pieces

    def tokens_copy(i):
        return pltpu.make_async_copy(x_ref.at[pl.ds(i * part, part)], xs.at[pl.ds(i * part, part)], sems.at[i])

    def weights_copy(i):
        return pltpu.make_async_copy(w_ref.at[pl.ds(i * deep, deep)], ws.at[pl.ds(i * deep, deep)], sems.at[8 + i])

    def gain_copy():
        return pltpu.make_async_copy(gain_hbm, gain_ref, sems.at[12])

    def segments_copy():
        return pltpu.make_async_copy(seg_hbm, seg_ref, sems.at[13])

    for i in range(4):
        tokens_copy(i).start()
    gain_copy().start()
    for i in range(pieces):
        weights_copy(i).start()
    for i in range(4, 8):
        tokens_copy(i).start()
    segments_copy().start()

    def wide(first, count, start):
        return xs[first:first + count, start:start + LANES].astype(jnp.float32)

    def stats(first, count):
        total = wide(first, count, 0)
        for start in range(LANES, width, LANES):
            total = total + wide(first, count, start)
        mean = jnp.broadcast_to(jnp.sum(total, axis=1, keepdims=True) * (1.0 / width), (count, LANES))
        square = jnp.zeros((count, LANES), jnp.float32)
        for start in range(0, width, LANES):
            center = wide(first, count, start) - mean
            square = square + center * center
        spread = jnp.sum(square, axis=1, keepdims=True) * (1.0 / width)
        return mean, jnp.broadcast_to(lax.rsqrt(spread + 1e-05), (count, LANES))

    for first in range(0, rows, tile):
        halves = []
        for at in range(first, first + tile, 2 * part):
            tokens_copy(at // part).wait()
            tokens_copy(at // part + 1).wait()
            halves.append(stats(at, 2 * part))
        mean = jnp.concatenate([h[0] for h in halves], axis=0)
        scale = jnp.concatenate([h[1] for h in halves], axis=0)
        if first == 0:
            gain_copy().wait()
        kv = jnp.zeros((tile, ws.shape[1]), jnp.float32)
        span = slice(first, first + tile)
        for start in range(0, width, deep):
            if first == 0:
                weights_copy(start // deep).wait()
            for at in range(start, start + deep, LANES):
                normed = (wide(first, tile, at) - mean) * scale * gain_ref[:, at:at + LANES]
                normed_ref[span, at:at + LANES] = normed.astype(jnp.bfloat16)
            kv = kv + jnp.dot(
                normed_ref[span, start:start + deep], ws[start:start + deep, :], preferred_element_type=jnp.float32
            )
        msg_ref[span, :] = kv.astype(jnp.bfloat16)
    segments_copy().wait()
    seg = seg_ref[...].astype(jnp.float32)
    low = jnp.broadcast_to(seg[:, :HD], (8, HD))
    high = jnp.broadcast_to(seg[:, HD:], (8, HD))
    msg_ref[rows:, :] = jnp.concatenate([low, high], axis=0).astype(jnp.bfloat16)


def in_hbm(x):
    return pltpu.with_memory_space_constraint(x, pltpu.HBM)


def in_vmem(x):
    return pltpu.with_memory_space_constraint(x, pltpu.VMEM)


def norm_kv(tokens, gain, w_keyval, segments):
    rows, width = tokens.shape
    cols = w_keyval.shape[1]
    vmem, hbm = pl.BlockSpec(memory_space=pltpu.VMEM), pl.BlockSpec(memory_space=pltpu.HBM)
    return pl.pallas_call(
        norm_kv_kernel,
        in_specs=[hbm] * 4,
        out_specs=[vmem, vmem],
        out_shape=[pltpu.VMEM((rows + SEG_ROWS, cols), jnp.bfloat16), pltpu.VMEM((rows, width), jnp.bfloat16)],
        scratch_shapes=[
            pltpu.VMEM((rows, width), jnp.bfloat16),
            pltpu.VMEM((width, cols), jnp.bfloat16),
            pltpu.VMEM((1, width), jnp.float32),
            pltpu.VMEM((1, rows), jnp.int32),
            pltpu.SemaphoreType.DMA((14,)),
        ],
        compiler_params=pltpu.CompilerParams(vmem_limit_bytes=24 * MIB),
        cost_estimate=pl.CostEstimate(
            flops=2 * rows * width * cols, bytes_accessed=4 * rows * width + 2 * width * cols, transcendentals=0
        ),
        name="norm_kv",
    )(in_hbm(tokens), in_hbm(gain.reshape(1, width)), in_hbm(w_keyval), in_hbm(segments.reshape(1, rows)))


def query_kernel(x_ref, w_ref, out_ref):
    out_ref[...] = jnp.dot(x_ref[...], w_ref[...], preferred_element_type=jnp.float32).astype(jnp.bfloat16)


def project_query(normed, w_query):
    rows, width = normed.shape
    cols = w_query.shape[1]
    vmem = pl.BlockSpec(memory_space=pltpu.VMEM)
    return pl.pallas_call(
        query_kernel,
        in_specs=[vmem, vmem],
        out_specs=vmem,
        out_shape=pltpu.VMEM((rows, cols), jnp.bfloat16),
        compiler_params=pltpu.CompilerParams(vmem_limit_bytes=8 * MIB),
        cost_estimate=pl.CostEstimate(
            flops=2 * rows * width * cols, bytes_accessed=2 * rows * width + 2 * width * cols, transcendentals=0
        ),
        name="project_query",
    )(in_vmem(normed), in_vmem(w_query))


def attend_kernel(plan, first, last, *refs):
    blocks = len(plan)
    q_ref, seg_ref = refs[:2]
    mine, other = refs[2:2 + blocks], refs[2 + blocks:2 + 2 * blocks]
    refs = refs[2 + 2 * blocks:]
    state_ref = None
    if not first:
        state_ref, refs = refs[0], refs[1:]
    out_ref, scores = refs
    rows = q_ref.shape[0]
    tile = rows // 2
    part = lax.axis_index("tp")
    place = lax.axis_index("seq")

    def finish(span, weighted, total):
        out_ref[span, :] = (weighted / jnp.sum(total, axis=1, keepdims=True)).astype(jnp.bfloat16)

    def update(count, keys, values):
        own_seg = jnp.transpose(jnp.broadcast_to(seg_ref[...].astype(jnp.float32), (8, rows)))[:, 0:1]
        key_segs = []
        for slot in range(count):
            packed = mine[slot][rows:, :].astype(jnp.float32)
            key_segs.append(jnp.concatenate([packed[0:1, :], packed[8:9, :]], axis=1))
        for start in range(0, rows, tile):
            span = slice(start, start + tile)
            query = q_ref[span, :]
            best = None if first else state_ref[span, HD:HD + LANES]
            bounds = []
            for slot, (back, furthest) in enumerate(plan[:count]):
                low, high = 0, rows
                if back == 0:
                    high = start + tile
                elif furthest:
                    low = start
                bounds.append((low, high))
                raw = lax.dot_general(query, keys[slot][low:high, :], NT, preferred_element_type=jnp.float32)
                allowed = key_segs[slot][:, low:high] == own_seg[span, :]
                if back == 0:
                    row_pos = start + lax.broadcasted_iota(jnp.int32, raw.shape, 0)
                    allowed = allowed & (lax.broadcasted_iota(jnp.int32, raw.shape, 1) <= row_pos)
                masked = jnp.where(allowed, raw, NEG)
                scores[slot, :, low:high] = masked
                for at in range(0, high - low, LANES):
                    piece = masked[:, at:at + LANES]
                    best = piece if best is None else jnp.maximum(best, piece)
            top = jnp.broadcast_to(jnp.max(best, axis=1, keepdims=True), (tile, LANES))
            if first:
                total = jnp.zeros((tile, LANES), jnp.float32)
                weighted = jnp.zeros((tile, HD), jnp.float32)
            else:
                shrink = jnp.exp2((state_ref[span, HD:HD + LANES] - top) * FACTOR)
                total = state_ref[span, HD + LANES:] * shrink
                weighted = state_ref[span, :HD] * jnp.concatenate([shrink, shrink], axis=1)
            for slot in range(count):
                low, high = bounds[slot]
                pieces = []
                for at in range(low, high, LANES):
                    weights = jnp.exp2((scores[slot, :, at:at + LANES] - top) * FACTOR)
                    total = total + weights
                    pieces.append(weights.astype(jnp.bfloat16))
                probs = jnp.concatenate(pieces, axis=1)
                weighted = weighted + jnp.dot(probs, values[slot][low:high, :], preferred_element_type=jnp.float32)
            if last:
                finish(span, weighted, total)
            else:
                out_ref[span, :HD] = weighted
                out_ref[span, HD:HD + LANES] = top
                out_ref[span, HD + LANES:] = total

    for count in range(1 if first else 0, blocks + 1):
        reached = place >= (plan[count - 1][0] if count > 0 else 0)
        if count < blocks:
            reached = reached & (place < plan[count][0])
        if count > 0:
            pl.when(reached & (part == 0))(functools.partial(update, count, mine, other))
            pl.when(reached & (part == 1))(functools.partial(update, count, other, mine))
        elif last:

            @pl.when(reached)
            def _():
                finish(slice(0, rows), state_ref[:, :HD], state_ref[:, HD + LANES:])


def attend(query, segments, plan, mine, other, state, last):
    rows = query.shape[0]
    blocks = len(plan)
    vmem = pl.BlockSpec(memory_space=pltpu.VMEM)
    first = state is None
    operands = [query, segments.reshape(1, rows), *mine, *other] + ([] if first else [state])
    return pl.pallas_call(
        functools.partial(attend_kernel, plan, first, last),
        in_specs=[vmem] * len(operands),
        out_specs=vmem,
        out_shape=pltpu.VMEM((rows, HD), jnp.bfloat16) if last else pltpu.VMEM((rows, HD + 2 * LANES), jnp.float32),
        scratch_shapes=[pltpu.VMEM((blocks, rows // 2, rows), jnp.float32)],
        input_output_aliases={} if first or last else {len(operands) - 1: 0},
        compiler_params=pltpu.CompilerParams(vmem_limit_bytes=12 * MIB),
        cost_estimate=pl.CostEstimate(
            flops=4 * rows * rows * blocks * HD, bytes_accessed=4 * rows * blocks * HD, transcendentals=rows * rows * blocks
        ),
        name="attend_last" if last else "attend_first" if first else "attend_more",
    )(*[in_vmem(operand) for operand in operands])


def bounds_kernel(sum_ref, out_exp_ref, x_ref, sum_bound_ref, out_bound_ref, wide_ref, near, sem):
    groups, rows = sum_ref.shape
    fetch = pltpu.make_async_copy(x_ref, near, sem)
    fetch.start()
    per = sum_bound_ref.shape[1] // groups
    for exps, bound_ref in ((sum_ref, sum_bound_ref), (out_exp_ref, out_bound_ref)):
        power = jnp.left_shift(jnp.int32(1), exps[...] - MIN_EXP).astype(jnp.float32)
        bound = jnp.transpose(power * (LIMIT * 2.0 ** MIN_EXP))
        for group in range(groups):
            wide = jnp.broadcast_to(bound[:, group:group + 1], (rows, per)).astype(jnp.bfloat16)
            bound_ref[:, group * per:(group + 1) * per] = wide
    fetch.wait()

    def widen(step, carry):
        span = pl.ds(pl.multiple_of(step * 64, 64), 64)
        wide_ref[span, :] = near[span, :].astype(jnp.float32)
        return carry

    lax.fori_loop(0, rows // 64, widen, 0)


def spread_bounds(sum_exps, out_exps, tokens):
    rows, width = tokens.shape
    groups = sum_exps.shape[1]
    vmem = pl.BlockSpec(memory_space=pltpu.VMEM)
    return pl.pallas_call(
        bounds_kernel,
        in_specs=[vmem, vmem, pl.BlockSpec(memory_space=pltpu.HBM)],
        out_specs=[vmem] * 3,
        out_shape=[pltpu.VMEM((rows, width), jnp.bfloat16)] * 2 + [pltpu.VMEM((rows, width), jnp.float32)],
        scratch_shapes=[pltpu.VMEM((rows, width), jnp.bfloat16), pltpu.SemaphoreType.DMA(())],
        compiler_params=pltpu.CompilerParams(vmem_limit_bytes=10 * MIB),
        cost_estimate=pl.CostEstimate(flops=8 * rows * width, bytes_accessed=8 * rows * groups, transcendentals=0),
        name="spread_bounds",
    )(in_vmem(sum_exps.T), in_vmem(out_exps.T), in_hbm(tokens))


def clip(value, bound):
    return jnp.minimum(jnp.maximum(value.astype(jnp.bfloat16), -bound), bound)


def own_kernel(a_ref, w_ref, sum_ref, out_ref):
    rows, width = out_ref.shape
    tile = rows
    chunk = width // 4

    def body(step, carry):
        for at in range(0, chunk, HD):
            cols = pl.ds(pl.multiple_of(step * chunk + at, HD), HD)
            weights = w_ref[:, cols]
            for start in range(0, rows, tile):
                span = slice(start, start + tile)
                term = jnp.dot(a_ref[span, :], weights, preferred_element_type=jnp.float32)
                out_ref[span, cols] = clip(term, sum_ref[span, cols])
        return carry

    lax.fori_loop(0, 4, body, 0)


def project_own(attended, w_out, sum_bound):
    rows, depth = attended.shape
    width = w_out.shape[1]
    vmem = pl.BlockSpec(memory_space=pltpu.VMEM)
    return pl.pallas_call(
        own_kernel,
        in_specs=[vmem] * 3,
        out_specs=vmem,
        out_shape=pltpu.VMEM((rows, width), jnp.bfloat16),
        compiler_params=pltpu.CompilerParams(vmem_limit_bytes=8 * MIB),
        cost_estimate=pl.CostEstimate(
            flops=2 * rows * width * depth, bytes_accessed=4 * rows * width + 2 * width * depth, transcendentals=0
        ),
        name="project_own",
    )(in_vmem(attended), in_vmem(w_out), in_vmem(sum_bound))


def output_kernel(b_ref, wb_ref, quant_ref, x_ref, sum_ref, last_ref, out_ref, staged, sems):
    rows, width = x_ref.shape
    pieces = sems.shape[0]
    piece = width // pieces
    chunk = width // 2
    tile = rows

    def copy(index):
        span = pl.ds(pl.multiple_of(index * piece, piece), piece)
        return pltpu.make_async_copy(staged.at[:, span], out_ref.at[:, span], sems.at[index])

    def body(step, carry):
        for at in range(0, chunk, HD):
            cols = pl.ds(pl.multiple_of(step * chunk + at, HD), HD)
            weights = wb_ref[:, cols]
            for start in range(0, rows, tile):
                span = slice(start, start + tile)
                term = jnp.dot(b_ref[span, :], weights, preferred_element_type=jnp.float32)
                other = clip(term, sum_ref[span, cols])
                quant = other.astype(jnp.float32) + quant_ref[span, cols].astype(jnp.float32)
                staged[span, cols] = clip(x_ref[span, cols] + quant, last_ref[span, cols])
            if (at + HD) % piece == 0:
                copy(step * (chunk // piece) + at // piece).start()
        return carry

    lax.fori_loop(0, width // chunk, body, 0)
    for index in range(pieces):
        copy(index).wait()


def project_out(att_other, w_other, quant_own, sum_bound, out_bound, tokens):
    rows, width = tokens.shape
    depth = att_other.shape[1]
    pieces = 8
    vmem = pl.BlockSpec(memory_space=pltpu.VMEM)
    operands = [att_other, w_other, quant_own, tokens, sum_bound, out_bound]
    return pl.pallas_call(
        output_kernel,
        in_specs=[vmem] * len(operands),
        out_specs=pl.BlockSpec(memory_space=pltpu.HBM),
        out_shape=jax.ShapeDtypeStruct((rows, width), jnp.bfloat16),
        scratch_shapes=[pltpu.VMEM((rows, width), jnp.bfloat16), pltpu.SemaphoreType.DMA((pieces,))],
        compiler_params=pltpu.CompilerParams(vmem_limit_bytes=10 * MIB),
        cost_estimate=pl.CostEstimate(
            flops=2 * rows * width * depth, bytes_accessed=4 * rows * width + 2 * width * depth, transcendentals=0
        ),
        name="project_out",
    )(*[in_vmem(operand) for operand in operands])


def on_device(seq_size, tokens, gain, segments, w_query, w_keyval, w_out, sum_exps, out_exps):
    window = seq_size // 2

    def swap_cores(x):
        return lax.ppermute(x, "tp", [(0, 1), (1, 0)])

    def shift(x, step, first):
        cycle = seq_size - first
        pairs = []
        for i in range(seq_size):
            for core in range(2):
                after = 2 * (first + (i - first + step) % cycle) + core if i >= first else 2 * i + 1 - core
                pairs.append((2 * i + core, after))
        return lax.ppermute(x, ("seq", "tp"), pairs)

    w_other = swap_cores(w_out)
    message, normed = norm_kv(tokens, gain, w_keyval, segments)
    query = project_query(normed, w_query)
    held, query = lax.optimization_barrier((shift(message, 2, 0), query))
    odd = lax.rem(lax.axis_index("seq"), 2) == 1
    beside = lax.ppermute(jnp.where(odd, held, message), "seq", [(i, i ^ 1) for i in range(seq_size)])
    parts = [[(0, message), (2, held)]]
    for back in range(2, window, 2):
        step = shift(held, 1, back)
        held = shift(held, 2, back)
        parts.append([(back + 1, step)] + ([(back + 2, held)] if back + 2 < window else []))
    parts.append([(1, beside), (window, held)])
    exps = lax.optimization_barrier((sum_exps, out_exps, query))[:2]
    bounds = spread_bounds(*exps, tokens)
    state = None
    for number, blocks in enumerate(parts):
        plan = [(back, back == window) for back, _ in blocks]
        mine = [block for _, block in blocks]
        if number == 1:
            bounds, state = early = lax.optimization_barrier((bounds, state))
        if number > 0:
            mine = [lax.optimization_barrier((block, early))[0] for block in mine]
        other = [swap_cores(m) for m in mine]
        state = attend(query, segments, plan, mine, other, state, number == len(parts) - 1)
    quant_own = project_own(state, w_out, bounds[0])
    return project_out(swap_cores(state), w_other, quant_own, *bounds)


def solution(mesh):
    in_specs = (
        P(("groups", "seq"), None),
        P(),
        P(("groups", "seq")),
        P(None, "tp"),
        P(None, "tp"),
        P("tp", None),
        P(("groups", "seq"), None),
        P(("groups", "seq"), None),
    )
    out_specs = P(("groups", "seq"), None)
    return jax.shard_map(
        functools.partial(on_device, mesh.shape["seq"]),
        mesh=mesh, in_specs=in_specs, out_specs=out_specs, check_vma=False,
    )
```

```python
import functools

import jax
import jax.numpy as jnp
from jax import lax
from jax.experimental import pallas as pl
from jax.experimental.pallas import tpu as pltpu
from jax.sharding import PartitionSpec as P

HD = 256
LANES = 128
SEG_ROWS = 16
LIMIT = 448.0
MIN_EXP = -9
NEG = -1e30
MIB = 1024 * 1024
NT = (((1,), (1,)), ((), ()))
FACTOR = HD ** (-0.5) * 1.4426950408889634


def norm_kv_kernel(x_ref, gain_hbm, w_ref, seg_hbm, next_ref, msg_ref, normed_ref, near_ref, xs, ws, gain_ref, seg_ref, sems):
    rows, width = xs.shape
    tile, part = rows // 2, rows // 4

    def tokens_copy(i):
        return pltpu.make_async_copy(x_ref.at[pl.ds(i * part, part)], xs.at[pl.ds(i * part, part)], sems.at[i])

    def weights_copy():
        return pltpu.make_async_copy(w_ref, ws, sems.at[4])

    def gain_copy():
        return pltpu.make_async_copy(gain_hbm, gain_ref, sems.at[5])

    def segments_copy():
        return pltpu.make_async_copy(seg_hbm, seg_ref, sems.at[6])

    def next_copy():
        return pltpu.make_async_copy(next_ref, near_ref, sems.at[7])

    def wide(first, count, start):
        return xs[first:first + count, start:start + LANES].astype(jnp.float32)

    def stats(first):
        total = wide(first, part, 0)
        for start in range(LANES, width, LANES):
            total = total + wide(first, part, start)
        mean = jnp.broadcast_to(jnp.sum(total, axis=1, keepdims=True) * (1.0 / width), (part, LANES))
        square = jnp.zeros((part, LANES), jnp.float32)
        for start in range(0, width, LANES):
            center = wide(first, part, start) - mean
            square = square + center * center
        spread = jnp.sum(square, axis=1, keepdims=True) * (1.0 / width)
        return mean, jnp.broadcast_to(lax.rsqrt(spread + 1e-05), (part, LANES))

    def project(first, halves):
        mean = jnp.concatenate([h[0] for h in halves], axis=0)
        scale = jnp.concatenate([h[1] for h in halves], axis=0)
        kv = jnp.zeros((tile, ws.shape[1]), jnp.float32)
        span = slice(first, first + tile)
        for start in range(0, width, HD):
            for at in (start, start + LANES):
                normed = (wide(first, tile, at) - mean) * scale * gain_ref[:, at:at + LANES]
                normed_ref[span, at:at + LANES] = normed.astype(jnp.bfloat16)
            kv = kv + jnp.dot(
                normed_ref[span, start:start + HD], ws[start:start + HD, :], preferred_element_type=jnp.float32
            )
        msg_ref[span, :] = kv.astype(jnp.bfloat16)

    tokens_copy(0).start()
    tokens_copy(1).start()
    tokens_copy(0).wait()
    gain_copy().start()
    weights_copy().start()
    halves = [stats(0)]
    tokens_copy(1).wait()
    tokens_copy(2).start()
    halves.append(stats(part))
    gain_copy().wait()
    weights_copy().wait()
    tokens_copy(3).start()
    segments_copy().start()
    project(0, halves)
    tokens_copy(2).wait()
    halves = [stats(tile)]
    tokens_copy(3).wait()
    next_copy().start()
    halves.append(stats(tile + part))
    project(tile, halves)
    segments_copy().wait()
    seg = seg_ref[...].astype(jnp.float32)
    low = jnp.broadcast_to(seg[:, :HD], (8, HD))
    high = jnp.broadcast_to(seg[:, HD:], (8, HD))
    msg_ref[rows:, :] = jnp.concatenate([low, high], axis=0).astype(jnp.bfloat16)
    next_copy().wait()


def in_hbm(x):
    return pltpu.with_memory_space_constraint(x, pltpu.HBM)


def in_vmem(x):
    return pltpu.with_memory_space_constraint(x, pltpu.VMEM)


def norm_kv(tokens, gain, w_keyval, segments, w_next):
    rows, width = tokens.shape
    cols = w_keyval.shape[1]
    vmem, hbm = pl.BlockSpec(memory_space=pltpu.VMEM), pl.BlockSpec(memory_space=pltpu.HBM)
    return pl.pallas_call(
        norm_kv_kernel,
        in_specs=[hbm] * 5,
        out_specs=[vmem] * 3,
        out_shape=[
            pltpu.VMEM((rows + SEG_ROWS, cols), jnp.bfloat16),
            pltpu.VMEM((rows, width), jnp.bfloat16),
            pltpu.VMEM(w_next.shape, w_next.dtype),
        ],
        scratch_shapes=[
            pltpu.VMEM((rows, width), jnp.bfloat16),
            pltpu.VMEM((width, cols), jnp.bfloat16),
            pltpu.VMEM((1, width), jnp.float32),
            pltpu.VMEM((1, rows), jnp.int32),
            pltpu.SemaphoreType.DMA((8,)),
        ],
        compiler_params=pltpu.CompilerParams(vmem_limit_bytes=24 * MIB),
        cost_estimate=pl.CostEstimate(
            flops=2 * rows * width * cols, bytes_accessed=4 * rows * width + 2 * width * cols, transcendentals=0
        ),
        name="norm_kv",
    )(*[in_hbm(x) for x in (tokens, gain.reshape(1, width), w_keyval, segments.reshape(1, rows), w_next)])


def query_kernel(x_ref, w_ref, out_ref):
    out_ref[...] = jnp.dot(x_ref[...], w_ref[...], preferred_element_type=jnp.float32).astype(jnp.bfloat16)


def project_query(normed, w_query):
    rows, width = normed.shape
    cols = w_query.shape[1]
    vmem = pl.BlockSpec(memory_space=pltpu.VMEM)
    return pl.pallas_call(
        query_kernel,
        in_specs=[vmem, vmem],
        out_specs=vmem,
        out_shape=pltpu.VMEM((rows, cols), jnp.bfloat16),
        compiler_params=pltpu.CompilerParams(vmem_limit_bytes=8 * MIB),
        cost_estimate=pl.CostEstimate(
            flops=2 * rows * width * cols, bytes_accessed=2 * rows * width + 2 * width * cols, transcendentals=0
        ),
        name="project_query",
    )(in_vmem(normed), in_vmem(w_query))


def attend_kernel(plan, first, last, *refs):
    blocks = len(plan)
    q_ref, seg_ref = refs[:2]
    mine, other = refs[2:2 + blocks], refs[2 + blocks:2 + 2 * blocks]
    refs = refs[2 + 2 * blocks:]
    state_ref = None
    if not first:
        state_ref, refs = refs[0], refs[1:]
    out_ref, scores = refs
    rows = q_ref.shape[0]
    tile = rows // 4
    part = lax.axis_index("tp")
    place = lax.axis_index("seq")

    def finish(span, weighted, total):
        out_ref[span, :] = (weighted / jnp.sum(total, axis=1, keepdims=True)).astype(jnp.bfloat16)

    def update(count, keys, values):
        own_seg = jnp.transpose(jnp.broadcast_to(seg_ref[...].astype(jnp.float32), (8, rows)))[:, 0:1]
        key_segs = []
        for slot in range(count):
            packed = mine[slot][rows:, :].astype(jnp.float32)
            key_segs.append(jnp.concatenate([packed[0:1, :], packed[8:9, :]], axis=1))
        for start in range(0, rows, tile):
            span = slice(start, start + tile)
            query = q_ref[span, :]
            best = None if first else state_ref[span, HD:HD + LANES]
            bounds = []
            for slot, (back, furthest) in enumerate(plan[:count]):
                low, high = 0, rows
                if back == 0:
                    high = start + tile
                elif furthest:
                    low = start
                bounds.append((low, high))
                raw = lax.dot_general(query, keys[slot][low:high, :], NT, preferred_element_type=jnp.float32)
                allowed = key_segs[slot][:, low:high] == own_seg[span, :]
                if back == 0:
                    row_pos = start + lax.broadcasted_iota(jnp.int32, raw.shape, 0)
                    allowed = allowed & (lax.broadcasted_iota(jnp.int32, raw.shape, 1) <= row_pos)
                masked = jnp.where(allowed, raw, NEG)
                scores[slot, :, low:high] = masked
                for at in range(0, high - low, LANES):
                    piece = masked[:, at:at + LANES]
                    best = piece if best is None else jnp.maximum(best, piece)
            top = jnp.broadcast_to(jnp.max(best, axis=1, keepdims=True), (tile, LANES))
            if first:
                total = jnp.zeros((tile, LANES), jnp.float32)
                weighted = jnp.zeros((tile, HD), jnp.float32)
            else:
                shrink = jnp.exp2((state_ref[span, HD:HD + LANES] - top) * FACTOR)
                total = state_ref[span, HD + LANES:] * shrink
                weighted = state_ref[span, :HD] * jnp.concatenate([shrink, shrink], axis=1)
            for slot in range(count):
                low, high = bounds[slot]
                pieces = []
                for at in range(low, high, LANES):
                    weights = jnp.exp2((scores[slot, :, at:at + LANES] - top) * FACTOR)
                    total = total + weights
                    pieces.append(weights.astype(jnp.bfloat16))
                probs = jnp.concatenate(pieces, axis=1)
                weighted = weighted + jnp.dot(probs, values[slot][low:high, :], preferred_element_type=jnp.float32)
            if last:
                finish(span, weighted, total)
            else:
                out_ref[span, :HD] = weighted
                out_ref[span, HD:HD + LANES] = top
                out_ref[span, HD + LANES:] = total

    for count in range(1 if first else 0, blocks + 1):
        reached = place >= (plan[count - 1][0] if count > 0 else 0)
        if count < blocks:
            reached = reached & (place < plan[count][0])
        if count > 0:
            pl.when(reached & (part == 0))(functools.partial(update, count, mine, other))
            pl.when(reached & (part == 1))(functools.partial(update, count, other, mine))
        elif last:

            @pl.when(reached)
            def _():
                finish(slice(0, rows), state_ref[:, :HD], state_ref[:, HD + LANES:])


def attend(query, segments, plan, mine, other, state, last):
    rows = query.shape[0]
    blocks = len(plan)
    vmem = pl.BlockSpec(memory_space=pltpu.VMEM)
    first = state is None
    operands = [query, segments.reshape(1, rows), *mine, *other] + ([] if first else [state])
    return pl.pallas_call(
        functools.partial(attend_kernel, plan, first, last),
        in_specs=[vmem] * len(operands),
        out_specs=vmem,
        out_shape=pltpu.VMEM((rows, HD), jnp.bfloat16) if last else pltpu.VMEM((rows, HD + 2 * LANES), jnp.float32),
        scratch_shapes=[pltpu.VMEM((blocks, rows // 4, rows), jnp.float32)],
        input_output_aliases={} if first or last else {len(operands) - 1: 0},
        compiler_params=pltpu.CompilerParams(vmem_limit_bytes=12 * MIB),
        cost_estimate=pl.CostEstimate(
            flops=4 * rows * rows * blocks * HD, bytes_accessed=4 * rows * blocks * HD, transcendentals=rows * rows * blocks
        ),
        name="attend_last" if last else "attend_first" if first else "attend_more",
    )(*[in_vmem(operand) for operand in operands])


def bounds_kernel(sum_ref, out_exp_ref, x_ref, sum_bound_ref, out_bound_ref, wide_ref, near, sem):
    groups, rows = sum_ref.shape
    fetch = pltpu.make_async_copy(x_ref, near, sem)
    fetch.start()
    per = sum_bound_ref.shape[1] // groups
    for exps, bound_ref in ((sum_ref, sum_bound_ref), (out_exp_ref, out_bound_ref)):
        power = jnp.left_shift(jnp.int32(1), exps[...] - MIN_EXP).astype(jnp.float32)
        bound = jnp.transpose(power * (LIMIT * 2.0 ** MIN_EXP))
        for group in range(groups):
            wide = jnp.broadcast_to(bound[:, group:group + 1], (rows, per)).astype(jnp.bfloat16)
            bound_ref[:, group * per:(group + 1) * per] = wide
    fetch.wait()

    def widen(step, carry):
        span = pl.ds(pl.multiple_of(step * 64, 64), 64)
        wide_ref[span, :] = near[span, :].astype(jnp.float32)
        return carry

    lax.fori_loop(0, rows // 64, widen, 0)


def spread_bounds(sum_exps, out_exps, tokens):
    rows, width = tokens.shape
    groups = sum_exps.shape[1]
    vmem = pl.BlockSpec(memory_space=pltpu.VMEM)
    return pl.pallas_call(
        bounds_kernel,
        in_specs=[vmem, vmem, pl.BlockSpec(memory_space=pltpu.HBM)],
        out_specs=[vmem] * 3,
        out_shape=[pltpu.VMEM((rows, width), jnp.bfloat16)] * 2 + [pltpu.VMEM((rows, width), jnp.float32)],
        scratch_shapes=[pltpu.VMEM((rows, width), jnp.bfloat16), pltpu.SemaphoreType.DMA(())],
        compiler_params=pltpu.CompilerParams(vmem_limit_bytes=10 * MIB),
        cost_estimate=pl.CostEstimate(flops=8 * rows * width, bytes_accessed=8 * rows * groups, transcendentals=0),
        name="spread_bounds",
    )(in_vmem(sum_exps.T), in_vmem(out_exps.T), in_hbm(tokens))


def clip(value, bound):
    return jnp.minimum(jnp.maximum(value.astype(jnp.bfloat16), -bound), bound)


def own_kernel(a_ref, w_ref, sum_ref, out_ref):
    rows, width = out_ref.shape
    tile = rows // 4
    chunk = width // 4

    def body(step, carry):
        for at in range(0, chunk, HD):
            cols = pl.ds(pl.multiple_of(step * chunk + at, HD), HD)
            weights = w_ref[:, cols]
            for start in range(0, rows, tile):
                span = slice(start, start + tile)
                term = jnp.dot(a_ref[span, :], weights, preferred_element_type=jnp.float32)
                out_ref[span, cols] = clip(term, sum_ref[span, cols])
        return carry

    lax.fori_loop(0, 4, body, 0)


def project_own(attended, w_out, sum_bound):
    rows, depth = attended.shape
    width = w_out.shape[1]
    vmem = pl.BlockSpec(memory_space=pltpu.VMEM)
    return pl.pallas_call(
        own_kernel,
        in_specs=[vmem] * 3,
        out_specs=vmem,
        out_shape=pltpu.VMEM((rows, width), jnp.bfloat16),
        compiler_params=pltpu.CompilerParams(vmem_limit_bytes=8 * MIB),
        cost_estimate=pl.CostEstimate(
            flops=2 * rows * width * depth, bytes_accessed=4 * rows * width + 2 * width * depth, transcendentals=0
        ),
        name="project_own",
    )(in_vmem(attended), in_vmem(w_out), in_vmem(sum_bound))


def output_kernel(b_ref, wb_ref, quant_ref, x_ref, sum_ref, last_ref, out_ref, staged, sems):
    rows, width = x_ref.shape
    pieces = sems.shape[0]
    piece = width // pieces
    chunk = width // 2
    tile = rows // 4

    def copy(index):
        span = pl.ds(pl.multiple_of(index * piece, piece), piece)
        return pltpu.make_async_copy(staged.at[:, span], out_ref.at[:, span], sems.at[index])

    def body(step, carry):
        for at in range(0, chunk, HD):
            cols = pl.ds(pl.multiple_of(step * chunk + at, HD), HD)
            weights = wb_ref[:, cols]
            for start in range(0, rows, tile):
                span = slice(start, start + tile)
                term = jnp.dot(b_ref[span, :], weights, preferred_element_type=jnp.float32)
                other = clip(term, sum_ref[span, cols])
                quant = other.astype(jnp.float32) + quant_ref[span, cols].astype(jnp.float32)
                staged[span, cols] = clip(x_ref[span, cols] + quant, last_ref[span, cols])
            if (at + HD) % piece == 0:
                copy(step * (chunk // piece) + at // piece).start()
        return carry

    lax.fori_loop(0, width // chunk, body, 0)
    for index in range(pieces):
        copy(index).wait()


def project_out(att_other, w_other, quant_own, sum_bound, out_bound, tokens):
    rows, width = tokens.shape
    depth = att_other.shape[1]
    pieces = 8
    vmem = pl.BlockSpec(memory_space=pltpu.VMEM)
    operands = [att_other, w_other, quant_own, tokens, sum_bound, out_bound]
    return pl.pallas_call(
        output_kernel,
        in_specs=[vmem] * len(operands),
        out_specs=pl.BlockSpec(memory_space=pltpu.HBM),
        out_shape=jax.ShapeDtypeStruct((rows, width), jnp.bfloat16),
        scratch_shapes=[pltpu.VMEM((rows, width), jnp.bfloat16), pltpu.SemaphoreType.DMA((pieces,))],
        compiler_params=pltpu.CompilerParams(vmem_limit_bytes=10 * MIB),
        cost_estimate=pl.CostEstimate(
            flops=2 * rows * width * depth, bytes_accessed=4 * rows * width + 2 * width * depth, transcendentals=0
        ),
        name="project_out",
    )(*[in_vmem(operand) for operand in operands])


def on_device(seq_size, tokens, gain, segments, w_query, w_keyval, w_out, sum_exps, out_exps):
    window = seq_size // 2

    def swap_cores(x):
        return lax.ppermute(x, "tp", [(0, 1), (1, 0)])

    def shift(x, step, first):
        cycle = seq_size - first
        pairs = []
        for i in range(seq_size):
            for core in range(2):
                after = 2 * (first + (i - first + step) % cycle) + core if i >= first else 2 * i + 1 - core
                pairs.append((2 * i + core, after))
        return lax.ppermute(x, ("seq", "tp"), pairs)

    w_other = swap_cores(w_out)
    message, normed, w_near = norm_kv(tokens, gain, w_keyval, segments, w_query)
    query = project_query(normed, w_near)
    held, query = lax.optimization_barrier((shift(message, 2, 0), query))
    odd = lax.rem(lax.axis_index("seq"), 2) == 1
    beside = lax.ppermute(jnp.where(odd, held, message), "seq", [(i, i ^ 1) for i in range(seq_size)])
    parts = [[(0, message), (2, held)]]
    for back in range(2, window, 2):
        step = shift(held, 1, back)
        held = shift(held, 2, back)
        parts.append([(back + 1, step)] + ([(back + 2, held)] if back + 2 < window else []))
    parts.append([(1, beside), (window, held)])
    exps = lax.optimization_barrier((sum_exps, out_exps, query))[:2]
    bounds = spread_bounds(*exps, tokens)
    state = None
    for number, blocks in enumerate(parts):
        plan = [(back, back == window) for back, _ in blocks]
        mine = [block for _, block in blocks]
        if number == 1:
            bounds, state = early = lax.optimization_barrier((bounds, state))
        if number > 0:
            mine = [lax.optimization_barrier((block, early))[0] for block in mine]
        other = [swap_cores(m) for m in mine]
        state = attend(query, segments, plan, mine, other, state, number == len(parts) - 1)
    quant_own = project_own(state, w_out, bounds[0])
    return project_out(swap_cores(state), w_other, quant_own, *bounds)


def solution(mesh):
    in_specs = (
        P(("groups", "seq"), None),
        P(),
        P(("groups", "seq")),
        P(None, "tp"),
        P(None, "tp"),
        P("tp", None),
        P(("groups", "seq"), None),
        P(("groups", "seq"), None),
    )
    out_specs = P(("groups", "seq"), None)
    return jax.shard_map(
        functools.partial(on_device, mesh.shape["seq"]),
        mesh=mesh, in_specs=in_specs, out_specs=out_specs, check_vma=False,
    )
```

```python
import functools

import jax
import jax.numpy as jnp
from jax import lax
from jax.experimental import pallas as pl
from jax.experimental.pallas import tpu as pltpu
from jax.sharding import PartitionSpec as P

HD = 256
LANES = 128
SEG_ROWS = 16
LIMIT = 448.0
MIN_EXP = -9
NEG = -1e30
MIB = 1024 * 1024
NT = (((1,), (1,)), ((), ()))
FACTOR = HD ** (-0.5) * 1.4426950408889634


def norm_kv_kernel(x_ref, gain_hbm, w_ref, seg_hbm, msg_ref, normed_ref, xs, ws, gain_ref, seg_ref, sems):
    rows, width = xs.shape
    steps = 2
    tile, part = rows // steps, rows // 4

    def tokens_copy(step):
        span = pl.ds(pl.multiple_of(step * tile, tile), tile)
        return pltpu.make_async_copy(x_ref.at[span], xs.at[span], sems.at[step])

    def weights_copy():
        return pltpu.make_async_copy(w_ref, ws, sems.at[2])

    def gain_copy():
        return pltpu.make_async_copy(gain_hbm, gain_ref, sems.at[3])

    def segments_copy():
        return pltpu.make_async_copy(seg_hbm, seg_ref, sems.at[4])

    tokens_copy(0).start()
    gain_copy().start()
    weights_copy().start()
    tokens_copy(1).start()
    segments_copy().start()

    def wide(first, count, start):
        return xs[pl.ds(pl.multiple_of(first, part), count), start:start + LANES].astype(jnp.float32)

    def stats(first):
        total = wide(first, part, 0)
        for start in range(LANES, width, LANES):
            total = total + wide(first, part, start)
        mean = jnp.broadcast_to(jnp.sum(total, axis=1, keepdims=True) * (1.0 / width), (part, LANES))
        square = jnp.zeros((part, LANES), jnp.float32)
        for start in range(0, width, LANES):
            center = wide(first, part, start) - mean
            square = square + center * center
        spread = jnp.sum(square, axis=1, keepdims=True) * (1.0 / width)
        return mean, jnp.broadcast_to(lax.rsqrt(spread + 1e-05), (part, LANES))

    def body(step, carry):
        first = step * tile
        tokens_copy(step).wait()
        halves = [stats(first + at) for at in range(0, tile, part)]
        mean = jnp.concatenate([h[0] for h in halves], axis=0)
        scale = jnp.concatenate([h[1] for h in halves], axis=0)

        @pl.when(step == 0)
        def _():
            gain_copy().wait()
            weights_copy().wait()

        kv = jnp.zeros((tile, ws.shape[1]), jnp.float32)
        span = pl.ds(pl.multiple_of(first, tile), tile)
        for start in range(0, width, HD):
            for at in (start, start + LANES):
                normed = (wide(first, tile, at) - mean) * scale * gain_ref[:, at:at + LANES]
                normed_ref[span, at:at + LANES] = normed.astype(jnp.bfloat16)
            kv = kv + jnp.dot(
                normed_ref[span, start:start + HD], ws[start:start + HD, :], preferred_element_type=jnp.float32
            )
        msg_ref[span, :] = kv.astype(jnp.bfloat16)
        return carry

    lax.fori_loop(0, steps, body, 0)
    segments_copy().wait()
    seg = seg_ref[...].astype(jnp.float32)
    low = jnp.broadcast_to(seg[:, :HD], (8, HD))
    high = jnp.broadcast_to(seg[:, HD:], (8, HD))
    msg_ref[rows:, :] = jnp.concatenate([low, high], axis=0).astype(jnp.bfloat16)


def in_hbm(x):
    return pltpu.with_memory_space_constraint(x, pltpu.HBM)


def in_vmem(x):
    return pltpu.with_memory_space_constraint(x, pltpu.VMEM)


def norm_kv(tokens, gain, w_keyval, segments):
    rows, width = tokens.shape
    cols = w_keyval.shape[1]
    vmem, hbm = pl.BlockSpec(memory_space=pltpu.VMEM), pl.BlockSpec(memory_space=pltpu.HBM)
    return pl.pallas_call(
        norm_kv_kernel,
        in_specs=[hbm] * 4,
        out_specs=[vmem, vmem],
        out_shape=[pltpu.VMEM((rows + SEG_ROWS, cols), jnp.bfloat16), pltpu.VMEM((rows, width), jnp.bfloat16)],
        scratch_shapes=[
            pltpu.VMEM((rows, width), jnp.bfloat16),
            pltpu.VMEM((width, cols), jnp.bfloat16),
            pltpu.VMEM((1, width), jnp.float32),
            pltpu.VMEM((1, rows), jnp.int32),
            pltpu.SemaphoreType.DMA((5,)),
        ],
        compiler_params=pltpu.CompilerParams(vmem_limit_bytes=24 * MIB),
        cost_estimate=pl.CostEstimate(
            flops=2 * rows * width * cols, bytes_accessed=4 * rows * width + 2 * width * cols, transcendentals=0
        ),
        name="norm_kv",
    )(in_hbm(tokens), in_hbm(gain.reshape(1, width)), in_hbm(w_keyval), in_hbm(segments.reshape(1, rows)))


def query_kernel(x_ref, w_ref, out_ref):
    out_ref[...] = jnp.dot(x_ref[...], w_ref[...], preferred_element_type=jnp.float32).astype(jnp.bfloat16)


def project_query(normed, w_query):
    rows, width = normed.shape
    cols = w_query.shape[1]
    vmem = pl.BlockSpec(memory_space=pltpu.VMEM)
    return pl.pallas_call(
        query_kernel,
        in_specs=[vmem, vmem],
        out_specs=vmem,
        out_shape=pltpu.VMEM((rows, cols), jnp.bfloat16),
        compiler_params=pltpu.CompilerParams(vmem_limit_bytes=8 * MIB),
        cost_estimate=pl.CostEstimate(
            flops=2 * rows * width * cols, bytes_accessed=2 * rows * width + 2 * width * cols, transcendentals=0
        ),
        name="project_query",
    )(in_vmem(normed), in_vmem(w_query))


def attend_kernel(plan, first, last, *refs):
    blocks = len(plan)
    q_ref, seg_ref = refs[:2]
    mine, other = refs[2:2 + blocks], refs[2 + blocks:2 + 2 * blocks]
    refs = refs[2 + 2 * blocks:]
    state_ref = None
    if not first:
        state_ref, refs = refs[0], refs[1:]
    out_ref, scores = refs
    rows = q_ref.shape[0]
    tile = rows
    part = lax.axis_index("tp")
    place = lax.axis_index("seq")

    def finish(span, weighted, total):
        out_ref[span, :] = (weighted / jnp.sum(total, axis=1, keepdims=True)).astype(jnp.bfloat16)

    def update(count, keys, values):
        own_seg = jnp.transpose(jnp.broadcast_to(seg_ref[...].astype(jnp.float32), (8, rows)))[:, 0:1]
        key_segs = []
        for slot in range(count):
            packed = mine[slot][rows:, :].astype(jnp.float32)
            key_segs.append(jnp.concatenate([packed[0:1, :], packed[8:9, :]], axis=1))
        for start in range(0, rows, tile):
            span = slice(start, start + tile)
            query = q_ref[span, :]
            best = None if first else state_ref[span, HD:HD + LANES]
            bounds = []
            for slot, (back, furthest) in enumerate(plan[:count]):
                low, high = 0, rows
                if back == 0:
                    high = start + tile
                elif furthest:
                    low = start
                bounds.append((low, high))
                raw = lax.dot_general(query, keys[slot][low:high, :], NT, preferred_element_type=jnp.float32)
                allowed = key_segs[slot][:, low:high] == own_seg[span, :]
                if back == 0:
                    row_pos = start + lax.broadcasted_iota(jnp.int32, raw.shape, 0)
                    allowed = allowed & (lax.broadcasted_iota(jnp.int32, raw.shape, 1) <= row_pos)
                masked = jnp.where(allowed, raw, NEG)
                scores[slot, :, low:high] = masked
                for at in range(0, high - low, LANES):
                    piece = masked[:, at:at + LANES]
                    best = piece if best is None else jnp.maximum(best, piece)
            top = jnp.broadcast_to(jnp.max(best, axis=1, keepdims=True), (tile, LANES))
            if first:
                total = jnp.zeros((tile, LANES), jnp.float32)
                weighted = jnp.zeros((tile, HD), jnp.float32)
            else:
                shrink = jnp.exp2((state_ref[span, HD:HD + LANES] - top) * FACTOR)
                total = state_ref[span, HD + LANES:] * shrink
                weighted = state_ref[span, :HD] * jnp.concatenate([shrink, shrink], axis=1)
            for slot in range(count):
                low, high = bounds[slot]
                pieces = []
                for at in range(low, high, LANES):
                    weights = jnp.exp2((scores[slot, :, at:at + LANES] - top) * FACTOR)
                    total = total + weights
                    pieces.append(weights.astype(jnp.bfloat16))
                probs = jnp.concatenate(pieces, axis=1)
                weighted = weighted + jnp.dot(probs, values[slot][low:high, :], preferred_element_type=jnp.float32)
            if last:
                finish(span, weighted, total)
            else:
                out_ref[span, :HD] = weighted
                out_ref[span, HD:HD + LANES] = top
                out_ref[span, HD + LANES:] = total

    for count in range(1 if first else 0, blocks + 1):
        reached = place >= (plan[count - 1][0] if count > 0 else 0)
        if count < blocks:
            reached = reached & (place < plan[count][0])
        if count > 0:
            pl.when(reached & (part == 0))(functools.partial(update, count, mine, other))
            pl.when(reached & (part == 1))(functools.partial(update, count, other, mine))
        elif last:

            @pl.when(reached)
            def _():
                finish(slice(0, rows), state_ref[:, :HD], state_ref[:, HD + LANES:])


def attend(query, segments, plan, mine, other, state, last):
    rows = query.shape[0]
    blocks = len(plan)
    vmem = pl.BlockSpec(memory_space=pltpu.VMEM)
    first = state is None
    operands = [query, segments.reshape(1, rows), *mine, *other] + ([] if first else [state])
    return pl.pallas_call(
        functools.partial(attend_kernel, plan, first, last),
        in_specs=[vmem] * len(operands),
        out_specs=vmem,
        out_shape=pltpu.VMEM((rows, HD), jnp.bfloat16) if last else pltpu.VMEM((rows, HD + 2 * LANES), jnp.float32),
        scratch_shapes=[pltpu.VMEM((blocks, rows, rows), jnp.float32)],
        input_output_aliases={} if first or last else {len(operands) - 1: 0},
        compiler_params=pltpu.CompilerParams(vmem_limit_bytes=12 * MIB),
        cost_estimate=pl.CostEstimate(
            flops=4 * rows * rows * blocks * HD, bytes_accessed=4 * rows * blocks * HD, transcendentals=rows * rows * blocks
        ),
        name="attend_last" if last else "attend_first" if first else "attend_more",
    )(*[in_vmem(operand) for operand in operands])


def bounds_kernel(sum_ref, out_exp_ref, x_ref, sum_bound_ref, out_bound_ref, wide_ref, near, sem):
    groups, rows = sum_ref.shape
    fetch = pltpu.make_async_copy(x_ref, near, sem)
    fetch.start()
    per = sum_bound_ref.shape[1] // groups
    for exps, bound_ref in ((sum_ref, sum_bound_ref), (out_exp_ref, out_bound_ref)):
        power = jnp.left_shift(jnp.int32(1), exps[...] - MIN_EXP).astype(jnp.float32)
        bound = jnp.transpose(power * (LIMIT * 2.0 ** MIN_EXP))
        for group in range(groups):
            wide = jnp.broadcast_to(bound[:, group:group + 1], (rows, per)).astype(jnp.bfloat16)
            bound_ref[:, group * per:(group + 1) * per] = wide
    fetch.wait()

    def widen(step, carry):
        span = pl.ds(pl.multiple_of(step * 64, 64), 64)
        wide_ref[span, :] = near[span, :].astype(jnp.float32)
        return carry

    lax.fori_loop(0, rows // 64, widen, 0)


def spread_bounds(sum_exps, out_exps, tokens):
    rows, width = tokens.shape
    groups = sum_exps.shape[1]
    vmem = pl.BlockSpec(memory_space=pltpu.VMEM)
    return pl.pallas_call(
        bounds_kernel,
        in_specs=[vmem, vmem, pl.BlockSpec(memory_space=pltpu.HBM)],
        out_specs=[vmem] * 3,
        out_shape=[pltpu.VMEM((rows, width), jnp.bfloat16)] * 2 + [pltpu.VMEM((rows, width), jnp.float32)],
        scratch_shapes=[pltpu.VMEM((rows, width), jnp.bfloat16), pltpu.SemaphoreType.DMA(())],
        compiler_params=pltpu.CompilerParams(vmem_limit_bytes=10 * MIB),
        cost_estimate=pl.CostEstimate(flops=8 * rows * width, bytes_accessed=8 * rows * groups, transcendentals=0),
        name="spread_bounds",
    )(in_vmem(sum_exps.T), in_vmem(out_exps.T), in_hbm(tokens))


def clip(value, bound):
    return jnp.minimum(jnp.maximum(value.astype(jnp.bfloat16), -bound), bound)


def own_kernel(a_ref, w_ref, sum_ref, out_ref):
    rows, width = out_ref.shape
    tile = rows // 2
    chunk = width // 4

    def body(step, carry):
        for at in range(0, chunk, HD):
            cols = pl.ds(pl.multiple_of(step * chunk + at, HD), HD)
            weights = w_ref[:, cols]
            for start in range(0, rows, tile):
                span = slice(start, start + tile)
                term = jnp.dot(a_ref[span, :], weights, preferred_element_type=jnp.float32)
                out_ref[span, cols] = clip(term, sum_ref[span, cols])
        return carry

    lax.fori_loop(0, 4, body, 0)


def project_own(attended, w_out, sum_bound):
    rows, depth = attended.shape
    width = w_out.shape[1]
    vmem = pl.BlockSpec(memory_space=pltpu.VMEM)
    return pl.pallas_call(
        own_kernel,
        in_specs=[vmem] * 3,
        out_specs=vmem,
        out_shape=pltpu.VMEM((rows, width), jnp.bfloat16),
        compiler_params=pltpu.CompilerParams(vmem_limit_bytes=8 * MIB),
        cost_estimate=pl.CostEstimate(
            flops=2 * rows * width * depth, bytes_accessed=4 * rows * width + 2 * width * depth, transcendentals=0
        ),
        name="project_own",
    )(in_vmem(attended), in_vmem(w_out), in_vmem(sum_bound))


def output_kernel(b_ref, wb_ref, quant_ref, x_ref, sum_ref, last_ref, out_ref, staged, sems):
    rows, width = x_ref.shape
    pieces = sems.shape[0]
    piece = width // pieces
    chunk = width // 2
    tile = rows // 2

    def copy(index):
        span = pl.ds(pl.multiple_of(index * piece, piece), piece)
        return pltpu.make_async_copy(staged.at[:, span], out_ref.at[:, span], sems.at[index])

    def body(step, carry):
        for at in range(0, chunk, HD):
            cols = pl.ds(pl.multiple_of(step * chunk + at, HD), HD)
            weights = wb_ref[:, cols]
            for start in range(0, rows, tile):
                span = slice(start, start + tile)
                term = jnp.dot(b_ref[span, :], weights, preferred_element_type=jnp.float32)
                other = clip(term, sum_ref[span, cols])
                quant = other.astype(jnp.float32) + quant_ref[span, cols].astype(jnp.float32)
                staged[span, cols] = clip(x_ref[span, cols] + quant, last_ref[span, cols])
            if (at + HD) % piece == 0:
                copy(step * (chunk // piece) + at // piece).start()
        return carry

    lax.fori_loop(0, width // chunk, body, 0)
    for index in range(pieces):
        copy(index).wait()


def project_out(att_other, w_other, quant_own, sum_bound, out_bound, tokens):
    rows, width = tokens.shape
    depth = att_other.shape[1]
    pieces = 8
    vmem = pl.BlockSpec(memory_space=pltpu.VMEM)
    operands = [att_other, w_other, quant_own, tokens, sum_bound, out_bound]
    return pl.pallas_call(
        output_kernel,
        in_specs=[vmem] * len(operands),
        out_specs=pl.BlockSpec(memory_space=pltpu.HBM),
        out_shape=jax.ShapeDtypeStruct((rows, width), jnp.bfloat16),
        scratch_shapes=[pltpu.VMEM((rows, width), jnp.bfloat16), pltpu.SemaphoreType.DMA((pieces,))],
        compiler_params=pltpu.CompilerParams(vmem_limit_bytes=10 * MIB),
        cost_estimate=pl.CostEstimate(
            flops=2 * rows * width * depth, bytes_accessed=4 * rows * width + 2 * width * depth, transcendentals=0
        ),
        name="project_out",
    )(*[in_vmem(operand) for operand in operands])


def on_device(seq_size, tokens, gain, segments, w_query, w_keyval, w_out, sum_exps, out_exps):
    window = seq_size // 2

    def swap_cores(x):
        return lax.ppermute(x, "tp", [(0, 1), (1, 0)])

    def shift(x, step, first):
        cycle = seq_size - first
        pairs = []
        for i in range(seq_size):
            for core in range(2):
                after = 2 * (first + (i - first + step) % cycle) + core if i >= first else 2 * i + 1 - core
                pairs.append((2 * i + core, after))
        return lax.ppermute(x, ("seq", "tp"), pairs)

    w_other = swap_cores(w_out)
    message, normed = norm_kv(tokens, gain, w_keyval, segments)
    query = project_query(normed, w_query)
    held, query = lax.optimization_barrier((shift(message, 2, 0), query))
    odd = lax.rem(lax.axis_index("seq"), 2) == 1
    beside = lax.ppermute(jnp.where(odd, held, message), "seq", [(i, i ^ 1) for i in range(seq_size)])
    parts = [[(0, message), (2, held)]]
    for back in range(2, window, 2):
        step = shift(held, 1, back)
        held = shift(held, 2, back)
        parts.append([(back + 1, step)] + ([(back + 2, held)] if back + 2 < window else []))
    parts.append([(1, beside), (window, held)])
    exps = lax.optimization_barrier((sum_exps, out_exps, query))[:2]
    bounds = spread_bounds(*exps, tokens)
    state = None
    for number, blocks in enumerate(parts):
        plan = [(back, back == window) for back, _ in blocks]
        mine = [block for _, block in blocks]
        if number == 1:
            bounds, state = early = lax.optimization_barrier((bounds, state))
        if number > 0:
            mine = [lax.optimization_barrier((block, early))[0] for block in mine]
        other = [swap_cores(m) for m in mine]
        state = attend(query, segments, plan, mine, other, state, number == len(parts) - 1)
    quant_own = project_own(state, w_out, bounds[0])
    return project_out(swap_cores(state), w_other, quant_own, *bounds)


def solution(mesh):
    in_specs = (
        P(("groups", "seq"), None),
        P(),
        P(("groups", "seq")),
        P(None, "tp"),
        P(None, "tp"),
        P("tp", None),
        P(("groups", "seq"), None),
        P(("groups", "seq"), None),
    )
    out_specs = P(("groups", "seq"), None)
    return jax.shard_map(
        functools.partial(on_device, mesh.shape["seq"]),
        mesh=mesh, in_specs=in_specs, out_specs=out_specs, check_vma=False,
    )
```

```python
import functools

import jax
import jax.numpy as jnp
from jax import lax
from jax.experimental import pallas as pl
from jax.experimental.pallas import tpu as pltpu
from jax.sharding import PartitionSpec as P

HD = 256
LANES = 128
SEG_ROWS = 16
LIMIT = 448.0
MIN_EXP = -9
NEG = -1e30
MIB = 1024 * 1024
NT = (((1,), (1,)), ((), ()))
FACTOR = HD ** (-0.5) * 1.4426950408889634


def norm_kv_kernel(x_ref, gain_hbm, w_ref, seg_hbm, msg_ref, normed_ref, xs, ws, gain_ref, seg_ref, sems):
    rows, width = xs.shape
    tile, part = rows // 2, rows // 4

    def cut(source, target, first, count, pieces, sem):
        size = count // pieces
        return [
            pltpu.make_async_copy(
                source.at[pl.ds(first + i * size, size)], target.at[pl.ds(first + i * size, size)], sems.at[sem + i]
            )
            for i in range(pieces)
        ]

    def early_tokens(half):
        return cut(x_ref, xs, half * part, part, 4, 4 * half)

    def late_tokens():
        return cut(x_ref, xs, tile, tile, 2, 8)

    def weights():
        return cut(w_ref, ws, 0, width, 4, 10)

    def gain_copy():
        return pltpu.make_async_copy(gain_hbm, gain_ref, sems.at[14])

    def segments_copy():
        return pltpu.make_async_copy(seg_hbm, seg_ref, sems.at[15])

    for copy in early_tokens(0) + early_tokens(1) + [gain_copy()] + weights() + late_tokens() + [segments_copy()]:
        copy.start()

    def wide(first, count, start):
        return xs[first:first + count, start:start + LANES].astype(jnp.float32)

    def stats(first):
        total = wide(first, part, 0)
        for start in range(LANES, width, LANES):
            total = total + wide(first, part, start)
        mean = jnp.broadcast_to(jnp.sum(total, axis=1, keepdims=True) * (1.0 / width), (part, LANES))
        square = jnp.zeros((part, LANES), jnp.float32)
        for start in range(0, width, LANES):
            center = wide(first, part, start) - mean
            square = square + center * center
        spread = jnp.sum(square, axis=1, keepdims=True) * (1.0 / width)
        return mean, jnp.broadcast_to(lax.rsqrt(spread + 1e-05), (part, LANES))

    def project(first, halves):
        mean = jnp.concatenate([h[0] for h in halves], axis=0)
        scale = jnp.concatenate([h[1] for h in halves], axis=0)
        kv = jnp.zeros((tile, ws.shape[1]), jnp.float32)
        span = slice(first, first + tile)
        for start in range(0, width, HD):
            for at in (start, start + LANES):
                normed = (wide(first, tile, at) - mean) * scale * gain_ref[:, at:at + LANES]
                normed_ref[span, at:at + LANES] = normed.astype(jnp.bfloat16)
            kv = kv + jnp.dot(
                normed_ref[span, start:start + HD], ws[start:start + HD, :], preferred_element_type=jnp.float32
            )
        msg_ref[span, :] = kv.astype(jnp.bfloat16)

    halves = []
    for half in range(2):
        for copy in early_tokens(half):
            copy.wait()
        halves.append(stats(half * part))
    for copy in [gain_copy()] + weights():
        copy.wait()
    project(0, halves)
    for copy in late_tokens():
        copy.wait()
    project(tile, [stats(tile), stats(tile + part)])
    segments_copy().wait()
    seg = seg_ref[...].astype(jnp.float32)
    low = jnp.broadcast_to(seg[:, :HD], (8, HD))
    high = jnp.broadcast_to(seg[:, HD:], (8, HD))
    msg_ref[rows:, :] = jnp.concatenate([low, high], axis=0).astype(jnp.bfloat16)


def in_hbm(x):
    return pltpu.with_memory_space_constraint(x, pltpu.HBM)


def in_vmem(x):
    return pltpu.with_memory_space_constraint(x, pltpu.VMEM)


def norm_kv(tokens, gain, w_keyval, segments):
    rows, width = tokens.shape
    cols = w_keyval.shape[1]
    vmem, hbm = pl.BlockSpec(memory_space=pltpu.VMEM), pl.BlockSpec(memory_space=pltpu.HBM)
    return pl.pallas_call(
        norm_kv_kernel,
        in_specs=[hbm] * 4,
        out_specs=[vmem, vmem],
        out_shape=[pltpu.VMEM((rows + SEG_ROWS, cols), jnp.bfloat16), pltpu.VMEM((rows, width), jnp.bfloat16)],
        scratch_shapes=[
            pltpu.VMEM((rows, width), jnp.bfloat16),
            pltpu.VMEM((width, cols), jnp.bfloat16),
            pltpu.VMEM((1, width), jnp.float32),
            pltpu.VMEM((1, rows), jnp.int32),
            pltpu.SemaphoreType.DMA((16,)),
        ],
        compiler_params=pltpu.CompilerParams(vmem_limit_bytes=24 * MIB),
        cost_estimate=pl.CostEstimate(
            flops=2 * rows * width * cols, bytes_accessed=4 * rows * width + 2 * width * cols, transcendentals=0
        ),
        name="norm_kv",
    )(in_hbm(tokens), in_hbm(gain.reshape(1, width)), in_hbm(w_keyval), in_hbm(segments.reshape(1, rows)))


def query_kernel(x_ref, w_ref, out_ref):
    out_ref[...] = jnp.dot(x_ref[...], w_ref[...], preferred_element_type=jnp.float32).astype(jnp.bfloat16)


def project_query(normed, w_query):
    rows, width = normed.shape
    cols = w_query.shape[1]
    vmem = pl.BlockSpec(memory_space=pltpu.VMEM)
    return pl.pallas_call(
        query_kernel,
        in_specs=[vmem, vmem],
        out_specs=vmem,
        out_shape=pltpu.VMEM((rows, cols), jnp.bfloat16),
        compiler_params=pltpu.CompilerParams(vmem_limit_bytes=8 * MIB),
        cost_estimate=pl.CostEstimate(
            flops=2 * rows * width * cols, bytes_accessed=2 * rows * width + 2 * width * cols, transcendentals=0
        ),
        name="project_query",
    )(in_vmem(normed), in_vmem(w_query))


def attend_kernel(plan, first, last, *refs):
    blocks = len(plan)
    q_ref, seg_ref = refs[:2]
    mine, other = refs[2:2 + blocks], refs[2 + blocks:2 + 2 * blocks]
    refs = refs[2 + 2 * blocks:]
    state_ref = None
    if not first:
        state_ref, refs = refs[0], refs[1:]
    out_ref, scores = refs
    rows = q_ref.shape[0]
    tile = rows // 2
    part = lax.axis_index("tp")
    place = lax.axis_index("seq")

    def finish(span, weighted, total):
        out_ref[span, :] = (weighted / jnp.sum(total, axis=1, keepdims=True)).astype(jnp.bfloat16)

    def update(slots, keys, values):
        own_seg = jnp.transpose(jnp.broadcast_to(seg_ref[...].astype(jnp.float32), (8, rows)))[:, 0:1]
        key_segs = {}
        for slot in slots:
            packed = mine[slot][rows:, :].astype(jnp.float32)
            key_segs[slot] = jnp.concatenate([packed[0:1, :], packed[8:9, :]], axis=1)
        for start in range(0, rows, tile):
            span = slice(start, start + tile)
            query = q_ref[span, :]
            best = None if first else state_ref[span, HD:HD + LANES]
            bounds = {}
            for slot in slots:
                back, furthest = plan[slot]
                low, high = 0, rows
                if back == 0:
                    high = start + tile
                elif furthest:
                    low = start
                bounds[slot] = (low, high)
                raw = lax.dot_general(query, keys[slot][low:high, :], NT, preferred_element_type=jnp.float32)
                allowed = key_segs[slot][:, low:high] == own_seg[span, :]
                if back == 0:
                    row_pos = start + lax.broadcasted_iota(jnp.int32, raw.shape, 0)
                    allowed = allowed & (lax.broadcasted_iota(jnp.int32, raw.shape, 1) <= row_pos)
                masked = jnp.where(allowed, raw, NEG)
                scores[slot, :, low:high] = masked
                for at in range(0, high - low, LANES):
                    piece = masked[:, at:at + LANES]
                    best = piece if best is None else jnp.maximum(best, piece)
            top = jnp.broadcast_to(jnp.max(best, axis=1, keepdims=True), (tile, LANES))
            if first:
                total = jnp.zeros((tile, LANES), jnp.float32)
                weighted = jnp.zeros((tile, HD), jnp.float32)
            else:
                shrink = jnp.exp2((state_ref[span, HD:HD + LANES] - top) * FACTOR)
                total = state_ref[span, HD + LANES:] * shrink
                weighted = state_ref[span, :HD] * jnp.concatenate([shrink, shrink], axis=1)
            for slot in slots:
                low, high = bounds[slot]
                pieces = []
                for at in range(low, high, LANES):
                    weights = jnp.exp2((scores[slot, :, at:at + LANES] - top) * FACTOR)
                    total = total + weights
                    pieces.append(weights.astype(jnp.bfloat16))
                probs = jnp.concatenate(pieces, axis=1)
                weighted = weighted + jnp.dot(probs, values[slot][low:high, :], preferred_element_type=jnp.float32)
            if last:
                finish(span, weighted, total)
            else:
                out_ref[span, :HD] = weighted
                out_ref[span, HD:HD + LANES] = top
                out_ref[span, HD + LANES:] = total

    order = sorted(range(blocks), key=lambda slot: plan[slot][0])
    for count in range(1 if first else 0, blocks + 1):
        reached = place >= (plan[order[count - 1]][0] if count > 0 else 0)
        if count < blocks:
            reached = reached & (place < plan[order[count]][0])
        if count > 0:
            pl.when(reached & (part == 0))(functools.partial(update, order[:count], mine, other))
            pl.when(reached & (part == 1))(functools.partial(update, order[:count], other, mine))
        elif last:

            @pl.when(reached)
            def _():
                finish(slice(0, rows), state_ref[:, :HD], state_ref[:, HD + LANES:])


def attend(query, segments, plan, mine, other, state, last):
    rows = query.shape[0]
    blocks = len(plan)
    vmem = pl.BlockSpec(memory_space=pltpu.VMEM)
    first = state is None
    operands = [query, segments.reshape(1, rows), *mine, *other] + ([] if first else [state])
    return pl.pallas_call(
        functools.partial(attend_kernel, plan, first, last),
        in_specs=[vmem] * len(operands),
        out_specs=vmem,
        out_shape=pltpu.VMEM((rows, HD), jnp.bfloat16) if last else pltpu.VMEM((rows, HD + 2 * LANES), jnp.float32),
        scratch_shapes=[pltpu.VMEM((blocks, rows // 2, rows), jnp.float32)],
        input_output_aliases={} if first or last else {len(operands) - 1: 0},
        compiler_params=pltpu.CompilerParams(vmem_limit_bytes=12 * MIB),
        cost_estimate=pl.CostEstimate(
            flops=4 * rows * rows * blocks * HD, bytes_accessed=4 * rows * blocks * HD, transcendentals=rows * rows * blocks
        ),
        name="attend_last" if last else "attend_first" if first else "attend_more",
    )(*[in_vmem(operand) for operand in operands])


def bounds_kernel(sum_ref, out_exp_ref, x_ref, sum_bound_ref, out_bound_ref, wide_ref, near, sem):
    groups, rows = sum_ref.shape
    fetch = pltpu.make_async_copy(x_ref, near, sem)
    fetch.start()
    per = sum_bound_ref.shape[1] // groups
    for exps, bound_ref in ((sum_ref, sum_bound_ref), (out_exp_ref, out_bound_ref)):
        power = jnp.left_shift(jnp.int32(1), exps[...] - MIN_EXP).astype(jnp.float32)
        bound = jnp.transpose(power * (LIMIT * 2.0 ** MIN_EXP))
        for group in range(groups):
            wide = jnp.broadcast_to(bound[:, group:group + 1], (rows, per)).astype(jnp.bfloat16)
            bound_ref[:, group * per:(group + 1) * per] = wide
    fetch.wait()

    def widen(step, carry):
        span = pl.ds(pl.multiple_of(step * 64, 64), 64)
        wide_ref[span, :] = near[span, :].astype(jnp.float32)
        return carry

    lax.fori_loop(0, rows // 64, widen, 0)


def spread_bounds(sum_exps, out_exps, tokens):
    rows, width = tokens.shape
    groups = sum_exps.shape[1]
    vmem = pl.BlockSpec(memory_space=pltpu.VMEM)
    return pl.pallas_call(
        bounds_kernel,
        in_specs=[vmem, vmem, pl.BlockSpec(memory_space=pltpu.HBM)],
        out_specs=[vmem] * 3,
        out_shape=[pltpu.VMEM((rows, width), jnp.bfloat16)] * 2 + [pltpu.VMEM((rows, width), jnp.float32)],
        scratch_shapes=[pltpu.VMEM((rows, width), jnp.bfloat16), pltpu.SemaphoreType.DMA(())],
        compiler_params=pltpu.CompilerParams(vmem_limit_bytes=10 * MIB),
        cost_estimate=pl.CostEstimate(flops=8 * rows * width, bytes_accessed=8 * rows * groups, transcendentals=0),
        name="spread_bounds",
    )(in_vmem(sum_exps.T), in_vmem(out_exps.T), in_hbm(tokens))


def clip(value, bound):
    return jnp.minimum(jnp.maximum(value.astype(jnp.bfloat16), -bound), bound)


def own_kernel(a_ref, w_ref, sum_ref, out_ref):
    rows, width = out_ref.shape
    tile = rows // 2
    chunk = width // 4

    def body(step, carry):
        for at in range(0, chunk, HD):
            cols = pl.ds(pl.multiple_of(step * chunk + at, HD), HD)
            weights = w_ref[:, cols]
            for start in range(0, rows, tile):
                span = slice(start, start + tile)
                term = jnp.dot(a_ref[span, :], weights, preferred_element_type=jnp.float32)
                out_ref[span, cols] = clip(term, sum_ref[span, cols])
        return carry

    lax.fori_loop(0, 4, body, 0)


def project_own(attended, w_out, sum_bound):
    rows, depth = attended.shape
    width = w_out.shape[1]
    vmem = pl.BlockSpec(memory_space=pltpu.VMEM)
    return pl.pallas_call(
        own_kernel,
        in_specs=[vmem] * 3,
        out_specs=vmem,
        out_shape=pltpu.VMEM((rows, width), jnp.bfloat16),
        compiler_params=pltpu.CompilerParams(vmem_limit_bytes=8 * MIB),
        cost_estimate=pl.CostEstimate(
            flops=2 * rows * width * depth, bytes_accessed=4 * rows * width + 2 * width * depth, transcendentals=0
        ),
        name="project_own",
    )(in_vmem(attended), in_vmem(w_out), in_vmem(sum_bound))


def output_kernel(b_ref, wb_ref, quant_ref, x_ref, sum_ref, last_ref, out_ref, staged, sems):
    rows, width = x_ref.shape
    pieces = sems.shape[0]
    piece = width // pieces
    chunk = width // 2
    tile = rows // 2

    def copy(index):
        span = pl.ds(pl.multiple_of(index * piece, piece), piece)
        return pltpu.make_async_copy(staged.at[:, span], out_ref.at[:, span], sems.at[index])

    def body(step, carry):
        for at in range(0, chunk, HD):
            cols = pl.ds(pl.multiple_of(step * chunk + at, HD), HD)
            weights = wb_ref[:, cols]
            for start in range(0, rows, tile):
                span = slice(start, start + tile)
                term = jnp.dot(b_ref[span, :], weights, preferred_element_type=jnp.float32)
                other = clip(term, sum_ref[span, cols])
                quant = other.astype(jnp.float32) + quant_ref[span, cols].astype(jnp.float32)
                staged[span, cols] = clip(x_ref[span, cols] + quant, last_ref[span, cols])
            if (at + HD) % piece == 0:
                copy(step * (chunk // piece) + at // piece).start()
        return carry

    lax.fori_loop(0, width // chunk, body, 0)
    for index in range(pieces):
        copy(index).wait()


def project_out(att_other, w_other, quant_own, sum_bound, out_bound, tokens):
    rows, width = tokens.shape
    depth = att_other.shape[1]
    pieces = 8
    vmem = pl.BlockSpec(memory_space=pltpu.VMEM)
    operands = [att_other, w_other, quant_own, tokens, sum_bound, out_bound]
    return pl.pallas_call(
        output_kernel,
        in_specs=[vmem] * len(operands),
        out_specs=pl.BlockSpec(memory_space=pltpu.HBM),
        out_shape=jax.ShapeDtypeStruct((rows, width), jnp.bfloat16),
        scratch_shapes=[pltpu.VMEM((rows, width), jnp.bfloat16), pltpu.SemaphoreType.DMA((pieces,))],
        compiler_params=pltpu.CompilerParams(vmem_limit_bytes=10 * MIB),
        cost_estimate=pl.CostEstimate(
            flops=2 * rows * width * depth, bytes_accessed=4 * rows * width + 2 * width * depth, transcendentals=0
        ),
        name="project_out",
    )(*[in_vmem(operand) for operand in operands])


def on_device(seq_size, tokens, gain, segments, w_query, w_keyval, w_out, sum_exps, out_exps):
    window = seq_size // 2

    def swap_cores(x):
        return lax.ppermute(x, "tp", [(0, 1), (1, 0)])

    def shift(x, step, first):
        cycle = seq_size - first
        pairs = []
        for i in range(seq_size):
            for core in range(2):
                after = 2 * (first + (i - first + step) % cycle) + core if i >= first else 2 * i + 1 - core
                pairs.append((2 * i + core, after))
        return lax.ppermute(x, ("seq", "tp"), pairs)

    w_other = swap_cores(w_out)
    message, normed = norm_kv(tokens, gain, w_keyval, segments)
    query = project_query(normed, w_query)
    held, query = lax.optimization_barrier((shift(message, 2, 0), query))
    odd = lax.rem(lax.axis_index("seq"), 2) == 1
    beside = lax.ppermute(jnp.where(odd, held, message), "seq", [(i, i ^ 1) for i in range(seq_size)])
    parts = [[(0, message), (2, held)]]
    for back in range(2, window, 2):
        step = shift(held, 1, back)
        held = shift(held, 2, back)
        parts.append([(back + 1, step)] + ([(back + 2, held)] if back + 2 < window else []))
    parts.append([(window, held), (1, beside)])
    exps = lax.optimization_barrier((sum_exps, out_exps, query))[:2]
    bounds = spread_bounds(*exps, tokens)
    state = None
    for number, blocks in enumerate(parts):
        plan = [(back, back == window) for back, _ in blocks]
        mine = [block for _, block in blocks]
        if number == 1:
            bounds, state = early = lax.optimization_barrier((bounds, state))
        if number > 0:
            mine = [lax.optimization_barrier((block, early))[0] for block in mine]
        other = [swap_cores(m) for m in mine]
        state = attend(query, segments, plan, mine, other, state, number == len(parts) - 1)
    quant_own = project_own(state, w_out, bounds[0])
    return project_out(swap_cores(state), w_other, quant_own, *bounds)


def solution(mesh):
    in_specs = (
        P(("groups", "seq"), None),
        P(),
        P(("groups", "seq")),
        P(None, "tp"),
        P(None, "tp"),
        P("tp", None),
        P(("groups", "seq"), None),
        P(("groups", "seq"), None),
    )
    out_specs = P(("groups", "seq"), None)
    return jax.shard_map(
        functools.partial(on_device, mesh.shape["seq"]),
        mesh=mesh, in_specs=in_specs, out_specs=out_specs, check_vma=False,
    )
```

```python
import functools

import jax
import jax.numpy as jnp
from jax import lax
from jax.experimental import pallas as pl
from jax.experimental.pallas import tpu as pltpu
from jax.sharding import PartitionSpec as P

HD = 256
LANES = 128
SEG_ROWS = 16
LIMIT = 448.0
MIN_EXP = -9
NEG = -1e30
MIB = 1024 * 1024
NT = (((1,), (1,)), ((), ()))
FACTOR = HD ** (-0.5) * 1.4426950408889634


def norm_kv_kernel(x_ref, gain_hbm, w_ref, seg_hbm, msg_ref, normed_ref, xs, ws, gain_ref, seg_ref, sems):
    rows, width = xs.shape
    tile, part = rows // 2, rows // 4

    def cut(source, target, first, count, pieces, sem):
        size = count // pieces
        return [
            pltpu.make_async_copy(
                source.at[pl.ds(first + i * size, size)], target.at[pl.ds(first + i * size, size)], sems.at[sem + i]
            )
            for i in range(pieces)
        ]

    def early_tokens(half):
        return cut(x_ref, xs, half * part, part, 8 - 4 * half, 8 * half)

    def late_tokens():
        return cut(x_ref, xs, tile, tile, 2, 12)

    def weights():
        return cut(w_ref, ws, 0, width, 4, 14)

    def gain_copy():
        return pltpu.make_async_copy(gain_hbm, gain_ref, sems.at[18])

    def segments_copy():
        return pltpu.make_async_copy(seg_hbm, seg_ref, sems.at[19])

    for copy in early_tokens(0) + early_tokens(1) + [gain_copy()] + weights() + late_tokens() + [segments_copy()]:
        copy.start()

    def wide(first, count, start):
        return xs[first:first + count, start:start + LANES].astype(jnp.float32)

    def stats(first):
        pivot = jnp.broadcast_to(jnp.sum(wide(first, part, 0), axis=1, keepdims=True) * (1.0 / LANES), (part, LANES))
        total = jnp.zeros((part, LANES), jnp.float32)
        square = jnp.zeros((part, LANES), jnp.float32)
        for start in range(0, width, LANES):
            away = wide(first, part, start) - pivot
            total = total + away
            square = square + away * away
        shift = jnp.sum(total, axis=1, keepdims=True) * (1.0 / width)
        spread = jnp.maximum(jnp.sum(square, axis=1, keepdims=True) * (1.0 / width) - shift * shift, 0.0)
        return pivot + shift, jnp.broadcast_to(lax.rsqrt(spread + 1e-05), (part, LANES))

    def project(first, halves):
        mean = jnp.concatenate([h[0] for h in halves], axis=0)
        scale = jnp.concatenate([h[1] for h in halves], axis=0)
        kv = jnp.zeros((tile, ws.shape[1]), jnp.float32)
        span = slice(first, first + tile)
        for start in range(0, width, HD):
            for at in (start, start + LANES):
                normed = (wide(first, tile, at) - mean) * scale * gain_ref[:, at:at + LANES]
                normed_ref[span, at:at + LANES] = normed.astype(jnp.bfloat16)
            kv = kv + jnp.dot(
                normed_ref[span, start:start + HD], ws[start:start + HD, :], preferred_element_type=jnp.float32
            )
        msg_ref[span, :] = kv.astype(jnp.bfloat16)

    halves = []
    for half in range(2):
        for copy in early_tokens(half):
            copy.wait()
        halves.append(stats(half * part))
    for copy in [gain_copy()] + weights():
        copy.wait()
    project(0, halves)
    for copy in late_tokens():
        copy.wait()
    project(tile, [stats(tile), stats(tile + part)])
    segments_copy().wait()
    seg = seg_ref[...].astype(jnp.float32)
    low = jnp.broadcast_to(seg[:, :HD], (8, HD))
    high = jnp.broadcast_to(seg[:, HD:], (8, HD))
    msg_ref[rows:, :] = jnp.concatenate([low, high], axis=0).astype(jnp.bfloat16)


def in_hbm(x):
    return pltpu.with_memory_space_constraint(x, pltpu.HBM)


def in_vmem(x):
    return pltpu.with_memory_space_constraint(x, pltpu.VMEM)


def norm_kv(tokens, gain, w_keyval, segments):
    rows, width = tokens.shape
    cols = w_keyval.shape[1]
    vmem, hbm = pl.BlockSpec(memory_space=pltpu.VMEM), pl.BlockSpec(memory_space=pltpu.HBM)
    return pl.pallas_call(
        norm_kv_kernel,
        in_specs=[hbm] * 4,
        out_specs=[vmem, vmem],
        out_shape=[pltpu.VMEM((rows + SEG_ROWS, cols), jnp.bfloat16), pltpu.VMEM((rows, width), jnp.bfloat16)],
        scratch_shapes=[
            pltpu.VMEM((rows, width), jnp.bfloat16),
            pltpu.VMEM((width, cols), jnp.bfloat16),
            pltpu.VMEM((1, width), jnp.float32),
            pltpu.VMEM((1, rows), jnp.int32),
            pltpu.SemaphoreType.DMA((20,)),
        ],
        compiler_params=pltpu.CompilerParams(vmem_limit_bytes=24 * MIB),
        cost_estimate=pl.CostEstimate(
            flops=2 * rows * width * cols, bytes_accessed=4 * rows * width + 2 * width * cols, transcendentals=0
        ),
        name="norm_kv",
    )(in_hbm(tokens), in_hbm(gain.reshape(1, width)), in_hbm(w_keyval), in_hbm(segments.reshape(1, rows)))


def query_kernel(x_ref, w_ref, out_ref):
    out_ref[...] = jnp.dot(x_ref[...], w_ref[...], preferred_element_type=jnp.float32).astype(jnp.bfloat16)


def project_query(normed, w_query):
    rows, width = normed.shape
    cols = w_query.shape[1]
    vmem = pl.BlockSpec(memory_space=pltpu.VMEM)
    return pl.pallas_call(
        query_kernel,
        in_specs=[vmem, vmem],
        out_specs=vmem,
        out_shape=pltpu.VMEM((rows, cols), jnp.bfloat16),
        compiler_params=pltpu.CompilerParams(vmem_limit_bytes=8 * MIB),
        cost_estimate=pl.CostEstimate(
            flops=2 * rows * width * cols, bytes_accessed=2 * rows * width + 2 * width * cols, transcendentals=0
        ),
        name="project_query",
    )(in_vmem(normed), in_vmem(w_query))


def attend_kernel(plan, first, last, *refs):
    blocks = len(plan)
    q_ref, seg_ref = refs[:2]
    mine, other = refs[2:2 + blocks], refs[2 + blocks:2 + 2 * blocks]
    refs = refs[2 + 2 * blocks:]
    state_ref = None
    if not first:
        state_ref, refs = refs[0], refs[1:]
    out_ref, scores = refs
    rows = q_ref.shape[0]
    tile = rows // 2
    part = lax.axis_index("tp")
    place = lax.axis_index("seq")

    def finish(span, weighted, total):
        out_ref[span, :] = (weighted / jnp.sum(total, axis=1, keepdims=True)).astype(jnp.bfloat16)

    def update(slots, keys, values):
        own_seg = jnp.transpose(jnp.broadcast_to(seg_ref[...].astype(jnp.float32), (8, rows)))[:, 0:1]
        key_segs = {}
        for slot in slots:
            packed = mine[slot][rows:, :].astype(jnp.float32)
            key_segs[slot] = jnp.concatenate([packed[0:1, :], packed[8:9, :]], axis=1)
        for start in range(0, rows, tile):
            span = slice(start, start + tile)
            query = q_ref[span, :]
            best = None if first else state_ref[span, HD:HD + LANES]
            bounds = {}
            for slot in slots:
                back, furthest = plan[slot]
                low, high = 0, rows
                if back == 0:
                    high = start + tile
                elif furthest:
                    low = start
                bounds[slot] = (low, high)
                raw = lax.dot_general(query, keys[slot][low:high, :], NT, preferred_element_type=jnp.float32)
                allowed = key_segs[slot][:, low:high] == own_seg[span, :]
                if back == 0:
                    row_pos = start + lax.broadcasted_iota(jnp.int32, raw.shape, 0)
                    allowed = allowed & (lax.broadcasted_iota(jnp.int32, raw.shape, 1) <= row_pos)
                masked = jnp.where(allowed, raw, NEG)
                scores[slot, :, low:high] = masked
                for at in range(0, high - low, LANES):
                    piece = masked[:, at:at + LANES]
                    best = piece if best is None else jnp.maximum(best, piece)
            top = jnp.broadcast_to(jnp.max(best, axis=1, keepdims=True), (tile, LANES))
            if first:
                total = jnp.zeros((tile, LANES), jnp.float32)
                weighted = jnp.zeros((tile, HD), jnp.float32)
            else:
                shrink = jnp.exp2((state_ref[span, HD:HD + LANES] - top) * FACTOR)
                total = state_ref[span, HD + LANES:] * shrink
                weighted = state_ref[span, :HD] * jnp.concatenate([shrink, shrink], axis=1)
            for slot in slots:
                low, high = bounds[slot]
                pieces = []
                for at in range(low, high, LANES):
                    weights = jnp.exp2((scores[slot, :, at:at + LANES] - top) * FACTOR)
                    total = total + weights
                    pieces.append(weights.astype(jnp.bfloat16))
                probs = jnp.concatenate(pieces, axis=1)
                weighted = weighted + jnp.dot(probs, values[slot][low:high, :], preferred_element_type=jnp.float32)
            if last:
                finish(span, weighted, total)
            else:
                out_ref[span, :HD] = weighted
                out_ref[span, HD:HD + LANES] = top
                out_ref[span, HD + LANES:] = total

    order = sorted(range(blocks), key=lambda slot: plan[slot][0])
    for count in range(1 if first else 0, blocks + 1):
        reached = place >= (plan[order[count - 1]][0] if count > 0 else 0)
        if count < blocks:
            reached = reached & (place < plan[order[count]][0])
        if count > 0:
            pl.when(reached & (part == 0))(functools.partial(update, order[:count], mine, other))
            pl.when(reached & (part == 1))(functools.partial(update, order[:count], other, mine))
        elif last:

            @pl.when(reached)
            def _():
                finish(slice(0, rows), state_ref[:, :HD], state_ref[:, HD + LANES:])


def attend(query, segments, plan, mine, other, state, last):
    rows = query.shape[0]
    blocks = len(plan)
    vmem = pl.BlockSpec(memory_space=pltpu.VMEM)
    first = state is None
    operands = [query, segments.reshape(1, rows), *mine, *other] + ([] if first else [state])
    return pl.pallas_call(
        functools.partial(attend_kernel, plan, first, last),
        in_specs=[vmem] * len(operands),
        out_specs=vmem,
        out_shape=pltpu.VMEM((rows, HD), jnp.bfloat16) if last else pltpu.VMEM((rows, HD + 2 * LANES), jnp.float32),
        scratch_shapes=[pltpu.VMEM((blocks, rows // 2, rows), jnp.float32)],
        input_output_aliases={} if first or last else {len(operands) - 1: 0},
        compiler_params=pltpu.CompilerParams(vmem_limit_bytes=12 * MIB),
        cost_estimate=pl.CostEstimate(
            flops=4 * rows * rows * blocks * HD, bytes_accessed=4 * rows * blocks * HD, transcendentals=rows * rows * blocks
        ),
        name="attend_last" if last else "attend_first" if first else "attend_more",
    )(*[in_vmem(operand) for operand in operands])


def bounds_kernel(sum_ref, out_exp_ref, x_ref, sum_bound_ref, out_bound_ref, wide_ref, near, sem):
    groups, rows = sum_ref.shape
    fetch = pltpu.make_async_copy(x_ref, near, sem)
    fetch.start()
    per = sum_bound_ref.shape[1] // groups
    for exps, bound_ref in ((sum_ref, sum_bound_ref), (out_exp_ref, out_bound_ref)):
        power = jnp.left_shift(jnp.int32(1), exps[...] - MIN_EXP).astype(jnp.float32)
        bound = jnp.transpose(power * (LIMIT * 2.0 ** MIN_EXP))
        for group in range(groups):
            wide = jnp.broadcast_to(bound[:, group:group + 1], (rows, per)).astype(jnp.bfloat16)
            bound_ref[:, group * per:(group + 1) * per] = wide
    fetch.wait()

    def widen(step, carry):
        span = pl.ds(pl.multiple_of(step * 64, 64), 64)
        wide_ref[span, :] = near[span, :].astype(jnp.float32)
        return carry

    lax.fori_loop(0, rows // 64, widen, 0)


def spread_bounds(sum_exps, out_exps, tokens):
    rows, width = tokens.shape
    groups = sum_exps.shape[1]
    vmem = pl.BlockSpec(memory_space=pltpu.VMEM)
    return pl.pallas_call(
        bounds_kernel,
        in_specs=[vmem, vmem, pl.BlockSpec(memory_space=pltpu.HBM)],
        out_specs=[vmem] * 3,
        out_shape=[pltpu.VMEM((rows, width), jnp.bfloat16)] * 2 + [pltpu.VMEM((rows, width), jnp.float32)],
        scratch_shapes=[pltpu.VMEM((rows, width), jnp.bfloat16), pltpu.SemaphoreType.DMA(())],
        compiler_params=pltpu.CompilerParams(vmem_limit_bytes=10 * MIB),
        cost_estimate=pl.CostEstimate(flops=8 * rows * width, bytes_accessed=8 * rows * groups, transcendentals=0),
        name="spread_bounds",
    )(in_vmem(sum_exps.T), in_vmem(out_exps.T), in_hbm(tokens))


def clip(value, bound):
    return jnp.minimum(jnp.maximum(value.astype(jnp.bfloat16), -bound), bound)


def own_kernel(a_ref, w_ref, sum_ref, out_ref):
    rows, width = out_ref.shape
    tile = rows // 2
    for at in range(0, width, HD):
        cols = slice(at, at + HD)
        for start in range(0, rows, tile):
            span = slice(start, start + tile)
            term = jnp.dot(a_ref[span, :], w_ref[:, cols], preferred_element_type=jnp.float32)
            out_ref[span, cols] = clip(term, sum_ref[span, cols])


def project_own(attended, w_out, sum_bound):
    rows, depth = attended.shape
    width = w_out.shape[1]
    vmem = pl.BlockSpec(memory_space=pltpu.VMEM)
    return pl.pallas_call(
        own_kernel,
        in_specs=[vmem] * 3,
        out_specs=vmem,
        out_shape=pltpu.VMEM((rows, width), jnp.bfloat16),
        compiler_params=pltpu.CompilerParams(vmem_limit_bytes=8 * MIB),
        cost_estimate=pl.CostEstimate(
            flops=2 * rows * width * depth, bytes_accessed=4 * rows * width + 2 * width * depth, transcendentals=0
        ),
        name="project_own",
    )(in_vmem(attended), in_vmem(w_out), in_vmem(sum_bound))


def output_kernel(b_ref, wb_ref, quant_ref, x_ref, sum_ref, last_ref, out_ref, staged, sems):
    rows, width = x_ref.shape
    tile = rows // 2

    def copy(index):
        span = slice(index * HD, (index + 1) * HD)
        return pltpu.make_async_copy(staged.at[:, span], out_ref.at[:, span], sems.at[index])

    for index in range(width // HD):
        cols = slice(index * HD, (index + 1) * HD)
        for start in range(0, rows, tile):
            span = slice(start, start + tile)
            term = jnp.dot(b_ref[span, :], wb_ref[:, cols], preferred_element_type=jnp.float32)
            quant = clip(term, sum_ref[span, cols]).astype(jnp.float32) + quant_ref[span, cols].astype(jnp.float32)
            staged[span, cols] = clip(x_ref[span, cols] + quant, last_ref[span, cols])
        copy(index).start()
    for index in range(width // HD):
        copy(index).wait()


def project_out(att_other, w_other, quant_own, sum_bound, out_bound, tokens):
    rows, width = tokens.shape
    depth = att_other.shape[1]
    pieces = width // HD
    vmem = pl.BlockSpec(memory_space=pltpu.VMEM)
    operands = [att_other, w_other, quant_own, tokens, sum_bound, out_bound]
    return pl.pallas_call(
        output_kernel,
        in_specs=[vmem] * len(operands),
        out_specs=pl.BlockSpec(memory_space=pltpu.HBM),
        out_shape=jax.ShapeDtypeStruct((rows, width), jnp.bfloat16),
        scratch_shapes=[pltpu.VMEM((rows, width), jnp.bfloat16), pltpu.SemaphoreType.DMA((pieces,))],
        compiler_params=pltpu.CompilerParams(vmem_limit_bytes=10 * MIB),
        cost_estimate=pl.CostEstimate(
            flops=2 * rows * width * depth, bytes_accessed=4 * rows * width + 2 * width * depth, transcendentals=0
        ),
        name="project_out",
    )(*[in_vmem(operand) for operand in operands])


def on_device(seq_size, tokens, gain, segments, w_query, w_keyval, w_out, sum_exps, out_exps):
    window = seq_size // 2

    def swap_cores(x):
        return lax.ppermute(x, "tp", [(0, 1), (1, 0)])

    def shift(x, step, first):
        cycle = seq_size - first
        pairs = []
        for i in range(seq_size):
            for core in range(2):
                after = 2 * (first + (i - first + step) % cycle) + core if i >= first else 2 * i + 1 - core
                pairs.append((2 * i + core, after))
        return lax.ppermute(x, ("seq", "tp"), pairs)

    w_other = swap_cores(w_out)
    message, normed = norm_kv(tokens, gain, w_keyval, segments)
    query = project_query(normed, w_query)
    held, query = lax.optimization_barrier((shift(message, 2, 0), query))
    odd = lax.rem(lax.axis_index("seq"), 2) == 1
    beside = lax.ppermute(jnp.where(odd, held, message), "seq", [(i, i ^ 1) for i in range(seq_size)])
    parts = [[(0, message), (2, held)]]
    for back in range(2, window, 2):
        step = shift(held, 1, back)
        held = shift(held, 2, back)
        parts.append([(back + 1, step)] + ([(back + 2, held)] if back + 2 < window else []))
    parts.append([(window, held), (1, beside)])
    exps = lax.optimization_barrier((sum_exps, out_exps, query))[:2]
    bounds = spread_bounds(*exps, tokens)
    state = None
    for number, blocks in enumerate(parts):
        plan = [(back, back == window) for back, _ in blocks]
        mine = [block for _, block in blocks]
        if number == 1:
            bounds, state = early = lax.optimization_barrier((bounds, state))
        if number > 0:
            mine = [lax.optimization_barrier((block, early))[0] for block in mine]
        other = [swap_cores(m) for m in mine]
        state = attend(query, segments, plan, mine, other, state, number == len(parts) - 1)
    quant_own = project_own(state, w_out, bounds[0])
    return project_out(swap_cores(state), w_other, quant_own, *bounds)


def solution(mesh):
    in_specs = (
        P(("groups", "seq"), None),
        P(),
        P(("groups", "seq")),
        P(None, "tp"),
        P(None, "tp"),
        P("tp", None),
        P(("groups", "seq"), None),
        P(("groups", "seq"), None),
    )
    out_specs = P(("groups", "seq"), None)
    return jax.shard_map(
        functools.partial(on_device, mesh.shape["seq"]),
        mesh=mesh, in_specs=in_specs, out_specs=out_specs, check_vma=False,
    )
```

```python
import functools

import jax
import jax.numpy as jnp
from jax import lax
from jax.experimental import pallas as pl
from jax.experimental.pallas import tpu as pltpu
from jax.sharding import PartitionSpec as P

HD = 256
LANES = 128
SEG_ROWS = 16
LIMIT = 448.0
MIN_EXP = -9
NEG = -1e30
MIB = 1024 * 1024
NT = (((1,), (1,)), ((), ()))
FACTOR = HD ** (-0.5) * 1.4426950408889634


def norm_kv_kernel(x_ref, gain_hbm, w_ref, seg_hbm, msg_ref, normed_ref, xs, ws, gain_ref, seg_ref, sems):
    rows, width = xs.shape
    tile, part = rows // 2, rows // 4

    def cut(source, target, first, count, pieces, sem):
        size = count // pieces
        return [
            pltpu.make_async_copy(
                source.at[pl.ds(first + i * size, size)], target.at[pl.ds(first + i * size, size)], sems.at[sem + i]
            )
            for i in range(pieces)
        ]

    def early_tokens(half):
        return cut(x_ref, xs, half * part, part, 8 - 4 * half, 8 * half)

    def late_tokens():
        return cut(x_ref, xs, tile, tile, 1, 12)

    def weights():
        return cut(w_ref, ws, 0, width, 4, 14)

    def gain_copy():
        return pltpu.make_async_copy(gain_hbm, gain_ref, sems.at[18])

    def segments_copy():
        return pltpu.make_async_copy(seg_hbm, seg_ref, sems.at[19])

    for copy in early_tokens(0) + early_tokens(1) + [gain_copy()] + weights() + late_tokens() + [segments_copy()]:
        copy.start()

    def wide(first, count, start):
        return xs[first:first + count, start:start + LANES].astype(jnp.float32)

    def stats(first):
        total = wide(first, part, 0)
        for start in range(LANES, width, LANES):
            total = total + wide(first, part, start)
        mean = jnp.broadcast_to(jnp.sum(total, axis=1, keepdims=True) * (1.0 / width), (part, LANES))
        square = jnp.zeros((part, LANES), jnp.float32)
        for start in range(0, width, LANES):
            center = wide(first, part, start) - mean
            square = square + center * center
        spread = jnp.sum(square, axis=1, keepdims=True) * (1.0 / width)
        return mean, jnp.broadcast_to(lax.rsqrt(spread + 1e-05), (part, LANES))

    def project(first, halves):
        mean = jnp.concatenate([h[0] for h in halves], axis=0)
        scale = jnp.concatenate([h[1] for h in halves], axis=0)
        kv = jnp.zeros((tile, ws.shape[1]), jnp.float32)
        span = slice(first, first + tile)
        for start in range(0, width, HD):
            if first == 0 and start % (width // 4) == 0:
                weights()[4 * start // width].wait()
            for at in (start, start + LANES):
                normed = (wide(first, tile, at) - mean) * scale * gain_ref[:, at:at + LANES]
                normed_ref[span, at:at + LANES] = normed.astype(jnp.bfloat16)
            kv = kv + jnp.dot(
                normed_ref[span, start:start + HD], ws[start:start + HD, :], preferred_element_type=jnp.float32
            )
        msg_ref[span, :] = kv.astype(jnp.bfloat16)

    halves = []
    for half in range(2):
        for copy in early_tokens(half):
            copy.wait()
        halves.append(stats(half * part))
    gain_copy().wait()
    project(0, halves)
    for copy in late_tokens():
        copy.wait()
    project(tile, [stats(tile), stats(tile + part)])
    segments_copy().wait()
    seg = seg_ref[...].astype(jnp.float32)
    low = jnp.broadcast_to(seg[:, :HD], (8, HD))
    high = jnp.broadcast_to(seg[:, HD:], (8, HD))
    msg_ref[rows:, :] = jnp.concatenate([low, high], axis=0).astype(jnp.bfloat16)


def in_hbm(x):
    return pltpu.with_memory_space_constraint(x, pltpu.HBM)


def in_vmem(x):
    return pltpu.with_memory_space_constraint(x, pltpu.VMEM)


def norm_kv(tokens, gain, w_keyval, segments):
    rows, width = tokens.shape
    cols = w_keyval.shape[1]
    vmem, hbm = pl.BlockSpec(memory_space=pltpu.VMEM), pl.BlockSpec(memory_space=pltpu.HBM)
    return pl.pallas_call(
        norm_kv_kernel,
        in_specs=[hbm] * 4,
        out_specs=[vmem, vmem],
        out_shape=[pltpu.VMEM((rows + SEG_ROWS, cols), jnp.bfloat16), pltpu.VMEM((rows, width), jnp.bfloat16)],
        scratch_shapes=[
            pltpu.VMEM((rows, width), jnp.bfloat16),
            pltpu.VMEM((width, cols), jnp.bfloat16),
            pltpu.VMEM((1, width), jnp.float32),
            pltpu.VMEM((1, rows), jnp.int32),
            pltpu.SemaphoreType.DMA((20,)),
        ],
        compiler_params=pltpu.CompilerParams(vmem_limit_bytes=24 * MIB),
        cost_estimate=pl.CostEstimate(
            flops=2 * rows * width * cols, bytes_accessed=4 * rows * width + 2 * width * cols, transcendentals=0
        ),
        name="norm_kv",
    )(in_hbm(tokens), in_hbm(gain.reshape(1, width)), in_hbm(w_keyval), in_hbm(segments.reshape(1, rows)))


def query_kernel(x_ref, w_ref, out_ref):
    out_ref[...] = jnp.dot(x_ref[...], w_ref[...], preferred_element_type=jnp.float32).astype(jnp.bfloat16)


def project_query(normed, w_query):
    rows, width = normed.shape
    cols = w_query.shape[1]
    vmem = pl.BlockSpec(memory_space=pltpu.VMEM)
    return pl.pallas_call(
        query_kernel,
        in_specs=[vmem, vmem],
        out_specs=vmem,
        out_shape=pltpu.VMEM((rows, cols), jnp.bfloat16),
        compiler_params=pltpu.CompilerParams(vmem_limit_bytes=8 * MIB),
        cost_estimate=pl.CostEstimate(
            flops=2 * rows * width * cols, bytes_accessed=2 * rows * width + 2 * width * cols, transcendentals=0
        ),
        name="project_query",
    )(in_vmem(normed), in_vmem(w_query))


def attend_kernel(plan, first, last, *refs):
    blocks = len(plan)
    q_ref, seg_ref = refs[:2]
    mine, other = refs[2:2 + blocks], refs[2 + blocks:2 + 2 * blocks]
    refs = refs[2 + 2 * blocks:]
    state_ref = None
    if not first:
        state_ref, refs = refs[0], refs[1:]
    out_ref, scores = refs
    rows = q_ref.shape[0]
    tile = rows // 2
    part = lax.axis_index("tp")
    place = lax.axis_index("seq")

    def finish(span, weighted, total):
        inverse = jnp.broadcast_to(1.0 / jnp.sum(total, axis=1, keepdims=True), total.shape)
        out_ref[span, :] = (weighted * jnp.concatenate([inverse, inverse], axis=1)).astype(jnp.bfloat16)

    def update(slots, keys, values):
        if first:
            out_ref[:, HD + 2 * LANES:] = jnp.transpose(
                jnp.broadcast_to(seg_ref[...].astype(jnp.float32), (LANES, rows))
            )
        key_segs = {}
        for slot in slots:
            packed = mine[slot][rows:, :].astype(jnp.float32)
            key_segs[slot] = jnp.concatenate([packed[0:1, :], packed[8:9, :]], axis=1)
        for start in range(0, rows, tile):
            span = slice(start, start + tile)
            query = q_ref[span, :]
            own_seg = (out_ref if first else state_ref)[span, HD + 2 * LANES:]
            best = before = None if first else state_ref[span, HD:HD + LANES]
            bounds = {}
            for slot in slots:
                back, furthest = plan[slot]
                low, high = 0, rows
                if back == 0:
                    high = start + tile
                elif furthest:
                    low = start
                bounds[slot] = (low, high)
                raw = lax.dot_general(query, keys[slot][low:high, :], NT, preferred_element_type=jnp.float32)
                for at in range(low, high, LANES):
                    allowed = key_segs[slot][:, at:at + LANES] == own_seg
                    if back == 0:
                        row_pos = start + lax.broadcasted_iota(jnp.int32, allowed.shape, 0)
                        allowed = allowed & (at + lax.broadcasted_iota(jnp.int32, allowed.shape, 1) <= row_pos)
                    piece = jnp.where(allowed, raw[:, at - low:at - low + LANES], NEG)
                    scores[slot, :, at:at + LANES] = piece
                    best = piece if best is None else jnp.maximum(best, piece)
            top = jnp.broadcast_to(jnp.max(best, axis=1, keepdims=True), (tile, LANES))
            if first:
                total = jnp.zeros((tile, LANES), jnp.float32)
                weighted = jnp.zeros((tile, HD), jnp.float32)
            else:
                shrink = jnp.exp2((before - top) * FACTOR)
                total = state_ref[span, HD + LANES:HD + 2 * LANES] * shrink
                weighted = state_ref[span, :HD] * jnp.concatenate([shrink, shrink], axis=1)
            for slot in slots:
                low, high = bounds[slot]
                pieces = []
                for at in range(low, high, LANES):
                    weights = jnp.exp2((scores[slot, :, at:at + LANES] - top) * FACTOR)
                    total = total + weights
                    pieces.append(weights.astype(jnp.bfloat16))
                probs = jnp.concatenate(pieces, axis=1)
                weighted = weighted + jnp.dot(probs, values[slot][low:high, :], preferred_element_type=jnp.float32)
            if last:
                finish(span, weighted, total)
            else:
                out_ref[span, :HD] = weighted
                out_ref[span, HD:HD + LANES] = top
                out_ref[span, HD + LANES:HD + 2 * LANES] = total

    order = sorted(range(blocks), key=lambda slot: plan[slot][0])
    for count in range(1 if first else 0, blocks + 1):
        reached = place >= (plan[order[count - 1]][0] if count > 0 else 0)
        if count < blocks:
            reached = reached & (place < plan[order[count]][0])
        if count > 0:
            pl.when(reached & (part == 0))(functools.partial(update, order[:count], mine, other))
            pl.when(reached & (part == 1))(functools.partial(update, order[:count], other, mine))
        elif last:

            @pl.when(reached)
            def _():
                finish(slice(0, rows), state_ref[:, :HD], state_ref[:, HD + LANES:HD + 2 * LANES])


def attend(query, segments, plan, mine, other, state, last):
    rows = query.shape[0]
    blocks = len(plan)
    vmem = pl.BlockSpec(memory_space=pltpu.VMEM)
    first = state is None
    operands = [query, segments.reshape(1, rows), *mine, *other] + ([] if first else [state])
    return pl.pallas_call(
        functools.partial(attend_kernel, plan, first, last),
        in_specs=[vmem] * len(operands),
        out_specs=vmem,
        out_shape=pltpu.VMEM((rows, HD), jnp.bfloat16) if last else pltpu.VMEM((rows, HD + 3 * LANES), jnp.float32),
        scratch_shapes=[pltpu.VMEM((blocks, rows // 2, rows), jnp.float32)],
        input_output_aliases={} if first or last else {len(operands) - 1: 0},
        compiler_params=pltpu.CompilerParams(vmem_limit_bytes=12 * MIB),
        cost_estimate=pl.CostEstimate(
            flops=4 * rows * rows * blocks * HD, bytes_accessed=4 * rows * blocks * HD, transcendentals=rows * rows * blocks
        ),
        name="attend_last" if last else "attend_first" if first else "attend_more",
    )(*[in_vmem(operand) for operand in operands])


def bounds_kernel(sum_ref, out_exp_ref, x_ref, sum_bound_ref, out_bound_ref, wide_ref, near, sem):
    groups, rows = sum_ref.shape
    fetch = pltpu.make_async_copy(x_ref, near, sem)
    fetch.start()
    per = sum_bound_ref.shape[1] // groups
    for exps, bound_ref in ((sum_ref, sum_bound_ref), (out_exp_ref, out_bound_ref)):
        power = jnp.left_shift(jnp.int32(1), exps[...] - MIN_EXP).astype(jnp.float32)
        bound = jnp.transpose(power * (LIMIT * 2.0 ** MIN_EXP))
        for group in range(groups):
            wide = jnp.broadcast_to(bound[:, group:group + 1], (rows, per)).astype(jnp.bfloat16)
            bound_ref[:, group * per:(group + 1) * per] = wide
    fetch.wait()

    def widen(step, carry):
        span = pl.ds(pl.multiple_of(step * 64, 64), 64)
        wide_ref[span, :] = near[span, :].astype(jnp.float32)
        return carry

    lax.fori_loop(0, rows // 64, widen, 0)


def spread_bounds(sum_exps, out_exps, tokens):
    rows, width = tokens.shape
    groups = sum_exps.shape[1]
    vmem = pl.BlockSpec(memory_space=pltpu.VMEM)
    return pl.pallas_call(
        bounds_kernel,
        in_specs=[vmem, vmem, pl.BlockSpec(memory_space=pltpu.HBM)],
        out_specs=[vmem] * 3,
        out_shape=[pltpu.VMEM((rows, width), jnp.bfloat16)] * 2 + [pltpu.VMEM((rows, width), jnp.float32)],
        scratch_shapes=[pltpu.VMEM((rows, width), jnp.bfloat16), pltpu.SemaphoreType.DMA(())],
        compiler_params=pltpu.CompilerParams(vmem_limit_bytes=10 * MIB),
        cost_estimate=pl.CostEstimate(flops=8 * rows * width, bytes_accessed=8 * rows * groups, transcendentals=0),
        name="spread_bounds",
    )(in_vmem(sum_exps.T), in_vmem(out_exps.T), in_hbm(tokens))


def clip(value, bound):
    return jnp.minimum(jnp.maximum(value.astype(jnp.bfloat16), -bound), bound)


def own_kernel(a_ref, w_ref, sum_ref, out_ref):
    rows, width = out_ref.shape
    tile = rows // 2
    for at in range(0, width, HD):
        cols = slice(at, at + HD)
        for start in range(0, rows, tile):
            span = slice(start, start + tile)
            term = jnp.dot(a_ref[span, :], w_ref[:, cols], preferred_element_type=jnp.float32)
            out_ref[span, cols] = clip(term, sum_ref[span, cols])


def project_own(attended, w_out, sum_bound):
    rows, depth = attended.shape
    width = w_out.shape[1]
    vmem = pl.BlockSpec(memory_space=pltpu.VMEM)
    return pl.pallas_call(
        own_kernel,
        in_specs=[vmem] * 3,
        out_specs=vmem,
        out_shape=pltpu.VMEM((rows, width), jnp.bfloat16),
        compiler_params=pltpu.CompilerParams(vmem_limit_bytes=8 * MIB),
        cost_estimate=pl.CostEstimate(
            flops=2 * rows * width * depth, bytes_accessed=4 * rows * width + 2 * width * depth, transcendentals=0
        ),
        name="project_own",
    )(in_vmem(attended), in_vmem(w_out), in_vmem(sum_bound))


def output_kernel(b_ref, wb_ref, quant_ref, x_ref, sum_ref, last_ref, out_ref, staged, sems):
    rows, width = x_ref.shape
    tile = rows // 2

    def copy(index):
        span = slice(index * HD, (index + 1) * HD)
        return pltpu.make_async_copy(staged.at[:, span], out_ref.at[:, span], sems.at[index])

    for index in range(width // HD):
        cols = slice(index * HD, (index + 1) * HD)
        for start in range(0, rows, tile):
            span = slice(start, start + tile)
            term = jnp.dot(b_ref[span, :], wb_ref[:, cols], preferred_element_type=jnp.float32)
            quant = clip(term, sum_ref[span, cols]).astype(jnp.float32) + quant_ref[span, cols].astype(jnp.float32)
            staged[span, cols] = clip(x_ref[span, cols] + quant, last_ref[span, cols])
        copy(index).start()
    for index in range(width // HD):
        copy(index).wait()


def project_out(att_other, w_other, quant_own, sum_bound, out_bound, tokens):
    rows, width = tokens.shape
    depth = att_other.shape[1]
    pieces = width // HD
    vmem = pl.BlockSpec(memory_space=pltpu.VMEM)
    operands = [att_other, w_other, quant_own, tokens, sum_bound, out_bound]
    return pl.pallas_call(
        output_kernel,
        in_specs=[vmem] * len(operands),
        out_specs=pl.BlockSpec(memory_space=pltpu.HBM),
        out_shape=jax.ShapeDtypeStruct((rows, width), jnp.bfloat16),
        scratch_shapes=[pltpu.VMEM((rows, width), jnp.bfloat16), pltpu.SemaphoreType.DMA((pieces,))],
        compiler_params=pltpu.CompilerParams(vmem_limit_bytes=10 * MIB),
        cost_estimate=pl.CostEstimate(
            flops=2 * rows * width * depth, bytes_accessed=4 * rows * width + 2 * width * depth, transcendentals=0
        ),
        name="project_out",
    )(*[in_vmem(operand) for operand in operands])


def on_device(seq_size, tokens, gain, segments, w_query, w_keyval, w_out, sum_exps, out_exps):
    window = seq_size // 2

    def swap_cores(x):
        return lax.ppermute(x, "tp", [(0, 1), (1, 0)])

    def shift(x, step, first):
        cycle = seq_size - first
        pairs = []
        for i in range(seq_size):
            for core in range(2):
                after = 2 * (first + (i - first + step) % cycle) + core if i >= first else 2 * i + 1 - core
                pairs.append((2 * i + core, after))
        return lax.ppermute(x, ("seq", "tp"), pairs)

    w_other = swap_cores(w_out)
    message, normed = norm_kv(tokens, gain, w_keyval, segments)
    query = project_query(normed, w_query)
    held, query = lax.optimization_barrier((shift(message, 2, 0), query))
    odd = lax.rem(lax.axis_index("seq"), 2) == 1
    beside = lax.ppermute(jnp.where(odd, held, message), "seq", [(i, i ^ 1) for i in range(seq_size)])
    parts = [[(0, message), (2, held)]]
    for back in range(2, window, 2):
        step = shift(held, 1, back)
        held = shift(held, 2, back)
        parts.append([(back + 1, step)] + ([(back + 2, held)] if back + 2 < window else []))
    parts.append([(window, held), (1, beside)])
    exps = lax.optimization_barrier((sum_exps, out_exps, query))[:2]
    bounds = spread_bounds(*exps, tokens)
    state = None
    for number, blocks in enumerate(parts):
        plan = [(back, back == window) for back, _ in blocks]
        mine = [block for _, block in blocks]
        if number == 1:
            bounds, state = early = lax.optimization_barrier((bounds, state))
        if number > 0:
            mine = [lax.optimization_barrier((block, early))[0] for block in mine]
        other = [swap_cores(m) for m in mine]
        state = attend(query, segments, plan, mine, other, state, number == len(parts) - 1)
    quant_own = project_own(state, w_out, bounds[0])
    return project_out(swap_cores(state), w_other, quant_own, *bounds)


def solution(mesh):
    in_specs = (
        P(("groups", "seq"), None),
        P(),
        P(("groups", "seq")),
        P(None, "tp"),
        P(None, "tp"),
        P("tp", None),
        P(("groups", "seq"), None),
        P(("groups", "seq"), None),
    )
    out_specs = P(("groups", "seq"), None)
    return jax.shard_map(
        functools.partial(on_device, mesh.shape["seq"]),
        mesh=mesh, in_specs=in_specs, out_specs=out_specs, check_vma=False,
    )
```

```python
import functools

import jax
import jax.numpy as jnp
from jax import lax
from jax.experimental import pallas as pl
from jax.experimental.pallas import tpu as pltpu
from jax.sharding import PartitionSpec as P

HD = 256
LANES = 128
SEG_ROWS = 16
LIMIT = 448.0
MIN_EXP = -9
NEG = -1e30
MIB = 1024 * 1024
NT = (((1,), (1,)), ((), ()))
FACTOR = HD ** (-0.5) * 1.4426950408889634


def norm_kv_kernel(x_ref, gain_hbm, w_ref, seg_hbm, msg_ref, normed_ref, xs, ws, gain_ref, seg_ref, sems):
    rows, width = xs.shape
    tile, part = rows // 2, rows // 4

    def cut(source, target, first, count, pieces, sem):
        size = count // pieces
        return [
            pltpu.make_async_copy(
                source.at[pl.ds(first + i * size, size)], target.at[pl.ds(first + i * size, size)], sems.at[sem + i]
            )
            for i in range(pieces)
        ]

    def early_tokens(half):
        return cut(x_ref, xs, half * part, part, 4, 4 * half)

    def late_tokens():
        return cut(x_ref, xs, tile, tile, 2, 8)

    def weights():
        return cut(w_ref, ws, 0, width, 4, 10)

    def gain_copy():
        return pltpu.make_async_copy(gain_hbm, gain_ref, sems.at[14])

    def segments_copy():
        return pltpu.make_async_copy(seg_hbm, seg_ref, sems.at[15])

    for copy in early_tokens(0) + early_tokens(1) + [gain_copy()] + weights() + late_tokens() + [segments_copy()]:
        copy.start()

    def wide(first, count, start):
        return xs[first:first + count, start:start + LANES].astype(jnp.float32)

    def stats(first):
        total = wide(first, part, 0)
        for start in range(LANES, width, LANES):
            total = total + wide(first, part, start)
        mean = jnp.broadcast_to(jnp.sum(total, axis=1, keepdims=True) * (1.0 / width), (part, LANES))
        square = jnp.zeros((part, LANES), jnp.float32)
        for start in range(0, width, LANES):
            center = wide(first, part, start) - mean
            square = square + center * center
        spread = jnp.sum(square, axis=1, keepdims=True) * (1.0 / width)
        return mean, jnp.broadcast_to(lax.rsqrt(spread + 1e-05), (part, LANES))

    pieces = []
    for half in range(2):
        for copy in early_tokens(half):
            copy.wait()
        pieces.append(stats(half * part))
    for copy in late_tokens():
        copy.wait()
    pieces += [stats(tile), stats(tile + part)]
    mean = [jnp.concatenate([p[0] for p in pieces[i:i + 2]], axis=0) for i in (0, 2)]
    scale = [jnp.concatenate([p[1] for p in pieces[i:i + 2]], axis=0) for i in (0, 2)]
    for copy in [gain_copy()] + weights():
        copy.wait()
    kv = jnp.zeros((rows, ws.shape[1]), jnp.float32)
    for start in range(0, width, HD):
        for half in range(2):
            for at in (start, start + LANES):
                normed = (wide(half * tile, tile, at) - mean[half]) * scale[half] * gain_ref[:, at:at + LANES]
                normed_ref[half * tile:(half + 1) * tile, at:at + LANES] = normed.astype(jnp.bfloat16)
        kv = kv + jnp.dot(normed_ref[:, start:start + HD], ws[start:start + HD, :], preferred_element_type=jnp.float32)
    msg_ref[:rows, :] = kv.astype(jnp.bfloat16)
    segments_copy().wait()
    seg = seg_ref[...].astype(jnp.float32)
    low = jnp.broadcast_to(seg[:, :HD], (8, HD))
    high = jnp.broadcast_to(seg[:, HD:], (8, HD))
    msg_ref[rows:, :] = jnp.concatenate([low, high], axis=0).astype(jnp.bfloat16)


def in_hbm(x):
    return pltpu.with_memory_space_constraint(x, pltpu.HBM)


def in_vmem(x):
    return pltpu.with_memory_space_constraint(x, pltpu.VMEM)


def norm_kv(tokens, gain, w_keyval, segments):
    rows, width = tokens.shape
    cols = w_keyval.shape[1]
    vmem, hbm = pl.BlockSpec(memory_space=pltpu.VMEM), pl.BlockSpec(memory_space=pltpu.HBM)
    return pl.pallas_call(
        norm_kv_kernel,
        in_specs=[hbm] * 4,
        out_specs=[vmem, vmem],
        out_shape=[pltpu.VMEM((rows + SEG_ROWS, cols), jnp.bfloat16), pltpu.VMEM((rows, width), jnp.bfloat16)],
        scratch_shapes=[
            pltpu.VMEM((rows, width), jnp.bfloat16),
            pltpu.VMEM((width, cols), jnp.bfloat16),
            pltpu.VMEM((1, width), jnp.float32),
            pltpu.VMEM((1, rows), jnp.int32),
            pltpu.SemaphoreType.DMA((16,)),
        ],
        compiler_params=pltpu.CompilerParams(vmem_limit_bytes=24 * MIB),
        cost_estimate=pl.CostEstimate(
            flops=2 * rows * width * cols, bytes_accessed=4 * rows * width + 2 * width * cols, transcendentals=0
        ),
        name="norm_kv",
    )(in_hbm(tokens), in_hbm(gain.reshape(1, width)), in_hbm(w_keyval), in_hbm(segments.reshape(1, rows)))


def query_kernel(x_ref, w_ref, out_ref):
    out_ref[...] = jnp.dot(x_ref[...], w_ref[...], preferred_element_type=jnp.float32).astype(jnp.bfloat16)


def project_query(normed, w_query):
    rows, width = normed.shape
    cols = w_query.shape[1]
    vmem = pl.BlockSpec(memory_space=pltpu.VMEM)
    return pl.pallas_call(
        query_kernel,
        in_specs=[vmem, vmem],
        out_specs=vmem,
        out_shape=pltpu.VMEM((rows, cols), jnp.bfloat16),
        compiler_params=pltpu.CompilerParams(vmem_limit_bytes=8 * MIB),
        cost_estimate=pl.CostEstimate(
            flops=2 * rows * width * cols, bytes_accessed=2 * rows * width + 2 * width * cols, transcendentals=0
        ),
        name="project_query",
    )(in_vmem(normed), in_vmem(w_query))


def attend_kernel(plan, first, last, *refs):
    blocks = len(plan)
    q_ref, seg_ref = refs[:2]
    mine, other = refs[2:2 + blocks], refs[2 + blocks:2 + 2 * blocks]
    refs = refs[2 + 2 * blocks:]
    state_ref = None
    if not first:
        state_ref, refs = refs[0], refs[1:]
    out_ref, scores = refs
    rows = q_ref.shape[0]
    tile = rows // 2
    part = lax.axis_index("tp")
    place = lax.axis_index("seq")

    def finish(span, weighted, total):
        inverse = jnp.broadcast_to(1.0 / jnp.sum(total, axis=1, keepdims=True), total.shape)
        out_ref[span, :] = (weighted * jnp.concatenate([inverse, inverse], axis=1)).astype(jnp.bfloat16)

    def update(slots, keys, values):
        if first:
            out_ref[:, HD + 2 * LANES:] = jnp.transpose(
                jnp.broadcast_to(seg_ref[...].astype(jnp.float32), (LANES, rows))
            )
        key_segs = {}
        for slot in slots:
            packed = mine[slot][rows:, :].astype(jnp.float32)
            key_segs[slot] = jnp.concatenate([packed[0:1, :], packed[8:9, :]], axis=1)
        for start in range(0, rows, tile):
            span = slice(start, start + tile)
            query = q_ref[span, :]
            own_seg = (out_ref if first else state_ref)[span, HD + 2 * LANES:]
            best = before = None if first else state_ref[span, HD:HD + LANES]
            bounds = {}
            for slot in slots:
                back, furthest = plan[slot]
                low, high = 0, rows
                if back == 0:
                    high = start + tile
                elif furthest:
                    low = start
                bounds[slot] = (low, high)
                raw = lax.dot_general(query, keys[slot][low:high, :], NT, preferred_element_type=jnp.float32)
                for at in range(low, high, LANES):
                    allowed = key_segs[slot][:, at:at + LANES] == own_seg
                    if back == 0:
                        row_pos = start + lax.broadcasted_iota(jnp.int32, allowed.shape, 0)
                        allowed = allowed & (at + lax.broadcasted_iota(jnp.int32, allowed.shape, 1) <= row_pos)
                    piece = jnp.where(allowed, raw[:, at - low:at - low + LANES], NEG)
                    scores[slot, :, at:at + LANES] = piece
                    best = piece if best is None else jnp.maximum(best, piece)
            top = jnp.broadcast_to(jnp.max(best, axis=1, keepdims=True), (tile, LANES))
            if first:
                total = jnp.zeros((tile, LANES), jnp.float32)
                weighted = jnp.zeros((tile, HD), jnp.float32)
            else:
                shrink = jnp.exp2((before - top) * FACTOR)
                total = state_ref[span, HD + LANES:HD + 2 * LANES] * shrink
                weighted = state_ref[span, :HD] * jnp.concatenate([shrink, shrink], axis=1)
            for slot in slots:
                low, high = bounds[slot]
                pieces = []
                for at in range(low, high, LANES):
                    weights = jnp.exp2((scores[slot, :, at:at + LANES] - top) * FACTOR)
                    total = total + weights
                    pieces.append(weights.astype(jnp.bfloat16))
                probs = jnp.concatenate(pieces, axis=1)
                weighted = weighted + jnp.dot(probs, values[slot][low:high, :], preferred_element_type=jnp.float32)
            if last:
                finish(span, weighted, total)
            else:
                out_ref[span, :HD] = weighted
                out_ref[span, HD:HD + LANES] = top
                out_ref[span, HD + LANES:HD + 2 * LANES] = total

    order = sorted(range(blocks), key=lambda slot: plan[slot][0])
    for count in range(1 if first else 0, blocks + 1):
        reached = place >= (plan[order[count - 1]][0] if count > 0 else 0)
        if count < blocks:
            reached = reached & (place < plan[order[count]][0])
        if count > 0:
            pl.when(reached & (part == 0))(functools.partial(update, order[:count], mine, other))
            pl.when(reached & (part == 1))(functools.partial(update, order[:count], other, mine))
        elif last:

            @pl.when(reached)
            def _():
                finish(slice(0, rows), state_ref[:, :HD], state_ref[:, HD + LANES:HD + 2 * LANES])


def attend(query, segments, plan, mine, other, state, last):
    rows = query.shape[0]
    blocks = len(plan)
    vmem = pl.BlockSpec(memory_space=pltpu.VMEM)
    first = state is None
    operands = [query, segments.reshape(1, rows), *mine, *other] + ([] if first else [state])
    return pl.pallas_call(
        functools.partial(attend_kernel, plan, first, last),
        in_specs=[vmem] * len(operands),
        out_specs=vmem,
        out_shape=pltpu.VMEM((rows, HD), jnp.bfloat16) if last else pltpu.VMEM((rows, HD + 3 * LANES), jnp.float32),
        scratch_shapes=[pltpu.VMEM((blocks, rows // 2, rows), jnp.float32)],
        input_output_aliases={} if first or last else {len(operands) - 1: 0},
        compiler_params=pltpu.CompilerParams(vmem_limit_bytes=12 * MIB),
        cost_estimate=pl.CostEstimate(
            flops=4 * rows * rows * blocks * HD, bytes_accessed=4 * rows * blocks * HD, transcendentals=rows * rows * blocks
        ),
        name="attend_last" if last else "attend_first" if first else "attend_more",
    )(*[in_vmem(operand) for operand in operands])


def bounds_kernel(sum_ref, out_exp_ref, x_ref, sum_bound_ref, out_bound_ref, wide_ref, near, sem):
    groups, rows = sum_ref.shape
    fetch = pltpu.make_async_copy(x_ref, near, sem)
    fetch.start()
    per = sum_bound_ref.shape[1] // groups
    for exps, bound_ref in ((sum_ref, sum_bound_ref), (out_exp_ref, out_bound_ref)):
        power = jnp.left_shift(jnp.int32(1), exps[...] - MIN_EXP).astype(jnp.float32)
        bound = jnp.transpose(power * (LIMIT * 2.0 ** MIN_EXP))
        for group in range(groups):
            wide = jnp.broadcast_to(bound[:, group:group + 1], (rows, per)).astype(jnp.bfloat16)
            bound_ref[:, group * per:(group + 1) * per] = wide
    fetch.wait()

    def widen(step, carry):
        span = pl.ds(pl.multiple_of(step * 64, 64), 64)
        wide_ref[span, :] = near[span, :].astype(jnp.float32)
        return carry

    lax.fori_loop(0, rows // 64, widen, 0)


def spread_bounds(sum_exps, out_exps, tokens):
    rows, width = tokens.shape
    groups = sum_exps.shape[1]
    vmem = pl.BlockSpec(memory_space=pltpu.VMEM)
    return pl.pallas_call(
        bounds_kernel,
        in_specs=[vmem, vmem, pl.BlockSpec(memory_space=pltpu.HBM)],
        out_specs=[vmem] * 3,
        out_shape=[pltpu.VMEM((rows, width), jnp.bfloat16)] * 2 + [pltpu.VMEM((rows, width), jnp.float32)],
        scratch_shapes=[pltpu.VMEM((rows, width), jnp.bfloat16), pltpu.SemaphoreType.DMA(())],
        compiler_params=pltpu.CompilerParams(vmem_limit_bytes=10 * MIB),
        cost_estimate=pl.CostEstimate(flops=8 * rows * width, bytes_accessed=8 * rows * groups, transcendentals=0),
        name="spread_bounds",
    )(in_vmem(sum_exps.T), in_vmem(out_exps.T), in_hbm(tokens))


def clip(value, bound):
    return jnp.minimum(jnp.maximum(value.astype(jnp.bfloat16), -bound), bound)


def in_tiles(a_ref, w_ref, finish):
    rows = a_ref.shape[0]
    tile = rows // 2
    waiting = None
    for at in range(0, w_ref.shape[1], HD):
        for start in range(0, rows, tile):
            span, cols = slice(start, start + tile), slice(at, at + HD)
            term = jnp.dot(a_ref[span, :], w_ref[:, cols], preferred_element_type=jnp.float32)
            if waiting is not None:
                finish(*waiting)
            waiting = (span, cols, term)
    finish(*waiting)


def own_kernel(a_ref, w_ref, sum_ref, out_ref):
    def finish(span, cols, term):
        out_ref[span, cols] = clip(term, sum_ref[span, cols])

    in_tiles(a_ref, w_ref, finish)


def project_own(attended, w_out, sum_bound):
    rows, depth = attended.shape
    width = w_out.shape[1]
    vmem = pl.BlockSpec(memory_space=pltpu.VMEM)
    return pl.pallas_call(
        own_kernel,
        in_specs=[vmem] * 3,
        out_specs=vmem,
        out_shape=pltpu.VMEM((rows, width), jnp.bfloat16),
        compiler_params=pltpu.CompilerParams(vmem_limit_bytes=8 * MIB),
        cost_estimate=pl.CostEstimate(
            flops=2 * rows * width * depth, bytes_accessed=4 * rows * width + 2 * width * depth, transcendentals=0
        ),
        name="project_own",
    )(in_vmem(attended), in_vmem(w_out), in_vmem(sum_bound))


def output_kernel(b_ref, wb_ref, quant_ref, x_ref, sum_ref, last_ref, out_ref, staged, sems):
    rows, width = x_ref.shape

    def copy(index):
        span = slice(index * HD, (index + 1) * HD)
        return pltpu.make_async_copy(staged.at[:, span], out_ref.at[:, span], sems.at[index])

    def finish(span, cols, term):
        quant = clip(term, sum_ref[span, cols]).astype(jnp.float32) + quant_ref[span, cols].astype(jnp.float32)
        staged[span, cols] = clip(x_ref[span, cols] + quant, last_ref[span, cols])
        if span.stop == rows:
            copy(cols.start // HD).start()

    in_tiles(b_ref, wb_ref, finish)
    for index in range(width // HD):
        copy(index).wait()


def project_out(att_other, w_other, quant_own, sum_bound, out_bound, tokens):
    rows, width = tokens.shape
    depth = att_other.shape[1]
    pieces = width // HD
    vmem = pl.BlockSpec(memory_space=pltpu.VMEM)
    operands = [att_other, w_other, quant_own, tokens, sum_bound, out_bound]
    return pl.pallas_call(
        output_kernel,
        in_specs=[vmem] * len(operands),
        out_specs=pl.BlockSpec(memory_space=pltpu.HBM),
        out_shape=jax.ShapeDtypeStruct((rows, width), jnp.bfloat16),
        scratch_shapes=[pltpu.VMEM((rows, width), jnp.bfloat16), pltpu.SemaphoreType.DMA((pieces,))],
        compiler_params=pltpu.CompilerParams(vmem_limit_bytes=10 * MIB),
        cost_estimate=pl.CostEstimate(
            flops=2 * rows * width * depth, bytes_accessed=4 * rows * width + 2 * width * depth, transcendentals=0
        ),
        name="project_out",
    )(*[in_vmem(operand) for operand in operands])


def on_device(seq_size, tokens, gain, segments, w_query, w_keyval, w_out, sum_exps, out_exps):
    window = seq_size // 2

    def swap_cores(x):
        return lax.ppermute(x, "tp", [(0, 1), (1, 0)])

    def shift(x, step, first):
        cycle = seq_size - first
        pairs = []
        for i in range(seq_size):
            for core in range(2):
                after = 2 * (first + (i - first + step) % cycle) + core if i >= first else 2 * i + 1 - core
                pairs.append((2 * i + core, after))
        return lax.ppermute(x, ("seq", "tp"), pairs)

    w_other = swap_cores(w_out)
    message, normed = norm_kv(tokens, gain, w_keyval, segments)
    query = project_query(normed, w_query)
    held, query = lax.optimization_barrier((shift(message, 2, 0), query))
    odd = lax.rem(lax.axis_index("seq"), 2) == 1
    beside = lax.ppermute(jnp.where(odd, held, message), "seq", [(i, i ^ 1) for i in range(seq_size)])
    parts = [[(0, message), (2, held)]]
    for back in range(2, window, 2):
        step = shift(held, 1, back)
        held = shift(held, 2, back)
        parts.append([(back + 1, step)] + ([(back + 2, held)] if back + 2 < window else []))
    parts.append([(window, held), (1, beside)])
    exps = lax.optimization_barrier((sum_exps, out_exps, query))[:2]
    bounds = spread_bounds(*exps, tokens)
    state = None
    for number, blocks in enumerate(parts):
        plan = [(back, back == window) for back, _ in blocks]
        mine = [block for _, block in blocks]
        if number == 1:
            bounds, state = early = lax.optimization_barrier((bounds, state))
        if number > 0:
            mine = [lax.optimization_barrier((block, early))[0] for block in mine]
        other = [swap_cores(m) for m in mine]
        state = attend(query, segments, plan, mine, other, state, number == len(parts) - 1)
    quant_own = project_own(state, w_out, bounds[0])
    return project_out(swap_cores(state), w_other, quant_own, *bounds)


def solution(mesh):
    in_specs = (
        P(("groups", "seq"), None),
        P(),
        P(("groups", "seq")),
        P(None, "tp"),
        P(None, "tp"),
        P("tp", None),
        P(("groups", "seq"), None),
        P(("groups", "seq"), None),
    )
    out_specs = P(("groups", "seq"), None)
    return jax.shard_map(
        functools.partial(on_device, mesh.shape["seq"]),
        mesh=mesh, in_specs=in_specs, out_specs=out_specs, check_vma=False,
    )
```

```python
import functools

import jax
import jax.numpy as jnp
from jax import lax
from jax.experimental import pallas as pl
from jax.experimental.pallas import tpu as pltpu
from jax.sharding import PartitionSpec as P

HD = 256
LANES = 128
SEG_ROWS = 16
LIMIT = 448.0
MIN_EXP = -9
NEG = -1e30
MIB = 1024 * 1024
NT = (((1,), (1,)), ((), ()))
FACTOR = HD ** (-0.5) * 1.4426950408889634


def norm_kv_kernel(x_ref, gain_hbm, w_ref, seg_hbm, next_ref, msg_ref, normed_ref, near_ref, xs, ws, gain_ref, seg_ref, sems):
    rows, width = xs.shape
    tile, part = rows // 2, rows // 4

    def cut(source, target, first, count, pieces, sem):
        size = count // pieces
        return [
            pltpu.make_async_copy(
                source.at[pl.ds(first + i * size, size)], target.at[pl.ds(first + i * size, size)], sems.at[sem + i]
            )
            for i in range(pieces)
        ]

    def early_tokens(half):
        return cut(x_ref, xs, half * part, part, 4, 4 * half)

    def late_tokens():
        return cut(x_ref, xs, tile, tile, 2, 8)

    def weights():
        return cut(w_ref, ws, 0, width, 4, 10)

    def gain_copy():
        return pltpu.make_async_copy(gain_hbm, gain_ref, sems.at[14])

    def segments_copy():
        return pltpu.make_async_copy(seg_hbm, seg_ref, sems.at[15])

    def next_copy():
        return pltpu.make_async_copy(next_ref, near_ref, sems.at[16])

    for copy in early_tokens(0) + early_tokens(1) + [gain_copy()] + weights() + late_tokens() + [segments_copy()]:
        copy.start()

    def wide(first, count, start):
        return xs[first:first + count, start:start + LANES].astype(jnp.float32)

    def stats(first):
        total = wide(first, part, 0)
        for start in range(LANES, width, LANES):
            total = total + wide(first, part, start)
        mean = jnp.broadcast_to(jnp.sum(total, axis=1, keepdims=True) * (1.0 / width), (part, LANES))
        square = jnp.zeros((part, LANES), jnp.float32)
        for start in range(0, width, LANES):
            center = wide(first, part, start) - mean
            square = square + center * center
        spread = jnp.sum(square, axis=1, keepdims=True) * (1.0 / width)
        return mean, jnp.broadcast_to(lax.rsqrt(spread + 1e-05), (part, LANES))

    def project(first, halves):
        mean = jnp.concatenate([h[0] for h in halves], axis=0)
        scale = jnp.concatenate([h[1] for h in halves], axis=0)
        kv = jnp.zeros((tile, ws.shape[1]), jnp.float32)
        span = slice(first, first + tile)
        for start in range(0, width, HD):
            for at in (start, start + LANES):
                normed = (wide(first, tile, at) - mean) * scale * gain_ref[:, at:at + LANES]
                normed_ref[span, at:at + LANES] = normed.astype(jnp.bfloat16)
            kv = kv + jnp.dot(
                normed_ref[span, start:start + HD], ws[start:start + HD, :], preferred_element_type=jnp.float32
            )
        msg_ref[span, :] = kv.astype(jnp.bfloat16)

    halves = []
    for half in range(2):
        for copy in early_tokens(half):
            copy.wait()
        halves.append(stats(half * part))
    for copy in [gain_copy()] + weights():
        copy.wait()
    next_copy().start()
    project(0, halves)
    for copy in late_tokens():
        copy.wait()
    project(tile, [stats(tile), stats(tile + part)])
    segments_copy().wait()
    seg = seg_ref[...].astype(jnp.float32)
    low = jnp.broadcast_to(seg[:, :HD], (8, HD))
    high = jnp.broadcast_to(seg[:, HD:], (8, HD))
    msg_ref[rows:, :] = jnp.concatenate([low, high], axis=0).astype(jnp.bfloat16)
    next_copy().wait()


def in_hbm(x):
    return pltpu.with_memory_space_constraint(x, pltpu.HBM)


def in_vmem(x):
    return pltpu.with_memory_space_constraint(x, pltpu.VMEM)


def norm_kv(tokens, gain, w_keyval, segments, w_next):
    rows, width = tokens.shape
    cols = w_keyval.shape[1]
    vmem, hbm = pl.BlockSpec(memory_space=pltpu.VMEM), pl.BlockSpec(memory_space=pltpu.HBM)
    return pl.pallas_call(
        norm_kv_kernel,
        in_specs=[hbm] * 5,
        out_specs=[vmem] * 3,
        out_shape=[
            pltpu.VMEM((rows + SEG_ROWS, cols), jnp.bfloat16),
            pltpu.VMEM((rows, width), jnp.bfloat16),
            pltpu.VMEM(w_next.shape, w_next.dtype),
        ],
        scratch_shapes=[
            pltpu.VMEM((rows, width), jnp.bfloat16),
            pltpu.VMEM((width, cols), jnp.bfloat16),
            pltpu.VMEM((1, width), jnp.float32),
            pltpu.VMEM((1, rows), jnp.int32),
            pltpu.SemaphoreType.DMA((17,)),
        ],
        compiler_params=pltpu.CompilerParams(vmem_limit_bytes=24 * MIB),
        cost_estimate=pl.CostEstimate(
            flops=2 * rows * width * cols, bytes_accessed=4 * rows * width + 2 * width * cols, transcendentals=0
        ),
        name="norm_kv",
    )(*[in_hbm(x) for x in (tokens, gain.reshape(1, width), w_keyval, segments.reshape(1, rows), w_next)])


def query_kernel(x_ref, w_ref, out_ref):
    out_ref[...] = jnp.dot(x_ref[...], w_ref[...], preferred_element_type=jnp.float32).astype(jnp.bfloat16)


def project_query(normed, w_query):
    rows, width = normed.shape
    cols = w_query.shape[1]
    vmem = pl.BlockSpec(memory_space=pltpu.VMEM)
    return pl.pallas_call(
        query_kernel,
        in_specs=[vmem, vmem],
        out_specs=vmem,
        out_shape=pltpu.VMEM((rows, cols), jnp.bfloat16),
        compiler_params=pltpu.CompilerParams(vmem_limit_bytes=8 * MIB),
        cost_estimate=pl.CostEstimate(
            flops=2 * rows * width * cols, bytes_accessed=2 * rows * width + 2 * width * cols, transcendentals=0
        ),
        name="project_query",
    )(in_vmem(normed), in_vmem(w_query))


def attend_kernel(plan, first, last, *refs):
    blocks = len(plan)
    q_ref, seg_ref = refs[:2]
    mine, other = refs[2:2 + blocks], refs[2 + blocks:2 + 2 * blocks]
    refs = refs[2 + 2 * blocks:]
    state_ref = None
    if not first:
        state_ref, refs = refs[0], refs[1:]
    out_ref, scores = refs
    rows = q_ref.shape[0]
    tile = rows // 2
    part = lax.axis_index("tp")
    place = lax.axis_index("seq")

    def finish(span, weighted, total):
        inverse = jnp.broadcast_to(1.0 / jnp.sum(total, axis=1, keepdims=True), total.shape)
        out_ref[span, :] = (weighted * jnp.concatenate([inverse, inverse], axis=1)).astype(jnp.bfloat16)

    def update(slots, keys, values):
        if first:
            out_ref[:, HD + 2 * LANES:] = jnp.transpose(
                jnp.broadcast_to(seg_ref[...].astype(jnp.float32), (LANES, rows))
            )
        key_segs = {}
        for slot in slots:
            packed = mine[slot][rows:, :].astype(jnp.float32)
            key_segs[slot] = jnp.concatenate([packed[0:1, :], packed[8:9, :]], axis=1)
        for start in range(0, rows, tile):
            span = slice(start, start + tile)
            query = q_ref[span, :]
            own_seg = (out_ref if first else state_ref)[span, HD + 2 * LANES:]
            best = before = None if first else state_ref[span, HD:HD + LANES]
            bounds = {}
            for slot in slots:
                back, furthest = plan[slot]
                low, high = 0, rows
                if back == 0:
                    high = start + tile
                elif furthest:
                    low = start
                bounds[slot] = (low, high)
                raw = lax.dot_general(query, keys[slot][low:high, :], NT, preferred_element_type=jnp.float32)
                for at in range(low, high, LANES):
                    allowed = key_segs[slot][:, at:at + LANES] == own_seg
                    if back == 0:
                        row_pos = start + lax.broadcasted_iota(jnp.int32, allowed.shape, 0)
                        allowed = allowed & (at + lax.broadcasted_iota(jnp.int32, allowed.shape, 1) <= row_pos)
                    piece = jnp.where(allowed, raw[:, at - low:at - low + LANES], NEG)
                    scores[slot, :, at:at + LANES] = piece
                    best = piece if best is None else jnp.maximum(best, piece)
            top = jnp.broadcast_to(jnp.max(best, axis=1, keepdims=True), (tile, LANES))
            if first:
                total = jnp.zeros((tile, LANES), jnp.float32)
                weighted = jnp.zeros((tile, HD), jnp.float32)
            else:
                shrink = jnp.exp2((before - top) * FACTOR)
                total = state_ref[span, HD + LANES:HD + 2 * LANES] * shrink
                weighted = state_ref[span, :HD] * jnp.concatenate([shrink, shrink], axis=1)
            for slot in slots:
                low, high = bounds[slot]
                pieces = []
                for at in range(low, high, LANES):
                    weights = jnp.exp2((scores[slot, :, at:at + LANES] - top) * FACTOR)
                    total = total + weights
                    pieces.append(weights.astype(jnp.bfloat16))
                probs = jnp.concatenate(pieces, axis=1)
                weighted = weighted + jnp.dot(probs, values[slot][low:high, :], preferred_element_type=jnp.float32)
            if last:
                finish(span, weighted, total)
            else:
                out_ref[span, :HD] = weighted
                out_ref[span, HD:HD + LANES] = top
                out_ref[span, HD + LANES:HD + 2 * LANES] = total

    order = sorted(range(blocks), key=lambda slot: plan[slot][0])
    for count in range(1 if first else 0, blocks + 1):
        reached = place >= (plan[order[count - 1]][0] if count > 0 else 0)
        if count < blocks:
            reached = reached & (place < plan[order[count]][0])
        if count > 0:
            pl.when(reached & (part == 0))(functools.partial(update, order[:count], mine, other))
            pl.when(reached & (part == 1))(functools.partial(update, order[:count], other, mine))
        elif last:

            @pl.when(reached)
            def _():
                finish(slice(0, rows), state_ref[:, :HD], state_ref[:, HD + LANES:HD + 2 * LANES])


def attend(query, segments, plan, mine, other, state, last):
    rows = query.shape[0]
    blocks = len(plan)
    vmem = pl.BlockSpec(memory_space=pltpu.VMEM)
    first = state is None
    operands = [query, segments.reshape(1, rows), *mine, *other] + ([] if first else [state])
    return pl.pallas_call(
        functools.partial(attend_kernel, plan, first, last),
        in_specs=[vmem] * len(operands),
        out_specs=vmem,
        out_shape=pltpu.VMEM((rows, HD), jnp.bfloat16) if last else pltpu.VMEM((rows, HD + 3 * LANES), jnp.float32),
        scratch_shapes=[pltpu.VMEM((blocks, rows // 2, rows), jnp.float32)],
        input_output_aliases={} if first or last else {len(operands) - 1: 0},
        compiler_params=pltpu.CompilerParams(vmem_limit_bytes=12 * MIB),
        cost_estimate=pl.CostEstimate(
            flops=4 * rows * rows * blocks * HD, bytes_accessed=4 * rows * blocks * HD, transcendentals=rows * rows * blocks
        ),
        name="attend_last" if last else "attend_first" if first else "attend_more",
    )(*[in_vmem(operand) for operand in operands])


def bounds_kernel(sum_ref, out_exp_ref, x_ref, sum_bound_ref, sum_low_ref, out_bound_ref, out_low_ref, wide_ref, near, sem):
    groups, rows = sum_ref.shape
    fetch = pltpu.make_async_copy(x_ref, near, sem)
    fetch.start()
    per = sum_bound_ref.shape[1] // groups
    for exps, bound_ref, low_ref in ((sum_ref, sum_bound_ref, sum_low_ref), (out_exp_ref, out_bound_ref, out_low_ref)):
        power = jnp.left_shift(jnp.int32(1), exps[...] - MIN_EXP).astype(jnp.float32)
        bound = jnp.transpose(power * (LIMIT * 2.0 ** MIN_EXP))
        for group in range(groups):
            wide = jnp.broadcast_to(bound[:, group:group + 1], (rows, per)).astype(jnp.bfloat16)
            bound_ref[:, group * per:(group + 1) * per] = wide
            low_ref[:, group * per:(group + 1) * per] = -wide
    fetch.wait()

    def widen(step, carry):
        span = pl.ds(pl.multiple_of(step * 64, 64), 64)
        wide_ref[span, :] = near[span, :].astype(jnp.float32)
        return carry

    lax.fori_loop(0, rows // 64, widen, 0)


def spread_bounds(sum_exps, out_exps, tokens):
    rows, width = tokens.shape
    groups = sum_exps.shape[1]
    vmem = pl.BlockSpec(memory_space=pltpu.VMEM)
    return pl.pallas_call(
        bounds_kernel,
        in_specs=[vmem, vmem, pl.BlockSpec(memory_space=pltpu.HBM)],
        out_specs=[vmem] * 5,
        out_shape=[pltpu.VMEM((rows, width), jnp.bfloat16)] * 4 + [pltpu.VMEM((rows, width), jnp.float32)],
        scratch_shapes=[pltpu.VMEM((rows, width), jnp.bfloat16), pltpu.SemaphoreType.DMA(())],
        compiler_params=pltpu.CompilerParams(vmem_limit_bytes=10 * MIB),
        cost_estimate=pl.CostEstimate(flops=8 * rows * width, bytes_accessed=8 * rows * groups, transcendentals=0),
        name="spread_bounds",
    )(in_vmem(sum_exps.T), in_vmem(out_exps.T), in_hbm(tokens))


def clip(value, bound, low):
    return jnp.minimum(jnp.maximum(value.astype(jnp.bfloat16), low), bound)


def own_kernel(a_ref, w_ref, sum_ref, low_ref, out_ref):
    rows, width = out_ref.shape
    tile = rows // 2
    for at in range(0, width, HD):
        cols = slice(at, at + HD)
        for start in range(0, rows, tile):
            span = slice(start, start + tile)
            term = jnp.dot(a_ref[span, :], w_ref[:, cols], preferred_element_type=jnp.float32)
            out_ref[span, cols] = clip(term, sum_ref[span, cols], low_ref[span, cols])


def project_own(attended, w_out, sum_bound, sum_low):
    rows, depth = attended.shape
    width = w_out.shape[1]
    vmem = pl.BlockSpec(memory_space=pltpu.VMEM)
    return pl.pallas_call(
        own_kernel,
        in_specs=[vmem] * 4,
        out_specs=vmem,
        out_shape=pltpu.VMEM((rows, width), jnp.bfloat16),
        compiler_params=pltpu.CompilerParams(vmem_limit_bytes=8 * MIB),
        cost_estimate=pl.CostEstimate(
            flops=2 * rows * width * depth, bytes_accessed=4 * rows * width + 2 * width * depth, transcendentals=0
        ),
        name="project_own",
    )(in_vmem(attended), in_vmem(w_out), in_vmem(sum_bound), in_vmem(sum_low))


def output_kernel(b_ref, wb_ref, quant_ref, x_ref, sum_ref, sum_low_ref, last_ref, last_low_ref, out_ref, staged, sems):
    rows, width = x_ref.shape
    tile = rows // 2

    def copy(index):
        span = slice(index * HD, (index + 1) * HD)
        return pltpu.make_async_copy(staged.at[:, span], out_ref.at[:, span], sems.at[index])

    for index in range(width // HD):
        cols = slice(index * HD, (index + 1) * HD)
        for start in range(0, rows, tile):
            span = slice(start, start + tile)
            term = jnp.dot(b_ref[span, :], wb_ref[:, cols], preferred_element_type=jnp.float32)
            other = clip(term, sum_ref[span, cols], sum_low_ref[span, cols])
            quant = other.astype(jnp.float32) + quant_ref[span, cols].astype(jnp.float32)
            staged[span, cols] = clip(x_ref[span, cols] + quant, last_ref[span, cols], last_low_ref[span, cols])
        copy(index).start()
    for index in range(width // HD):
        copy(index).wait()


def project_out(att_other, w_other, quant_own, sum_bound, sum_low, out_bound, out_low, tokens):
    rows, width = tokens.shape
    depth = att_other.shape[1]
    pieces = width // HD
    vmem = pl.BlockSpec(memory_space=pltpu.VMEM)
    operands = [att_other, w_other, quant_own, tokens, sum_bound, sum_low, out_bound, out_low]
    return pl.pallas_call(
        output_kernel,
        in_specs=[vmem] * len(operands),
        out_specs=pl.BlockSpec(memory_space=pltpu.HBM),
        out_shape=jax.ShapeDtypeStruct((rows, width), jnp.bfloat16),
        scratch_shapes=[pltpu.VMEM((rows, width), jnp.bfloat16), pltpu.SemaphoreType.DMA((pieces,))],
        compiler_params=pltpu.CompilerParams(vmem_limit_bytes=10 * MIB),
        cost_estimate=pl.CostEstimate(
            flops=2 * rows * width * depth, bytes_accessed=4 * rows * width + 2 * width * depth, transcendentals=0
        ),
        name="project_out",
    )(*[in_vmem(operand) for operand in operands])


def on_device(seq_size, tokens, gain, segments, w_query, w_keyval, w_out, sum_exps, out_exps):
    window = seq_size // 2

    def swap_cores(x):
        return lax.ppermute(x, "tp", [(0, 1), (1, 0)])

    def shift(x, step, first):
        cycle = seq_size - first
        pairs = []
        for i in range(seq_size):
            for core in range(2):
                after = 2 * (first + (i - first + step) % cycle) + core if i >= first else 2 * i + 1 - core
                pairs.append((2 * i + core, after))
        return lax.ppermute(x, ("seq", "tp"), pairs)

    w_other = swap_cores(w_out)
    message, normed, w_near = norm_kv(tokens, gain, w_keyval, segments, w_query)
    query = project_query(normed, w_near)
    held, query = lax.optimization_barrier((shift(message, 2, 0), query))
    odd = lax.rem(lax.axis_index("seq"), 2) == 1
    beside = lax.ppermute(jnp.where(odd, held, message), "seq", [(i, i ^ 1) for i in range(seq_size)])
    parts = [[(0, message), (2, held)]]
    for back in range(2, window, 2):
        step = shift(held, 1, back)
        held = shift(held, 2, back)
        parts.append([(back + 1, step)] + ([(back + 2, held)] if back + 2 < window else []))
    parts.append([(window, held), (1, beside)])
    exps = lax.optimization_barrier((sum_exps, out_exps, query))[:2]
    bounds = spread_bounds(*exps, tokens)
    state = None
    for number, blocks in enumerate(parts):
        plan = [(back, back == window) for back, _ in blocks]
        mine = [block for _, block in blocks]
        if number == 1:
            bounds, state = early = lax.optimization_barrier((bounds, state))
        if number > 0:
            mine = [lax.optimization_barrier((block, early))[0] for block in mine]
        other = [swap_cores(m) for m in mine]
        state = attend(query, segments, plan, mine, other, state, number == len(parts) - 1)
    quant_own = project_own(state, w_out, *bounds[:2])
    return project_out(swap_cores(state), w_other, quant_own, *bounds)


def solution(mesh):
    in_specs = (
        P(("groups", "seq"), None),
        P(),
        P(("groups", "seq")),
        P(None, "tp"),
        P(None, "tp"),
        P("tp", None),
        P(("groups", "seq"), None),
        P(("groups", "seq"), None),
    )
    out_specs = P(("groups", "seq"), None)
    return jax.shard_map(
        functools.partial(on_device, mesh.shape["seq"]),
        mesh=mesh, in_specs=in_specs, out_specs=out_specs, check_vma=False,
    )
```

```python
import functools

import jax
import jax.numpy as jnp
from jax import lax
from jax.experimental import pallas as pl
from jax.experimental.pallas import tpu as pltpu
from jax.sharding import PartitionSpec as P

HD = 256
LANES = 128
SEG_ROWS = 16
LIMIT = 448.0
MIN_EXP = -9
NEG = -1e30
MIB = 1024 * 1024
NT = (((1,), (1,)), ((), ()))
FACTOR = HD ** (-0.5) * 1.4426950408889634


def norm_kv_kernel(x_ref, gain_hbm, w_ref, seg_hbm, next_ref, msg_ref, normed_ref, near_ref, xs, ws, gain_ref, seg_ref, sems):
    rows, width = xs.shape
    tile, part = rows // 2, rows // 4

    def cut(source, target, first, count, pieces, sem):
        size = count // pieces
        return [
            pltpu.make_async_copy(
                source.at[pl.ds(first + i * size, size)], target.at[pl.ds(first + i * size, size)], sems.at[sem + i]
            )
            for i in range(pieces)
        ]

    def early_tokens(half):
        return cut(x_ref, xs, half * part, part, 4, 4 * half)

    def late_tokens():
        return cut(x_ref, xs, tile, tile, 2, 8)

    def weights():
        return cut(w_ref, ws, 0, width, 4, 10)

    def gain_copy():
        return pltpu.make_async_copy(gain_hbm, gain_ref, sems.at[14])

    def segments_copy():
        return pltpu.make_async_copy(seg_hbm, seg_ref, sems.at[15])

    def next_copy():
        return pltpu.make_async_copy(next_ref, near_ref, sems.at[16])

    for copy in early_tokens(0) + early_tokens(1) + [gain_copy()] + weights() + late_tokens() + [segments_copy()]:
        copy.start()

    def wide(first, count, start):
        return xs[first:first + count, start:start + LANES].astype(jnp.float32)

    def stats(first):
        total = wide(first, part, 0)
        for start in range(LANES, width, LANES):
            total = total + wide(first, part, start)
        mean = jnp.broadcast_to(jnp.sum(total, axis=1, keepdims=True) * (1.0 / width), (part, LANES))
        square = jnp.zeros((part, LANES), jnp.float32)
        for start in range(0, width, LANES):
            center = wide(first, part, start) - mean
            square = square + center * center
        spread = jnp.sum(square, axis=1, keepdims=True) * (1.0 / width)
        return mean, jnp.broadcast_to(lax.rsqrt(spread + 1e-05), (part, LANES))

    def project(first, halves):
        mean = jnp.concatenate([h[0] for h in halves], axis=0)
        scale = jnp.concatenate([h[1] for h in halves], axis=0)
        kv = jnp.zeros((tile, ws.shape[1]), jnp.float32)
        span = slice(first, first + tile)
        for start in range(0, width, HD):
            for at in (start, start + LANES):
                normed = (wide(first, tile, at) - mean) * scale * gain_ref[:, at:at + LANES]
                normed_ref[span, at:at + LANES] = normed.astype(jnp.bfloat16)
            kv = kv + jnp.dot(
                normed_ref[span, start:start + HD], ws[start:start + HD, :], preferred_element_type=jnp.float32
            )
        msg_ref[span, :] = kv.astype(jnp.bfloat16)

    halves = []
    for half in range(2):
        for copy in early_tokens(half):
            copy.wait()
        halves.append(stats(half * part))
    for copy in [gain_copy()] + weights():
        copy.wait()
    next_copy().start()
    project(0, halves)
    for copy in late_tokens():
        copy.wait()
    project(tile, [stats(tile), stats(tile + part)])
    segments_copy().wait()
    seg = seg_ref[...].astype(jnp.float32)
    low = jnp.broadcast_to(seg[:, :HD], (8, HD))
    high = jnp.broadcast_to(seg[:, HD:], (8, HD))
    msg_ref[rows:, :] = jnp.concatenate([low, high], axis=0).astype(jnp.bfloat16)
    next_copy().wait()


def in_hbm(x):
    return pltpu.with_memory_space_constraint(x, pltpu.HBM)


def in_vmem(x):
    return pltpu.with_memory_space_constraint(x, pltpu.VMEM)


def norm_kv(tokens, gain, w_keyval, segments, w_next):
    rows, width = tokens.shape
    cols = w_keyval.shape[1]
    vmem, hbm = pl.BlockSpec(memory_space=pltpu.VMEM), pl.BlockSpec(memory_space=pltpu.HBM)
    return pl.pallas_call(
        norm_kv_kernel,
        in_specs=[hbm] * 5,
        out_specs=[vmem] * 3,
        out_shape=[
            pltpu.VMEM((rows + SEG_ROWS, cols), jnp.bfloat16),
            pltpu.VMEM((rows, width), jnp.bfloat16),
            pltpu.VMEM(w_next.shape, w_next.dtype),
        ],
        scratch_shapes=[
            pltpu.VMEM((rows, width), jnp.bfloat16),
            pltpu.VMEM((width, cols), jnp.bfloat16),
            pltpu.VMEM((1, width), jnp.float32),
            pltpu.VMEM((1, rows), jnp.int32),
            pltpu.SemaphoreType.DMA((17,)),
        ],
        compiler_params=pltpu.CompilerParams(vmem_limit_bytes=24 * MIB),
        cost_estimate=pl.CostEstimate(
            flops=2 * rows * width * cols, bytes_accessed=4 * rows * width + 2 * width * cols, transcendentals=0
        ),
        name="norm_kv",
    )(*[in_hbm(x) for x in (tokens, gain.reshape(1, width), w_keyval, segments.reshape(1, rows), w_next)])


def query_kernel(x_ref, w_ref, out_ref):
    out_ref[...] = jnp.dot(x_ref[...], w_ref[...], preferred_element_type=jnp.float32).astype(jnp.bfloat16)


def project_query(normed, w_query):
    rows, width = normed.shape
    cols = w_query.shape[1]
    vmem = pl.BlockSpec(memory_space=pltpu.VMEM)
    return pl.pallas_call(
        query_kernel,
        in_specs=[vmem, vmem],
        out_specs=vmem,
        out_shape=pltpu.VMEM((rows, cols), jnp.bfloat16),
        compiler_params=pltpu.CompilerParams(vmem_limit_bytes=8 * MIB),
        cost_estimate=pl.CostEstimate(
            flops=2 * rows * width * cols, bytes_accessed=2 * rows * width + 2 * width * cols, transcendentals=0
        ),
        name="project_query",
    )(in_vmem(normed), in_vmem(w_query))


def attend_kernel(plan, first, last, *refs):
    blocks = len(plan)
    q_ref, seg_ref = refs[:2]
    mine, other = refs[2:2 + blocks], refs[2 + blocks:2 + 2 * blocks]
    refs = refs[2 + 2 * blocks:]
    state_ref = None
    if not first:
        state_ref, refs = refs[0], refs[1:]
    out_ref, scores = refs
    rows = q_ref.shape[0]
    tile = rows // 2
    part = lax.axis_index("tp")
    place = lax.axis_index("seq")

    def finish(span, weighted, total):
        inverse = jnp.broadcast_to(1.0 / jnp.sum(total, axis=1, keepdims=True), total.shape)
        out_ref[span, :] = (weighted * jnp.concatenate([inverse, inverse], axis=1)).astype(jnp.bfloat16)

    def update(slots, keys, values):
        if first:
            out_ref[:, HD + 2 * LANES:] = jnp.transpose(
                jnp.broadcast_to(seg_ref[...].astype(jnp.float32), (LANES, rows))
            )
        key_segs = {}
        for slot in slots:
            packed = mine[slot][rows:, :].astype(jnp.float32)
            key_segs[slot] = jnp.concatenate([packed[0:1, :], packed[8:9, :]], axis=1)
        for start in range(0, rows, tile):
            span = slice(start, start + tile)
            query = q_ref[span, :]
            own_seg = (out_ref if first else state_ref)[span, HD + 2 * LANES:]
            best = before = None if first else state_ref[span, HD:HD + LANES]
            bounds = {}
            for slot in slots:
                back, furthest = plan[slot]
                low, high = 0, rows
                if back == 0:
                    high = start + tile
                elif furthest:
                    low = start
                bounds[slot] = (low, high)
                raw = lax.dot_general(query, keys[slot][low:high, :], NT, preferred_element_type=jnp.float32)
                for at in range(low, high, LANES):
                    allowed = key_segs[slot][:, at:at + LANES] == own_seg
                    if back == 0:
                        row_pos = start + lax.broadcasted_iota(jnp.int32, allowed.shape, 0)
                        allowed = allowed & (at + lax.broadcasted_iota(jnp.int32, allowed.shape, 1) <= row_pos)
                    piece = jnp.where(allowed, raw[:, at - low:at - low + LANES], NEG)
                    scores[slot, :, at:at + LANES] = piece
                    best = piece if best is None else jnp.maximum(best, piece)
            top = jnp.broadcast_to(jnp.max(best, axis=1, keepdims=True), (tile, LANES))
            if first:
                total = jnp.zeros((tile, LANES), jnp.float32)
                weighted = jnp.zeros((tile, HD), jnp.float32)
            else:
                shrink = jnp.exp2((before - top) * FACTOR)
                total = state_ref[span, HD + LANES:HD + 2 * LANES] * shrink
                weighted = state_ref[span, :HD] * jnp.concatenate([shrink, shrink], axis=1)
            for slot in slots:
                low, high = bounds[slot]
                pieces = []
                for at in range(low, high, LANES):
                    weights = jnp.exp2((scores[slot, :, at:at + LANES] - top) * FACTOR)
                    total = total + weights
                    pieces.append(weights.astype(jnp.bfloat16))
                probs = jnp.concatenate(pieces, axis=1)
                weighted = weighted + jnp.dot(probs, values[slot][low:high, :], preferred_element_type=jnp.float32)
            if last:
                finish(span, weighted, total)
            else:
                out_ref[span, :HD] = weighted
                out_ref[span, HD:HD + LANES] = top
                out_ref[span, HD + LANES:HD + 2 * LANES] = total

    order = sorted(range(blocks), key=lambda slot: plan[slot][0])
    for count in range(1 if first else 0, blocks + 1):
        reached = place >= (plan[order[count - 1]][0] if count > 0 else 0)
        if count < blocks:
            reached = reached & (place < plan[order[count]][0])
        if count > 0:
            pl.when(reached & (part == 0))(functools.partial(update, order[:count], mine, other))
            pl.when(reached & (part == 1))(functools.partial(update, order[:count], other, mine))
        elif last:

            @pl.when(reached)
            def _():
                finish(slice(0, rows), state_ref[:, :HD], state_ref[:, HD + LANES:HD + 2 * LANES])


def attend(query, segments, plan, mine, other, state, last):
    rows = query.shape[0]
    blocks = len(plan)
    vmem = pl.BlockSpec(memory_space=pltpu.VMEM)
    first = state is None
    operands = [query, segments.reshape(1, rows), *mine, *other] + ([] if first else [state])
    return pl.pallas_call(
        functools.partial(attend_kernel, plan, first, last),
        in_specs=[vmem] * len(operands),
        out_specs=vmem,
        out_shape=pltpu.VMEM((rows, HD), jnp.bfloat16) if last else pltpu.VMEM((rows, HD + 3 * LANES), jnp.float32),
        scratch_shapes=[pltpu.VMEM((blocks, rows // 2, rows), jnp.float32)],
        input_output_aliases={} if first or last else {len(operands) - 1: 0},
        compiler_params=pltpu.CompilerParams(vmem_limit_bytes=12 * MIB),
        cost_estimate=pl.CostEstimate(
            flops=4 * rows * rows * blocks * HD, bytes_accessed=4 * rows * blocks * HD, transcendentals=rows * rows * blocks
        ),
        name="attend_last" if last else "attend_first" if first else "attend_more",
    )(*[in_vmem(operand) for operand in operands])


def bounds_kernel(sum_ref, out_exp_ref, x_ref, sum_bound_ref, out_bound_ref, near_ref, sem):
    groups, rows = sum_ref.shape
    fetch = pltpu.make_async_copy(x_ref, near_ref, sem)
    fetch.start()
    per = sum_bound_ref.shape[1] // groups
    for exps, bound_ref in ((sum_ref, sum_bound_ref), (out_exp_ref, out_bound_ref)):
        power = jnp.left_shift(jnp.int32(1), exps[...] - MIN_EXP).astype(jnp.float32)
        bound = jnp.transpose(power * (LIMIT * 2.0 ** MIN_EXP))
        for group in range(groups):
            wide = jnp.broadcast_to(bound[:, group:group + 1], (rows, per)).astype(jnp.bfloat16)
            bound_ref[:, group * per:(group + 1) * per] = wide
    fetch.wait()


def spread_bounds(sum_exps, out_exps, tokens):
    rows, width = tokens.shape
    groups = sum_exps.shape[1]
    vmem = pl.BlockSpec(memory_space=pltpu.VMEM)
    return pl.pallas_call(
        bounds_kernel,
        in_specs=[vmem, vmem, pl.BlockSpec(memory_space=pltpu.HBM)],
        out_specs=[vmem] * 3,
        out_shape=[pltpu.VMEM((rows, width), jnp.bfloat16)] * 3,
        scratch_shapes=[pltpu.SemaphoreType.DMA(())],
        compiler_params=pltpu.CompilerParams(vmem_limit_bytes=10 * MIB),
        cost_estimate=pl.CostEstimate(flops=8 * rows * width, bytes_accessed=8 * rows * groups, transcendentals=0),
        name="spread_bounds",
    )(in_vmem(sum_exps.T), in_vmem(out_exps.T), in_hbm(tokens))


def clip(value, bound):
    return jnp.minimum(jnp.maximum(value.astype(jnp.bfloat16), -bound), bound)


def own_kernel(a_ref, w_ref, sum_ref, out_ref):
    rows, width = out_ref.shape
    tile = rows // 2
    for at in range(0, width, HD):
        cols = slice(at, at + HD)
        for start in range(0, rows, tile):
            span = slice(start, start + tile)
            term = jnp.dot(a_ref[span, :], w_ref[:, cols], preferred_element_type=jnp.float32)
            out_ref[span, cols] = clip(term, sum_ref[span, cols])


def project_own(attended, w_out, sum_bound):
    rows, depth = attended.shape
    width = w_out.shape[1]
    vmem = pl.BlockSpec(memory_space=pltpu.VMEM)
    return pl.pallas_call(
        own_kernel,
        in_specs=[vmem] * 3,
        out_specs=vmem,
        out_shape=pltpu.VMEM((rows, width), jnp.bfloat16),
        compiler_params=pltpu.CompilerParams(vmem_limit_bytes=8 * MIB),
        cost_estimate=pl.CostEstimate(
            flops=2 * rows * width * depth, bytes_accessed=4 * rows * width + 2 * width * depth, transcendentals=0
        ),
        name="project_own",
    )(in_vmem(attended), in_vmem(w_out), in_vmem(sum_bound))


def output_kernel(b_ref, wb_ref, quant_ref, x_ref, sum_ref, last_ref, out_ref, staged, sems):
    rows, width = x_ref.shape
    tile = rows // 2

    def copy(index):
        span = slice(index * HD, (index + 1) * HD)
        return pltpu.make_async_copy(staged.at[:, span], out_ref.at[:, span], sems.at[index])

    for index in range(width // HD):
        cols = slice(index * HD, (index + 1) * HD)
        for start in range(0, rows, tile):
            span = slice(start, start + tile)
            term = jnp.dot(b_ref[span, :], wb_ref[:, cols], preferred_element_type=jnp.float32)
            quant = clip(term, sum_ref[span, cols]).astype(jnp.float32) + quant_ref[span, cols].astype(jnp.float32)
            staged[span, cols] = clip(x_ref[span, cols].astype(jnp.float32) + quant, last_ref[span, cols])
        copy(index).start()
    for index in range(width // HD):
        copy(index).wait()


def project_out(att_other, w_other, quant_own, sum_bound, out_bound, tokens):
    rows, width = tokens.shape
    depth = att_other.shape[1]
    pieces = width // HD
    vmem = pl.BlockSpec(memory_space=pltpu.VMEM)
    operands = [att_other, w_other, quant_own, tokens, sum_bound, out_bound]
    return pl.pallas_call(
        output_kernel,
        in_specs=[vmem] * len(operands),
        out_specs=pl.BlockSpec(memory_space=pltpu.HBM),
        out_shape=jax.ShapeDtypeStruct((rows, width), jnp.bfloat16),
        scratch_shapes=[pltpu.VMEM((rows, width), jnp.bfloat16), pltpu.SemaphoreType.DMA((pieces,))],
        compiler_params=pltpu.CompilerParams(vmem_limit_bytes=10 * MIB),
        cost_estimate=pl.CostEstimate(
            flops=2 * rows * width * depth, bytes_accessed=4 * rows * width + 2 * width * depth, transcendentals=0
        ),
        name="project_out",
    )(*[in_vmem(operand) for operand in operands])


def on_device(seq_size, tokens, gain, segments, w_query, w_keyval, w_out, sum_exps, out_exps):
    window = seq_size // 2

    def swap_cores(x):
        return lax.ppermute(x, "tp", [(0, 1), (1, 0)])

    def shift(x, step, first):
        cycle = seq_size - first
        pairs = []
        for i in range(seq_size):
            for core in range(2):
                after = 2 * (first + (i - first + step) % cycle) + core if i >= first else 2 * i + 1 - core
                pairs.append((2 * i + core, after))
        return lax.ppermute(x, ("seq", "tp"), pairs)

    w_other = swap_cores(w_out)
    message, normed, w_near = norm_kv(tokens, gain, w_keyval, segments, w_query)
    query = project_query(normed, w_near)
    held, query = lax.optimization_barrier((shift(message, 2, 0), query))
    odd = lax.rem(lax.axis_index("seq"), 2) == 1
    beside = lax.ppermute(jnp.where(odd, held, message), "seq", [(i, i ^ 1) for i in range(seq_size)])
    parts = [[(0, message), (2, held)]]
    for back in range(2, window, 2):
        step = shift(held, 1, back)
        held = shift(held, 2, back)
        parts.append([(back + 1, step)] + ([(back + 2, held)] if back + 2 < window else []))
    parts.append([(window, held), (1, beside)])
    exps = lax.optimization_barrier((sum_exps, out_exps, query))[:2]
    bounds = spread_bounds(*exps, tokens)
    state = None
    for number, blocks in enumerate(parts):
        plan = [(back, back == window) for back, _ in blocks]
        mine = [block for _, block in blocks]
        if number == 1:
            bounds, state = early = lax.optimization_barrier((bounds, state))
        if number > 0:
            mine = [lax.optimization_barrier((block, early))[0] for block in mine]
        other = [swap_cores(m) for m in mine]
        state = attend(query, segments, plan, mine, other, state, number == len(parts) - 1)
    quant_own = project_own(state, w_out, bounds[0])
    return project_out(swap_cores(state), w_other, quant_own, *bounds)


def solution(mesh):
    in_specs = (
        P(("groups", "seq"), None),
        P(),
        P(("groups", "seq")),
        P(None, "tp"),
        P(None, "tp"),
        P("tp", None),
        P(("groups", "seq"), None),
        P(("groups", "seq"), None),
    )
    out_specs = P(("groups", "seq"), None)
    return jax.shard_map(
        functools.partial(on_device, mesh.shape["seq"]),
        mesh=mesh, in_specs=in_specs, out_specs=out_specs, check_vma=False,
    )
```

```python
import functools

import jax
import jax.numpy as jnp
from jax import lax
from jax.experimental import pallas as pl
from jax.experimental.pallas import tpu as pltpu
from jax.sharding import PartitionSpec as P

HD = 256
LANES = 128
SEG_ROWS = 16
LIMIT = 448.0
MIN_EXP = -9
NEG = -1e30
MIB = 1024 * 1024
NT = (((1,), (1,)), ((), ()))
FACTOR = HD ** (-0.5) * 1.4426950408889634


def norm_kv_kernel(x_ref, gain_hbm, w_ref, seg_hbm, next_ref, msg_ref, normed_ref, near_ref, xs, ws, gain_ref, seg_ref, sems):
    rows, width = xs.shape
    tile, part = rows // 2, rows // 4

    def cut(source, target, first, count, pieces, sem):
        size = count // pieces
        return [
            pltpu.make_async_copy(
                source.at[pl.ds(first + i * size, size)], target.at[pl.ds(first + i * size, size)], sems.at[sem + i]
            )
            for i in range(pieces)
        ]

    def early_tokens(half):
        return cut(x_ref, xs, half * part, part, 4, 4 * half)

    def late_tokens():
        return cut(x_ref, xs, tile, tile, 2, 8)

    def weights():
        return cut(w_ref, ws, 0, width, 4, 10)

    def gain_copy():
        return pltpu.make_async_copy(gain_hbm, gain_ref, sems.at[14])

    def segments_copy():
        return pltpu.make_async_copy(seg_hbm, seg_ref, sems.at[15])

    def next_copy():
        return pltpu.make_async_copy(next_ref, near_ref, sems.at[16])

    for copy in early_tokens(0) + early_tokens(1) + [gain_copy()] + weights() + late_tokens() + [segments_copy()]:
        copy.start()

    def wide(first, count, start):
        return xs[first:first + count, start:start + LANES].astype(jnp.float32)

    def stats(first):
        total = wide(first, part, 0)
        for start in range(LANES, width, LANES):
            total = total + wide(first, part, start)
        mean = jnp.broadcast_to(jnp.sum(total, axis=1, keepdims=True) * (1.0 / width), (part, LANES))
        square = jnp.zeros((part, LANES), jnp.float32)
        for start in range(0, width, LANES):
            center = wide(first, part, start) - mean
            square = square + center * center
        spread = jnp.sum(square, axis=1, keepdims=True) * (1.0 / width)
        return mean, jnp.broadcast_to(lax.rsqrt(spread + 1e-05), (part, LANES))

    def project(first, halves):
        mean = jnp.concatenate([h[0] for h in halves], axis=0)
        scale = jnp.concatenate([h[1] for h in halves], axis=0)
        kv = jnp.zeros((tile, ws.shape[1]), jnp.float32)
        span = slice(first, first + tile)
        for start in range(0, width, HD):
            for at in (start, start + LANES):
                normed = (wide(first, tile, at) - mean) * scale * gain_ref[:, at:at + LANES]
                normed_ref[span, at:at + LANES] = normed.astype(jnp.bfloat16)
            kv = kv + jnp.dot(
                normed_ref[span, start:start + HD], ws[start:start + HD, :], preferred_element_type=jnp.float32
            )
        msg_ref[span, :] = kv.astype(jnp.bfloat16)

    halves = []
    for half in range(2):
        for copy in early_tokens(half):
            copy.wait()
        halves.append(stats(half * part))
    for copy in [gain_copy()] + weights():
        copy.wait()
    next_copy().start()
    project(0, halves)
    for copy in late_tokens():
        copy.wait()
    project(tile, [stats(tile), stats(tile + part)])
    segments_copy().wait()
    seg = seg_ref[...].astype(jnp.float32)
    low = jnp.broadcast_to(seg[:, :HD], (8, HD))
    high = jnp.broadcast_to(seg[:, HD:], (8, HD))
    msg_ref[rows:, :] = jnp.concatenate([low, high], axis=0).astype(jnp.bfloat16)
    next_copy().wait()


def in_hbm(x):
    return pltpu.with_memory_space_constraint(x, pltpu.HBM)


def in_vmem(x):
    return pltpu.with_memory_space_constraint(x, pltpu.VMEM)


def norm_kv(tokens, gain, w_keyval, segments, w_next):
    rows, width = tokens.shape
    cols = w_keyval.shape[1]
    vmem, hbm = pl.BlockSpec(memory_space=pltpu.VMEM), pl.BlockSpec(memory_space=pltpu.HBM)
    return pl.pallas_call(
        norm_kv_kernel,
        in_specs=[hbm] * 5,
        out_specs=[vmem] * 3,
        out_shape=[
            pltpu.VMEM((rows + SEG_ROWS, cols), jnp.bfloat16),
            pltpu.VMEM((rows, width), jnp.bfloat16),
            pltpu.VMEM(w_next.shape, w_next.dtype),
        ],
        scratch_shapes=[
            pltpu.VMEM((rows, width), jnp.bfloat16),
            pltpu.VMEM((width, cols), jnp.bfloat16),
            pltpu.VMEM((1, width), jnp.float32),
            pltpu.VMEM((1, rows), jnp.int32),
            pltpu.SemaphoreType.DMA((17,)),
        ],
        compiler_params=pltpu.CompilerParams(vmem_limit_bytes=24 * MIB),
        cost_estimate=pl.CostEstimate(
            flops=2 * rows * width * cols, bytes_accessed=4 * rows * width + 2 * width * cols, transcendentals=0
        ),
        name="norm_kv",
    )(*[in_hbm(x) for x in (tokens, gain.reshape(1, width), w_keyval, segments.reshape(1, rows), w_next)])


def query_kernel(x_ref, w_ref, out_ref):
    out_ref[...] = jnp.dot(x_ref[...], w_ref[...], preferred_element_type=jnp.float32).astype(jnp.bfloat16)


def project_query(normed, w_query):
    rows, width = normed.shape
    cols = w_query.shape[1]
    vmem = pl.BlockSpec(memory_space=pltpu.VMEM)
    return pl.pallas_call(
        query_kernel,
        in_specs=[vmem, vmem],
        out_specs=vmem,
        out_shape=pltpu.VMEM((rows, cols), jnp.bfloat16),
        compiler_params=pltpu.CompilerParams(vmem_limit_bytes=8 * MIB),
        cost_estimate=pl.CostEstimate(
            flops=2 * rows * width * cols, bytes_accessed=2 * rows * width + 2 * width * cols, transcendentals=0
        ),
        name="project_query",
    )(in_vmem(normed), in_vmem(w_query))


def attend_kernel(plan, first, last, *refs):
    blocks = len(plan)
    q_ref, seg_ref = refs[:2]
    mine, other = refs[2:2 + blocks], refs[2 + blocks:2 + 2 * blocks]
    refs = refs[2 + 2 * blocks:]
    state_ref = None
    if not first:
        state_ref, refs = refs[0], refs[1:]
    out_ref, scores = refs
    rows = q_ref.shape[0]
    tile = rows // 2
    part = lax.axis_index("tp")
    place = lax.axis_index("seq")

    def finish(span, weighted, total):
        inverse = jnp.broadcast_to(1.0 / jnp.sum(total, axis=1, keepdims=True), total.shape)
        out_ref[span, :] = (weighted * jnp.concatenate([inverse, inverse], axis=1)).astype(jnp.bfloat16)

    def update(slots, keys, values):
        if first:
            out_ref[:, HD + 2 * LANES:] = jnp.transpose(
                jnp.broadcast_to(seg_ref[...].astype(jnp.float32), (LANES, rows))
            )
        key_segs = {}
        for slot in slots:
            packed = mine[slot][rows:, :].astype(jnp.float32)
            key_segs[slot] = jnp.concatenate([packed[0:1, :], packed[8:9, :]], axis=1)
        for start in range(0, rows, tile):
            span = slice(start, start + tile)
            query = q_ref[span, :]
            own_seg = (out_ref if first else state_ref)[span, HD + 2 * LANES:]
            best = before = None if first else state_ref[span, HD:HD + LANES]
            bounds = {}
            for slot in slots:
                back, furthest = plan[slot]
                low, high = 0, rows
                if back == 0:
                    high = start + tile
                elif furthest:
                    low = start
                bounds[slot] = (low, high)
                raw = lax.dot_general(query, keys[slot][low:high, :], NT, preferred_element_type=jnp.float32)
                for at in range(low, high, LANES):
                    allowed = key_segs[slot][:, at:at + LANES] == own_seg
                    if back == 0:
                        row_pos = start + lax.broadcasted_iota(jnp.int32, allowed.shape, 0)
                        allowed = allowed & (at + lax.broadcasted_iota(jnp.int32, allowed.shape, 1) <= row_pos)
                    piece = jnp.where(allowed, raw[:, at - low:at - low + LANES], NEG)
                    scores[slot, :, at:at + LANES] = piece
                    best = piece if best is None else jnp.maximum(best, piece)
            top = jnp.broadcast_to(jnp.max(best, axis=1, keepdims=True), (tile, LANES))
            if first:
                total = jnp.zeros((tile, LANES), jnp.float32)
                weighted = jnp.zeros((tile, HD), jnp.float32)
            else:
                shrink = jnp.exp2((before - top) * FACTOR)
                total = state_ref[span, HD + LANES:HD + 2 * LANES] * shrink
                weighted = state_ref[span, :HD] * jnp.concatenate([shrink, shrink], axis=1)
            for slot in slots:
                low, high = bounds[slot]
                pieces = []
                for at in range(low, high, LANES):
                    weights = jnp.exp2((scores[slot, :, at:at + LANES] - top) * FACTOR)
                    total = total + weights
                    pieces.append(weights.astype(jnp.bfloat16))
                probs = jnp.concatenate(pieces, axis=1)
                weighted = weighted + jnp.dot(probs, values[slot][low:high, :], preferred_element_type=jnp.float32)
            if last:
                finish(span, weighted, total)
            else:
                out_ref[span, :HD] = weighted
                out_ref[span, HD:HD + LANES] = top
                out_ref[span, HD + LANES:HD + 2 * LANES] = total

    order = sorted(range(blocks), key=lambda slot: plan[slot][0])
    for count in range(1 if first else 0, blocks + 1):
        reached = place >= (plan[order[count - 1]][0] if count > 0 else 0)
        if count < blocks:
            reached = reached & (place < plan[order[count]][0])
        if count > 0:
            pl.when(reached & (part == 0))(functools.partial(update, order[:count], mine, other))
            pl.when(reached & (part == 1))(functools.partial(update, order[:count], other, mine))
        elif last:

            @pl.when(reached)
            def _():
                finish(slice(0, rows), state_ref[:, :HD], state_ref[:, HD + LANES:HD + 2 * LANES])


def attend(query, segments, plan, mine, other, state, last):
    rows = query.shape[0]
    blocks = len(plan)
    vmem = pl.BlockSpec(memory_space=pltpu.VMEM)
    first = state is None
    operands = [query, segments.reshape(1, rows), *mine, *other] + ([] if first else [state])
    return pl.pallas_call(
        functools.partial(attend_kernel, plan, first, last),
        in_specs=[vmem] * len(operands),
        out_specs=vmem,
        out_shape=pltpu.VMEM((rows, HD), jnp.bfloat16) if last else pltpu.VMEM((rows, HD + 3 * LANES), jnp.float32),
        scratch_shapes=[pltpu.VMEM((blocks, rows // 2, rows), jnp.float32)],
        input_output_aliases={} if first or last else {len(operands) - 1: 0},
        compiler_params=pltpu.CompilerParams(vmem_limit_bytes=12 * MIB),
        cost_estimate=pl.CostEstimate(
            flops=4 * rows * rows * blocks * HD, bytes_accessed=4 * rows * blocks * HD, transcendentals=rows * rows * blocks
        ),
        name="attend_last" if last else "attend_first" if first else "attend_more",
    )(*[in_vmem(operand) for operand in operands])


def bounds_kernel(sum_ref, out_exp_ref, x_ref, sum_bound_ref, out_bound_ref, wide_ref, near, sem):
    groups, rows = sum_ref.shape
    fetch = pltpu.make_async_copy(x_ref, near, sem)
    fetch.start()
    per = sum_bound_ref.shape[1] // groups
    for exps, bound_ref in ((sum_ref, sum_bound_ref), (out_exp_ref, out_bound_ref)):
        power = jnp.left_shift(jnp.int32(1), exps[...] - MIN_EXP).astype(jnp.float32)
        bound = jnp.transpose(power * (LIMIT * 2.0 ** MIN_EXP))
        for group in range(groups):
            wide = jnp.broadcast_to(bound[:, group:group + 1], (rows, per)).astype(jnp.bfloat16)
            bound_ref[:, group * per:(group + 1) * per] = wide
    fetch.wait()

    def widen(step, carry):
        span = pl.ds(pl.multiple_of(step * 64, 64), 64)
        wide_ref[span, :] = near[span, :].astype(jnp.float32)
        return carry

    lax.fori_loop(0, rows // 64, widen, 0)


def spread_bounds(sum_exps, out_exps, tokens):
    rows, width = tokens.shape
    groups = sum_exps.shape[1]
    vmem = pl.BlockSpec(memory_space=pltpu.VMEM)
    return pl.pallas_call(
        bounds_kernel,
        in_specs=[vmem, vmem, pl.BlockSpec(memory_space=pltpu.HBM)],
        out_specs=[vmem] * 3,
        out_shape=[pltpu.VMEM((rows, width), jnp.bfloat16)] * 2 + [pltpu.VMEM((rows, width), jnp.float32)],
        scratch_shapes=[pltpu.VMEM((rows, width), jnp.bfloat16), pltpu.SemaphoreType.DMA(())],
        compiler_params=pltpu.CompilerParams(vmem_limit_bytes=10 * MIB),
        cost_estimate=pl.CostEstimate(flops=8 * rows * width, bytes_accessed=8 * rows * groups, transcendentals=0),
        name="spread_bounds",
    )(in_vmem(sum_exps.T), in_vmem(out_exps.T), in_hbm(tokens))


def clip(value, bound):
    return jnp.minimum(jnp.maximum(value.astype(jnp.bfloat16), -bound), bound)


def own_kernel(a_ref, w_ref, sum_ref, out_ref):
    rows, width = out_ref.shape
    tile = rows // 2
    for at in range(0, width, HD):
        cols = slice(at, at + HD)
        for start in range(0, rows, tile):
            span = slice(start, start + tile)
            term = jnp.dot(a_ref[span, :], w_ref[:, cols], preferred_element_type=jnp.float32)
            out_ref[span, cols] = clip(term, sum_ref[span, cols])


def project_own(attended, w_out, sum_bound):
    rows, depth = attended.shape
    width = w_out.shape[1]
    vmem = pl.BlockSpec(memory_space=pltpu.VMEM)
    return pl.pallas_call(
        own_kernel,
        in_specs=[vmem] * 3,
        out_specs=vmem,
        out_shape=pltpu.VMEM((rows, width), jnp.bfloat16),
        compiler_params=pltpu.CompilerParams(vmem_limit_bytes=8 * MIB),
        cost_estimate=pl.CostEstimate(
            flops=2 * rows * width * depth, bytes_accessed=4 * rows * width + 2 * width * depth, transcendentals=0
        ),
        name="project_own",
    )(in_vmem(attended), in_vmem(w_out), in_vmem(sum_bound))


def output_kernel(b_ref, wb_ref, quant_ref, x_ref, sum_ref, last_ref, out_ref, staged, sems):
    rows, width = x_ref.shape
    tile = rows // 2

    def copy(index):
        span = slice(index * HD, (index + 1) * HD)
        return pltpu.make_async_copy(staged.at[:, span], out_ref.at[:, span], sems.at[index])

    for index in range(width // HD):
        cols = slice(index * HD, (index + 1) * HD)
        for start in range(0, rows, tile):
            span = slice(start, start + tile)
            term = jnp.dot(b_ref[span, :], wb_ref[:, cols], preferred_element_type=jnp.float32)
            quant = clip(term, sum_ref[span, cols]).astype(jnp.float32) + quant_ref[span, cols].astype(jnp.float32)
            staged[span, cols] = clip(x_ref[span, cols] + quant, last_ref[span, cols])
        copy(index).start()
    for index in range(width // HD):
        copy(index).wait()


def project_out(att_other, w_other, quant_own, sum_bound, out_bound, tokens):
    rows, width = tokens.shape
    depth = att_other.shape[1]
    pieces = width // HD
    vmem = pl.BlockSpec(memory_space=pltpu.VMEM)
    operands = [att_other, w_other, quant_own, tokens, sum_bound, out_bound]
    return pl.pallas_call(
        output_kernel,
        in_specs=[vmem] * len(operands),
        out_specs=pl.BlockSpec(memory_space=pltpu.HBM),
        out_shape=jax.ShapeDtypeStruct((rows, width), jnp.bfloat16),
        scratch_shapes=[pltpu.VMEM((rows, width), jnp.bfloat16), pltpu.SemaphoreType.DMA((pieces,))],
        compiler_params=pltpu.CompilerParams(vmem_limit_bytes=10 * MIB),
        cost_estimate=pl.CostEstimate(
            flops=2 * rows * width * depth, bytes_accessed=4 * rows * width + 2 * width * depth, transcendentals=0
        ),
        name="project_out",
    )(*[in_vmem(operand) for operand in operands])


def on_device(seq_size, tokens, gain, segments, w_query, w_keyval, w_out, sum_exps, out_exps):
    window = seq_size // 2

    def swap_cores(x):
        return lax.ppermute(x, "tp", [(0, 1), (1, 0)])

    def shift(x, step, first):
        cycle = seq_size - first
        pairs = []
        for i in range(seq_size):
            for core in range(2):
                after = 2 * (first + (i - first + step) % cycle) + core if i >= first else 2 * i + 1 - core
                pairs.append((2 * i + core, after))
        return lax.ppermute(x, ("seq", "tp"), pairs)

    w_other = swap_cores(w_out)
    message, normed, w_near = norm_kv(tokens, gain, w_keyval, segments, w_query)
    query = project_query(normed, w_near)
    held, query = lax.optimization_barrier((shift(message, 2, 0), query))
    odd = lax.rem(lax.axis_index("seq"), 2) == 1
    beside = lax.ppermute(jnp.where(odd, held, message), "seq", [(i, i ^ 1) for i in range(seq_size)])
    parts = [[(0, message), (2, held)]]
    for back in range(2, window, 2):
        step = shift(held, 1, back)
        held = shift(held, 2, back)
        parts.append([(back + 1, step)] + ([(back + 2, held)] if back + 2 < window else []))
    parts.append([(window, held), (1, beside)])
    exps = lax.optimization_barrier((sum_exps, out_exps, query))[:2]
    bounds = spread_bounds(*exps, tokens)
    state = None
    for number, blocks in enumerate(parts):
        plan = [(back, back == window) for back, _ in blocks]
        mine = [block for _, block in blocks]
        if number == 1:
            bounds, state = early = lax.optimization_barrier((bounds, state))
        if number > 0:
            mine = [lax.optimization_barrier((block, early))[0] for block in mine]
        other = [swap_cores(m) for m in mine]
        state = attend(query, segments, plan, mine, other, state, number == len(parts) - 1)
    quant_own = project_own(state, w_out, bounds[0])
    return project_out(swap_cores(state), w_other, quant_own, *bounds)


def solution(mesh):
    in_specs = (
        P(("groups", "seq"), None),
        P(),
        P(("groups", "seq")),
        P(None, "tp"),
        P(None, "tp"),
        P("tp", None),
        P(("groups", "seq"), None),
        P(("groups", "seq"), None),
    )
    out_specs = P(("groups", "seq"), None)
    return jax.shard_map(
        functools.partial(on_device, mesh.shape["seq"]),
        mesh=mesh, in_specs=in_specs, out_specs=out_specs, check_vma=False,
    )
```

```python
import functools

import jax
import jax.numpy as jnp
from jax import lax
from jax.experimental import pallas as pl
from jax.experimental.pallas import tpu as pltpu
from jax.sharding import PartitionSpec as P

HD = 256
LANES = 128
SEG_ROWS = 16
LIMIT = 448.0
MIN_EXP = -9
NEG = -1e30
MIB = 1024 * 1024
NT = (((1,), (1,)), ((), ()))
FACTOR = HD ** (-0.5) * 1.4426950408889634


def norm_kv_kernel(x_ref, gain_hbm, w_ref, seg_hbm, next_ref, msg_ref, normed_ref, near_ref, xs, ws, gain_ref, seg_ref, sems):
    rows, width = xs.shape
    tile, part = rows // 2, rows // 4

    def cut(source, target, first, count, pieces, sem):
        size = count // pieces
        return [
            pltpu.make_async_copy(
                source.at[pl.ds(first + i * size, size)], target.at[pl.ds(first + i * size, size)], sems.at[sem + i]
            )
            for i in range(pieces)
        ]

    def early_tokens(half):
        return cut(x_ref, xs, half * part, part, 4, 4 * half)

    def late_tokens():
        return cut(x_ref, xs, tile, tile, 2, 8)

    def weights():
        return cut(w_ref, ws, 0, width, 4, 10)

    def gain_copy():
        return pltpu.make_async_copy(gain_hbm, gain_ref, sems.at[14])

    def segments_copy():
        return pltpu.make_async_copy(seg_hbm, seg_ref, sems.at[15])

    def next_copy():
        return pltpu.make_async_copy(next_ref, near_ref, sems.at[16])

    for copy in early_tokens(0) + early_tokens(1) + [gain_copy()] + weights() + late_tokens() + [segments_copy()]:
        copy.start()

    def wide(first, count, start):
        return xs[first:first + count, start:start + LANES].astype(jnp.float32)

    def stats(first):
        total = wide(first, part, 0)
        for start in range(LANES, width, LANES):
            total = total + wide(first, part, start)
        mean = jnp.broadcast_to(jnp.sum(total, axis=1, keepdims=True) * (1.0 / width), (part, LANES))
        square = jnp.zeros((part, LANES), jnp.float32)
        for start in range(0, width, LANES):
            center = wide(first, part, start) - mean
            square = square + center * center
        spread = jnp.sum(square, axis=1, keepdims=True) * (1.0 / width)
        return mean, jnp.broadcast_to(lax.rsqrt(spread + 1e-05), (part, LANES))

    def project(first, halves):
        mean = jnp.concatenate([h[0] for h in halves], axis=0)
        scale = jnp.concatenate([h[1] for h in halves], axis=0)
        kv = jnp.zeros((tile, ws.shape[1]), jnp.float32)
        span = slice(first, first + tile)
        for start in range(0, width, HD):
            for at in (start, start + LANES):
                normed = (wide(first, tile, at) - mean) * scale * gain_ref[:, at:at + LANES]
                normed_ref[span, at:at + LANES] = normed.astype(jnp.bfloat16)
            kv = kv + jnp.dot(
                normed_ref[span, start:start + HD], ws[start:start + HD, :], preferred_element_type=jnp.float32
            )
        msg_ref[span, :] = kv.astype(jnp.bfloat16)

    halves = []
    for half in range(2):
        for copy in early_tokens(half):
            copy.wait()
        halves.append(stats(half * part))
    for copy in [gain_copy()] + weights():
        copy.wait()
    next_copy().start()
    project(0, halves)
    for copy in late_tokens():
        copy.wait()
    project(tile, [stats(tile), stats(tile + part)])
    segments_copy().wait()
    seg = seg_ref[...].astype(jnp.float32)
    low = jnp.broadcast_to(seg[:, :HD], (8, HD))
    high = jnp.broadcast_to(seg[:, HD:], (8, HD))
    msg_ref[rows:, :] = jnp.concatenate([low, high], axis=0).astype(jnp.bfloat16)
    next_copy().wait()


def in_hbm(x):
    return pltpu.with_memory_space_constraint(x, pltpu.HBM)


def in_vmem(x):
    return pltpu.with_memory_space_constraint(x, pltpu.VMEM)


def norm_kv(tokens, gain, w_keyval, segments, w_next):
    rows, width = tokens.shape
    cols = w_keyval.shape[1]
    vmem, hbm = pl.BlockSpec(memory_space=pltpu.VMEM), pl.BlockSpec(memory_space=pltpu.HBM)
    return pl.pallas_call(
        norm_kv_kernel,
        in_specs=[hbm] * 5,
        out_specs=[vmem] * 3,
        out_shape=[
            pltpu.VMEM((rows + SEG_ROWS, cols), jnp.bfloat16),
            pltpu.VMEM((rows, width), jnp.bfloat16),
            pltpu.VMEM(w_next.shape, w_next.dtype),
        ],
        scratch_shapes=[
            pltpu.VMEM((rows, width), jnp.bfloat16),
            pltpu.VMEM((width, cols), jnp.bfloat16),
            pltpu.VMEM((1, width), jnp.float32),
            pltpu.VMEM((1, rows), jnp.int32),
            pltpu.SemaphoreType.DMA((17,)),
        ],
        compiler_params=pltpu.CompilerParams(vmem_limit_bytes=24 * MIB),
        cost_estimate=pl.CostEstimate(
            flops=2 * rows * width * cols, bytes_accessed=4 * rows * width + 2 * width * cols, transcendentals=0
        ),
        name="norm_kv",
    )(*[in_hbm(x) for x in (tokens, gain.reshape(1, width), w_keyval, segments.reshape(1, rows), w_next)])


def query_kernel(x_ref, w_ref, out_ref):
    out_ref[...] = jnp.dot(x_ref[...], w_ref[...], preferred_element_type=jnp.float32).astype(jnp.bfloat16)


def project_query(normed, w_query):
    rows, width = normed.shape
    cols = w_query.shape[1]
    vmem = pl.BlockSpec(memory_space=pltpu.VMEM)
    return pl.pallas_call(
        query_kernel,
        in_specs=[vmem, vmem],
        out_specs=vmem,
        out_shape=pltpu.VMEM((rows, cols), jnp.bfloat16),
        compiler_params=pltpu.CompilerParams(vmem_limit_bytes=8 * MIB),
        cost_estimate=pl.CostEstimate(
            flops=2 * rows * width * cols, bytes_accessed=2 * rows * width + 2 * width * cols, transcendentals=0
        ),
        name="project_query",
    )(in_vmem(normed), in_vmem(w_query))


def attend_kernel(plan, first, last, *refs):
    blocks = len(plan)
    q_ref, seg_ref = refs[:2]
    mine, other = refs[2:2 + blocks], refs[2 + blocks:2 + 2 * blocks]
    refs = refs[2 + 2 * blocks:]
    state_ref = None
    if not first:
        state_ref, refs = refs[0], refs[1:]
    out_ref, scores = refs
    rows = q_ref.shape[0]
    tile = rows // 2
    part = lax.axis_index("tp")
    place = lax.axis_index("seq")

    def finish(span, weighted, total):
        inverse = jnp.broadcast_to(1.0 / jnp.sum(total, axis=1, keepdims=True), total.shape)
        out_ref[span, :] = (weighted * jnp.concatenate([inverse, inverse], axis=1)).astype(jnp.bfloat16)

    def update(slots, keys, values):
        if first:
            out_ref[:, HD + 2 * LANES:] = jnp.transpose(
                jnp.broadcast_to(seg_ref[...].astype(jnp.float32), (LANES, rows))
            )
        key_segs = {}
        for slot in slots:
            packed = mine[slot][rows:, :].astype(jnp.float32)
            key_segs[slot] = jnp.concatenate([packed[0:1, :], packed[8:9, :]], axis=1)
        for start in range(0, rows, tile):
            span = slice(start, start + tile)
            query = q_ref[span, :]
            own_seg = (out_ref if first else state_ref)[span, HD + 2 * LANES:]
            best = before = None if first else state_ref[span, HD:HD + LANES]
            bounds = {}
            for slot in slots:
                back, furthest = plan[slot]
                low, high = 0, rows
                if back == 0:
                    high = start + tile
                elif furthest:
                    low = start
                bounds[slot] = (low, high)
                raw = lax.dot_general(query, keys[slot][low:high, :], NT, preferred_element_type=jnp.float32)
                for at in range(low, high, LANES):
                    allowed = key_segs[slot][:, at:at + LANES] == own_seg
                    if back == 0:
                        row_pos = start + lax.broadcasted_iota(jnp.int32, allowed.shape, 0)
                        allowed = allowed & (at + lax.broadcasted_iota(jnp.int32, allowed.shape, 1) <= row_pos)
                    piece = jnp.where(allowed, raw[:, at - low:at - low + LANES], NEG)
                    scores[slot, :, at:at + LANES] = piece
                    best = piece if best is None else jnp.maximum(best, piece)
            top = jnp.broadcast_to(jnp.max(best, axis=1, keepdims=True), (tile, LANES))
            if first:
                total = jnp.zeros((tile, LANES), jnp.float32)
                weighted = jnp.zeros((tile, HD), jnp.float32)
            else:
                shrink = jnp.exp2((before - top) * FACTOR)
                total = state_ref[span, HD + LANES:HD + 2 * LANES] * shrink
                weighted = state_ref[span, :HD] * jnp.concatenate([shrink, shrink], axis=1)
            for slot in slots:
                low, high = bounds[slot]
                pieces = []
                for at in range(low, high, LANES):
                    weights = jnp.exp2((scores[slot, :, at:at + LANES] - top) * FACTOR)
                    total = total + weights
                    pieces.append(weights.astype(jnp.bfloat16))
                probs = jnp.concatenate(pieces, axis=1)
                weighted = weighted + jnp.dot(probs, values[slot][low:high, :], preferred_element_type=jnp.float32)
            if last:
                finish(span, weighted, total)
            else:
                out_ref[span, :HD] = weighted
                out_ref[span, HD:HD + LANES] = top
                out_ref[span, HD + LANES:HD + 2 * LANES] = total

    order = sorted(range(blocks), key=lambda slot: plan[slot][0])
    for count in range(1 if first else 0, blocks + 1):
        reached = place >= (plan[order[count - 1]][0] if count > 0 else 0)
        if count < blocks:
            reached = reached & (place < plan[order[count]][0])
        if count > 0:
            pl.when(reached & (part == 0))(functools.partial(update, order[:count], mine, other))
            pl.when(reached & (part == 1))(functools.partial(update, order[:count], other, mine))
        elif last:

            @pl.when(reached)
            def _():
                finish(slice(0, rows), state_ref[:, :HD], state_ref[:, HD + LANES:HD + 2 * LANES])


def attend(query, segments, plan, mine, other, state, last):
    rows = query.shape[0]
    blocks = len(plan)
    vmem = pl.BlockSpec(memory_space=pltpu.VMEM)
    first = state is None
    operands = [query, segments.reshape(1, rows), *mine, *other] + ([] if first else [state])
    return pl.pallas_call(
        functools.partial(attend_kernel, plan, first, last),
        in_specs=[vmem] * len(operands),
        out_specs=vmem,
        out_shape=pltpu.VMEM((rows, HD), jnp.bfloat16) if last else pltpu.VMEM((rows, HD + 3 * LANES), jnp.float32),
        scratch_shapes=[pltpu.VMEM((blocks, rows // 2, rows), jnp.float32)],
        input_output_aliases={} if first or last else {len(operands) - 1: 0},
        compiler_params=pltpu.CompilerParams(vmem_limit_bytes=12 * MIB),
        cost_estimate=pl.CostEstimate(
            flops=4 * rows * rows * blocks * HD, bytes_accessed=4 * rows * blocks * HD, transcendentals=rows * rows * blocks
        ),
        name="attend_last" if last else "attend_first" if first else "attend_more",
    )(*[in_vmem(operand) for operand in operands])


def bounds_kernel(sum_ref, out_exp_ref, x_ref, sum_bound_ref, out_bound_ref, wide_ref, near, sem):
    groups, rows = sum_ref.shape
    fetch = pltpu.make_async_copy(x_ref, near, sem)
    fetch.start()
    per = sum_bound_ref.shape[1] // groups
    for exps, bound_ref in ((sum_ref, sum_bound_ref), (out_exp_ref, out_bound_ref)):
        power = jnp.left_shift(jnp.int32(1), exps[...] - MIN_EXP).astype(jnp.float32)
        bound = jnp.transpose(power * (LIMIT * 2.0 ** MIN_EXP))
        for group in range(groups):
            wide = jnp.broadcast_to(bound[:, group:group + 1], (rows, per)).astype(jnp.bfloat16)
            bound_ref[:, group * per:(group + 1) * per] = wide
    fetch.wait()

    def widen(step, carry):
        span = pl.ds(pl.multiple_of(step * 64, 64), 64)
        wide_ref[span, :] = near[span, :].astype(jnp.float32)
        return carry

    lax.fori_loop(0, rows // 64, widen, 0)


def spread_bounds(sum_exps, out_exps, tokens):
    rows, width = tokens.shape
    groups = sum_exps.shape[1]
    vmem = pl.BlockSpec(memory_space=pltpu.VMEM)
    return pl.pallas_call(
        bounds_kernel,
        in_specs=[vmem, vmem, pl.BlockSpec(memory_space=pltpu.HBM)],
        out_specs=[vmem] * 3,
        out_shape=[pltpu.VMEM((rows, width), jnp.bfloat16)] * 2 + [pltpu.VMEM((rows, width), jnp.float32)],
        scratch_shapes=[pltpu.VMEM((rows, width), jnp.bfloat16), pltpu.SemaphoreType.DMA(())],
        compiler_params=pltpu.CompilerParams(vmem_limit_bytes=10 * MIB),
        cost_estimate=pl.CostEstimate(flops=8 * rows * width, bytes_accessed=8 * rows * groups, transcendentals=0),
        name="spread_bounds",
    )(in_vmem(sum_exps.T), in_vmem(out_exps.T), in_hbm(tokens))


def clip(value, bound):
    return jnp.minimum(jnp.maximum(value.astype(jnp.bfloat16), -bound), bound)


def own_kernel(a_ref, w_ref, sum_ref, out_ref):
    rows, width = out_ref.shape
    tile = rows // 2
    for at in range(0, width, HD):
        cols = slice(at, at + HD)
        for start in range(0, rows, tile):
            span = slice(start, start + tile)
            term = jnp.dot(a_ref[span, :], w_ref[:, cols], preferred_element_type=jnp.float32)
            out_ref[span, cols] = clip(term, sum_ref[span, cols])


def project_own(attended, w_out, sum_bound):
    rows, depth = attended.shape
    width = w_out.shape[1]
    vmem = pl.BlockSpec(memory_space=pltpu.VMEM)
    return pl.pallas_call(
        own_kernel,
        in_specs=[vmem] * 3,
        out_specs=vmem,
        out_shape=pltpu.VMEM((rows, width), jnp.bfloat16),
        compiler_params=pltpu.CompilerParams(vmem_limit_bytes=8 * MIB),
        cost_estimate=pl.CostEstimate(
            flops=2 * rows * width * depth, bytes_accessed=4 * rows * width + 2 * width * depth, transcendentals=0
        ),
        name="project_own",
    )(in_vmem(attended), in_vmem(w_out), in_vmem(sum_bound))


def output_kernel(b_ref, wb_ref, quant_ref, x_ref, sum_ref, last_ref, out_ref, staged, sems):
    rows, width = x_ref.shape
    tile = rows // 2

    def copy(index):
        span = slice(index * HD, (index + 1) * HD)
        return pltpu.make_async_copy(staged.at[:, span], out_ref.at[:, span], sems.at[index])

    for index in range(width // HD):
        cols = slice(index * HD, (index + 1) * HD)
        for start in range(0, rows, tile):
            span = slice(start, start + tile)
            term = jnp.dot(b_ref[span, :], wb_ref[:, cols], preferred_element_type=jnp.float32)
            quant = clip(term, sum_ref[span, cols]).astype(jnp.float32) + quant_ref[span, cols].astype(jnp.float32)
            staged[span, cols] = clip(x_ref[span, cols] + quant, last_ref[span, cols])
        copy(index).start()
    for index in range(width // HD):
        copy(index).wait()


def project_out(att_other, w_other, quant_own, sum_bound, out_bound, tokens):
    rows, width = tokens.shape
    depth = att_other.shape[1]
    pieces = width // HD
    vmem = pl.BlockSpec(memory_space=pltpu.VMEM)
    operands = [att_other, w_other, quant_own, tokens, sum_bound, out_bound]
    return pl.pallas_call(
        output_kernel,
        in_specs=[vmem] * len(operands),
        out_specs=pl.BlockSpec(memory_space=pltpu.HBM),
        out_shape=jax.ShapeDtypeStruct((rows, width), jnp.bfloat16),
        scratch_shapes=[pltpu.VMEM((rows, width), jnp.bfloat16), pltpu.SemaphoreType.DMA((pieces,))],
        compiler_params=pltpu.CompilerParams(vmem_limit_bytes=10 * MIB),
        cost_estimate=pl.CostEstimate(
            flops=2 * rows * width * depth, bytes_accessed=4 * rows * width + 2 * width * depth, transcendentals=0
        ),
        name="project_out",
    )(*[in_vmem(operand) for operand in operands])


def on_device(seq_size, tokens, gain, segments, w_query, w_keyval, w_out, sum_exps, out_exps):
    window = seq_size // 2

    def swap_cores(x):
        return lax.ppermute(x, "tp", [(0, 1), (1, 0)])

    def shift(x, step, first):
        cycle = seq_size - first
        pairs = []
        for i in range(seq_size):
            for core in range(2):
                after = 2 * (first + (i - first + step) % cycle) + core if i >= first else 2 * i + 1 - core
                pairs.append((2 * i + core, after))
        return lax.ppermute(x, ("seq", "tp"), pairs)

    w_other = swap_cores(w_out)
    message, normed, w_near = norm_kv(tokens, gain, w_keyval, segments, w_query)
    query = project_query(normed, w_near)
    held, query = lax.optimization_barrier((shift(message, 2, 0), query))
    odd = lax.rem(lax.axis_index("seq"), 2) == 1
    beside = lax.ppermute(jnp.where(odd, held, message), "seq", [(i, i ^ 1) for i in range(seq_size)])
    parts = [[(0, message), (2, held)]]
    for back in range(2, window, 2):
        step = shift(held, 1, back)
        held = shift(held, 2, back)
        parts.append([(back + 1, step)] + ([(back + 2, held)] if back + 2 < window else []))
    parts.append([(window, held), (1, beside)])
    exps = lax.optimization_barrier((sum_exps, out_exps, query))[:2]
    bounds = spread_bounds(*exps, tokens)
    state = None
    for number, blocks in enumerate(parts):
        plan = [(back, back == window) for back, _ in blocks]
        mine = [block for _, block in blocks]
        if number == 1:
            bounds, state = early = lax.optimization_barrier((bounds, state))
        if number > 0:
            mine = [lax.optimization_barrier((block, early))[0] for block in mine]
        other = []
        for block in mine:
            if number == len(parts) - 1 and other:
                block = lax.optimization_barrier((block, other[-1]))[0]
            other.append(swap_cores(block))
        state = attend(query, segments, plan, mine, other, state, number == len(parts) - 1)
    quant_own = project_own(state, w_out, bounds[0])
    return project_out(swap_cores(state), w_other, quant_own, *bounds)


def solution(mesh):
    in_specs = (
        P(("groups", "seq"), None),
        P(),
        P(("groups", "seq")),
        P(None, "tp"),
        P(None, "tp"),
        P("tp", None),
        P(("groups", "seq"), None),
        P(("groups", "seq"), None),
    )
    out_specs = P(("groups", "seq"), None)
    return jax.shard_map(
        functools.partial(on_device, mesh.shape["seq"]),
        mesh=mesh, in_specs=in_specs, out_specs=out_specs, check_vma=False,
    )
```

```python
import functools

import jax
import jax.numpy as jnp
from jax import lax
from jax.experimental import pallas as pl
from jax.experimental.pallas import tpu as pltpu
from jax.sharding import PartitionSpec as P

HD = 256
LANES = 128
SEG_ROWS = 16
LIMIT = 448.0
MIN_EXP = -9
NEG = -1e30
MIB = 1024 * 1024
NT = (((1,), (1,)), ((), ()))
FACTOR = HD ** (-0.5) * 1.4426950408889634


def norm_kv_kernel(x_ref, gain_hbm, w_ref, seg_hbm, next_ref, msg_ref, normed_ref, near_ref, xs, ws, gain_ref, seg_ref, sems):
    rows, width = xs.shape
    tile, part = rows // 2, rows // 4

    def cut(source, target, first, count, pieces, sem):
        size = count // pieces
        return [
            pltpu.make_async_copy(
                source.at[pl.ds(first + i * size, size)], target.at[pl.ds(first + i * size, size)], sems.at[sem + i]
            )
            for i in range(pieces)
        ]

    def early_tokens(half):
        return cut(x_ref, xs, half * part, part, 4, 4 * half)

    def late_tokens():
        return cut(x_ref, xs, tile, tile, 2, 8)

    def weights():
        return cut(w_ref, ws, 0, width, 4, 10)

    def gain_copy():
        return pltpu.make_async_copy(gain_hbm, gain_ref, sems.at[14])

    def segments_copy():
        return pltpu.make_async_copy(seg_hbm, seg_ref, sems.at[15])

    def next_copy():
        return pltpu.make_async_copy(next_ref, near_ref, sems.at[16])

    for copy in early_tokens(0) + early_tokens(1) + [gain_copy()] + weights() + late_tokens() + [segments_copy()]:
        copy.start()

    def wide(first, count, start):
        return xs[first:first + count, start:start + LANES].astype(jnp.float32)

    def stats(first):
        total = wide(first, part, 0)
        for start in range(LANES, width, LANES):
            total = total + wide(first, part, start)
        mean = jnp.broadcast_to(jnp.sum(total, axis=1, keepdims=True) * (1.0 / width), (part, LANES))
        square = jnp.zeros((part, LANES), jnp.float32)
        for start in range(0, width, LANES):
            center = wide(first, part, start) - mean
            square = square + center * center
        spread = jnp.sum(square, axis=1, keepdims=True) * (1.0 / width)
        return mean, jnp.broadcast_to(lax.rsqrt(spread + 1e-05), (part, LANES))

    def project(first, halves):
        mean = jnp.concatenate([h[0] for h in halves], axis=0)
        scale = jnp.concatenate([h[1] for h in halves], axis=0)
        kv = jnp.zeros((tile, ws.shape[1]), jnp.float32)
        span = slice(first, first + tile)
        for start in range(0, width, HD):
            for at in (start, start + LANES):
                normed = (wide(first, tile, at) - mean) * scale * gain_ref[:, at:at + LANES]
                normed_ref[span, at:at + LANES] = normed.astype(jnp.bfloat16)
            kv = kv + jnp.dot(
                normed_ref[span, start:start + HD], ws[start:start + HD, :], preferred_element_type=jnp.float32
            )
        msg_ref[span, :] = kv.astype(jnp.bfloat16)

    halves = []
    for half in range(2):
        for copy in early_tokens(half):
            copy.wait()
        halves.append(stats(half * part))
    for copy in [gain_copy()] + weights():
        copy.wait()
    next_copy().start()
    project(0, halves)
    for copy in late_tokens():
        copy.wait()
    project(tile, [stats(tile), stats(tile + part)])
    segments_copy().wait()
    seg = seg_ref[...].astype(jnp.float32)
    low = jnp.broadcast_to(seg[:, :HD], (8, HD))
    high = jnp.broadcast_to(seg[:, HD:], (8, HD))
    msg_ref[rows:, :] = jnp.concatenate([low, high], axis=0).astype(jnp.bfloat16)
    next_copy().wait()


def in_hbm(x):
    return pltpu.with_memory_space_constraint(x, pltpu.HBM)


def in_vmem(x):
    return pltpu.with_memory_space_constraint(x, pltpu.VMEM)


def norm_kv(tokens, gain, w_keyval, segments, w_next):
    rows, width = tokens.shape
    cols = w_keyval.shape[1]
    vmem, hbm = pl.BlockSpec(memory_space=pltpu.VMEM), pl.BlockSpec(memory_space=pltpu.HBM)
    return pl.pallas_call(
        norm_kv_kernel,
        in_specs=[hbm] * 5,
        out_specs=[vmem] * 3,
        out_shape=[
            pltpu.VMEM((rows + SEG_ROWS, cols), jnp.bfloat16),
            pltpu.VMEM((rows, width), jnp.bfloat16),
            pltpu.VMEM(w_next.shape, w_next.dtype),
        ],
        scratch_shapes=[
            pltpu.VMEM((rows, width), jnp.bfloat16),
            pltpu.VMEM((width, cols), jnp.bfloat16),
            pltpu.VMEM((1, width), jnp.float32),
            pltpu.VMEM((1, rows), jnp.int32),
            pltpu.SemaphoreType.DMA((17,)),
        ],
        compiler_params=pltpu.CompilerParams(vmem_limit_bytes=24 * MIB),
        cost_estimate=pl.CostEstimate(
            flops=2 * rows * width * cols, bytes_accessed=4 * rows * width + 2 * width * cols, transcendentals=0
        ),
        name="norm_kv",
    )(*[in_hbm(x) for x in (tokens, gain.reshape(1, width), w_keyval, segments.reshape(1, rows), w_next)])


def query_kernel(x_ref, w_ref, out_ref):
    out_ref[...] = jnp.dot(x_ref[...], w_ref[...], preferred_element_type=jnp.float32).astype(jnp.bfloat16)


def project_query(normed, w_query):
    rows, width = normed.shape
    cols = w_query.shape[1]
    vmem = pl.BlockSpec(memory_space=pltpu.VMEM)
    return pl.pallas_call(
        query_kernel,
        in_specs=[vmem, vmem],
        out_specs=vmem,
        out_shape=pltpu.VMEM((rows, cols), jnp.bfloat16),
        compiler_params=pltpu.CompilerParams(vmem_limit_bytes=8 * MIB),
        cost_estimate=pl.CostEstimate(
            flops=2 * rows * width * cols, bytes_accessed=2 * rows * width + 2 * width * cols, transcendentals=0
        ),
        name="project_query",
    )(in_vmem(normed), in_vmem(w_query))


def attend_kernel(plan, first, last, *refs):
    blocks = len(plan)
    q_ref, seg_ref = refs[:2]
    mine, other = refs[2:2 + blocks], refs[2 + blocks:2 + 2 * blocks]
    refs = refs[2 + 2 * blocks:]
    state_ref = None
    if not first:
        state_ref, refs = refs[0], refs[1:]
    out_ref, scores = refs
    rows = q_ref.shape[0]
    tile = rows // 2
    part = lax.axis_index("tp")
    place = lax.axis_index("seq")

    def finish(span, weighted, total):
        inverse = jnp.broadcast_to(1.0 / jnp.sum(total, axis=1, keepdims=True), total.shape)
        out_ref[span, :] = (weighted * jnp.concatenate([inverse, inverse], axis=1)).astype(jnp.bfloat16)

    def update(slots, keys, values):
        if first:
            out_ref[:, HD + 2 * LANES:] = jnp.transpose(
                jnp.broadcast_to(seg_ref[...].astype(jnp.float32), (LANES, rows))
            )
        key_segs = {}
        for slot in slots:
            packed = mine[slot][rows:, :].astype(jnp.float32)
            key_segs[slot] = jnp.concatenate([packed[0:1, :], packed[8:9, :]], axis=1)
        for start in range(0, rows, tile):
            span = slice(start, start + tile)
            query = q_ref[span, :]
            own_seg = (out_ref if first else state_ref)[span, HD + 2 * LANES:]
            best = before = None if first else state_ref[span, HD:HD + LANES]
            bounds = {}
            for slot in slots:
                back, furthest = plan[slot]
                low, high = 0, rows
                if back == 0:
                    high = start + tile
                elif furthest:
                    low = start
                bounds[slot] = (low, high)
                raw = lax.dot_general(query, keys[slot][low:high, :], NT, preferred_element_type=jnp.float32)
                for at in range(low, high, LANES):
                    allowed = key_segs[slot][:, at:at + LANES] == own_seg
                    if back == 0:
                        row_pos = start + lax.broadcasted_iota(jnp.int32, allowed.shape, 0)
                        allowed = allowed & (at + lax.broadcasted_iota(jnp.int32, allowed.shape, 1) <= row_pos)
                    piece = jnp.where(allowed, raw[:, at - low:at - low + LANES], NEG)
                    scores[slot, :, at:at + LANES] = piece
                    best = piece if best is None else jnp.maximum(best, piece)
            top = jnp.broadcast_to(jnp.max(best, axis=1, keepdims=True), (tile, LANES))
            if first:
                total = jnp.zeros((tile, LANES), jnp.float32)
                weighted = jnp.zeros((tile, HD), jnp.float32)
            else:
                shrink = jnp.exp2((before - top) * FACTOR)
                total = state_ref[span, HD + LANES:HD + 2 * LANES] * shrink
                weighted = state_ref[span, :HD] * jnp.concatenate([shrink, shrink], axis=1)
            for slot in slots:
                low, high = bounds[slot]
                pieces = []
                for at in range(low, high, LANES):
                    weights = jnp.exp2((scores[slot, :, at:at + LANES] - top) * FACTOR)
                    total = total + weights
                    pieces.append(weights.astype(jnp.bfloat16))
                probs = jnp.concatenate(pieces, axis=1)
                weighted = weighted + jnp.dot(probs, values[slot][low:high, :], preferred_element_type=jnp.float32)
            if last:
                finish(span, weighted, total)
            else:
                out_ref[span, :HD] = weighted
                out_ref[span, HD:HD + LANES] = top
                out_ref[span, HD + LANES:HD + 2 * LANES] = total

    order = sorted(range(blocks), key=lambda slot: plan[slot][0])
    for count in range(1 if first else 0, blocks + 1):
        reached = place >= (plan[order[count - 1]][0] if count > 0 else 0)
        if count < blocks:
            reached = reached & (place < plan[order[count]][0])
        if count > 0:
            pl.when(reached & (part == 0))(functools.partial(update, order[:count], mine, other))
            pl.when(reached & (part == 1))(functools.partial(update, order[:count], other, mine))
        elif last:

            @pl.when(reached)
            def _():
                finish(slice(0, rows), state_ref[:, :HD], state_ref[:, HD + LANES:HD + 2 * LANES])


def attend(query, segments, plan, mine, other, state, last):
    rows = query.shape[0]
    blocks = len(plan)
    vmem = pl.BlockSpec(memory_space=pltpu.VMEM)
    first = state is None
    operands = [query, segments.reshape(1, rows), *mine, *other] + ([] if first else [state])
    return pl.pallas_call(
        functools.partial(attend_kernel, plan, first, last),
        in_specs=[vmem] * len(operands),
        out_specs=vmem,
        out_shape=pltpu.VMEM((rows, HD), jnp.bfloat16) if last else pltpu.VMEM((rows, HD + 3 * LANES), jnp.float32),
        scratch_shapes=[pltpu.VMEM((blocks, rows // 2, rows), jnp.float32)],
        input_output_aliases={} if first or last else {len(operands) - 1: 0},
        compiler_params=pltpu.CompilerParams(vmem_limit_bytes=12 * MIB),
        cost_estimate=pl.CostEstimate(
            flops=4 * rows * rows * blocks * HD, bytes_accessed=4 * rows * blocks * HD, transcendentals=rows * rows * blocks
        ),
        name="attend_last" if last else "attend_first" if first else "attend_more",
    )(*[in_vmem(operand) for operand in operands])


def bounds_kernel(sum_ref, out_exp_ref, x_ref, sum_bound_ref, out_bound_ref, wide_ref, near, sem):
    groups, rows = sum_ref.shape
    fetch = pltpu.make_async_copy(x_ref, near, sem)
    fetch.start()
    per = sum_bound_ref.shape[1] // groups
    for exps, bound_ref in ((sum_ref, sum_bound_ref), (out_exp_ref, out_bound_ref)):
        power = jnp.left_shift(jnp.int32(1), exps[...] - MIN_EXP).astype(jnp.float32)
        bound = jnp.transpose(power * (LIMIT * 2.0 ** MIN_EXP))
        for group in range(groups):
            wide = jnp.broadcast_to(bound[:, group:group + 1], (rows, per)).astype(jnp.bfloat16)
            bound_ref[:, group * per:(group + 1) * per] = wide
    fetch.wait()

    def widen(step, carry):
        span = pl.ds(pl.multiple_of(step * 64, 64), 64)
        wide_ref[span, :] = near[span, :].astype(jnp.float32)
        return carry

    lax.fori_loop(0, rows // 64, widen, 0)


def spread_bounds(sum_exps, out_exps, tokens):
    rows, width = tokens.shape
    groups = sum_exps.shape[1]
    vmem = pl.BlockSpec(memory_space=pltpu.VMEM)
    return pl.pallas_call(
        bounds_kernel,
        in_specs=[vmem, vmem, pl.BlockSpec(memory_space=pltpu.HBM)],
        out_specs=[vmem] * 3,
        out_shape=[pltpu.VMEM((rows, width), jnp.bfloat16)] * 2 + [pltpu.VMEM((rows, width), jnp.float32)],
        scratch_shapes=[pltpu.VMEM((rows, width), jnp.bfloat16), pltpu.SemaphoreType.DMA(())],
        compiler_params=pltpu.CompilerParams(vmem_limit_bytes=10 * MIB),
        cost_estimate=pl.CostEstimate(flops=8 * rows * width, bytes_accessed=8 * rows * groups, transcendentals=0),
        name="spread_bounds",
    )(in_vmem(sum_exps.T), in_vmem(out_exps.T), in_hbm(tokens))


def clip(value, bound):
    return jnp.minimum(jnp.maximum(value.astype(jnp.bfloat16), -bound), bound)


def own_kernel(a_ref, w_ref, sum_ref, out_ref):
    rows, width = out_ref.shape
    tile = rows // 2
    for at in range(0, width, HD):
        cols = slice(at, at + HD)
        for start in range(0, rows, tile):
            span = slice(start, start + tile)
            term = jnp.dot(a_ref[span, :], w_ref[:, cols], preferred_element_type=jnp.float32)
            out_ref[span, cols] = clip(term, sum_ref[span, cols])


def project_own(attended, w_out, sum_bound):
    rows, depth = attended.shape
    width = w_out.shape[1]
    vmem = pl.BlockSpec(memory_space=pltpu.VMEM)
    return pl.pallas_call(
        own_kernel,
        in_specs=[vmem] * 3,
        out_specs=vmem,
        out_shape=pltpu.VMEM((rows, width), jnp.bfloat16),
        compiler_params=pltpu.CompilerParams(vmem_limit_bytes=8 * MIB),
        cost_estimate=pl.CostEstimate(
            flops=2 * rows * width * depth, bytes_accessed=4 * rows * width + 2 * width * depth, transcendentals=0
        ),
        name="project_own",
    )(in_vmem(attended), in_vmem(w_out), in_vmem(sum_bound))


def output_kernel(b_ref, wb_ref, quant_ref, x_ref, sum_ref, last_ref, out_ref, staged, sems):
    rows, width = x_ref.shape
    tile = rows // 2

    def copy(index):
        span = slice(index * HD, (index + 1) * HD)
        return pltpu.make_async_copy(staged.at[:, span], out_ref.at[:, span], sems.at[index])

    for index in range(width // HD):
        cols = slice(index * HD, (index + 1) * HD)
        for start in range(0, rows, tile):
            span = slice(start, start + tile)
            term = jnp.dot(b_ref[span, :], wb_ref[:, cols], preferred_element_type=jnp.float32)
            quant = clip(term, sum_ref[span, cols]).astype(jnp.float32) + quant_ref[span, cols].astype(jnp.float32)
            staged[span, cols] = clip(x_ref[span, cols] + quant, last_ref[span, cols])
        copy(index).start()
    for index in range(width // HD):
        copy(index).wait()


def project_out(att_other, w_other, quant_own, sum_bound, out_bound, tokens):
    rows, width = tokens.shape
    depth = att_other.shape[1]
    pieces = width // HD
    vmem = pl.BlockSpec(memory_space=pltpu.VMEM)
    operands = [att_other, w_other, quant_own, tokens, sum_bound, out_bound]
    return pl.pallas_call(
        output_kernel,
        in_specs=[vmem] * len(operands),
        out_specs=pl.BlockSpec(memory_space=pltpu.HBM),
        out_shape=jax.ShapeDtypeStruct((rows, width), jnp.bfloat16),
        scratch_shapes=[pltpu.VMEM((rows, width), jnp.bfloat16), pltpu.SemaphoreType.DMA((pieces,))],
        compiler_params=pltpu.CompilerParams(vmem_limit_bytes=10 * MIB),
        cost_estimate=pl.CostEstimate(
            flops=2 * rows * width * depth, bytes_accessed=4 * rows * width + 2 * width * depth, transcendentals=0
        ),
        name="project_out",
    )(*[in_vmem(operand) for operand in operands])


def on_device(seq_size, tokens, gain, segments, w_query, w_keyval, w_out, sum_exps, out_exps):
    window = seq_size // 2

    def swap_cores(x):
        return lax.ppermute(x, "tp", [(0, 1), (1, 0)])

    def shift(x, step, first):
        cycle = seq_size - first
        pairs = []
        for i in range(seq_size):
            for core in range(2):
                after = 2 * (first + (i - first + step) % cycle) + core if i >= first else 2 * i + 1 - core
                pairs.append((2 * i + core, after))
        return lax.ppermute(x, ("seq", "tp"), pairs)

    w_other = swap_cores(w_out)
    message, normed, w_near = norm_kv(tokens, gain, w_keyval, segments, w_query)
    query = project_query(normed, w_near)
    held, query = lax.optimization_barrier((shift(message, 2, 0), query))
    odd = lax.rem(lax.axis_index("seq"), 2) == 1
    beside = lax.ppermute(jnp.where(odd, held, message), "seq", [(i, i ^ 1) for i in range(seq_size)])
    parts = [[(0, message), (2, held)]]
    for back in range(2, window, 2):
        step = shift(held, 1, 0)
        held = shift(held, 2, back)
        parts.append([(back + 1, step)] + ([(back + 2, held)] if back + 2 < window else []))
    parts.append([(window, held), (1, beside)])
    exps = lax.optimization_barrier((sum_exps, out_exps, query))[:2]
    bounds = spread_bounds(*exps, tokens)
    state = None
    for number, blocks in enumerate(parts):
        plan = [(back, back == window) for back, _ in blocks]
        mine = [block for _, block in blocks]
        if number == 1:
            bounds, state = early = lax.optimization_barrier((bounds, state))
        if number > 0:
            mine = [lax.optimization_barrier((block, early))[0] for block in mine]
        other = [swap_cores(m) for m in mine]
        state = attend(query, segments, plan, mine, other, state, number == len(parts) - 1)
    quant_own = project_own(state, w_out, bounds[0])
    return project_out(swap_cores(state), w_other, quant_own, *bounds)


def solution(mesh):
    in_specs = (
        P(("groups", "seq"), None),
        P(),
        P(("groups", "seq")),
        P(None, "tp"),
        P(None, "tp"),
        P("tp", None),
        P(("groups", "seq"), None),
        P(("groups", "seq"), None),
    )
    out_specs = P(("groups", "seq"), None)
    return jax.shard_map(
        functools.partial(on_device, mesh.shape["seq"]),
        mesh=mesh, in_specs=in_specs, out_specs=out_specs, check_vma=False,
    )
```
